32 devices in a mesh: face: 2 (over x), px: 4 (over y, core), py: 4 (over z).
Axes of the slice: x: 2, y: 2, z: 4, core: 2. Of those that a mesh axis runs over, the one named last changes fastest.
Arguments:
- tracer_mass: float32 [40, 128, 512], P(None, ('face', 'px'), 'py'), may hold values from -6 to 6
- recon_table: float32 [10, 25], replicated, may hold values from -1.25 to 1.25
- intersection_weights: float32 [4, 10, 128, 512], P(None, None, ('face', 'px'), 'py'), may hold values from -1 to 1
- intersection_cells: int32 [4, 128, 512], P(None, ('face', 'px'), 'py'), may hold values from 0 to 8
- rotation_codes: int32 [4, 128, 512], P(None, ('face', 'px'), 'py'), may hold values from 0 to 3
Outputs:
- advected: float32 [40, 128, 512], P(None, ('face', 'px'), 'py')
The draws below stay inside these ranges and needn't reach their ends.
Inputs may be any that keep to these rules, and one draw needn't show every extreme that they name: `intersection_cells`: the index of the 3 x 3 neighbour, row-major from offset (-1, -1). `rotation_codes`: a count of quarter turns.
All inputs are finite; a program needn't handle non-finite values.
Results may differ from the reference program's by a relative error of at most 0.0001.
Values sent between devices are 32-bit elements; how exact they have to be, the bound alone decides.
No kernel may reach another device: no remote copies, remote signals or barrier semaphores. Data moves between devices by JAX's collectives and lax.ppermute only.
A program may use at most 256 MiB of HBM per device.

```python
import jax
import jax.numpy as jnp
import numpy as np
from jax import lax

TRACERS = 20
LEV = 2
OVL = 4
TERMS = 10
TAPS = 25
STEPS = 2
STACKS = 40
NX = 128
NY = 512


def plant(entries, stream_key, low, top_value):
    index_at = [jax.random.randint(jax.random.fold_in(stream_key, axis), (), 0, length) for axis, length in enumerate(entries.shape)]
    widest = entries.shape.index(max(entries.shape))
    beside = index_at[:widest] + [(index_at[widest] + 1) % entries.shape[widest]] + index_at[widest + 1:]
    return entries.at[tuple(index_at)].set(low).at[tuple(beside)].set(top_value)


def steps_of(rng, shape, shards, smallest, largest):
    def one(axis_at, blocks):
        steps = jax.random.uniform(jax.random.fold_in(jax.random.fold_in(rng, 6), axis_at), (blocks,), jnp.float32, smallest / len(shards), largest / len(shards))
        return jnp.repeat(jnp.exp(steps), shape[axis_at] // blocks).reshape((-1,) + (1,) * (len(shape) - axis_at - 1))

    level = one(*shards[0])
    for cut in shards[1:]:
        level = level * one(*cut)
    return level


def gaussian(rng, dims, width, bound, pieces=(), kind=jnp.bfloat16):
    factor_of = steps_of(rng, dims, pieces, -0.22, 0.18) if pieces else 1.0
    values = jax.random.normal(rng, dims, jnp.float32) * width * factor_of
    return jnp.minimum(jnp.maximum(values, -bound), bound).astype(kind)


def setup_inputs(seed: int = 0) -> dict:
    key_of = jax.random.split(jax.random.key(seed), 6)
    tracer_mass = gaussian(key_of[0], (STACKS, NX, NY), 1.0, 6.0, ((1, 8), (2, 4)), jnp.float32)
    recon_table = gaussian(key_of[1], (TERMS, TAPS), TAPS ** -0.5, 1.25, (), jnp.float32)
    intersection_weights = gaussian(key_of[2], (OVL, TERMS, NX, NY), 0.16, 1.0, ((2, 8), (3, 4)), jnp.float32)
    intersection_cells = plant(jax.random.randint(key_of[3], (OVL, NX, NY), 0, 9), jax.random.fold_in(key_of[3], 1), 0, 8).astype(jnp.int32)
    rotation_codes = plant(jax.random.randint(key_of[4], (OVL, NX, NY), 0, 4), jax.random.fold_in(key_of[4], 1), 0, 3).astype(jnp.int32)
    return dict(tracer_mass=tracer_mass, recon_table=recon_table, intersection_weights=intersection_weights, intersection_cells=intersection_cells, rotation_codes=rotation_codes)


def rotation_tables():
    exponents = [(0, 0), (1, 0), (0, 1), (2, 0), (1, 1), (0, 2), (3, 0), (2, 1), (1, 2), (0, 3)]
    quarter = np.zeros((10, 10))
    for place, powers in enumerate(exponents):
        target = exponents.index((powers[1], powers[0]))
        quarter[target, place] = (-1.0) ** powers[1]
    tables = [np.eye(10)]
    for turn in range(3):
        tables.append(quarter @ tables[-1])
    return np.stack(tables)


def neighbour_weights(intersection_weights, intersection_cells, rotation_codes):
    tables = jnp.asarray(rotation_tables(), dtype=jnp.float32)
    rotated = jnp.zeros_like(intersection_weights)
    for turn in range(4):
        picked = (rotation_codes == turn).astype(jnp.float32)[:, None]
        turned = jnp.einsum("kl,mkxy->mlxy", tables[turn], intersection_weights, precision=lax.Precision.HIGHEST)
        rotated = rotated + picked * turned
    choose = (intersection_cells[:, None] == jnp.arange(9, dtype=jnp.int32)[None, :, None, None]).astype(jnp.float32)
    return jnp.einsum("mnxy,mlxy->nlxy", choose, rotated, precision=lax.Precision.HIGHEST)


def combine_stencil(weights, recon_table):
    parts = [jnp.zeros(weights.shape[2:], jnp.float32) for offset in range(49)]
    for near in range(9):
        spread = jnp.einsum("lxy,lj->jxy", weights[near], recon_table, precision=lax.Precision.HIGHEST)
        for tap in range(25):
            offset = (near // 3 + tap // 5) * 7 + near % 3 + tap % 5
            parts[offset] = parts[offset] + spread[tap]
    return jnp.stack(parts)


def reference(tracer_mass, recon_table, intersection_weights, intersection_cells, rotation_codes):
    stencil = combine_stencil(neighbour_weights(intersection_weights, intersection_cells, rotation_codes), recon_table)
    blocks = tracer_mass.reshape(LEV, TRACERS, NX, NY)

    def advance(block):
        for step in range(STEPS):
            padded = jnp.pad(block, ((0, 0), (3, 3), (3, 3)))
            total = jnp.zeros_like(block)
            for offset in range(49):
                shift_x = offset // 7
                shift_y = offset % 7
                total = total + stencil[offset][None] * padded[:, shift_x:shift_x + NX, shift_y:shift_y + NY]
            block = total
        return block

    return lax.map(advance, blocks).reshape(STACKS, NX, NY)
```

```python
import functools

import jax
import jax.numpy as jnp
from jax import lax
from jax.experimental import pallas as pl
from jax.experimental.pallas import tpu as pltpu
from jax.sharding import PartitionSpec as P

F32 = jnp.float32
SWAPPED = (0, 2, 1, 5, 4, 3, 9, 8, 7, 6)
POWERS = ((0, 0), (1, 0), (0, 1), (2, 0), (1, 1), (0, 2), (3, 0), (2, 1), (1, 2), (0, 3))
TERMS = 10
GROUP = 4
VMEM = pl.BlockSpec(memory_space=pltpu.VMEM)
SMEM = pl.BlockSpec(memory_space=pltpu.SMEM)
PARAMS = pltpu.CompilerParams(vmem_limit_bytes=40 * 1024 * 1024)


def swap(block, axes, odd_first):
    count = lax.axis_size(axes)
    pairs = []
    for low in range(1 if odd_first else 0, count - 1, 2):
        pairs += [(low, low + 1), (low + 1, low)]
    return lax.ppermute(block, axes, pairs)


def fill_stencil(recon, weights, cells, codes, turned, spread, stencil, tiles):
    zero = jnp.zeros((8, 128), F32)
    for g in range(tiles):
        rows = pl.ds(8 * g, 8)
        for m in range(4):
            code = codes[m, rows, :]
            odd = (code & 1) == 1
            sign_x = jnp.where(code >= 2, -1.0, 1.0).astype(F32)
            sign_y = jnp.where((code == 1) | (code == 2), -1.0, 1.0).astype(F32)
            sign_xy = sign_x * sign_y
            values = [weights[m, t, rows, :] for t in range(TERMS)]
            for t, (a, b) in enumerate(POWERS):
                value = values[t]
                if SWAPPED[t] != t:
                    value = jnp.where(odd, values[SWAPPED[t]], value)
                if a % 2 and b % 2:
                    value = value * sign_xy
                elif a % 2:
                    value = value * sign_x
                elif b % 2:
                    value = value * sign_y
                turned[t, m * tiles + g] = value

    combos = 4 * tiles

    def one_tap(tap, carry):
        total = [None] * combos
        for t in range(TERMS):
            scale = recon[t, tap]
            for c in range(combos):
                term = turned[t, c] * scale
                total[c] = term if t == 0 else total[c] + term
        for c in range(combos):
            spread[tap, c] = total[c]
        return carry

    lax.fori_loop(0, 25, one_tap, 0)

    for g in range(tiles):
        rows = pl.ds(8 * g, 8)
        masks = []
        for m in range(4):
            cell = cells[m, rows, :]
            first = jnp.where(cell < 3, 0, jnp.where(cell < 6, 3, 6))
            across = cell - first
            masks.append((cell < 3, cell < 6, across == 0, across <= 1))
        for ox in range(7):
            total = [None] * 7
            for m in range(4):
                low_x, mid_x, low_y, mid_y = masks[m]

                def tap(jx, jy):
                    if 0 <= jx < 5 and 0 <= jy < 5:
                        return spread[jx * 5 + jy, m * tiles + g]
                    return zero

                line = [
                    jnp.where(low_x, tap(ox, jy), jnp.where(mid_x, tap(ox - 1, jy), tap(ox - 2, jy)))
                    for jy in range(5)
                ]
                padded = [zero, zero] + line + [zero, zero]
                for oy in range(7):
                    value = jnp.where(
                        low_y, padded[oy + 2], jnp.where(mid_y, padded[oy + 1], padded[oy])
                    )
                    total[oy] = value if m == 0 else total[oy] + value
            for oy in range(7):
                stencil[ox * 7 + oy, rows, :] = total[oy]


def first_kernel(parity, recon, mass, weights, cells, codes, stencil, send_a, send_b, turned, spread):
    fill_stencil(recon, weights, cells, codes, turned, spread, stencil, 2)
    stacks, width = mass.shape[:2]
    even = parity[0] == 0
    for send, low_edge in ((send_a, jnp.logical_not(even)), (send_b, even)):
        mass_at = jnp.where(low_edge, 0, width - 6)
        stencil_at = jnp.where(low_edge, 0, width - 3)
        for s in range(stacks):
            send[6 * s : 6 * s + 6, :] = mass[s, pl.ds(mass_at, 6), :]
        for o in range(49):
            at = 6 * stacks + 3 * o
            send[at : at + 3, :] = stencil[o, pl.ds(stencil_at, 3), :]


def pack_columns(field, tiles, even, send_a, send_b):
    stacks = field.shape[0]
    lane = lax.broadcasted_iota(jnp.int32, (8, 128), 1)
    for tile in range(tiles):
        rows = pl.ds(8 * tile, 8)
        left = jnp.zeros((8, 128), F32)
        right = jnp.zeros((8, 128), F32)
        for s in range(stacks):
            here = (lane >= 3 * s) & (lane < 3 * s + 3)
            value = field[s, rows, :]
            left = jnp.where(here, pltpu.roll(value, (3 * s) % 128, 1), left)
            right = jnp.where(here, pltpu.roll(value, (3 * s - 125) % 128, 1), right)
        send_a[rows, :] = jnp.where(even, right, left)
        send_b[rows, :] = jnp.where(even, left, right)


def second_kernel(parity, mass, stencil, got_a, got_b, field, wide, send_a, send_b):
    stacks, width = mass.shape[:2]
    even = parity[0] == 0

    def place(above, below):
        for s in range(stacks):
            field[s, 0:6, :] = above[6 * s : 6 * s + 6, :]
            field[s, width + 6 : width + 12, :] = below[6 * s : 6 * s + 6, :]
        for o in range(49):
            at = 6 * stacks + 3 * o
            wide[o, 0:3, :] = above[at : at + 3, :]
            wide[o, width + 3 : width + 6, :] = below[at : at + 3, :]

    @pl.when(even)
    def _():
        place(got_b, got_a)

    @pl.when(jnp.logical_not(even))
    def _():
        place(got_a, got_b)

    for s in range(stacks):
        field[s, 6 : width + 6, :] = mass[s, :, :]
        field[s, width + 12 : width + 16, :] = jnp.zeros((4, 128), F32)
    for o in range(49):
        wide[o, 3 : width + 3, :] = stencil[o, :, :]
        wide[o, width + 6 : width + 8, :] = jnp.zeros((2, 128), F32)
    pack_columns(field, 4, parity[1] == 0, send_a, send_b)


def apply_stencil(even, field, stencil, got_a, got_b, out, shifted, in_tiles, out_tiles):
    stacks = field.shape[0]
    lane = lax.broadcasted_iota(jnp.int32, (8, 128), 1)

    def some_stacks(group, carry):
        for k in range(GROUP):
            s = group * GROUP + k
            for tile in range(in_tiles):
                rows = pl.ds(8 * tile, 8)
                one, two = got_a[rows, :], got_b[rows, :]
                after = jnp.where(even, one, two)
                before = jnp.where(even, two, one)
                halo = jnp.where(
                    lane < 64,
                    pltpu.roll(after, lax.rem(128 - 3 * s, 128), 1),
                    pltpu.roll(before, 125 - 3 * s, 1),
                )
                value = field[s, rows, :]
                for dy in range(-3, 4):
                    if dy > 0:
                        moved = pltpu.roll(jnp.where(lane < dy, halo, value), 128 - dy, 1)
                    elif dy < 0:
                        moved = pltpu.roll(jnp.where(lane >= 128 + dy, halo, value), -dy, 1)
                    else:
                        moved = value
                    shifted[k, dy + 3, rows, :] = moved
        for tile in range(out_tiles):
            total = [None] * GROUP
            for dy in range(7):
                for dx in range(7):
                    scale = stencil[dx * 7 + dy, 8 * tile : 8 * tile + 8, :]
                    for k in range(GROUP):
                        at = 8 * tile + dx
                        term = scale * shifted[k, dy, at : at + 8, :]
                        total[k] = term if total[k] is None else total[k] + term
            for k in range(GROUP):
                out[group * GROUP + k, 8 * tile : 8 * tile + 8, :] = total[k]
        return carry

    lax.fori_loop(0, stacks // GROUP, some_stacks, 0)


def third_kernel(parity, field, wide, got_a, got_b, out, send_a, send_b, shifted):
    even = parity[1] == 0
    apply_stencil(even, field, wide, got_a, got_b, out, shifted, 4, 3)
    pack_columns(out, 3, even, send_a, send_b)


def fourth_kernel(parity, field, stencil, got_a, got_b, out, shifted):
    apply_stencil(parity[1] == 0, field, stencil, got_a, got_b, out, shifted, 3, 2)


def local(tracer_mass, recon_table, intersection_weights, intersection_cells, rotation_codes):
    stacks, width_x, width_y = tracer_mass.shape
    row_axes, column_axes = ("face", "px"), "py"
    shape = lambda *sizes: jax.ShapeDtypeStruct(sizes, F32)
    parity = jnp.stack([lax.axis_index(row_axes) % 2, lax.axis_index(column_axes) % 2]).astype(jnp.int32)
    edge = -(-(6 * stacks + 3 * 49) // 8) * 8

    stencil, send_a, send_b = pl.pallas_call(
        first_kernel,
        out_shape=(shape(49, width_x, 128), shape(edge, 128), shape(edge, 128)),
        in_specs=[SMEM, SMEM, VMEM, VMEM, VMEM, VMEM],
        out_specs=(VMEM, VMEM, VMEM),
        scratch_shapes=[pltpu.VMEM((TERMS, 8, 8, 128), F32), pltpu.VMEM((25, 8, 8, 128), F32)],
        compiler_params=PARAMS,
        name="coefficients",
    )(parity, recon_table, tracer_mass, intersection_weights, intersection_cells, rotation_codes)
    got_a = swap(send_a, row_axes, False)
    got_b = swap(send_b, row_axes, True)

    field, wide, send_a, send_b = pl.pallas_call(
        second_kernel,
        out_shape=(shape(stacks, 32, 128), shape(49, 24, 128), shape(32, 128), shape(32, 128)),
        in_specs=[SMEM, VMEM, VMEM, VMEM, VMEM],
        out_specs=(VMEM,) * 4,
        compiler_params=PARAMS,
        name="assemble",
    )(parity, tracer_mass, stencil, got_a, got_b)
    got_a = swap(send_a, column_axes, False)
    got_b = swap(send_b, column_axes, True)

    field, send_a, send_b = pl.pallas_call(
        third_kernel,
        out_shape=(shape(stacks, 24, 128), shape(24, 128), shape(24, 128)),
        in_specs=[SMEM, VMEM, VMEM, VMEM, VMEM],
        out_specs=(VMEM,) * 3,
        scratch_shapes=[pltpu.VMEM((GROUP, 7, 32, 128), F32)],
        compiler_params=PARAMS,
        name="step_one",
    )(parity, field, wide, got_a, got_b)
    got_a = swap(send_a, column_axes, False)
    got_b = swap(send_b, column_axes, True)

    return pl.pallas_call(
        fourth_kernel,
        out_shape=shape(stacks, width_x, 128),
        in_specs=[SMEM, VMEM, VMEM, VMEM, VMEM],
        out_specs=VMEM,
        scratch_shapes=[pltpu.VMEM((GROUP, 7, 24, 128), F32)],
        compiler_params=PARAMS,
        name="step_two",
    )(parity, field, stencil, got_a, got_b)


def solution(mesh):
    in_specs = (
        P(None, ("face", "px"), "py"),
        P(),
        P(None, None, ("face", "px"), "py"),
        P(None, ("face", "px"), "py"),
        P(None, ("face", "px"), "py"),
    )
    out_specs = P(None, ("face", "px"), "py")
    return jax.shard_map(local, mesh=mesh, in_specs=in_specs, out_specs=out_specs, check_vma=False)
```

```python
import functools

import jax
import jax.numpy as jnp
from jax import lax
from jax.experimental import pallas as pl
from jax.experimental.pallas import tpu as pltpu
from jax.sharding import PartitionSpec as P

F32 = jnp.float32
ROW_AXES = ("face", "px")
COLUMN_AXES = "py"
SWAPPED = (0, 2, 1, 5, 4, 3, 9, 8, 7, 6)
POWERS = ((0, 0), (1, 0), (0, 1), (2, 0), (1, 1), (0, 2), (3, 0), (2, 1), (1, 2), (0, 3))
TERMS = 10
GROUP = 4
VMEM = pl.BlockSpec(memory_space=pltpu.VMEM)
HBM = pl.BlockSpec(memory_space=pltpu.HBM)
PARAMS = pltpu.CompilerParams(vmem_limit_bytes=40 * 1024 * 1024)


def swap(block, axes, odd_first):
    count = lax.axis_size(axes)
    partner = list(range(count))
    for low in range(1 if odd_first else 0, count - 1, 2):
        partner[low], partner[low + 1] = low + 1, low
    pairs = list(enumerate(partner))
    return lax.ppermute(block, axes, pairs)


def position(axes):
    index = lax.axis_index(axes)
    return lax.rem(index, 2) == 0, index == 0, index == lax.axis_size(axes) - 1


def fill_stencil(recon, weights, cells, codes, turned, spread, stencil, tiles):
    zero = jnp.zeros((8, 128), F32)
    for g in range(tiles):
        rows = pl.ds(8 * g, 8)
        for m in range(4):
            code = codes[m, rows, :]
            odd = (code & 1) == 1
            sign_x = jnp.where(code >= 2, -1.0, 1.0).astype(F32)
            sign_y = jnp.where((code == 1) | (code == 2), -1.0, 1.0).astype(F32)
            sign_xy = sign_x * sign_y
            values = [weights[m, t, rows, :] for t in range(TERMS)]
            for t, (a, b) in enumerate(POWERS):
                value = values[t]
                if SWAPPED[t] != t:
                    value = jnp.where(odd, values[SWAPPED[t]], value)
                if a % 2 and b % 2:
                    value = value * sign_xy
                elif a % 2:
                    value = value * sign_x
                elif b % 2:
                    value = value * sign_y
                turned[t, m * tiles + g] = value

    combos = 4 * tiles

    def one_tap(tap, carry):
        total = [None] * combos
        for t in range(TERMS):
            scale = recon[t, tap]
            for c in range(combos):
                term = turned[t, c] * scale
                total[c] = term if t == 0 else total[c] + term
        for c in range(combos):
            spread[tap, c] = total[c]
        return carry

    lax.fori_loop(0, 25, one_tap, 0)

    for g in range(tiles):
        rows = pl.ds(8 * g, 8)
        masks = []
        for m in range(4):
            cell = cells[m, rows, :]
            first = jnp.where(cell < 3, 0, jnp.where(cell < 6, 3, 6))
            across = cell - first
            masks.append((cell < 3, cell < 6, across == 0, across <= 1))
        for ox in range(7):
            total = [None] * 7
            for m in range(4):
                low_x, mid_x, low_y, mid_y = masks[m]

                def tap(jx, jy):
                    if 0 <= jx < 5 and 0 <= jy < 5:
                        return spread[jx * 5 + jy, m * tiles + g]
                    return zero

                line = [
                    jnp.where(low_x, tap(ox, jy), jnp.where(mid_x, tap(ox - 1, jy), tap(ox - 2, jy)))
                    for jy in range(5)
                ]
                padded = [zero, zero] + line + [zero, zero]
                for oy in range(7):
                    value = jnp.where(
                        low_y, padded[oy + 2], jnp.where(mid_y, padded[oy + 1], padded[oy])
                    )
                    total[oy] = value if m == 0 else total[oy] + value
            for oy in range(7):
                stencil[ox * 7 + oy, rows, :] = total[oy]


def first_kernel(
    recon_hbm, mass_hbm, weights_hbm, cells_hbm, codes_hbm, mass, stencil, send_a, send_b,
    recon, weights, cells, codes, turned, spread, sems,
):
    sources = (recon_hbm, codes_hbm, weights_hbm, cells_hbm, mass_hbm)
    targets = (recon, codes, weights, cells, mass)
    copies = [pltpu.make_async_copy(a, b, sems.at[i]) for i, (a, b) in enumerate(zip(sources, targets))]
    for copy in copies:
        copy.start()
    for copy in copies:
        copy.wait()
    fill_stencil(recon, weights, cells, codes, turned, spread, stencil, 2)
    stacks, width = mass.shape[:2]
    even = position(ROW_AXES)[0]
    for send, low_edge in ((send_a, jnp.logical_not(even)), (send_b, even)):
        mass_at = jnp.where(low_edge, 0, width - 6)
        stencil_at = jnp.where(low_edge, 0, width - 3)
        for s in range(stacks):
            send[6 * s : 6 * s + 6, :] = mass[s, pl.ds(mass_at, 6), :]
        for o in range(49):
            at = 6 * stacks + 3 * o
            send[at : at + 3, :] = stencil[o, pl.ds(stencil_at, 3), :]


def pack_columns(field, tiles, send_a, send_b):
    stacks = field.shape[0]
    even = position(COLUMN_AXES)[0]
    lane = lax.broadcasted_iota(jnp.int32, (8, 128), 1)
    for tile in range(tiles):
        rows = pl.ds(8 * tile, 8)
        left = jnp.zeros((8, 128), F32)
        right = jnp.zeros((8, 128), F32)
        for s in range(stacks):
            here = (lane >= 3 * s) & (lane < 3 * s + 3)
            value = field[s, rows, :]
            left = jnp.where(here, pltpu.roll(value, (3 * s) % 128, 1), left)
            right = jnp.where(here, pltpu.roll(value, (3 * s - 125) % 128, 1), right)
        send_a[rows, :] = jnp.where(even, right, left)
        send_b[rows, :] = jnp.where(even, left, right)


def second_kernel(mass, stencil, got_a, got_b, field, wide, send_a, send_b):
    stacks, width = mass.shape[:2]
    even, first, last = position(ROW_AXES)

    def place(above, below):
        for s in range(stacks):
            field[s, 0:6, :] = jnp.where(first, 0.0, above[6 * s : 6 * s + 6, :])
            field[s, width + 6 : width + 12, :] = jnp.where(last, 0.0, below[6 * s : 6 * s + 6, :])
        for o in range(49):
            at = 6 * stacks + 3 * o
            wide[o, 0:3, :] = jnp.where(first, 0.0, above[at : at + 3, :])
            wide[o, width + 3 : width + 6, :] = jnp.where(last, 0.0, below[at : at + 3, :])

    @pl.when(even)
    def _():
        place(got_b, got_a)

    @pl.when(jnp.logical_not(even))
    def _():
        place(got_a, got_b)

    for s in range(stacks):
        field[s, 6 : width + 6, :] = mass[s, :, :]
        field[s, width + 12 : width + 16, :] = jnp.zeros((4, 128), F32)
    for o in range(49):
        wide[o, 3 : width + 3, :] = stencil[o, :, :]
        wide[o, width + 6 : width + 8, :] = jnp.zeros((2, 128), F32)
    pack_columns(field, 4, send_a, send_b)


def apply_stencil(field, stencil, got_a, got_b, out, shifted, in_tiles, out_tiles):
    stacks = field.shape[0]
    even, first, last = position(COLUMN_AXES)
    lane = lax.broadcasted_iota(jnp.int32, (8, 128), 1)

    def some_stacks(group, carry):
        for k in range(GROUP):
            s = group * GROUP + k
            for tile in range(in_tiles):
                rows = pl.ds(8 * tile, 8)
                one, two = got_a[rows, :], got_b[rows, :]
                after = jnp.where(last, 0.0, jnp.where(even, one, two))
                before = jnp.where(first, 0.0, jnp.where(even, two, one))
                halo = jnp.where(
                    lane < 64,
                    pltpu.roll(after, lax.rem(128 - 3 * s, 128), 1),
                    pltpu.roll(before, 125 - 3 * s, 1),
                )
                value = field[s, rows, :]
                for dy in range(-3, 4):
                    if dy > 0:
                        moved = pltpu.roll(jnp.where(lane < dy, halo, value), 128 - dy, 1)
                    elif dy < 0:
                        moved = pltpu.roll(jnp.where(lane >= 128 + dy, halo, value), -dy, 1)
                    else:
                        moved = value
                    shifted[k, dy + 3, rows, :] = moved
        for tile in range(out_tiles):
            total = [None] * GROUP
            for dy in range(7):
                for dx in range(7):
                    scale = stencil[dx * 7 + dy, 8 * tile : 8 * tile + 8, :]
                    for k in range(GROUP):
                        at = 8 * tile + dx
                        term = scale * shifted[k, dy, at : at + 8, :]
                        total[k] = term if total[k] is None else total[k] + term
            for k in range(GROUP):
                out[group * GROUP + k, 8 * tile : 8 * tile + 8, :] = total[k]
        return carry

    lax.fori_loop(0, stacks // GROUP, some_stacks, 0)


def third_kernel(field, wide, got_a, got_b, out, send_a, send_b, shifted):
    apply_stencil(field, wide, got_a, got_b, out, shifted, 4, 3)
    pack_columns(out, 3, send_a, send_b)


def fourth_kernel(field, stencil, got_a, got_b, out, shifted):
    apply_stencil(field, stencil, got_a, got_b, out, shifted, 3, 2)


def local(tracer_mass, recon_table, intersection_weights, intersection_cells, rotation_codes):
    stacks, width_x, width_y = tracer_mass.shape
    row_axes, column_axes = ROW_AXES, COLUMN_AXES
    shape = lambda *sizes: jax.ShapeDtypeStruct(sizes, F32)
    edge = -(-(6 * stacks + 3 * 49) // 8) * 8

    mass, stencil, send_a, send_b = pl.pallas_call(
        first_kernel,
        out_shape=(shape(*tracer_mass.shape), shape(49, width_x, 128), shape(edge, 128), shape(edge, 128)),
        in_specs=[HBM] * 5,
        out_specs=(VMEM,) * 4,
        scratch_shapes=[
            pltpu.SMEM(recon_table.shape, F32),
            pltpu.VMEM(intersection_weights.shape, F32),
            pltpu.VMEM(intersection_cells.shape, jnp.int32),
            pltpu.VMEM(rotation_codes.shape, jnp.int32),
            pltpu.VMEM((TERMS, 8, 8, 128), F32),
            pltpu.VMEM((25, 8, 8, 128), F32),
            pltpu.SemaphoreType.DMA((5,)),
        ],
        compiler_params=PARAMS,
        name="coefficients",
    )(*(
        pltpu.with_memory_space_constraint(value, pltpu.HBM)
        for value in (recon_table, tracer_mass, intersection_weights, intersection_cells, rotation_codes)
    ))
    got_a = swap(send_a, row_axes, False)
    got_b = swap(send_b, row_axes, True)

    field, wide, send_a, send_b = pl.pallas_call(
        second_kernel,
        out_shape=(shape(stacks, 32, 128), shape(49, 24, 128), shape(32, 128), shape(32, 128)),
        in_specs=[VMEM] * 4,
        out_specs=(VMEM,) * 4,
        compiler_params=PARAMS,
        name="assemble",
    )(mass, stencil, got_a, got_b)
    got_a = swap(send_a, column_axes, False)
    got_b = swap(send_b, column_axes, True)

    field, send_a, send_b = pl.pallas_call(
        third_kernel,
        out_shape=(shape(stacks, 24, 128), shape(24, 128), shape(24, 128)),
        in_specs=[VMEM] * 4,
        out_specs=(VMEM,) * 3,
        scratch_shapes=[pltpu.VMEM((GROUP, 7, 32, 128), F32)],
        compiler_params=PARAMS,
        name="step_one",
    )(field, wide, got_a, got_b)
    got_a = swap(send_a, column_axes, False)
    got_b = swap(send_b, column_axes, True)

    return pl.pallas_call(
        fourth_kernel,
        out_shape=shape(stacks, width_x, 128),
        in_specs=[VMEM] * 4,
        out_specs=VMEM,
        scratch_shapes=[pltpu.VMEM((GROUP, 7, 24, 128), F32)],
        compiler_params=PARAMS,
        name="step_two",
    )(field, stencil, got_a, got_b)


def solution(mesh):
    in_specs = (
        P(None, ("face", "px"), "py"),
        P(),
        P(None, None, ("face", "px"), "py"),
        P(None, ("face", "px"), "py"),
        P(None, ("face", "px"), "py"),
    )
    out_specs = P(None, ("face", "px"), "py")
    return jax.shard_map(local, mesh=mesh, in_specs=in_specs, out_specs=out_specs, check_vma=False)
```

```python
import functools

import jax
import jax.numpy as jnp
from jax import lax
from jax.experimental import pallas as pl
from jax.experimental.pallas import tpu as pltpu
from jax.sharding import PartitionSpec as P

F32 = jnp.float32
ROW_AXES = ("face", "px")
COLUMN_AXES = "py"
SWAPPED = (0, 2, 1, 5, 4, 3, 9, 8, 7, 6)
POWERS = ((0, 0), (1, 0), (0, 1), (2, 0), (1, 1), (0, 2), (3, 0), (2, 1), (1, 2), (0, 3))
TERMS = 10
GROUP = 4
VMEM = pl.BlockSpec(memory_space=pltpu.VMEM)
HBM = pl.BlockSpec(memory_space=pltpu.HBM)
PARAMS = pltpu.CompilerParams(vmem_limit_bytes=40 * 1024 * 1024)


def swap(block, axes, odd_first):
    count = lax.axis_size(axes)
    partner = list(range(count))
    for low in range(1 if odd_first else 0, count - 1, 2):
        partner[low], partner[low + 1] = low + 1, low
    pairs = list(enumerate(partner))
    return lax.ppermute(block, axes, pairs)


def position(axes):
    index = lax.axis_index(axes)
    return lax.rem(index, 2) == 0, index == 0, index == lax.axis_size(axes) - 1


def fill_stencil(recon, weights, cells, codes, turned, spread, stencil, tiles):
    zero = jnp.zeros((8, 128), F32)
    for g in range(tiles):
        rows = pl.ds(8 * g, 8)
        for m in range(4):
            code = codes[m, rows, :]
            odd = (code & 1) == 1
            sign_x = jnp.where(code >= 2, -1.0, 1.0).astype(F32)
            sign_y = jnp.where((code == 1) | (code == 2), -1.0, 1.0).astype(F32)
            sign_xy = sign_x * sign_y
            values = [weights[m, t, rows, :] for t in range(TERMS)]
            for t, (a, b) in enumerate(POWERS):
                value = values[t]
                if SWAPPED[t] != t:
                    value = jnp.where(odd, values[SWAPPED[t]], value)
                if a % 2 and b % 2:
                    value = value * sign_xy
                elif a % 2:
                    value = value * sign_x
                elif b % 2:
                    value = value * sign_y
                turned[t, m * tiles + g] = value

    combos = 4 * tiles

    def one_tap(tap, carry):
        total = [None] * combos
        for t in range(TERMS):
            scale = recon[t, tap]
            for c in range(combos):
                term = turned[t, c] * scale
                total[c] = term if t == 0 else total[c] + term
        for c in range(combos):
            spread[tap, c] = total[c]
        return carry

    lax.fori_loop(0, 25, one_tap, 0)

    for g in range(tiles):
        rows = pl.ds(8 * g, 8)
        masks = []
        for m in range(4):
            cell = cells[m, rows, :]
            first = jnp.where(cell < 3, 0, jnp.where(cell < 6, 3, 6))
            across = cell - first
            masks.append((cell < 3, cell < 6, across == 0, across <= 1))
        for ox in range(7):
            total = [None] * 7
            for m in range(4):
                low_x, mid_x, low_y, mid_y = masks[m]

                def tap(jx, jy):
                    if 0 <= jx < 5 and 0 <= jy < 5:
                        return spread[jx * 5 + jy, m * tiles + g]
                    return zero

                line = [
                    jnp.where(low_x, tap(ox, jy), jnp.where(mid_x, tap(ox - 1, jy), tap(ox - 2, jy)))
                    for jy in range(5)
                ]
                padded = [zero, zero] + line + [zero, zero]
                for oy in range(7):
                    value = jnp.where(
                        low_y, padded[oy + 2], jnp.where(mid_y, padded[oy + 1], padded[oy])
                    )
                    total[oy] = value if m == 0 else total[oy] + value
            for oy in range(7):
                stencil[ox * 7 + oy, rows, :] = total[oy]


def first_kernel(
    recon_hbm, mass_hbm, weights_hbm, cells_hbm, codes_hbm, mass, stencil, send_a, send_b,
    recon, weights, cells, codes, turned, spread, sems,
):
    sources = (recon_hbm, codes_hbm, weights_hbm, cells_hbm, mass_hbm)
    targets = (recon, codes, weights, cells, mass)
    copies = [pltpu.make_async_copy(a, b, sems.at[i]) for i, (a, b) in enumerate(zip(sources, targets))]
    for copy in copies:
        copy.start()
    for copy in copies:
        copy.wait()
    fill_stencil(recon, weights, cells, codes, turned, spread, stencil, 2)
    stacks, width = mass.shape[:2]
    even = position(ROW_AXES)[0]
    for send, low_edge in ((send_a, jnp.logical_not(even)), (send_b, even)):
        mass_at = jnp.where(low_edge, 0, width - 6)
        stencil_at = jnp.where(low_edge, 0, width - 3)
        for s in range(stacks):
            send[6 * s : 6 * s + 6, :] = mass[s, pl.ds(mass_at, 6), :]
        for o in range(49):
            at = 6 * stacks + 3 * o
            send[at : at + 3, :] = stencil[o, pl.ds(stencil_at, 3), :]


def pack_columns(field, tiles, send):
    stacks = field.shape[0]
    here_at = lax.axis_index(COLUMN_AXES)
    lane = lax.broadcasted_iota(jnp.int32, (8, 128), 1)
    for tile in range(tiles):
        rows = pl.ds(8 * tile, 8)
        left = jnp.zeros((8, 128), F32)
        right = jnp.zeros((8, 128), F32)
        for s in range(stacks):
            here = (lane >= 3 * s) & (lane < 3 * s + 3)
            value = field[s, rows, :]
            left = jnp.where(here, pltpu.roll(value, (3 * s) % 128, 1), left)
            right = jnp.where(here, pltpu.roll(value, (3 * s - 125) % 128, 1), right)
        for target in range(send.shape[0]):
            send[target, rows, :] = jnp.where(
                target == here_at + 1, right, jnp.where(target == here_at - 1, left, 0.0)
            )


def second_kernel(mass, stencil, got_a, got_b, field, wide, send):
    stacks, width = mass.shape[:2]
    even, first, last = position(ROW_AXES)

    def place(above, below):
        for s in range(stacks):
            field[s, 0:6, :] = jnp.where(first, 0.0, above[6 * s : 6 * s + 6, :])
            field[s, width + 6 : width + 12, :] = jnp.where(last, 0.0, below[6 * s : 6 * s + 6, :])
        for o in range(49):
            at = 6 * stacks + 3 * o
            wide[o, 0:3, :] = jnp.where(first, 0.0, above[at : at + 3, :])
            wide[o, width + 3 : width + 6, :] = jnp.where(last, 0.0, below[at : at + 3, :])

    @pl.when(even)
    def _():
        place(got_b, got_a)

    @pl.when(jnp.logical_not(even))
    def _():
        place(got_a, got_b)

    for s in range(stacks):
        field[s, 6 : width + 6, :] = mass[s, :, :]
        field[s, width + 12 : width + 16, :] = jnp.zeros((4, 128), F32)
    for o in range(49):
        wide[o, 3 : width + 3, :] = stencil[o, :, :]
        wide[o, width + 6 : width + 8, :] = jnp.zeros((2, 128), F32)
    pack_columns(field, 4, send)


def apply_stencil(field, stencil, got, out, shifted, in_tiles, out_tiles):
    stacks = field.shape[0]
    _, first, last = position(COLUMN_AXES)
    here_at = lax.axis_index(COLUMN_AXES)
    after_at = jnp.where(last, 0, here_at + 1)
    before_at = jnp.where(first, 0, here_at - 1)
    lane = lax.broadcasted_iota(jnp.int32, (8, 128), 1)

    def some_stacks(group, carry):
        for k in range(GROUP):
            s = group * GROUP + k
            for tile in range(in_tiles):
                rows = pl.ds(8 * tile, 8)
                after = jnp.where(last, 0.0, got[after_at, rows, :])
                before = jnp.where(first, 0.0, got[before_at, rows, :])
                halo = jnp.where(
                    lane < 64,
                    pltpu.roll(after, lax.rem(128 - 3 * s, 128), 1),
                    pltpu.roll(before, 125 - 3 * s, 1),
                )
                value = field[s, rows, :]
                for dy in range(-3, 4):
                    if dy > 0:
                        moved = pltpu.roll(jnp.where(lane < dy, halo, value), 128 - dy, 1)
                    elif dy < 0:
                        moved = pltpu.roll(jnp.where(lane >= 128 + dy, halo, value), -dy, 1)
                    else:
                        moved = value
                    shifted[k, dy + 3, rows, :] = moved
        for tile in range(out_tiles):
            total = [None] * GROUP
            for dy in range(7):
                for dx in range(7):
                    scale = stencil[dx * 7 + dy, 8 * tile : 8 * tile + 8, :]
                    for k in range(GROUP):
                        at = 8 * tile + dx
                        term = scale * shifted[k, dy, at : at + 8, :]
                        total[k] = term if total[k] is None else total[k] + term
            for k in range(GROUP):
                out[group * GROUP + k, 8 * tile : 8 * tile + 8, :] = total[k]
        return carry

    lax.fori_loop(0, stacks // GROUP, some_stacks, 0)


def third_kernel(field, wide, got, out, send, shifted):
    apply_stencil(field, wide, got, out, shifted, 4, 3)
    pack_columns(out, 3, send)


def fourth_kernel(field, stencil, got, out, shifted):
    apply_stencil(field, stencil, got, out, shifted, 3, 2)


def local(tracer_mass, recon_table, intersection_weights, intersection_cells, rotation_codes):
    stacks, width_x, width_y = tracer_mass.shape
    row_axes, column_axes = ROW_AXES, COLUMN_AXES
    shape = lambda *sizes: jax.ShapeDtypeStruct(sizes, F32)
    edge = -(-(6 * stacks + 3 * 49) // 8) * 8

    mass, stencil, send_a, send_b = pl.pallas_call(
        first_kernel,
        out_shape=(shape(*tracer_mass.shape), shape(49, width_x, 128), shape(edge, 128), shape(edge, 128)),
        in_specs=[HBM] * 5,
        out_specs=(VMEM,) * 4,
        scratch_shapes=[
            pltpu.SMEM(recon_table.shape, F32),
            pltpu.VMEM(intersection_weights.shape, F32),
            pltpu.VMEM(intersection_cells.shape, jnp.int32),
            pltpu.VMEM(rotation_codes.shape, jnp.int32),
            pltpu.VMEM((TERMS, 8, 8, 128), F32),
            pltpu.VMEM((25, 8, 8, 128), F32),
            pltpu.SemaphoreType.DMA((5,)),
        ],
        compiler_params=PARAMS,
        name="coefficients",
    )(*(
        pltpu.with_memory_space_constraint(value, pltpu.HBM)
        for value in (recon_table, tracer_mass, intersection_weights, intersection_cells, rotation_codes)
    ))
    got_a = swap(send_a, row_axes, False)
    got_b = swap(send_b, row_axes, True)

    across = lax.axis_size(column_axes)
    field, wide, send = pl.pallas_call(
        second_kernel,
        out_shape=(shape(stacks, 32, 128), shape(49, 24, 128), shape(across, 32, 128)),
        in_specs=[VMEM] * 4,
        out_specs=(VMEM,) * 3,
        compiler_params=PARAMS,
        name="assemble",
    )(mass, stencil, got_a, got_b)
    got = lax.all_to_all(send, column_axes, 0, 0, tiled=True)

    field, send = pl.pallas_call(
        third_kernel,
        out_shape=(shape(stacks, 24, 128), shape(across, 24, 128)),
        in_specs=[VMEM] * 3,
        out_specs=(VMEM,) * 2,
        scratch_shapes=[pltpu.VMEM((GROUP, 7, 32, 128), F32)],
        compiler_params=PARAMS,
        name="step_one",
    )(field, wide, got)
    got = lax.all_to_all(send, column_axes, 0, 0, tiled=True)

    return pl.pallas_call(
        fourth_kernel,
        out_shape=shape(stacks, width_x, 128),
        in_specs=[VMEM] * 3,
        out_specs=VMEM,
        scratch_shapes=[pltpu.VMEM((GROUP, 7, 24, 128), F32)],
        compiler_params=PARAMS,
        name="step_two",
    )(field, stencil, got)


def solution(mesh):
    in_specs = (
        P(None, ("face", "px"), "py"),
        P(),
        P(None, None, ("face", "px"), "py"),
        P(None, ("face", "px"), "py"),
        P(None, ("face", "px"), "py"),
    )
    out_specs = P(None, ("face", "px"), "py")
    return jax.shard_map(local, mesh=mesh, in_specs=in_specs, out_specs=out_specs, check_vma=False)
```

```python
import jax
import jax.numpy as jnp
import numpy as np
from jax import lax
from jax.experimental import pallas as pl
from jax.experimental.pallas import tpu as pltpu
from jax.sharding import PartitionSpec as P

F32 = jnp.float32
ROW_AXES = ("face", "px")
COLUMN_AXES = "py"
SWAPPED = (0, 2, 1, 5, 4, 3, 9, 8, 7, 6)
POWERS = ((0, 0), (1, 0), (0, 1), (2, 0), (1, 1), (0, 2), (3, 0), (2, 1), (1, 2), (0, 3))
TERMS = 10
OFFSETS = 49
GROUP = 4
SPAN = 9
PER = 14
COEF_PER = 42
VMEM = pl.BlockSpec(memory_space=pltpu.VMEM)
HBM = pl.BlockSpec(memory_space=pltpu.HBM)


def params():
    return pltpu.CompilerParams(vmem_limit_bytes=40 * 1024 * 1024)


def cost(operations):
    return pl.CostEstimate(flops=operations, bytes_accessed=1 << 20, transcendentals=0)


def swap(block, axes, odd_first):
    count = lax.axis_size(axes)
    pairs = []
    for low in range(1 if odd_first else 0, count - 1, 2):
        pairs += [(low, low + 1), (low + 1, low)]
    return lax.ppermute(block, axes, pairs)


def is_even(axes):
    return lax.rem(lax.axis_index(axes), 2) == 0


def turn(value, amount):
    amount %= 128
    return pltpu.roll(value, amount, 1) if amount else value


def lanes(rows=8):
    return lax.broadcasted_iota(jnp.int32, (rows, 128), 1)


def fill_stencil(recon, weights, cells, codes, turned, spread, stencil, tiles):
    zero = jnp.zeros((8, 128), F32)
    for g in range(tiles):
        rows = pl.ds(8 * g, 8)
        for m in range(4):
            code = codes[m, rows, :]
            odd = (code & 1) == 1
            sign_x = jnp.where(code >= 2, -1.0, 1.0).astype(F32)
            sign_y = jnp.where((code == 1) | (code == 2), -1.0, 1.0).astype(F32)
            sign_xy = sign_x * sign_y
            values = [weights[m, t, rows, :] for t in range(TERMS)]
            for t, (a, b) in enumerate(POWERS):
                value = values[t]
                if SWAPPED[t] != t:
                    value = jnp.where(odd, values[SWAPPED[t]], value)
                if a % 2 and b % 2:
                    value = value * sign_xy
                elif a % 2:
                    value = value * sign_x
                elif b % 2:
                    value = value * sign_y
                turned[t, m * tiles + g] = value

    combos = 4 * tiles

    def one_tap(tap, carry):
        total = [None] * combos
        for t in range(TERMS):
            scale = recon[t, tap]
            for c in range(combos):
                term = turned[t, c] * scale
                total[c] = term if t == 0 else total[c] + term
        for c in range(combos):
            spread[tap, c] = total[c]
        return carry

    lax.fori_loop(0, 25, one_tap, 0)

    for g in range(tiles):
        rows = pl.ds(8 * g, 8)
        masks = []
        for m in range(4):
            cell = cells[m, rows, :]
            first = jnp.where(cell < 3, 0, jnp.where(cell < 6, 3, 6))
            across = cell - first
            masks.append((cell < 3, cell < 6, across == 0, across <= 1))
        for ox in range(7):
            total = [None] * 7
            for m in range(4):
                low_x, mid_x, low_y, mid_y = masks[m]

                def tap(jx, jy):
                    if 0 <= jx < 5 and 0 <= jy < 5:
                        return spread[jx * 5 + jy, m * tiles + g]
                    return zero

                line = [
                    jnp.where(low_x, tap(ox, jy), jnp.where(mid_x, tap(ox - 1, jy), tap(ox - 2, jy)))
                    for jy in range(5)
                ]
                padded = [zero, zero] + line + [zero, zero]
                for oy in range(7):
                    value = jnp.where(
                        low_y, padded[oy + 2], jnp.where(mid_y, padded[oy + 1], padded[oy])
                    )
                    total[oy] = value if m == 0 else total[oy] + value
            for oy in range(7):
                stencil[ox * 7 + oy, rows, :] = total[oy]


def coefficients(
    recon_hbm, mass_hbm, weights_hbm, cells_hbm, codes_hbm, mass, stencil, send_a, send_b,
    recon, weights, cells, codes, turned, spread, sems,
):
    sources = (recon_hbm, codes_hbm, weights_hbm, cells_hbm, mass_hbm)
    targets = (recon, codes, weights, cells, mass)
    copies = [pltpu.make_async_copy(a, b, sems.at[i]) for i, (a, b) in enumerate(zip(sources, targets))]
    for copy in copies:
        copy.start()
    for copy in copies:
        copy.wait()
    stacks, width = mass.shape[:2]
    fill_stencil(recon, weights, cells, codes, turned, spread, stencil, width // 8)
    even = is_even(ROW_AXES)
    for send, low_edge in ((send_a, jnp.logical_not(even)), (send_b, even)):
        mass_at = jnp.where(low_edge, 0, width - 6)
        stencil_at = jnp.where(low_edge, 0, width - 3)
        for s in range(stacks):
            send[6 * s : 6 * s + 6, :] = mass[s, pl.ds(mass_at, 6), :]
        for o in range(OFFSETS):
            at = 6 * stacks + 3 * o
            send[at : at + 3, :] = stencil[o, pl.ds(stencil_at, 3), :]


def pack_stacks(load, stacks, tile):
    lane = lanes()
    left = jnp.zeros((8, 128), F32)
    right = jnp.zeros((8, 128), F32)
    for s in range(PER * tile, min(stacks, PER * tile + PER)):
        at = SPAN * (s % PER)
        value = load(s)
        left = jnp.where((lane >= at + 3) & (lane < at + 9), turn(value, at + 3), left)
        right = jnp.where((lane >= at) & (lane < at + 6), turn(value, at - 122), right)
    return left, right


def pack_coefficients(load, tile):
    lane = lanes()
    left = jnp.zeros((8, 128), F32)
    right = jnp.zeros((8, 128), F32)
    for o in range(COEF_PER * tile, min(OFFSETS, COEF_PER * tile + COEF_PER)):
        at = 3 * (o % COEF_PER)
        here = (lane >= at) & (lane < at + 3)
        value = load(o)
        left = jnp.where(here, turn(value, at), left)
        right = jnp.where(here, turn(value, at - 125), right)
    return left, right


def pack_own(mass, stencil, left, right):
    stacks, width = mass.shape[:2]
    tiles = -(-stacks // PER)
    for half in range(width // 8):
        rows = pl.ds(8 * half, 8)
        for tile in range(tiles):
            at = width * tile + 8 * half
            left[at : at + 8, :], right[at : at + 8, :] = pack_stacks(
                lambda s: mass[s, rows, :], stacks, tile
            )
        for tile in range(2):
            at = width * (tiles + tile) + 8 * half
            left[at : at + 8, :], right[at : at + 8, :] = pack_coefficients(
                lambda o: stencil[o, rows, :], tile
            )


def join_halo(own_left, own_right, got_a, got_b, send_left, send_right, stacks, width):
    tiles = -(-stacks // PER)
    for send, own in ((send_left, own_left), (send_right, own_right)):
        for tile in range(tiles):
            send[tile, 0:width, :] = own[width * tile : width * tile + width, :]
            send[tile, width + 12 : width + 16, :] = jnp.zeros((4, 128), F32)
        for tile in range(2):
            at = width * (tiles + tile)
            send[tiles + tile, 0:width, :] = own[at : at + width, :]
            send[tiles + tile, width + 6 : width + 16, :] = jnp.zeros((10, 128), F32)

    def place(above, below):
        for got, mass_at, coef_at in ((above, width, width), (below, width + 6, width + 3)):
            for tile in range(tiles):
                left, right = pack_stacks(lambda s: got[6 * s : 6 * s + 8, :], stacks, tile)
                send_left[tile, mass_at : mass_at + 6, :] = left[0:6]
                send_right[tile, mass_at : mass_at + 6, :] = right[0:6]
            for tile in range(2):
                base = 6 * stacks
                left, right = pack_coefficients(lambda o: got[base + 3 * o : base + 3 * o + 8, :], tile)
                send_left[tiles + tile, coef_at : coef_at + 3, :] = left[0:3]
                send_right[tiles + tile, coef_at : coef_at + 3, :] = right[0:3]

    even = is_even(ROW_AXES)

    @pl.when(even)
    def _():
        place(got_b, got_a)

    @pl.when(jnp.logical_not(even))
    def _():
        place(got_a, got_b)


def choose(even, first, second, first_out, second_out):
    @pl.when(even)
    def _():
        first_out[...] = first[...]
        second_out[...] = second[...]

    @pl.when(jnp.logical_not(even))
    def _():
        first_out[...] = second[...]
        second_out[...] = first[...]


def pack_all(mass, own_left, own_right, got_a, got_b, send_a, send_b, left, right):
    stacks, width = mass.shape[:2]
    join_halo(own_left, own_right, got_a, got_b, left, right, stacks, width)
    choose(is_even(COLUMN_AXES), right, left, send_a, send_b)


def main_sum(load, coef, coef_at, tile):
    fields = [[load(k, 8 * tile + dx) for k in range(GROUP)] for dx in range(7)]
    total = [None] * GROUP
    for dy in range(7):
        part = [None] * GROUP
        for dx in range(7):
            at = coef_at + 8 * tile
            scale = coef[dx * 7 + dy, at : at + 8, :]
            for k in range(GROUP):
                term = scale * fields[dx][k]
                part[k] = term if dx == 0 else part[k] + term
        for k in range(GROUP):
            moved = turn(part[k], 3 - dy)
            total[k] = moved if dy == 0 else total[k] + moved
    return total


def step_one(mass, stencil, got_a, got_b, partial, wide, shifted, field):
    stacks, width = mass.shape[:2]

    def place(above, below):
        for s in range(stacks):
            field[s, 0:6, :] = above[6 * s : 6 * s + 6, :]
            field[s, width + 6 : width + 12, :] = below[6 * s : 6 * s + 6, :]
        for o in range(OFFSETS):
            at = 6 * stacks + 3 * o
            wide[o, 0:3, :] = above[at : at + 3, :]
            wide[o, width + 3 : width + 6, :] = below[at : at + 3, :]

    even = is_even(ROW_AXES)

    @pl.when(even)
    def _():
        place(got_b, got_a)

    @pl.when(jnp.logical_not(even))
    def _():
        place(got_a, got_b)

    for s in range(stacks):
        field[s, 6 : width + 6, :] = mass[s, :, :]
        field[s, width + 12 : width + 16, :] = jnp.zeros((4, 128), F32)
    lane = lanes()
    for o in range(OFFSETS):
        wide[o, 3 : width + 3, :] = stencil[o, :, :]
        wide[o, width + 6 : width + 8, :] = jnp.zeros((2, 128), F32)
        dy = o % 7 - 3
        for tile in range(3):
            rows = pl.ds(8 * tile, 8)
            value = turn(wide[o, rows, :], dy)
            if dy > 0:
                value = jnp.where(lane >= dy, value, 0.0)
            elif dy < 0:
                value = jnp.where(lane < 128 + dy, value, 0.0)
            shifted[o, rows, :] = value

    def some_stacks(group, carry):
        for tile in range(3):
            total = main_sum(lambda k, at: field[group * GROUP + k, at : at + 8, :], shifted, 0, tile)
            for k in range(GROUP):
                partial[group * GROUP + k, 8 * tile : 8 * tile + 8, :] = total[k]
        return carry

    lax.fori_loop(0, stacks // GROUP, some_stacks, 0)


def packed_sum(load, coef, coef_at, tile, tiles, dys):
    fields = [[load(t, 8 * tile + dx) for t in range(tiles)] for dx in range(7)]
    total = [None] * tiles
    for dy in dys:
        part = [None] * tiles
        for dx in range(7):
            at = coef_at + 8 * tile
            scale = coef[dx * 7 + dy + 3, at : at + 8, :]
            for t in range(tiles):
                term = scale * fields[dx][t]
                part[t] = term if dx == 0 else part[t] + term
        for t in range(tiles):
            moved = turn(part[t], -dy)
            total[t] = moved if total[t] is None else total[t] + moved
    return total


def step_two(
    partial, wide, shifted, send_a, send_b, got_a, got_b, out,
    right_set, left_set, right_halo, left_halo, right_coef, left_coef,
    right_next, left_next, edge_one, edge_two, field,
):
    stacks, width = out.shape[:2]
    tiles = -(-stacks // PER)
    lane = lanes()
    place_in = lax.rem(lane, SPAN)

    def gather(sent_right, sent_left, from_right, from_left):
        wide_place = lax.rem(lanes(width + 16), SPAN)
        for tile in range(tiles):
            right = jnp.where(wide_place < 3, turn(sent_right[tile], -3), from_right[tile])
            left = jnp.where(wide_place >= 6, turn(sent_left[tile], 3), from_left[tile])
            for target, value in ((right_set, right), (left_set, left)):
                target[tile, 6 : width + 6, :] = value[0:width]
                target[tile, 0:6, :] = value[width : width + 6]
                target[tile, width + 6 : width + 16, :] = value[width + 6 : width + 16]
        for tile in range(2):
            for target, source in ((right_halo, from_right), (left_halo, from_left)):
                target[tile, 3 : width + 3, :] = source[tiles + tile, 0:width, :]
                target[tile, 0:3, :] = source[tiles + tile, width : width + 3, :]
                target[tile, width + 3 : width + 8, :] = source[tiles + tile, width + 3 : width + 8, :]

    even = is_even(COLUMN_AXES)

    @pl.when(even)
    def _():
        gather(send_a, send_b, got_a, got_b)

    @pl.when(jnp.logical_not(even))
    def _():
        gather(send_b, send_a, got_b, got_a)

    for o in range(OFFSETS):
        dy = o % 7 - 3
        at = 3 * (o % COEF_PER)
        for tile in range(3):
            rows = pl.ds(8 * tile, 8)
            right = turn(right_halo[o // COEF_PER, rows, :], 3 + dy - at)
            left = turn(left_halo[o // COEF_PER, rows, :], 3 + dy - at)
            own = wide[o, rows, :]
            if dy > 0:
                right = jnp.where(lane < 3 + dy, turn(own, 3 + dy), right)
                right = jnp.where((lane >= 3) & (lane < 6 + dy), right, 0.0)
            else:
                right = jnp.where((lane >= 3 + dy) & (lane < 6 + dy), right, 0.0)
            if dy < 0:
                left = jnp.where(lane < 6 + dy, left, turn(own, 6 + dy))
                left = jnp.where((lane >= 3 + dy) & (lane < 6), left, 0.0)
            else:
                left = jnp.where((lane >= 3 + dy) & (lane < 6 + dy), left, 0.0)
            for target, value in ((right_coef, right), (left_coef, left)):
                value = value + turn(value, SPAN)
                value = value + turn(value, 2 * SPAN)
                value = value + turn(value, 4 * SPAN)
                target[o, rows, :] = jnp.where(lane < 8 * SPAN, value, turn(value, 6 * SPAN))

    everywhere = range(-3, 4)
    for tile in range(3):
        rows = pl.ds(8 * tile, 8)
        right = packed_sum(
            lambda t, at: right_set[t, at : at + 8, :], right_coef, 0, tile, tiles, everywhere
        )
        left = packed_sum(
            lambda t, at: left_set[t, at : at + 8, :], left_coef, 0, tile, tiles, everywhere
        )
        halo = (place_in >= 3) & (place_in < 6)
        for t in range(tiles):
            right_next[t, rows, :] = jnp.where(halo, right[t], 0.0)
            left_next[t, rows, :] = jnp.where(halo, left[t], 0.0)
            edge_one[t, rows, :] = jnp.where(place_in < 3, right[t], turn(left[t], -3))

    for tile in range(2):
        rows = pl.ds(8 * tile, 8)
        right = packed_sum(
            lambda t, at: right_next[t, at : at + 8, :], right_coef, 3, tile, tiles, range(1, 4)
        )
        left = packed_sum(
            lambda t, at: left_next[t, at : at + 8, :], left_coef, 3, tile, tiles, range(-3, 0)
        )
        for t in range(tiles):
            edge_two[t, rows, :] = jnp.where(place_in < 3, right[t], turn(left[t], -3))

    at_edge = (lane < 3) | (lane >= 125)

    def some_stacks(group, carry):
        def edges(packed, k, rows):
            s = group * GROUP + k
            amount = lax.rem(253 - SPAN * lax.rem(s, PER), 128)
            return jnp.where(at_edge, pltpu.roll(packed[s // PER, rows, :], amount, 1), 0.0)

        for k in range(GROUP):
            for tile in range(3):
                rows = pl.ds(8 * tile, 8)
                field[k, rows, :] = partial[group * GROUP + k, rows, :] + edges(edge_one, k, rows)
        for tile in range(2):
            total = main_sum(lambda k, at: field[k, at : at + 8, :], shifted, 3, tile)
            rows = pl.ds(8 * tile, 8)
            for k in range(GROUP):
                out[group * GROUP + k, rows, :] = total[k] + edges(edge_two, k, rows)
        return carry

    lax.fori_loop(0, stacks // GROUP, some_stacks, 0)


def local(tracer_mass, recon_table, intersection_weights, intersection_cells, rotation_codes):
    stacks, width, columns = tracer_mass.shape
    shape = lambda *sizes: jax.ShapeDtypeStruct(sizes, F32)
    scratch = lambda *sizes: pltpu.VMEM(sizes, F32)
    edge = -(-(6 * stacks + 3 * OFFSETS) // 8) * 8
    tiles = -(-stacks // PER)
    combos = 4 * (width // 8)

    mass, stencil, send_a, send_b = pl.pallas_call(
        coefficients,
        out_shape=(shape(*tracer_mass.shape), shape(OFFSETS, width, 128), shape(edge, 128), shape(edge, 128)),
        in_specs=[HBM] * 5,
        out_specs=(VMEM,) * 4,
        scratch_shapes=[
            pltpu.SMEM(recon_table.shape, F32),
            scratch(*intersection_weights.shape),
            pltpu.VMEM(intersection_cells.shape, jnp.int32),
            pltpu.VMEM(rotation_codes.shape, jnp.int32),
            scratch(TERMS, combos, 8, 128),
            scratch(25, combos, 8, 128),
            pltpu.SemaphoreType.DMA((5,)),
        ],
        compiler_params=params(),
        cost_estimate=cost(8 * 10**6),
        name="coefficients",
    )(*(
        pltpu.with_memory_space_constraint(value, pltpu.HBM)
        for value in (recon_table, tracer_mass, intersection_weights, intersection_cells, rotation_codes)
    ))
    got_a = swap(send_a, ROW_AXES, False)
    got_b = swap(send_b, ROW_AXES, True)

    own_left, own_right = pl.pallas_call(
        pack_own,
        out_shape=(shape(width * (tiles + 2), 128),) * 2,
        in_specs=[VMEM] * 2,
        out_specs=(VMEM,) * 2,
        compiler_params=params(),
        cost_estimate=cost(10**6),
        name="pack_own",
    )(mass, stencil)

    send = (tiles + 2, width + 16, 128)
    send_left, send_right = pl.pallas_call(
        pack_all,
        out_shape=(shape(*send),) * 2,
        in_specs=[VMEM] * 5,
        out_specs=(VMEM,) * 2,
        scratch_shapes=[scratch(*send)] * 2,
        compiler_params=params(),
        cost_estimate=cost(10**6),
        name="pack_all",
    )(mass, own_left, own_right, got_a, got_b)
    column_a = swap(send_left, COLUMN_AXES, False)
    column_b = swap(send_right, COLUMN_AXES, True)

    partial, wide, shifted = pl.pallas_call(
        step_one,
        out_shape=(
            shape(stacks, width + 8, 128), shape(OFFSETS, width + 8, 128), shape(OFFSETS, width + 8, 128)
        ),
        in_specs=[VMEM] * 4,
        out_specs=(VMEM,) * 3,
        scratch_shapes=[scratch(stacks, width + 16, 128)],
        compiler_params=params(),
        cost_estimate=cost(12 * 10**6),
        name="step_one",
    )(mass, stencil, got_a, got_b)

    return pl.pallas_call(
        step_two,
        out_shape=shape(stacks, width, columns),
        in_specs=[VMEM] * 7,
        out_specs=VMEM,
        scratch_shapes=[
            scratch(tiles, width + 16, 128),
            scratch(tiles, width + 16, 128),
            scratch(2, width + 8, 128),
            scratch(2, width + 8, 128),
            scratch(OFFSETS, width + 8, 128),
            scratch(OFFSETS, width + 8, 128),
            scratch(tiles, width + 8, 128),
            scratch(tiles, width + 8, 128),
            scratch(tiles, width + 8, 128),
            scratch(tiles, width, 128),
            scratch(GROUP, width + 8, 128),
        ],
        compiler_params=params(),
        cost_estimate=cost(12 * 10**6),
        name="step_two",
    )(partial, wide, shifted, send_left, send_right, column_a, column_b)


def solution(mesh):
    in_specs = (
        P(None, ("face", "px"), "py"),
        P(),
        P(None, None, ("face", "px"), "py"),
        P(None, ("face", "px"), "py"),
        P(None, ("face", "px"), "py"),
    )
    out_specs = P(None, ("face", "px"), "py")
    return jax.shard_map(local, mesh=mesh, in_specs=in_specs, out_specs=out_specs, check_vma=False)
```

```python
import jax
import jax.numpy as jnp
from jax import lax
from jax.experimental import pallas as pl
from jax.experimental.pallas import tpu as pltpu
from jax.sharding import PartitionSpec as P

F32 = jnp.float32
ROW_AXES = ("face", "px")
COLUMN_AXES = "py"
SWAPPED = (0, 2, 1, 5, 4, 3, 9, 8, 7, 6)
POWERS = ((0, 0), (1, 0), (0, 1), (2, 0), (1, 1), (0, 2), (3, 0), (2, 1), (1, 2), (0, 3))
TERMS = 10
OFFSETS = 49
GROUP = 4
SPAN = 9
PER = 14
COEF_PER = 42
VMEM = pl.BlockSpec(memory_space=pltpu.VMEM)
HBM = pl.BlockSpec(memory_space=pltpu.HBM)


def params():
    return pltpu.CompilerParams(vmem_limit_bytes=40 * 1024 * 1024)


def cost(operations):
    return pl.CostEstimate(flops=operations, bytes_accessed=1 << 20, transcendentals=0)


def swap(block, axes, odd_first):
    count = lax.axis_size(axes)
    pairs = []
    for low in range(1 if odd_first else 0, count - 1, 2):
        pairs += [(low, low + 1), (low + 1, low)]
    return lax.ppermute(block, axes, pairs)


def is_even(axes):
    return lax.rem(lax.axis_index(axes), 2) == 0


def turn(value, amount):
    amount %= 128
    return pltpu.roll(value, amount, 1) if amount else value


def lanes(rows=8):
    return lax.broadcasted_iota(jnp.int32, (rows, 128), 1)


def fill_stencil(recon, weights, cells, codes, turned, spread, stencil, tiles):
    zero = jnp.zeros((8, 128), F32)
    for g in range(tiles):
        rows = pl.ds(8 * g, 8)
        for m in range(4):
            code = codes[m, rows, :]
            odd = (code & 1) == 1
            sign_x = jnp.where(code >= 2, -1.0, 1.0).astype(F32)
            sign_y = jnp.where((code == 1) | (code == 2), -1.0, 1.0).astype(F32)
            sign_xy = sign_x * sign_y
            values = [weights[m, t, rows, :] for t in range(TERMS)]
            for t, (a, b) in enumerate(POWERS):
                value = values[t]
                if SWAPPED[t] != t:
                    value = jnp.where(odd, values[SWAPPED[t]], value)
                if a % 2 and b % 2:
                    value = value * sign_xy
                elif a % 2:
                    value = value * sign_x
                elif b % 2:
                    value = value * sign_y
                turned[t, m * tiles + g] = value

    combos = 4 * tiles

    def one_tap(tap, carry):
        total = [None] * combos
        for t in range(TERMS):
            scale = recon[t, tap]
            for c in range(combos):
                term = turned[t, c] * scale
                total[c] = term if t == 0 else total[c] + term
        for c in range(combos):
            spread[tap, c] = total[c]
        return carry

    lax.fori_loop(0, 25, one_tap, 0)

    for g in range(tiles):
        rows = pl.ds(8 * g, 8)
        masks = []
        for m in range(4):
            cell = cells[m, rows, :]
            first = jnp.where(cell < 3, 0, jnp.where(cell < 6, 3, 6))
            across = cell - first
            masks.append((cell < 3, cell < 6, across == 0, across <= 1))
        for ox in range(7):
            total = [None] * 7
            for m in range(4):
                low_x, mid_x, low_y, mid_y = masks[m]

                def tap(jx, jy):
                    if 0 <= jx < 5 and 0 <= jy < 5:
                        return spread[jx * 5 + jy, m * tiles + g]
                    return zero

                line = [
                    jnp.where(low_x, tap(ox, jy), jnp.where(mid_x, tap(ox - 1, jy), tap(ox - 2, jy)))
                    for jy in range(5)
                ]
                padded = [zero, zero] + line + [zero, zero]
                for oy in range(7):
                    value = jnp.where(
                        low_y, padded[oy + 2], jnp.where(mid_y, padded[oy + 1], padded[oy])
                    )
                    total[oy] = value if m == 0 else total[oy] + value
            for oy in range(7):
                stencil[ox * 7 + oy, rows, :] = total[oy]


def coefficients(
    recon_hbm, mass_hbm, weights_hbm, cells_hbm, codes_hbm, mass, stencil, send_a, send_b,
    recon, weights, cells, codes, turned, spread, sems,
):
    sources = (recon_hbm, codes_hbm, weights_hbm, cells_hbm, mass_hbm)
    targets = (recon, codes, weights, cells, mass)
    copies = [pltpu.make_async_copy(a, b, sems.at[i]) for i, (a, b) in enumerate(zip(sources, targets))]
    for copy in copies:
        copy.start()
    for copy in copies:
        copy.wait()
    stacks, width = mass.shape[:2]
    fill_stencil(recon, weights, cells, codes, turned, spread, stencil, width // 8)
    even = is_even(ROW_AXES)
    for send, low_edge in ((send_a, jnp.logical_not(even)), (send_b, even)):
        mass_at = jnp.where(low_edge, 0, width - 6)
        stencil_at = jnp.where(low_edge, 0, width - 3)
        for s in range(stacks):
            send[6 * s : 6 * s + 6, :] = mass[s, pl.ds(mass_at, 6), :]
        for o in range(OFFSETS):
            at = 6 * stacks + 3 * o
            send[at : at + 3, :] = stencil[o, pl.ds(stencil_at, 3), :]


def pack_stacks(load, stacks, tile):
    lane = lanes()
    left = jnp.zeros((8, 128), F32)
    right = jnp.zeros((8, 128), F32)
    for s in range(PER * tile, min(stacks, PER * tile + PER)):
        at = SPAN * (s % PER)
        value = load(s)
        left = jnp.where((lane >= at + 3) & (lane < at + 9), turn(value, at + 3), left)
        right = jnp.where((lane >= at) & (lane < at + 6), turn(value, at - 122), right)
    return left, right


def pack_coefficients(load, tile):
    lane = lanes()
    left = jnp.zeros((8, 128), F32)
    right = jnp.zeros((8, 128), F32)
    for o in range(COEF_PER * tile, min(OFFSETS, COEF_PER * tile + COEF_PER)):
        at = 3 * (o % COEF_PER)
        here = (lane >= at) & (lane < at + 3)
        value = load(o)
        left = jnp.where(here, turn(value, at), left)
        right = jnp.where(here, turn(value, at - 125), right)
    return left, right


def pack_own(mass, stencil, left, right):
    stacks, width = mass.shape[:2]
    tiles = -(-stacks // PER)
    for half in range(width // 8):
        rows = pl.ds(8 * half, 8)
        for tile in range(tiles):
            at = width * tile + 8 * half
            left[at : at + 8, :], right[at : at + 8, :] = pack_stacks(
                lambda s: mass[s, rows, :], stacks, tile
            )
        for tile in range(2):
            at = width * (tiles + tile) + 8 * half
            left[at : at + 8, :], right[at : at + 8, :] = pack_coefficients(
                lambda o: stencil[o, rows, :], tile
            )


def join_halo(own_left, own_right, got_a, got_b, send_left, send_right, stacks, width):
    tiles = -(-stacks // PER)
    for send, own in ((send_left, own_left), (send_right, own_right)):
        for tile in range(tiles):
            send[tile, 0:width, :] = own[width * tile : width * tile + width, :]
            send[tile, width + 12 : width + 16, :] = jnp.zeros((4, 128), F32)
        for tile in range(2):
            at = width * (tiles + tile)
            send[tiles + tile, 0:width, :] = own[at : at + width, :]
            send[tiles + tile, width + 6 : width + 16, :] = jnp.zeros((10, 128), F32)

    def place(above, below):
        for got, mass_at, coef_at in ((above, width, width), (below, width + 6, width + 3)):
            for tile in range(tiles):
                left, right = pack_stacks(lambda s: got[6 * s : 6 * s + 8, :], stacks, tile)
                send_left[tile, mass_at : mass_at + 6, :] = left[0:6]
                send_right[tile, mass_at : mass_at + 6, :] = right[0:6]
            for tile in range(2):
                base = 6 * stacks
                left, right = pack_coefficients(lambda o: got[base + 3 * o : base + 3 * o + 8, :], tile)
                send_left[tiles + tile, coef_at : coef_at + 3, :] = left[0:3]
                send_right[tiles + tile, coef_at : coef_at + 3, :] = right[0:3]

    even = is_even(ROW_AXES)

    @pl.when(even)
    def _():
        place(got_b, got_a)

    @pl.when(jnp.logical_not(even))
    def _():
        place(got_a, got_b)


def choose(even, first, second, first_out, second_out):
    @pl.when(even)
    def _():
        first_out[...] = first[...]
        second_out[...] = second[...]

    @pl.when(jnp.logical_not(even))
    def _():
        first_out[...] = second[...]
        second_out[...] = first[...]


def pack_all(mass, own_left, own_right, got_a, got_b, send_a, send_b, left, right):
    stacks, width = mass.shape[:2]
    join_halo(own_left, own_right, got_a, got_b, left, right, stacks, width)
    choose(is_even(COLUMN_AXES), right, left, send_a, send_b)


def main_sum(load, coef, coef_at, tile):
    fields = [[load(k, 8 * tile + dx) for k in range(GROUP)] for dx in range(7)]
    total = [None] * GROUP
    for dy in range(7):
        part = [None] * GROUP
        for dx in range(7):
            at = coef_at + 8 * tile
            scale = coef[dx * 7 + dy, at : at + 8, :]
            for k in range(GROUP):
                term = scale * fields[dx][k]
                part[k] = term if dx == 0 else part[k] + term
        for k in range(GROUP):
            moved = turn(part[k], 3 - dy)
            total[k] = moved if dy == 0 else total[k] + moved
    return total


def step_one(mass, stencil, got_a, got_b, partial, wide, shifted, field):
    stacks, width = mass.shape[:2]

    def place(above, below):
        for s in range(stacks):
            field[s, 0:6, :] = above[6 * s : 6 * s + 6, :]
            field[s, width + 6 : width + 12, :] = below[6 * s : 6 * s + 6, :]
        for o in range(OFFSETS):
            at = 6 * stacks + 3 * o
            wide[o, 0:3, :] = above[at : at + 3, :]
            wide[o, width + 3 : width + 6, :] = below[at : at + 3, :]

    even = is_even(ROW_AXES)

    @pl.when(even)
    def _():
        place(got_b, got_a)

    @pl.when(jnp.logical_not(even))
    def _():
        place(got_a, got_b)

    for s in range(stacks):
        field[s, 6 : width + 6, :] = mass[s, :, :]
        field[s, width + 12 : width + 16, :] = jnp.zeros((4, 128), F32)
    lane = lanes()
    for o in range(OFFSETS):
        wide[o, 3 : width + 3, :] = stencil[o, :, :]
        wide[o, width + 6 : width + 8, :] = jnp.zeros((2, 128), F32)
        dy = o % 7 - 3
        for tile in range(3):
            rows = pl.ds(8 * tile, 8)
            value = turn(wide[o, rows, :], dy)
            if dy > 0:
                value = jnp.where(lane >= dy, value, 0.0)
            elif dy < 0:
                value = jnp.where(lane < 128 + dy, value, 0.0)
            shifted[o, rows, :] = value

    def some_stacks(group, carry):
        for tile in range(3):
            total = main_sum(lambda k, at: field[group * GROUP + k, at : at + 8, :], shifted, 0, tile)
            for k in range(GROUP):
                partial[group * GROUP + k, 8 * tile : 8 * tile + 8, :] = total[k]
        return carry

    lax.fori_loop(0, stacks // GROUP, some_stacks, 0)


def packed_sum(load, coef, coef_at, tile, tiles, dys):
    fields = [[load(t, 8 * tile + dx) for t in range(tiles)] for dx in range(7)]
    total = [None] * tiles
    for dy in dys:
        part = [None] * tiles
        for dx in range(7):
            at = coef_at + 8 * tile
            scale = coef[dx * 7 + dy + 3, at : at + 8, :]
            for t in range(tiles):
                term = scale * fields[dx][t]
                part[t] = term if dx == 0 else part[t] + term
        for t in range(tiles):
            moved = turn(part[t], -dy)
            total[t] = moved if total[t] is None else total[t] + moved
    return total


def place_in_group(rows=8):
    lane = lanes(rows)
    return lane - SPAN * ((lane * 57) >> 9)


def side_coefficients(
    wide, send_a, send_b, got_a, got_b, right_set, left_set, right_coef, left_coef, right_halo, left_halo
):
    width = wide.shape[1] - 8
    tiles = right_set.shape[0]
    lane = lanes()

    def gather(sent_right, sent_left, from_right, from_left):
        place = place_in_group(width + 16)
        for tile in range(tiles):
            right = jnp.where(place < 3, turn(sent_right[tile], -3), from_right[tile])
            left = jnp.where(place >= 6, turn(sent_left[tile], 3), from_left[tile])
            for target, value in ((right_set, right), (left_set, left)):
                target[tile, 6 : width + 6, :] = value[0:width]
                target[tile, 0:6, :] = value[width : width + 6]
                target[tile, width + 6 : width + 16, :] = value[width + 6 : width + 16]
        for tile in range(2):
            for target, source in ((right_halo, from_right), (left_halo, from_left)):
                target[tile, 3 : width + 3, :] = source[tiles + tile, 0:width, :]
                target[tile, 0:3, :] = source[tiles + tile, width : width + 3, :]
                target[tile, width + 3 : width + 8, :] = source[tiles + tile, width + 3 : width + 8, :]

    even = is_even(COLUMN_AXES)

    @pl.when(even)
    def _():
        gather(send_a, send_b, got_a, got_b)

    @pl.when(jnp.logical_not(even))
    def _():
        gather(send_b, send_a, got_b, got_a)

    def one_tile(tile, carry):
        rows = pl.ds(pl.multiple_of(8 * tile, 8), 8)
        for dy in range(-3, 4):
            offsets = [dx * 7 + dy + 3 for dx in range(7)]
            for side, target in ((right_halo, right_coef), (left_halo, left_coef)):
                keep_low, keep_high = 3 + dy, 6 + dy
                if side is right_halo and dy > 0:
                    keep_low = 3
                if side is left_halo and dy < 0:
                    keep_high = 6
                keep = (lane >= keep_low) & (lane < keep_high)
                values = []
                for o in offsets:
                    value = turn(side[o // COEF_PER, rows, :], 3 + dy - 3 * (o % COEF_PER))
                    if side is right_halo and dy > 0:
                        value = jnp.where(lane < 3 + dy, turn(wide[o, rows, :], 3 + dy), value)
                    if side is left_halo and dy < 0:
                        value = jnp.where(lane < 6 + dy, value, turn(wide[o, rows, :], 6 + dy))
                    values.append(jnp.where(keep, value, 0.0))
                for groups in (1, 2, 4):
                    values = [value + turn(value, groups * SPAN) for value in values]
                values = [jnp.where(lane < 8 * SPAN, value, turn(value, 6 * SPAN)) for value in values]
                for o, value in zip(offsets, values):
                    target[o, rows, :] = value
        return carry

    lax.fori_loop(0, (width + 8) // 8, one_tile, 0)


def halo_steps(right_set, left_set, right_coef, left_coef, edge_one, edge_two, right_next, left_next):
    tiles = right_set.shape[0]
    place = place_in_group()
    everywhere = range(-3, 4)
    for tile in range(edge_one.shape[1] // 8):
        rows = pl.ds(8 * tile, 8)
        right = packed_sum(
            lambda t, at: right_set[t, at : at + 8, :], right_coef, 0, tile, tiles, everywhere
        )
        left = packed_sum(
            lambda t, at: left_set[t, at : at + 8, :], left_coef, 0, tile, tiles, everywhere
        )
        halo = (place >= 3) & (place < 6)
        for t in range(tiles):
            right_next[t, rows, :] = jnp.where(halo, right[t], 0.0)
            left_next[t, rows, :] = jnp.where(halo, left[t], 0.0)
            edge_one[t, rows, :] = jnp.where(place < 3, right[t], turn(left[t], -3))
    for tile in range(edge_two.shape[1] // 8):
        rows = pl.ds(8 * tile, 8)
        right = packed_sum(
            lambda t, at: right_next[t, at : at + 8, :], right_coef, 3, tile, tiles, range(1, 4)
        )
        left = packed_sum(
            lambda t, at: left_next[t, at : at + 8, :], left_coef, 3, tile, tiles, range(-3, 0)
        )
        for t in range(tiles):
            edge_two[t, rows, :] = jnp.where(place < 3, right[t], turn(left[t], -3))


def step_two(partial, shifted, edge_one, edge_two, out, field):
    lane = lanes()
    at_edge = (lane < 3) | (lane >= 125)

    def some_stacks(group, carry):
        def edges(packed, k, rows):
            s = group * GROUP + k
            tile = lax.div(s, PER)
            amount = lax.rem(253 - SPAN * (s - PER * tile), 128)
            return jnp.where(at_edge, pltpu.roll(packed[tile, rows, :], amount, 1), 0.0)

        for tile in range(partial.shape[1] // 8):
            rows = pl.ds(8 * tile, 8)
            values = [partial[group * GROUP + k, rows, :] + edges(edge_one, k, rows) for k in range(GROUP)]
            for k in range(GROUP):
                field[k, rows, :] = values[k]
        for tile in range(out.shape[1] // 8):
            total = main_sum(lambda k, at: field[k, at : at + 8, :], shifted, 3, tile)
            rows = pl.ds(8 * tile, 8)
            values = [total[k] + edges(edge_two, k, rows) for k in range(GROUP)]
            for k in range(GROUP):
                out[group * GROUP + k, rows, :] = values[k]
        return carry

    lax.fori_loop(0, out.shape[0] // GROUP, some_stacks, 0)


def local(tracer_mass, recon_table, intersection_weights, intersection_cells, rotation_codes):
    stacks, width, columns = tracer_mass.shape
    shape = lambda *sizes: jax.ShapeDtypeStruct(sizes, F32)
    scratch = lambda *sizes: pltpu.VMEM(sizes, F32)
    edge = -(-(6 * stacks + 3 * OFFSETS) // 8) * 8
    tiles = -(-stacks // PER)
    combos = 4 * (width // 8)

    mass, stencil, send_a, send_b = pl.pallas_call(
        coefficients,
        out_shape=(shape(*tracer_mass.shape), shape(OFFSETS, width, 128), shape(edge, 128), shape(edge, 128)),
        in_specs=[HBM] * 5,
        out_specs=(VMEM,) * 4,
        scratch_shapes=[
            pltpu.SMEM(recon_table.shape, F32),
            scratch(*intersection_weights.shape),
            pltpu.VMEM(intersection_cells.shape, jnp.int32),
            pltpu.VMEM(rotation_codes.shape, jnp.int32),
            scratch(TERMS, combos, 8, 128),
            scratch(25, combos, 8, 128),
            pltpu.SemaphoreType.DMA((5,)),
        ],
        compiler_params=params(),
        cost_estimate=cost(8 * 10**6),
        name="coefficients",
    )(*(
        pltpu.with_memory_space_constraint(value, pltpu.HBM)
        for value in (recon_table, tracer_mass, intersection_weights, intersection_cells, rotation_codes)
    ))
    got_a = swap(send_a, ROW_AXES, False)
    got_b = swap(send_b, ROW_AXES, True)

    own_left, own_right = pl.pallas_call(
        pack_own,
        out_shape=(shape(width * (tiles + 2), 128),) * 2,
        in_specs=[VMEM] * 2,
        out_specs=(VMEM,) * 2,
        compiler_params=params(),
        cost_estimate=cost(10**6),
        name="pack_own",
    )(mass, stencil)

    send = (tiles + 2, width + 16, 128)
    send_a, send_b = pl.pallas_call(
        pack_all,
        out_shape=(shape(*send),) * 2,
        in_specs=[VMEM] * 5,
        out_specs=(VMEM,) * 2,
        scratch_shapes=[scratch(*send)] * 2,
        compiler_params=params(),
        cost_estimate=cost(10**6),
        name="pack_all",
    )(mass, own_left, own_right, got_a, got_b)
    column_a = swap(send_a, COLUMN_AXES, False)
    column_b = swap(send_b, COLUMN_AXES, True)

    partial, wide, shifted = pl.pallas_call(
        step_one,
        out_shape=(
            shape(stacks, width + 8, 128), shape(OFFSETS, width + 8, 128), shape(OFFSETS, width + 8, 128)
        ),
        in_specs=[VMEM] * 4,
        out_specs=(VMEM,) * 3,
        scratch_shapes=[scratch(stacks, width + 16, 128)],
        compiler_params=params(),
        cost_estimate=cost(12 * 10**6),
        name="step_one",
    )(mass, stencil, got_a, got_b)

    tall, low = width + 16, width + 8
    sides = pl.pallas_call(
        side_coefficients,
        out_shape=(shape(tiles, tall, 128),) * 2 + (shape(OFFSETS, low, 128),) * 2,
        in_specs=[VMEM] * 5,
        out_specs=(VMEM,) * 4,
        scratch_shapes=[scratch(2, low, 128)] * 2,
        compiler_params=params(),
        cost_estimate=cost(4 * 10**6),
        name="side_coefficients",
    )(wide, send_a, send_b, column_a, column_b)

    edge_one, edge_two = pl.pallas_call(
        halo_steps,
        out_shape=(shape(tiles, low, 128), shape(tiles, width, 128)),
        in_specs=[VMEM] * 4,
        out_specs=(VMEM,) * 2,
        scratch_shapes=[scratch(tiles, low, 128)] * 2,
        compiler_params=params(),
        cost_estimate=cost(4 * 10**6),
        name="halo_steps",
    )(*sides)

    return pl.pallas_call(
        step_two,
        out_shape=shape(stacks, width, columns),
        in_specs=[VMEM] * 4,
        out_specs=VMEM,
        scratch_shapes=[scratch(GROUP, low, 128)],
        compiler_params=params(),
        cost_estimate=cost(8 * 10**6),
        name="step_two",
    )(partial, shifted, edge_one, edge_two)


def solution(mesh):
    in_specs = (
        P(None, ("face", "px"), "py"),
        P(),
        P(None, None, ("face", "px"), "py"),
        P(None, ("face", "px"), "py"),
        P(None, ("face", "px"), "py"),
    )
    out_specs = P(None, ("face", "px"), "py")
    return jax.shard_map(local, mesh=mesh, in_specs=in_specs, out_specs=out_specs, check_vma=False)
```

```python
import jax
import jax.numpy as jnp
from jax import lax
from jax.experimental import pallas as pl
from jax.experimental.pallas import tpu as pltpu
from jax.sharding import PartitionSpec as P

F32 = jnp.float32
ROW_AXES = ("face", "px")
COLUMN_AXES = "py"
SWAPPED = (0, 2, 1, 5, 4, 3, 9, 8, 7, 6)
POWERS = ((0, 0), (1, 0), (0, 1), (2, 0), (1, 1), (0, 2), (3, 0), (2, 1), (1, 2), (0, 3))
TERMS = 10
OFFSETS = 49
GROUP = 4
SPAN = 9
PER = 14
COEF_PER = 42
VMEM = pl.BlockSpec(memory_space=pltpu.VMEM)
ANY = pl.BlockSpec(memory_space=pl.ANY)
HBM = pl.BlockSpec(memory_space=pltpu.HBM)


def params():
    return pltpu.CompilerParams(vmem_limit_bytes=40 * 1024 * 1024)


def cost(operations):
    return pl.CostEstimate(flops=operations, bytes_accessed=1 << 20, transcendentals=0)


def swap(block, axes, odd_first):
    count = lax.axis_size(axes)
    pairs = []
    for low in range(1 if odd_first else 0, count - 1, 2):
        pairs += [(low, low + 1), (low + 1, low)]
    return lax.ppermute(block, axes, pairs)


def is_even(axes):
    return lax.rem(lax.axis_index(axes), 2) == 0


def turn(value, amount):
    amount %= 128
    return pltpu.roll(value, amount, 1) if amount else value


def lanes(rows=8):
    return lax.broadcasted_iota(jnp.int32, (rows, 128), 1)


def fill_stencil(recon, weights, cells, codes, turned, spread, stencil, tiles):
    zero = jnp.zeros((8, 128), F32)
    for g in range(tiles):
        rows = pl.ds(8 * g, 8)
        for m in range(4):
            code = codes[m, rows, :]
            odd = (code & 1) == 1
            sign_x = jnp.where(code >= 2, -1.0, 1.0).astype(F32)
            sign_y = jnp.where((code == 1) | (code == 2), -1.0, 1.0).astype(F32)
            sign_xy = sign_x * sign_y
            values = [weights[m, t, rows, :] for t in range(TERMS)]
            for t, (a, b) in enumerate(POWERS):
                value = values[t]
                if SWAPPED[t] != t:
                    value = jnp.where(odd, values[SWAPPED[t]], value)
                if a % 2 and b % 2:
                    value = value * sign_xy
                elif a % 2:
                    value = value * sign_x
                elif b % 2:
                    value = value * sign_y
                turned[t, m * tiles + g] = value

    combos = 4 * tiles

    def one_tap(tap, carry):
        total = [None] * combos
        for t in range(TERMS):
            scale = recon[t, tap]
            for c in range(combos):
                term = turned[t, c] * scale
                total[c] = term if t == 0 else total[c] + term
        for c in range(combos):
            spread[tap, c] = total[c]
        return carry

    lax.fori_loop(0, 25, one_tap, 0)

    for g in range(tiles):
        rows = pl.ds(8 * g, 8)
        masks = []
        for m in range(4):
            cell = cells[m, rows, :]
            first = jnp.where(cell < 3, 0, jnp.where(cell < 6, 3, 6))
            across = cell - first
            masks.append((cell < 3, cell < 6, across == 0, across <= 1))
        for ox in range(7):
            total = [None] * 7
            for m in range(4):
                low_x, mid_x, low_y, mid_y = masks[m]

                def tap(jx, jy):
                    if 0 <= jx < 5 and 0 <= jy < 5:
                        return spread[jx * 5 + jy, m * tiles + g]
                    return zero

                line = [
                    jnp.where(low_x, tap(ox, jy), jnp.where(mid_x, tap(ox - 1, jy), tap(ox - 2, jy)))
                    for jy in range(5)
                ]
                padded = [zero, zero] + line + [zero, zero]
                for oy in range(7):
                    value = jnp.where(
                        low_y, padded[oy + 2], jnp.where(mid_y, padded[oy + 1], padded[oy])
                    )
                    total[oy] = value if m == 0 else total[oy] + value
            for oy in range(7):
                stencil[ox * 7 + oy, rows, :] = total[oy]


def coefficients(
    recon_hbm, mass_hbm, weights_hbm, cells_hbm, codes_hbm, mass, stencil, send_a, send_b,
    recon, weights, cells, codes, turned, spread, sems,
):
    sources = (recon_hbm, codes_hbm, weights_hbm, cells_hbm, mass_hbm)
    targets = (recon, codes, weights, cells, mass)
    copies = [pltpu.make_async_copy(a, b, sems.at[i]) for i, (a, b) in enumerate(zip(sources, targets))]
    for copy in copies:
        copy.start()
    for copy in copies:
        copy.wait()
    stacks, width = mass.shape[:2]
    fill_stencil(recon, weights, cells, codes, turned, spread, stencil, width // 8)
    even = is_even(ROW_AXES)
    for send, low_edge in ((send_a, jnp.logical_not(even)), (send_b, even)):
        mass_at = jnp.where(low_edge, 0, width - 6)
        stencil_at = jnp.where(low_edge, 0, width - 3)
        for s in range(stacks):
            send[6 * s : 6 * s + 6, :] = mass[s, pl.ds(mass_at, 6), :]
        for o in range(OFFSETS):
            at = 6 * stacks + 3 * o
            send[at : at + 3, :] = stencil[o, pl.ds(stencil_at, 3), :]


def pack_stacks(load, stacks, tile):
    lane = lanes()
    left = jnp.zeros((8, 128), F32)
    right = jnp.zeros((8, 128), F32)
    for s in range(PER * tile, min(stacks, PER * tile + PER)):
        at = SPAN * (s % PER)
        value = load(s)
        left = jnp.where((lane >= at + 3) & (lane < at + 9), turn(value, at + 3), left)
        right = jnp.where((lane >= at) & (lane < at + 6), turn(value, at - 122), right)
    return left, right


def pack_coefficients(load, tile):
    lane = lanes()
    left = jnp.zeros((8, 128), F32)
    right = jnp.zeros((8, 128), F32)
    for o in range(COEF_PER * tile, min(OFFSETS, COEF_PER * tile + COEF_PER)):
        at = 3 * (o % COEF_PER)
        here = (lane >= at) & (lane < at + 3)
        value = load(o)
        left = jnp.where(here, turn(value, at), left)
        right = jnp.where(here, turn(value, at - 125), right)
    return left, right


def fill_picks(picks):
    lane = lanes(1)
    group = (lane * 57) >> 9
    at = lane - SPAN * group
    source = lax.broadcasted_iota(jnp.int32, (128, 128), 0)
    for dy in range(-3, 4):
        q = at - dy
        halo = (q >= 3) & (q < 6)
        right = jnp.where(halo, 57 + q, jnp.where((q >= 0) & (q < 3) & (at >= 3), 125 + q, -1))
        left = jnp.where(halo, 61 + q, jnp.where((q >= 6) & (q < 9) & (at < 6), q - 6, -1))
        for side, wanted in enumerate((right, left)):
            wanted = jnp.where(group < PER, wanted, -1)
            picked = jnp.where(source == wanted, 1.0, 0.0).astype(jnp.bfloat16)
            picks[dy + 3, 0:128, 128 * side : 128 * side + 128] = picked
            picks[dy + 3, 128:256, 128 * side : 128 * side + 128] = picked


def pack_own(mass, stencil, left, right, picks):
    fill_picks(picks)
    stacks, width = mass.shape[:2]
    tiles = -(-stacks // PER)
    for half in range(width // 8):
        rows = pl.ds(8 * half, 8)
        for tile in range(tiles):
            at = width * tile + 8 * half
            left[at : at + 8, :], right[at : at + 8, :] = pack_stacks(
                lambda s: mass[s, rows, :], stacks, tile
            )
        for tile in range(2):
            at = width * (tiles + tile) + 8 * half
            left[at : at + 8, :], right[at : at + 8, :] = pack_coefficients(
                lambda o: stencil[o, rows, :], tile
            )


def join_halo(own_left, own_right, got_a, got_b, send_left, send_right, stacks, width):
    tiles = -(-stacks // PER)
    for send, own in ((send_left, own_left), (send_right, own_right)):
        for tile in range(tiles):
            send[tile, 0:width, :] = own[width * tile : width * tile + width, :]
            send[tile, width + 12 : width + 16, :] = jnp.zeros((4, 128), F32)
        for tile in range(2):
            at = width * (tiles + tile)
            send[tiles + tile, 0:width, :] = own[at : at + width, :]
            send[tiles + tile, width + 6 : width + 16, :] = jnp.zeros((10, 128), F32)

    def place(above, below):
        for got, mass_at, coef_at in ((above, width, width), (below, width + 6, width + 3)):
            for tile in range(tiles):
                left, right = pack_stacks(lambda s: got[6 * s : 6 * s + 8, :], stacks, tile)
                send_left[tile, mass_at : mass_at + 6, :] = left[0:6]
                send_right[tile, mass_at : mass_at + 6, :] = right[0:6]
            for tile in range(2):
                base = 6 * stacks
                left, right = pack_coefficients(lambda o: got[base + 3 * o : base + 3 * o + 8, :], tile)
                send_left[tiles + tile, coef_at : coef_at + 3, :] = left[0:3]
                send_right[tiles + tile, coef_at : coef_at + 3, :] = right[0:3]

    even = is_even(ROW_AXES)

    @pl.when(even)
    def _():
        place(got_b, got_a)

    @pl.when(jnp.logical_not(even))
    def _():
        place(got_a, got_b)


def choose(even, first, second, first_out, second_out):
    @pl.when(even)
    def _():
        first_out[...] = first[...]
        second_out[...] = second[...]

    @pl.when(jnp.logical_not(even))
    def _():
        first_out[...] = second[...]
        second_out[...] = first[...]


def pack_all(mass, own_left, own_right, got_a, got_b, send_a, send_b, left, right):
    stacks, width = mass.shape[:2]
    join_halo(own_left, own_right, got_a, got_b, left, right, stacks, width)
    choose(is_even(COLUMN_AXES), right, left, send_a, send_b)


def main_sum(load, coef, coef_at, tile):
    fields = [[load(k, 8 * tile + dx) for k in range(GROUP)] for dx in range(7)]
    total = [None] * GROUP
    for dy in range(7):
        part = [None] * GROUP
        for dx in range(7):
            at = coef_at + 8 * tile
            scale = coef[dx * 7 + dy, at : at + 8, :]
            for k in range(GROUP):
                term = scale * fields[dx][k]
                part[k] = term if dx == 0 else part[k] + term
        for k in range(GROUP):
            moved = turn(part[k], 3 - dy)
            total[k] = moved if dy == 0 else total[k] + moved
    return total


def some_steps(field, shifted, partial, stacks, first):
    def some_stacks(group, carry):
        for tile in range(partial.shape[1] // 8):
            total = main_sum(
                lambda k, at: field[first + group * GROUP + k, at : at + 8, :], shifted, 0, tile
            )
            for k in range(GROUP):
                partial[group * GROUP + k, 8 * tile : 8 * tile + 8, :] = total[k]
        return carry

    lax.fori_loop(0, stacks // GROUP, some_stacks, 0)


def hand_on(send, got, partial, out):
    out[...] = send[...]


def step_one(mass, stencil, got_a, got_b, partial, wide, shifted, field):
    stacks, width = mass.shape[:2]

    def place(above, below):
        for s in range(stacks):
            field[s, 0:6, :] = above[6 * s : 6 * s + 6, :]
            field[s, width + 6 : width + 12, :] = below[6 * s : 6 * s + 6, :]
        for o in range(OFFSETS):
            at = 6 * stacks + 3 * o
            wide[o, 0:3, :] = above[at : at + 3, :]
            wide[o, width + 3 : width + 6, :] = below[at : at + 3, :]

    even = is_even(ROW_AXES)

    @pl.when(even)
    def _():
        place(got_b, got_a)

    @pl.when(jnp.logical_not(even))
    def _():
        place(got_a, got_b)

    for s in range(stacks):
        field[s, 6 : width + 6, :] = mass[s, :, :]
        field[s, width + 12 : width + 16, :] = jnp.zeros((4, 128), F32)
    for o in range(OFFSETS):
        wide[o, 3 : width + 3, :] = stencil[o, :, :]
        wide[o, width + 6 : width + 8, :] = jnp.zeros((2, 128), F32)
    lane = lanes()
    for tile in range((width + 8) // 8):
        rows = pl.ds(8 * tile, 8)
        for dy in range(-3, 4):
            values = [turn(wide[dx * 7 + dy + 3, rows, :], dy) for dx in range(7)]
            if dy > 0:
                values = [jnp.where(lane >= dy, value, 0.0) for value in values]
            elif dy < 0:
                values = [jnp.where(lane < 128 + dy, value, 0.0) for value in values]
            for dx in range(7):
                shifted[dx * 7 + dy + 3, rows, :] = values[dx]
    some_steps(field, shifted, partial, partial.shape[0], 0)


def more_step_one(field, shifted, partial, own_shifted):
    width = own_shifted.shape[1]
    for o in range(OFFSETS):
        own_shifted[o, :, :] = shifted[o, 3 : width + 3, :]
    some_steps(field, shifted, partial, partial.shape[0], field.shape[0] - partial.shape[0])


def packed_sum(load, coef, coef_at, tile, tiles, dys):
    fields = [[load(t, 8 * tile + dx) for t in range(tiles)] for dx in range(7)]
    total = [None] * tiles
    for dy in dys:
        part = [None] * tiles
        for dx in range(7):
            at = coef_at + 8 * tile
            scale = coef[dx * 7 + dy + 3, at : at + 8, :]
            for t in range(tiles):
                term = scale * fields[dx][t]
                part[t] = term if dx == 0 else part[t] + term
        for t in range(tiles):
            moved = turn(part[t], -dy)
            total[t] = moved if total[t] is None else total[t] + moved
    return total


def place_in_group(rows=8):
    lane = lanes(rows)
    return lane - SPAN * ((lane * 57) >> 9)


def side_coefficients(
    wide, send_a, send_b, got_a, got_b, picks,
    right_set, left_set, right_coef, left_coef, right_halo, left_halo, rows_of,
):
    tall = wide.shape[1]
    width = tall - 8
    tiles = right_set.shape[0]
    lane = lanes()

    def gather(sent_right, sent_left, from_right, from_left):
        place = place_in_group(width + 16)
        for tile in range(tiles):
            right = jnp.where(place < 3, turn(sent_right[tile], -3), from_right[tile])
            left = jnp.where(place >= 6, turn(sent_left[tile], 3), from_left[tile])
            for target, value in ((right_set, right), (left_set, left)):
                target[tile, 6 : width + 6, :] = value[0:width]
                target[tile, 0:6, :] = value[width : width + 6]
                target[tile, width + 6 : width + 16, :] = value[width + 6 : width + 16]
        for tile in range(2):
            for target, source in ((right_halo, from_right), (left_halo, from_left)):
                target[tile, 3 : width + 3, :] = source[tiles + tile, 0:width, :]
                target[tile, 0:3, :] = source[tiles + tile, width : width + 3, :]
                target[tile, width + 3 : width + 8, :] = source[tiles + tile, width + 3 : width + 8, :]

    even = is_even(COLUMN_AXES)

    @pl.when(even)
    def _():
        gather(send_a, send_b, got_a, got_b)

    @pl.when(jnp.logical_not(even))
    def _():
        gather(send_b, send_a, got_b, got_a)

    from_right = (lane >= 60) & (lane < 63)
    from_left = (lane >= 64) & (lane < 67)
    for tile in range(tall // 8):
        rows = pl.ds(8 * tile, 8)
        right_rows = [right_halo[t, rows, :] for t in range(2)]
        left_rows = [left_halo[t, rows, :] for t in range(2)]
        for dy in range(7):
            values = []
            for dx in range(7):
                o = dx * 7 + dy
                at = 3 * (o % COEF_PER)
                right = turn(right_rows[o // COEF_PER], 60 - at)
                left = turn(left_rows[o // COEF_PER], 64 - at)
                values.append(
                    jnp.where(from_right, right, jnp.where(from_left, left, wide[o, rows, :]))
                )
            for dx in range(7):
                at = tall * dx + 8 * tile
                rows_of[dy, at : at + 8, :] = values[dx]

    for dy in range(7):
        value = rows_of[dy]
        high = value.astype(jnp.bfloat16)
        low = (value - high.astype(F32)).astype(jnp.bfloat16)
        both = jnp.concatenate([high, low], axis=1)
        spread = jnp.dot(both, picks[dy], preferred_element_type=F32)
        for dx in range(7):
            right_coef[dx * 7 + dy, :, :] = spread[tall * dx : tall * dx + tall, 0:128]
            left_coef[dx * 7 + dy, :, :] = spread[tall * dx : tall * dx + tall, 128:256]


def halo_steps(
    right_set, left_set, right_coef, left_coef, partial, more_partial, field, edges,
    edge_one, edge_two, right_next, left_next,
):
    tiles = right_set.shape[0]
    place = place_in_group()
    everywhere = range(-3, 4)
    for tile in range(edge_one.shape[1] // 8):
        rows = pl.ds(8 * tile, 8)
        right = packed_sum(
            lambda t, at: right_set[t, at : at + 8, :], right_coef, 0, tile, tiles, everywhere
        )
        left = packed_sum(
            lambda t, at: left_set[t, at : at + 8, :], left_coef, 0, tile, tiles, everywhere
        )
        halo = (place >= 3) & (place < 6)
        for t in range(tiles):
            right_next[t, rows, :] = jnp.where(halo, right[t], 0.0)
            left_next[t, rows, :] = jnp.where(halo, left[t], 0.0)
            edge_one[t, rows, :] = jnp.where(place < 3, right[t], turn(left[t], -3))
    for tile in range(edge_two.shape[1] // 8):
        rows = pl.ds(8 * tile, 8)
        right = packed_sum(
            lambda t, at: right_next[t, at : at + 8, :], right_coef, 3, tile, tiles, range(1, 4)
        )
        left = packed_sum(
            lambda t, at: left_next[t, at : at + 8, :], left_coef, 3, tile, tiles, range(-3, 0)
        )
        for t in range(tiles):
            edge_two[t, rows, :] = jnp.where(place < 3, right[t], turn(left[t], -3))

    lane = lanes()
    at_edge = (lane < 3) | (lane >= 125)
    stacks, more = field.shape[0], partial.shape[0]
    for t in range(tiles):
        members = range(PER * t, min(stacks, PER * t + PER))
        for tile in range(edge_one.shape[1] // 8):
            rows = pl.ds(8 * tile, 8)
            packed = edge_one[t, rows, :]
            values = []
            for s in members:
                value = partial[s, rows, :] if s < more else more_partial[s - more, rows, :]
                values.append(value + jnp.where(at_edge, turn(packed, 125 - SPAN * (s % PER)), 0.0))
            for s, value in zip(members, values):
                field[s, rows, :] = value
        for tile in range(edge_two.shape[1] // 8):
            rows = pl.ds(8 * tile, 8)
            packed = edge_two[t, rows, :]
            values = [jnp.where(at_edge, turn(packed, 125 - SPAN * (s % PER)), 0.0) for s in members]
            for s, value in zip(members, values):
                edges[s, rows, :] = value


def step_two(field, own_shifted, edges, out):
    def some_stacks(group, carry):
        for tile in range(out.shape[1] // 8):
            total = main_sum(lambda k, at: field[group * GROUP + k, at : at + 8, :], own_shifted, 0, tile)
            rows = pl.ds(8 * tile, 8)
            values = [total[k] + edges[group * GROUP + k, rows, :] for k in range(GROUP)]
            for k in range(GROUP):
                out[group * GROUP + k, rows, :] = values[k]
        return carry

    lax.fori_loop(0, out.shape[0] // GROUP, some_stacks, 0)


def local(tracer_mass, recon_table, intersection_weights, intersection_cells, rotation_codes):
    stacks, width, columns = tracer_mass.shape
    shape = lambda *sizes: jax.ShapeDtypeStruct(sizes, F32)
    scratch = lambda *sizes: pltpu.VMEM(sizes, F32)
    edge = -(-(6 * stacks + 3 * OFFSETS) // 8) * 8
    tiles = -(-stacks // PER)
    combos = 4 * (width // 8)

    mass, stencil, send_a, send_b = pl.pallas_call(
        coefficients,
        out_shape=(shape(*tracer_mass.shape), shape(OFFSETS, width, 128), shape(edge, 128), shape(edge, 128)),
        in_specs=[HBM] * 5,
        out_specs=(VMEM,) * 4,
        scratch_shapes=[
            pltpu.SMEM(recon_table.shape, F32),
            scratch(*intersection_weights.shape),
            pltpu.VMEM(intersection_cells.shape, jnp.int32),
            pltpu.VMEM(rotation_codes.shape, jnp.int32),
            scratch(TERMS, combos, 8, 128),
            scratch(25, combos, 8, 128),
            pltpu.SemaphoreType.DMA((5,)),
        ],
        compiler_params=params(),
        cost_estimate=cost(8 * 10**6),
        name="coefficients",
    )(*(
        pltpu.with_memory_space_constraint(value, pltpu.HBM)
        for value in (recon_table, tracer_mass, intersection_weights, intersection_cells, rotation_codes)
    ))
    got_a = swap(send_a, ROW_AXES, False)
    got_b = swap(send_b, ROW_AXES, True)

    tall, low = width + 16, width + 8
    picks = jax.ShapeDtypeStruct((7, 256, 256), jnp.bfloat16)
    own_left, own_right, picks = pl.pallas_call(
        pack_own,
        out_shape=(shape(width * (tiles + 2), 128),) * 2 + (picks,),
        in_specs=[VMEM] * 2,
        out_specs=(VMEM,) * 3,
        compiler_params=params(),
        cost_estimate=cost(10**6),
        name="pack_own",
    )(mass, stencil)

    send = (tiles + 2, tall, 128)
    send_a, send_b = pl.pallas_call(
        pack_all,
        out_shape=(shape(*send),) * 2,
        in_specs=[VMEM] * 5,
        out_specs=(VMEM,) * 2,
        scratch_shapes=[scratch(*send)] * 2,
        compiler_params=params(),
        cost_estimate=cost(10**6),
        name="pack_all",
    )(mass, own_left, own_right, got_a, got_b)
    column_a = swap(send_a, COLUMN_AXES, False)

    later = GROUP * (stacks // (2 * GROUP) - 1)
    partial, wide, shifted, field = pl.pallas_call(
        step_one,
        out_shape=(
            shape(stacks - later, low, 128), shape(OFFSETS, low, 128), shape(OFFSETS, low, 128),
            shape(stacks, tall, 128),
        ),
        in_specs=[VMEM] * 4,
        out_specs=(VMEM,) * 4,
        compiler_params=params(),
        cost_estimate=cost(8 * 10**6),
        name="step_one",
    )(mass, stencil, got_a, got_b)

    send_b = pl.pallas_call(
        hand_on,
        out_shape=shape(*send),
        in_specs=[VMEM, ANY, ANY],
        out_specs=VMEM,
        compiler_params=params(),
        cost_estimate=cost(10**4),
        name="hand_on",
    )(send_b, column_a, partial)
    column_b = swap(send_b, COLUMN_AXES, True)

    more_partial, own_shifted = pl.pallas_call(
        more_step_one,
        out_shape=(shape(later, low, 128), shape(OFFSETS, width, 128)),
        in_specs=[VMEM] * 2,
        out_specs=(VMEM,) * 2,
        compiler_params=params(),
        cost_estimate=cost(4 * 10**6),
        name="more_step_one",
    )(field, shifted)

    sides = pl.pallas_call(
        side_coefficients,
        out_shape=(shape(tiles, tall, 128),) * 2 + (shape(OFFSETS, low, 128),) * 2,
        in_specs=[VMEM] * 6,
        out_specs=(VMEM,) * 4,
        scratch_shapes=[scratch(2, low, 128)] * 2 + [scratch(7, 7 * low, 128)],
        compiler_params=params(),
        cost_estimate=cost(4 * 10**6),
        name="side_coefficients",
    )(wide, send_a, send_b, column_a, column_b, picks)

    field, edges = pl.pallas_call(
        halo_steps,
        out_shape=(shape(stacks, low, 128), shape(stacks, width, 128)),
        in_specs=[VMEM] * 6,
        out_specs=(VMEM,) * 2,
        scratch_shapes=[scratch(tiles, low, 128), scratch(tiles, width, 128)] + [scratch(tiles, low, 128)] * 2,
        compiler_params=params(),
        cost_estimate=cost(4 * 10**6),
        name="halo_steps",
    )(*sides, partial, more_partial)

    return pl.pallas_call(
        step_two,
        out_shape=shape(stacks, width, columns),
        in_specs=[VMEM] * 3,
        out_specs=VMEM,
        compiler_params=params(),
        cost_estimate=cost(8 * 10**6),
        name="step_two",
    )(field, own_shifted, edges)


def solution(mesh):
    in_specs = (
        P(None, ("face", "px"), "py"),
        P(),
        P(None, None, ("face", "px"), "py"),
        P(None, ("face", "px"), "py"),
        P(None, ("face", "px"), "py"),
    )
    out_specs = P(None, ("face", "px"), "py")
    return jax.shard_map(local, mesh=mesh, in_specs=in_specs, out_specs=out_specs, check_vma=False)
```

```python
import jax
import jax.numpy as jnp
from jax import lax
from jax.experimental import pallas as pl
from jax.experimental.pallas import tpu as pltpu
from jax.sharding import PartitionSpec as P

F32 = jnp.float32
ROW_AXES = ("face", "px")
COLUMN_AXES = "py"
SWAPPED = (0, 2, 1, 5, 4, 3, 9, 8, 7, 6)
POWERS = ((0, 0), (1, 0), (0, 1), (2, 0), (1, 1), (0, 2), (3, 0), (2, 1), (1, 2), (0, 3))
TERMS = 10
OFFSETS = 49
GROUP = 4
SPAN = 9
PER = 14
COEF_PER = 42
VMEM = pl.BlockSpec(memory_space=pltpu.VMEM)
HBM = pl.BlockSpec(memory_space=pltpu.HBM)


def params():
    return pltpu.CompilerParams(vmem_limit_bytes=40 * 1024 * 1024)


def cost(operations):
    return pl.CostEstimate(flops=operations, bytes_accessed=1 << 20, transcendentals=0)


def swap(block, axes, odd_first):
    count = lax.axis_size(axes)
    partner = list(range(count))
    for low in range(1 if odd_first else 0, count, 2):
        high = (low + 1) % count
        partner[low], partner[high] = high, low
    return lax.ppermute(block, axes, list(enumerate(partner)))


def shift(block, axes, step):
    count = lax.axis_size(axes)
    return lax.ppermute(block, axes, [(index, (index + step) % count) for index in range(count)])


def ends(axes):
    index = lax.axis_index(axes)
    return index == 0, index == lax.axis_size(axes) - 1


def is_even(axes):
    return lax.rem(lax.axis_index(axes), 2) == 0


def turn(value, amount):
    amount %= 128
    return pltpu.roll(value, amount, 1) if amount else value


def lanes(rows=8):
    return lax.broadcasted_iota(jnp.int32, (rows, 128), 1)


def fill_stencil(recon, weights, cells, codes, turned, spread, stencil, tiles):
    zero = jnp.zeros((8, 128), F32)
    for g in range(tiles):
        rows = pl.ds(8 * g, 8)
        for m in range(4):
            code = codes[m, rows, :]
            odd = (code & 1) == 1
            sign_x = jnp.where(code >= 2, -1.0, 1.0).astype(F32)
            sign_y = jnp.where((code == 1) | (code == 2), -1.0, 1.0).astype(F32)
            sign_xy = sign_x * sign_y
            values = [weights[m, t, rows, :] for t in range(TERMS)]
            for t, (a, b) in enumerate(POWERS):
                value = values[t]
                if SWAPPED[t] != t:
                    value = jnp.where(odd, values[SWAPPED[t]], value)
                if a % 2 and b % 2:
                    value = value * sign_xy
                elif a % 2:
                    value = value * sign_x
                elif b % 2:
                    value = value * sign_y
                turned[t, m * tiles + g] = value

    combos = 4 * tiles

    def one_tap(tap, carry):
        total = [None] * combos
        for t in range(TERMS):
            scale = recon[t, tap]
            for c in range(combos):
                term = turned[t, c] * scale
                total[c] = term if t == 0 else total[c] + term
        for c in range(combos):
            spread[tap, c] = total[c]
        return carry

    lax.fori_loop(0, 25, one_tap, 0)

    for g in range(tiles):
        rows = pl.ds(8 * g, 8)
        masks = []
        for m in range(4):
            cell = cells[m, rows, :]
            first = jnp.where(cell < 3, 0, jnp.where(cell < 6, 3, 6))
            across = cell - first
            masks.append((cell < 3, cell < 6, across == 0, across <= 1))
        for ox in range(7):
            total = [None] * 7
            for m in range(4):
                low_x, mid_x, low_y, mid_y = masks[m]

                def tap(jx, jy):
                    if 0 <= jx < 5 and 0 <= jy < 5:
                        return spread[jx * 5 + jy, m * tiles + g]
                    return zero

                line = [
                    jnp.where(low_x, tap(ox, jy), jnp.where(mid_x, tap(ox - 1, jy), tap(ox - 2, jy)))
                    for jy in range(5)
                ]
                padded = [zero, zero] + line + [zero, zero]
                for oy in range(7):
                    value = jnp.where(
                        low_y, padded[oy + 2], jnp.where(mid_y, padded[oy + 1], padded[oy])
                    )
                    total[oy] = value if m == 0 else total[oy] + value
            for oy in range(7):
                stencil[ox * 7 + oy, rows, :] = total[oy]


def coefficients(
    recon_hbm, mass_hbm, weights_hbm, cells_hbm, codes_hbm, mass, stencil, send_down, send_up,
    recon, weights, cells, codes, turned, spread, sems,
):
    sources = (recon_hbm, codes_hbm, weights_hbm, cells_hbm, mass_hbm)
    targets = (recon, codes, weights, cells, mass)
    copies = [pltpu.make_async_copy(a, b, sems.at[i]) for i, (a, b) in enumerate(zip(sources, targets))]
    for copy in copies:
        copy.start()
    for copy in copies:
        copy.wait()
    stacks, width = mass.shape[:2]
    fill_stencil(recon, weights, cells, codes, turned, spread, stencil, width // 8)
    for send, mass_at, stencil_at in ((send_down, width - 6, width - 3), (send_up, 0, 0)):
        for s in range(stacks):
            send[6 * s : 6 * s + 6, :] = mass[s, mass_at : mass_at + 6, :]
        for o in range(OFFSETS):
            at = 6 * stacks + 3 * o
            send[at : at + 3, :] = stencil[o, stencil_at : stencil_at + 3, :]


def pack_stacks(load, stacks, tile):
    lane = lanes()
    left = jnp.zeros((8, 128), F32)
    right = jnp.zeros((8, 128), F32)
    for s in range(PER * tile, min(stacks, PER * tile + PER)):
        at = SPAN * (s % PER)
        value = load(s)
        left = jnp.where((lane >= at + 3) & (lane < at + 9), turn(value, at + 3), left)
        right = jnp.where((lane >= at) & (lane < at + 6), turn(value, at - 122), right)
    return left, right


def pack_coefficients(load, tile):
    lane = lanes()
    left = jnp.zeros((8, 128), F32)
    right = jnp.zeros((8, 128), F32)
    for o in range(COEF_PER * tile, min(OFFSETS, COEF_PER * tile + COEF_PER)):
        at = 3 * (o % COEF_PER)
        here = (lane >= at) & (lane < at + 3)
        value = load(o)
        left = jnp.where(here, turn(value, at), left)
        right = jnp.where(here, turn(value, at - 125), right)
    return left, right


def fill_picks(picks):
    lane = lanes(1)
    group = (lane * 57) >> 9
    at = lane - SPAN * group
    source = lax.broadcasted_iota(jnp.int32, (128, 128), 0)
    for dy in range(-3, 4):
        q = at - dy
        halo = (q >= 3) & (q < 6)
        right = jnp.where(halo, 57 + q, jnp.where((q >= 0) & (q < 3) & (at >= 3), 125 + q, -1))
        left = jnp.where(halo, 61 + q, jnp.where((q >= 6) & (q < 9) & (at < 6), q - 6, -1))
        for side, wanted in enumerate((right, left)):
            wanted = jnp.where(group < PER, wanted, -1)
            picked = jnp.where(source == wanted, 1.0, 0.0).astype(jnp.bfloat16)
            picks[dy + 3, 0:128, 128 * side : 128 * side + 128] = picked
            picks[dy + 3, 128:256, 128 * side : 128 * side + 128] = picked


def pack_own(mass, stencil, left, right, picks):
    fill_picks(picks)
    stacks, width = mass.shape[:2]
    tiles = -(-stacks // PER)
    for half in range(width // 8):
        rows = pl.ds(8 * half, 8)
        for tile in range(tiles):
            at = width * tile + 8 * half
            left[at : at + 8, :], right[at : at + 8, :] = pack_stacks(
                lambda s: mass[s, rows, :], stacks, tile
            )
        for tile in range(2):
            at = width * (tiles + tile) + 8 * half
            left[at : at + 8, :], right[at : at + 8, :] = pack_coefficients(
                lambda o: stencil[o, rows, :], tile
            )


def join_halo(own_left, own_right, above, below, send_left, send_right, stacks, width):
    tiles = -(-stacks // PER)
    for send, own in ((send_left, own_left), (send_right, own_right)):
        for tile in range(tiles):
            send[tile, 0:width, :] = own[width * tile : width * tile + width, :]
            send[tile, width + 12 : width + 16, :] = jnp.zeros((4, 128), F32)
        for tile in range(2):
            at = width * (tiles + tile)
            send[tiles + tile, 0:width, :] = own[at : at + width, :]
            send[tiles + tile, width + 6 : width + 16, :] = jnp.zeros((10, 128), F32)

    first, last = ends(ROW_AXES)
    for got, outside, mass_at, coef_at in (
        (above, first, width, width), (below, last, width + 6, width + 3)
    ):
        for tile in range(tiles):
            left, right = pack_stacks(lambda s: got[6 * s : 6 * s + 8, :], stacks, tile)
            send_left[tile, mass_at : mass_at + 6, :] = jnp.where(outside, 0.0, left[0:6])
            send_right[tile, mass_at : mass_at + 6, :] = jnp.where(outside, 0.0, right[0:6])
        for tile in range(2):
            base = 6 * stacks
            left, right = pack_coefficients(lambda o: got[base + 3 * o : base + 3 * o + 8, :], tile)
            send_left[tiles + tile, coef_at : coef_at + 3, :] = jnp.where(outside, 0.0, left[0:3])
            send_right[tiles + tile, coef_at : coef_at + 3, :] = jnp.where(outside, 0.0, right[0:3])


def choose(even, first, second, first_out, second_out):
    @pl.when(even)
    def _():
        first_out[...] = first[...]
        second_out[...] = second[...]

    @pl.when(jnp.logical_not(even))
    def _():
        first_out[...] = second[...]
        second_out[...] = first[...]


def pack_all(mass, own_left, own_right, above, below, send_a, send_b, left, right):
    stacks, width = mass.shape[:2]
    join_halo(own_left, own_right, above, below, left, right, stacks, width)
    choose(is_even(COLUMN_AXES), right, left, send_a, send_b)


def main_sum(load, coef, coef_at, tile):
    fields = [[load(k, 8 * tile + dx) for k in range(GROUP)] for dx in range(7)]
    total = [None] * GROUP
    for dy in range(7):
        part = [None] * GROUP
        for dx in range(7):
            at = coef_at + 8 * tile
            scale = coef[dx * 7 + dy, at : at + 8, :]
            for k in range(GROUP):
                term = scale * fields[dx][k]
                part[k] = term if dx == 0 else part[k] + term
        for k in range(GROUP):
            moved = turn(part[k], 3 - dy)
            total[k] = moved if dy == 0 else total[k] + moved
    return total


def step_one(mass, stencil, above, below, partial, wide, shifted, own_shifted, field):
    stacks, width = mass.shape[:2]
    first, last = ends(ROW_AXES)
    for s in range(stacks):
        at = 6 * s
        field[s, 0:6, :] = jnp.where(first, 0.0, above[at : at + 6, :])
        field[s, 6 : width + 6, :] = mass[s, :, :]
        field[s, width + 6 : width + 12, :] = jnp.where(last, 0.0, below[at : at + 6, :])
        field[s, width + 12 : width + 16, :] = jnp.zeros((4, 128), F32)
    for o in range(OFFSETS):
        at = 6 * stacks + 3 * o
        wide[o, 0:3, :] = jnp.where(first, 0.0, above[at : at + 3, :])
        wide[o, 3 : width + 3, :] = stencil[o, :, :]
        wide[o, width + 3 : width + 6, :] = jnp.where(last, 0.0, below[at : at + 3, :])
        wide[o, width + 6 : width + 8, :] = jnp.zeros((2, 128), F32)
    lane = lanes()
    for tile in range((width + 8) // 8):
        rows = pl.ds(8 * tile, 8)
        for dy in range(-3, 4):
            values = [turn(wide[dx * 7 + dy + 3, rows, :], dy) for dx in range(7)]
            if dy > 0:
                values = [jnp.where(lane >= dy, value, 0.0) for value in values]
            elif dy < 0:
                values = [jnp.where(lane < 128 + dy, value, 0.0) for value in values]
            for dx in range(7):
                shifted[dx * 7 + dy + 3, rows, :] = values[dx]
    for o in range(OFFSETS):
        own_shifted[o, :, :] = shifted[o, 3 : width + 3, :]

    def some_stacks(group, carry):
        for tile in range(partial.shape[1] // 8):
            total = main_sum(lambda k, at: field[group * GROUP + k, at : at + 8, :], shifted, 0, tile)
            for k in range(GROUP):
                partial[group * GROUP + k, 8 * tile : 8 * tile + 8, :] = total[k]
        return carry

    lax.fori_loop(0, stacks // GROUP, some_stacks, 0)


def packed_sum(load, coef, coef_at, tile, tiles, dys):
    fields = [[load(t, 8 * tile + dx) for t in range(tiles)] for dx in range(7)]
    total = [None] * tiles
    for dy in dys:
        part = [None] * tiles
        for dx in range(7):
            at = coef_at + 8 * tile
            scale = coef[dx * 7 + dy + 3, at : at + 8, :]
            for t in range(tiles):
                term = scale * fields[dx][t]
                part[t] = term if dx == 0 else part[t] + term
        for t in range(tiles):
            moved = turn(part[t], -dy)
            total[t] = moved if total[t] is None else total[t] + moved
    return total


def place_in_group(rows=8):
    lane = lanes(rows)
    return lane - SPAN * ((lane * 57) >> 9)


def side_coefficients(
    wide, send_a, send_b, got_a, got_b, picks,
    right_set, left_set, right_coef, left_coef, right_halo, left_halo, rows_of,
):
    tall = wide.shape[1]
    width = tall - 8
    tiles = right_set.shape[0]
    lane = lanes()

    first, last = ends(COLUMN_AXES)

    def gather(sent_right, sent_left, got_right, got_left):
        place = place_in_group(width + 16)
        from_right = [jnp.where(last, 0.0, got_right[tile]) for tile in range(tiles + 2)]
        from_left = [jnp.where(first, 0.0, got_left[tile]) for tile in range(tiles + 2)]
        for tile in range(tiles):
            right = jnp.where(place < 3, turn(sent_right[tile], -3), from_right[tile])
            left = jnp.where(place >= 6, turn(sent_left[tile], 3), from_left[tile])
            for target, value in ((right_set, right), (left_set, left)):
                target[tile, 6 : width + 6, :] = value[0:width]
                target[tile, 0:6, :] = value[width : width + 6]
                target[tile, width + 6 : width + 16, :] = value[width + 6 : width + 16]
        for tile in range(2):
            for target, source in ((right_halo, from_right), (left_halo, from_left)):
                value = source[tiles + tile]
                target[tile, 3 : width + 3, :] = value[0:width]
                target[tile, 0:3, :] = value[width : width + 3]
                target[tile, width + 3 : width + 8, :] = value[width + 3 : width + 8]

    even = is_even(COLUMN_AXES)

    @pl.when(even)
    def _():
        gather(send_a, send_b, got_a, got_b)

    @pl.when(jnp.logical_not(even))
    def _():
        gather(send_b, send_a, got_b, got_a)

    from_right = (lane >= 60) & (lane < 63)
    from_left = (lane >= 64) & (lane < 67)
    for tile in range(tall // 8):
        rows = pl.ds(8 * tile, 8)
        right_rows = [right_halo[t, rows, :] for t in range(2)]
        left_rows = [left_halo[t, rows, :] for t in range(2)]
        for dy in range(7):
            values = []
            for dx in range(7):
                o = dx * 7 + dy
                at = 3 * (o % COEF_PER)
                right = turn(right_rows[o // COEF_PER], 60 - at)
                left = turn(left_rows[o // COEF_PER], 64 - at)
                values.append(
                    jnp.where(from_right, right, jnp.where(from_left, left, wide[o, rows, :]))
                )
            for dx in range(7):
                at = tall * dx + 8 * tile
                rows_of[dy, at : at + 8, :] = values[dx]

    for dy in range(7):
        value = rows_of[dy]
        high = value.astype(jnp.bfloat16)
        low = (value - high.astype(F32)).astype(jnp.bfloat16)
        both = jnp.concatenate([high, low], axis=1)
        spread = jnp.dot(both, picks[dy], preferred_element_type=F32)
        for dx in range(7):
            right_coef[dx * 7 + dy, :, :] = spread[tall * dx : tall * dx + tall, 0:128]
            left_coef[dx * 7 + dy, :, :] = spread[tall * dx : tall * dx + tall, 128:256]


def halo_steps(
    right_set, left_set, right_coef, left_coef, partial, field, edges,
    edge_one, edge_two, right_next, left_next,
):
    tiles = right_set.shape[0]
    place = place_in_group()
    everywhere = range(-3, 4)
    for tile in range(edge_one.shape[1] // 8):
        rows = pl.ds(8 * tile, 8)
        right = packed_sum(
            lambda t, at: right_set[t, at : at + 8, :], right_coef, 0, tile, tiles, everywhere
        )
        left = packed_sum(
            lambda t, at: left_set[t, at : at + 8, :], left_coef, 0, tile, tiles, everywhere
        )
        halo = (place >= 3) & (place < 6)
        for t in range(tiles):
            right_next[t, rows, :] = jnp.where(halo, right[t], 0.0)
            left_next[t, rows, :] = jnp.where(halo, left[t], 0.0)
            edge_one[t, rows, :] = jnp.where(place < 3, right[t], turn(left[t], -3))
    for tile in range(edge_two.shape[1] // 8):
        rows = pl.ds(8 * tile, 8)
        right = packed_sum(
            lambda t, at: right_next[t, at : at + 8, :], right_coef, 3, tile, tiles, range(1, 4)
        )
        left = packed_sum(
            lambda t, at: left_next[t, at : at + 8, :], left_coef, 3, tile, tiles, range(-3, 0)
        )
        for t in range(tiles):
            edge_two[t, rows, :] = jnp.where(place < 3, right[t], turn(left[t], -3))

    lane = lanes()
    at_edge = (lane < 3) | (lane >= 125)
    stacks = field.shape[0]
    for t in range(tiles):
        members = range(PER * t, min(stacks, PER * t + PER))
        for tile in range(edge_one.shape[1] // 8):
            rows = pl.ds(8 * tile, 8)
            packed = edge_one[t, rows, :]
            values = [
                partial[s, rows, :] + jnp.where(at_edge, turn(packed, 125 - SPAN * (s % PER)), 0.0)
                for s in members
            ]
            for s, value in zip(members, values):
                field[s, rows, :] = value
        for tile in range(edge_two.shape[1] // 8):
            rows = pl.ds(8 * tile, 8)
            packed = edge_two[t, rows, :]
            values = [jnp.where(at_edge, turn(packed, 125 - SPAN * (s % PER)), 0.0) for s in members]
            for s, value in zip(members, values):
                edges[s, rows, :] = value


def step_two(field, own_shifted, edges, out):
    def some_stacks(group, carry):
        for tile in range(out.shape[1] // 8):
            total = main_sum(lambda k, at: field[group * GROUP + k, at : at + 8, :], own_shifted, 0, tile)
            rows = pl.ds(8 * tile, 8)
            values = [total[k] + edges[group * GROUP + k, rows, :] for k in range(GROUP)]
            for k in range(GROUP):
                out[group * GROUP + k, rows, :] = values[k]
        return carry

    lax.fori_loop(0, out.shape[0] // GROUP, some_stacks, 0)


def local(tracer_mass, recon_table, intersection_weights, intersection_cells, rotation_codes):
    stacks, width, columns = tracer_mass.shape
    shape = lambda *sizes: jax.ShapeDtypeStruct(sizes, F32)
    scratch = lambda *sizes: pltpu.VMEM(sizes, F32)
    edge = -(-(6 * stacks + 3 * OFFSETS) // 8) * 8
    tiles = -(-stacks // PER)
    combos = 4 * (width // 8)

    mass, stencil, send_down, send_up = pl.pallas_call(
        coefficients,
        out_shape=(shape(*tracer_mass.shape), shape(OFFSETS, width, 128), shape(edge, 128), shape(edge, 128)),
        in_specs=[HBM] * 5,
        out_specs=(VMEM,) * 4,
        scratch_shapes=[
            pltpu.SMEM(recon_table.shape, F32),
            scratch(*intersection_weights.shape),
            pltpu.VMEM(intersection_cells.shape, jnp.int32),
            pltpu.VMEM(rotation_codes.shape, jnp.int32),
            scratch(TERMS, combos, 8, 128),
            scratch(25, combos, 8, 128),
            pltpu.SemaphoreType.DMA((5,)),
        ],
        compiler_params=params(),
        cost_estimate=cost(8 * 10**6),
        name="coefficients",
    )(*(
        pltpu.with_memory_space_constraint(value, pltpu.HBM)
        for value in (recon_table, tracer_mass, intersection_weights, intersection_cells, rotation_codes)
    ))
    above = shift(send_down, ROW_AXES, 1)
    below = shift(send_up, ROW_AXES, -1)

    tall, low = width + 16, width + 8
    picks = jax.ShapeDtypeStruct((7, 256, 256), jnp.bfloat16)
    own_left, own_right, picks = pl.pallas_call(
        pack_own,
        out_shape=(shape(width * (tiles + 2), 128),) * 2 + (picks,),
        in_specs=[VMEM] * 2,
        out_specs=(VMEM,) * 3,
        compiler_params=params(),
        cost_estimate=cost(10**6),
        name="pack_own",
    )(mass, stencil)

    send = (tiles + 2, tall, 128)
    send_a, send_b = pl.pallas_call(
        pack_all,
        out_shape=(shape(*send),) * 2,
        in_specs=[VMEM] * 5,
        out_specs=(VMEM,) * 2,
        scratch_shapes=[scratch(*send)] * 2,
        compiler_params=params(),
        cost_estimate=cost(10**6),
        name="pack_all",
    )(mass, own_left, own_right, above, below)
    column_a = swap(send_a, COLUMN_AXES, False)

    column_b = swap(send_b, COLUMN_AXES, True)

    partial, wide, shifted, own_shifted = pl.pallas_call(
        step_one,
        out_shape=(
            shape(stacks, low, 128), shape(OFFSETS, low, 128), shape(OFFSETS, low, 128),
            shape(OFFSETS, width, 128),
        ),
        in_specs=[VMEM] * 4,
        out_specs=(VMEM,) * 4,
        scratch_shapes=[scratch(stacks, tall, 128)],
        compiler_params=params(),
        cost_estimate=cost(12 * 10**6),
        name="step_one",
    )(mass, stencil, above, below)

    sides = pl.pallas_call(
        side_coefficients,
        out_shape=(shape(tiles, tall, 128),) * 2 + (shape(OFFSETS, low, 128),) * 2,
        in_specs=[VMEM] * 6,
        out_specs=(VMEM,) * 4,
        scratch_shapes=[scratch(2, low, 128)] * 2 + [scratch(7, 7 * low, 128)],
        compiler_params=params(),
        cost_estimate=cost(4 * 10**6),
        name="side_coefficients",
    )(wide, send_a, send_b, column_a, column_b, picks)

    field, edges = pl.pallas_call(
        halo_steps,
        out_shape=(shape(stacks, low, 128), shape(stacks, width, 128)),
        in_specs=[VMEM] * 5,
        out_specs=(VMEM,) * 2,
        scratch_shapes=[scratch(tiles, low, 128), scratch(tiles, width, 128)] + [scratch(tiles, low, 128)] * 2,
        compiler_params=params(),
        cost_estimate=cost(4 * 10**6),
        name="halo_steps",
    )(*sides, partial)

    return pl.pallas_call(
        step_two,
        out_shape=shape(stacks, width, columns),
        in_specs=[VMEM] * 3,
        out_specs=VMEM,
        compiler_params=params(),
        cost_estimate=cost(8 * 10**6),
        name="step_two",
    )(field, own_shifted, edges)


def solution(mesh):
    in_specs = (
        P(None, ("face", "px"), "py"),
        P(),
        P(None, None, ("face", "px"), "py"),
        P(None, ("face", "px"), "py"),
        P(None, ("face", "px"), "py"),
    )
    out_specs = P(None, ("face", "px"), "py")
    return jax.shard_map(local, mesh=mesh, in_specs=in_specs, out_specs=out_specs, check_vma=False)
```

```python
import functools

import jax
import jax.numpy as jnp
from jax import lax
from jax.experimental import pallas as pl
from jax.experimental.pallas import tpu as pltpu
from jax.sharding import PartitionSpec as P

F32 = jnp.float32
ROW_AXES = ("face", "px")
COLUMN_AXES = "py"
SWAPPED = (0, 2, 1, 5, 4, 3, 9, 8, 7, 6)
POWERS = ((0, 0), (1, 0), (0, 1), (2, 0), (1, 1), (0, 2), (3, 0), (2, 1), (1, 2), (0, 3))
TERMS = 10
OFFSETS = 49
GROUP = 4
SPAN = 9
PER = 14
COEF_PER = 42
VMEM = pl.BlockSpec(memory_space=pltpu.VMEM)
HBM = pl.BlockSpec(memory_space=pltpu.HBM)


def params():
    return pltpu.CompilerParams(vmem_limit_bytes=40 * 1024 * 1024)


def cost(operations):
    return pl.CostEstimate(flops=operations, bytes_accessed=1 << 20, transcendentals=0)


def swap(block, axes, odd_first):
    count = lax.axis_size(axes)
    partner = list(range(count))
    for low in range(1 if odd_first else 0, count, 2):
        high = (low + 1) % count
        partner[low], partner[high] = high, low
    return lax.ppermute(block, axes, list(enumerate(partner)))


def shift(block, axes, step):
    count = lax.axis_size(axes)
    return lax.ppermute(block, axes, [(index, (index + step) % count) for index in range(count)])


def ends(axes):
    index = lax.axis_index(axes)
    return index == 0, index == lax.axis_size(axes) - 1


def is_even(axes):
    return lax.rem(lax.axis_index(axes), 2) == 0


def turn(value, amount):
    amount %= 128
    return pltpu.roll(value, amount, 1) if amount else value


def lanes(rows=8):
    return lax.broadcasted_iota(jnp.int32, (rows, 128), 1)


def fill_stencil(recon, weights, cells, codes, turned, spread, stencil, tiles):
    zero = jnp.zeros((8, 128), F32)
    for g in range(tiles):
        rows = pl.ds(8 * g, 8)
        for m in range(4):
            code = codes[m, rows, :]
            odd = (code & 1) == 1
            sign_x = jnp.where(code >= 2, -1.0, 1.0).astype(F32)
            sign_y = jnp.where((code == 1) | (code == 2), -1.0, 1.0).astype(F32)
            sign_xy = sign_x * sign_y
            values = [weights[m, t, rows, :] for t in range(TERMS)]
            for t, (a, b) in enumerate(POWERS):
                value = values[t]
                if SWAPPED[t] != t:
                    value = jnp.where(odd, values[SWAPPED[t]], value)
                if a % 2 and b % 2:
                    value = value * sign_xy
                elif a % 2:
                    value = value * sign_x
                elif b % 2:
                    value = value * sign_y
                turned[t, m * tiles + g] = value

    combos = 4 * tiles

    def one_tap(tap, carry):
        total = [None] * combos
        for t in range(TERMS):
            scale = recon[t, tap]
            for c in range(combos):
                term = turned[t, c] * scale
                total[c] = term if t == 0 else total[c] + term
        for c in range(combos):
            spread[tap, c] = total[c]
        return carry

    lax.fori_loop(0, 25, one_tap, 0)

    for g in range(tiles):
        rows = pl.ds(8 * g, 8)
        masks = []
        for m in range(4):
            cell = cells[m, rows, :]
            first = jnp.where(cell < 3, 0, jnp.where(cell < 6, 3, 6))
            across = cell - first
            masks.append((cell < 3, cell < 6, across == 0, across <= 1))
        for ox in range(7):
            total = [None] * 7
            for m in range(4):
                low_x, mid_x, low_y, mid_y = masks[m]

                def tap(jx, jy):
                    if 0 <= jx < 5 and 0 <= jy < 5:
                        return spread[jx * 5 + jy, m * tiles + g]
                    return zero

                line = [
                    jnp.where(low_x, tap(ox, jy), jnp.where(mid_x, tap(ox - 1, jy), tap(ox - 2, jy)))
                    for jy in range(5)
                ]
                padded = [zero, zero] + line + [zero, zero]
                for oy in range(7):
                    value = jnp.where(
                        low_y, padded[oy + 2], jnp.where(mid_y, padded[oy + 1], padded[oy])
                    )
                    total[oy] = value if m == 0 else total[oy] + value
            for oy in range(7):
                stencil[ox * 7 + oy, rows, :] = total[oy]


def mass_rows(
    mass_hbm, weights_hbm, cells_hbm, codes_hbm, mass, weights, cells, codes, send_down, send_up, sems
):
    sources = (mass_hbm, weights_hbm, cells_hbm, codes_hbm)
    targets = (mass, weights, cells, codes)
    copies = [pltpu.make_async_copy(a, b, sems.at[i]) for i, (a, b) in enumerate(zip(sources, targets))]
    for copy in copies:
        copy.start()
    copies[0].wait()
    stacks, width = mass.shape[:2]
    for send, at in ((send_down, width - 6), (send_up, 0)):
        for s in range(stacks):
            send[6 * s : 6 * s + 6, :] = mass[s, at : at + 6, :]
    for copy in copies[1:]:
        copy.wait()


def coefficients(recon_hbm, weights, cells, codes, stencil, send_down, send_up, recon, turned, spread, sem):
    copy = pltpu.make_async_copy(recon_hbm, recon, sem.at[0])
    copy.start()
    copy.wait()
    width = stencil.shape[1]
    fill_stencil(recon, weights, cells, codes, turned, spread, stencil, width // 8)
    for send, at in ((send_down, width - 3), (send_up, 0)):
        for o in range(OFFSETS):
            send[3 * o : 3 * o + 3, :] = stencil[o, at : at + 3, :]


def pack_stacks(load, stacks, tile):
    lane = lanes()
    left = jnp.zeros((8, 128), F32)
    right = jnp.zeros((8, 128), F32)
    for s in range(PER * tile, min(stacks, PER * tile + PER)):
        at = SPAN * (s % PER)
        value = load(s)
        left = jnp.where((lane >= at + 3) & (lane < at + 9), turn(value, at + 3), left)
        right = jnp.where((lane >= at) & (lane < at + 6), turn(value, at - 122), right)
    return left, right


def pack_coefficients(load):
    lane = lanes()
    left = jnp.zeros((8, 128), F32)
    right = jnp.zeros((8, 128), F32)
    for o in range(COEF_PER):
        at = 3 * o
        here = (lane >= at) & (lane < at + 3)
        value = load(o)
        left = jnp.where(here, turn(value, at), left)
        right = jnp.where(here, turn(value, at - 125), right)
    return left, right


def add_spare(load, left, right):
    lane = lanes()
    for o in range(COEF_PER, OFFSETS):
        at = SPAN * (o - COEF_PER)
        value = load(o)
        left = jnp.where((lane >= at) & (lane < at + 3), turn(value, at), left)
        right = jnp.where((lane >= at + 6) & (lane < at + 9), turn(value, at - 119), right)
    return left, right


def fill_picks(picks):
    lane = lanes(1)
    group = (lane * 57) >> 9
    at = lane - SPAN * group
    source = lax.broadcasted_iota(jnp.int32, (128, 128), 0)
    for dy in range(-3, 4):
        q = at - dy
        halo = (q >= 3) & (q < 6)
        right = jnp.where(halo, 57 + q, jnp.where((q >= 0) & (q < 3) & (at >= 3), 125 + q, -1))
        left = jnp.where(halo, 61 + q, jnp.where((q >= 6) & (q < 9) & (at < 6), q - 6, -1))
        for side, wanted in enumerate((right, left)):
            wanted = jnp.where(group < PER, wanted, -1)
            picked = jnp.where(source == wanted, 1.0, 0.0).astype(jnp.bfloat16)
            picks[dy + 3, 0:128, 128 * side : 128 * side + 128] = picked
            picks[dy + 3, 128:256, 128 * side : 128 * side + 128] = picked


def pack_own(mass, stencil, left, right, picks):
    fill_picks(picks)
    stacks, width = mass.shape[:2]
    tiles = -(-stacks // PER)
    for half in range(width // 8):
        rows = pl.ds(8 * half, 8)
        for tile in range(tiles):
            at = width * tile + 8 * half
            values = pack_stacks(lambda s: mass[s, rows, :], stacks, tile)
            if tile == 0:
                values = add_spare(lambda o: stencil[o, rows, :], *values)
            left[at : at + 8, :], right[at : at + 8, :] = values
        at = width * tiles + 8 * half
        left[at : at + 8, :], right[at : at + 8, :] = pack_coefficients(lambda o: stencil[o, rows, :])


def pack_mass(own_left, own_right, above, below, left, right):
    stacks = (above.shape[0] - 8) // 6
    tiles = -(-stacks // PER)
    width = own_left.shape[0] // (tiles + 1)
    tall = width + 12
    for send, own in ((left, own_left), (right, own_right)):
        for tile in range(tiles + 1):
            send[tall * tile : tall * tile + width, :] = own[width * tile : width * tile + width, :]
        end = tall * tiles + width + 6
        send[end:, :] = jnp.zeros((send.shape[0] - end, 128), F32)
    first, last = ends(ROW_AXES)
    for got, outside, place in ((above, first, width), (below, last, width + 6)):
        for tile in range(tiles):
            at = tall * tile + place
            packed = pack_stacks(lambda s: got[6 * s : 6 * s + 8, :], stacks, tile)
            left[at : at + 6, :] = jnp.where(outside, 0.0, packed[0][0:6])
            right[at : at + 6, :] = jnp.where(outside, 0.0, packed[1][0:6])


def pack_all(width, mass_left, mass_right, above, below, send_a, send_b, left, right):
    left[...] = mass_left[...]
    right[...] = mass_right[...]
    coef_at = left.shape[0] - (width + 12)
    first, last = ends(ROW_AXES)
    for got, outside, mass_at, place in (
        (above, first, width, width), (below, last, width + 6, width + 3)
    ):
        load = lambda o: jnp.where(outside, 0.0, got[3 * o : 3 * o + 8, :])
        at = coef_at + place
        packed = pack_coefficients(load)
        left[at : at + 3, :] = packed[0][0:3]
        right[at : at + 3, :] = packed[1][0:3]
        packed = add_spare(load, left[mass_at : mass_at + 8, :], right[mass_at : mass_at + 8, :])
        left[mass_at : mass_at + 3, :] = packed[0][0:3]
        right[mass_at : mass_at + 3, :] = packed[1][0:3]
    choose(is_even(COLUMN_AXES), right, left, send_a, send_b)


def choose(even, first, second, first_out, second_out):
    @pl.when(even)
    def _():
        first_out[...] = first[...]
        second_out[...] = second[...]

    @pl.when(jnp.logical_not(even))
    def _():
        first_out[...] = second[...]
        second_out[...] = first[...]


def main_sum(load, coef, coef_at, tile):
    fields = [[load(k, 8 * tile + dx) for k in range(GROUP)] for dx in range(7)]
    total = [None] * GROUP
    for dy in range(7):
        part = [None] * GROUP
        for dx in range(7):
            at = coef_at + 8 * tile
            scale = coef[dx * 7 + dy, at : at + 8, :]
            for k in range(GROUP):
                term = scale * fields[dx][k]
                part[k] = term if dx == 0 else part[k] + term
        for k in range(GROUP):
            moved = turn(part[k], 3 - dy)
            total[k] = moved if dy == 0 else total[k] + moved
    return total


def step_one(mass, stencil, above, below, coef_above, coef_below, partial, wide, shifted, own_shifted, field):
    stacks, width = mass.shape[:2]
    first, last = ends(ROW_AXES)
    for s in range(stacks):
        at = 6 * s
        field[s, 0:6, :] = jnp.where(first, 0.0, above[at : at + 6, :])
        field[s, 6 : width + 6, :] = mass[s, :, :]
        field[s, width + 6 : width + 12, :] = jnp.where(last, 0.0, below[at : at + 6, :])
        field[s, width + 12 : width + 16, :] = jnp.zeros((4, 128), F32)
    for o in range(OFFSETS):
        at = 3 * o
        wide[o, 0:3, :] = jnp.where(first, 0.0, coef_above[at : at + 3, :])
        wide[o, 3 : width + 3, :] = stencil[o, :, :]
        wide[o, width + 3 : width + 6, :] = jnp.where(last, 0.0, coef_below[at : at + 3, :])
        wide[o, width + 6 : width + 8, :] = jnp.zeros((2, 128), F32)
    lane = lanes()
    for tile in range((width + 8) // 8):
        rows = pl.ds(8 * tile, 8)
        for dy in range(-3, 4):
            values = [turn(wide[dx * 7 + dy + 3, rows, :], dy) for dx in range(7)]
            if dy > 0:
                values = [jnp.where(lane >= dy, value, 0.0) for value in values]
            elif dy < 0:
                values = [jnp.where(lane < 128 + dy, value, 0.0) for value in values]
            for dx in range(7):
                shifted[dx * 7 + dy + 3, rows, :] = values[dx]
    for o in range(OFFSETS):
        own_shifted[o, :, :] = shifted[o, 3 : width + 3, :]

    def some_stacks(group, carry):
        for tile in range(partial.shape[1] // 8):
            total = main_sum(lambda k, at: field[group * GROUP + k, at : at + 8, :], shifted, 0, tile)
            for k in range(GROUP):
                partial[group * GROUP + k, 8 * tile : 8 * tile + 8, :] = total[k]
        return carry

    lax.fori_loop(0, stacks // GROUP, some_stacks, 0)


def packed_sum(load, coef, coef_at, tile, tiles, dys):
    fields = [[load(t, 8 * tile + dx) for t in range(tiles)] for dx in range(7)]
    total = [None] * tiles
    for dy in dys:
        part = [None] * tiles
        for dx in range(7):
            at = coef_at + 8 * tile
            scale = coef[dx * 7 + dy + 3, at : at + 8, :]
            for t in range(tiles):
                term = scale * fields[dx][t]
                part[t] = term if dx == 0 else part[t] + term
        for t in range(tiles):
            moved = turn(part[t], -dy)
            total[t] = moved if total[t] is None else total[t] + moved
    return total


def place_in_group(rows=8):
    lane = lanes(rows)
    return lane - SPAN * ((lane * 57) >> 9)


def side_coefficients(
    wide, send_a, send_b, got_a, got_b, picks,
    right_set, left_set, right_coef, left_coef, right_halo, left_halo, rows_of,
):
    tall = wide.shape[1]
    width = tall - 8
    tiles = right_set.shape[0]
    lane = lanes()

    first, last = ends(COLUMN_AXES)

    def gather(sent_right, sent_left, got_right, got_left):
        part = width + 12
        place = place_in_group(part)
        rows = [slice(part * tile, part * tile + part) for tile in range(tiles)]
        from_right = [jnp.where(last, 0.0, got_right[at, :]) for at in rows]
        from_left = [jnp.where(first, 0.0, got_left[at, :]) for at in rows]
        for tile, at in enumerate(rows):
            right = jnp.where(place < 3, turn(sent_right[at, :], -3), from_right[tile])
            left = jnp.where(place >= 6, turn(sent_left[at, :], 3), from_left[tile])
            for target, value in ((right_set, right), (left_set, left)):
                target[tile, 6 : width + 6, :] = value[0:width]
                target[tile, 0:6, :] = value[width : width + 6]
                target[tile, width + 6 : width + 12, :] = value[width + 6 : width + 12]
                target[tile, width + 12 : width + 16, :] = jnp.zeros((4, 128), F32)
        coefs = slice(part * tiles, part * tiles + width + 6)
        for target, source, got, outside in (
            (right_halo, from_right, got_right, last), (left_halo, from_left, got_left, first)
        ):
            value = jnp.where(outside, 0.0, got[coefs, :])
            spare = source[0]
            for tile, own, above, below in (
                (0, value[0:width], value[width : width + 3], value[width + 3 : width + 6]),
                (1, spare[0:width], spare[width : width + 3], spare[width + 6 : width + 9]),
            ):
                target[tile, 3 : width + 3, :] = own
                target[tile, 0:3, :] = above
                target[tile, width + 3 : width + 6, :] = below
                target[tile, width + 6 : width + 8, :] = jnp.zeros((2, 128), F32)

    even = is_even(COLUMN_AXES)

    @pl.when(even)
    def _():
        gather(send_a, send_b, got_a, got_b)

    @pl.when(jnp.logical_not(even))
    def _():
        gather(send_b, send_a, got_b, got_a)

    from_right = (lane >= 60) & (lane < 63)
    from_left = (lane >= 64) & (lane < 67)
    for tile in range(tall // 8):
        rows = pl.ds(8 * tile, 8)
        right_rows = [right_halo[t, rows, :] for t in range(2)]
        left_rows = [left_halo[t, rows, :] for t in range(2)]
        for dy in range(7):
            values = []
            for dx in range(7):
                o = dx * 7 + dy
                if o < COEF_PER:
                    right = turn(right_rows[0], 60 - 3 * o)
                    left = turn(left_rows[0], 64 - 3 * o)
                else:
                    at = SPAN * (o - COEF_PER)
                    right = turn(right_rows[1], 60 - at)
                    left = turn(left_rows[1], 58 - at)
                values.append(
                    jnp.where(from_right, right, jnp.where(from_left, left, wide[o, rows, :]))
                )
            for dx in range(7):
                at = tall * dx + 8 * tile
                rows_of[dy, at : at + 8, :] = values[dx]

    for dy in range(7):
        value = rows_of[dy]
        high = value.astype(jnp.bfloat16)
        low = (value - high.astype(F32)).astype(jnp.bfloat16)
        both = jnp.concatenate([high, low], axis=1)
        spread = jnp.dot(both, picks[dy], preferred_element_type=F32)
        for dx in range(7):
            right_coef[dx * 7 + dy, :, :] = spread[tall * dx : tall * dx + tall, 0:128]
            left_coef[dx * 7 + dy, :, :] = spread[tall * dx : tall * dx + tall, 128:256]


def halo_steps(
    right_set, left_set, right_coef, left_coef, partial, field, edges,
    edge_one, edge_two, right_next, left_next,
):
    tiles = right_set.shape[0]
    place = place_in_group()
    everywhere = range(-3, 4)
    for tile in range(edge_one.shape[1] // 8):
        rows = pl.ds(8 * tile, 8)
        right = packed_sum(
            lambda t, at: right_set[t, at : at + 8, :], right_coef, 0, tile, tiles, everywhere
        )
        left = packed_sum(
            lambda t, at: left_set[t, at : at + 8, :], left_coef, 0, tile, tiles, everywhere
        )
        halo = (place >= 3) & (place < 6)
        for t in range(tiles):
            right_next[t, rows, :] = jnp.where(halo, right[t], 0.0)
            left_next[t, rows, :] = jnp.where(halo, left[t], 0.0)
            edge_one[t, rows, :] = jnp.where(place < 3, right[t], turn(left[t], -3))
    for tile in range(edge_two.shape[1] // 8):
        rows = pl.ds(8 * tile, 8)
        right = packed_sum(
            lambda t, at: right_next[t, at : at + 8, :], right_coef, 3, tile, tiles, range(1, 4)
        )
        left = packed_sum(
            lambda t, at: left_next[t, at : at + 8, :], left_coef, 3, tile, tiles, range(-3, 0)
        )
        for t in range(tiles):
            edge_two[t, rows, :] = jnp.where(place < 3, right[t], turn(left[t], -3))

    lane = lanes()
    at_edge = (lane < 3) | (lane >= 125)
    stacks = field.shape[0]
    for t in range(tiles):
        members = range(PER * t, min(stacks, PER * t + PER))
        for tile in range(edge_one.shape[1] // 8):
            rows = pl.ds(8 * tile, 8)
            packed = edge_one[t, rows, :]
            values = [
                partial[s, rows, :] + jnp.where(at_edge, turn(packed, 125 - SPAN * (s % PER)), 0.0)
                for s in members
            ]
            for s, value in zip(members, values):
                field[s, rows, :] = value
        for tile in range(edge_two.shape[1] // 8):
            rows = pl.ds(8 * tile, 8)
            packed = edge_two[t, rows, :]
            values = [jnp.where(at_edge, turn(packed, 125 - SPAN * (s % PER)), 0.0) for s in members]
            for s, value in zip(members, values):
                edges[s, rows, :] = value


def step_two(field, own_shifted, edges, out_hbm, out, sems):
    groups = out.shape[0] // GROUP

    def piece(group):
        stacks = pl.ds(group * GROUP, GROUP)
        return pltpu.make_async_copy(out.at[stacks], out_hbm.at[stacks], sems.at[group])

    def some_stacks(group, carry):
        for tile in range(out.shape[1] // 8):
            total = main_sum(lambda k, at: field[group * GROUP + k, at : at + 8, :], own_shifted, 0, tile)
            rows = pl.ds(8 * tile, 8)
            values = [total[k] + edges[group * GROUP + k, rows, :] for k in range(GROUP)]
            for k in range(GROUP):
                out[group * GROUP + k, rows, :] = values[k]
        piece(group).start()
        return carry

    lax.fori_loop(0, groups, some_stacks, 0)
    for group in range(groups):
        piece(group).wait()


def local(tracer_mass, recon_table, intersection_weights, intersection_cells, rotation_codes):
    stacks, width, columns = tracer_mass.shape
    shape = lambda *sizes: jax.ShapeDtypeStruct(sizes, F32)
    scratch = lambda *sizes: pltpu.VMEM(sizes, F32)
    tiles = -(-stacks // PER)
    combos = 4 * (width // 8)
    tall, low = width + 16, width + 8
    fixed = lambda *values: [pltpu.with_memory_space_constraint(value, pltpu.HBM) for value in values]
    whole = lambda value: jax.ShapeDtypeStruct(value.shape, value.dtype)
    mass_edge, coef_edge = 6 * stacks + 8, -(-(3 * OFFSETS + 5) // 8) * 8

    mass, weights, cells, codes, mass_down, mass_up = pl.pallas_call(
        mass_rows,
        out_shape=(
            whole(tracer_mass), whole(intersection_weights), whole(intersection_cells),
            whole(rotation_codes), shape(mass_edge, 128), shape(mass_edge, 128),
        ),
        in_specs=[HBM] * 4,
        out_specs=(VMEM,) * 6,
        scratch_shapes=[pltpu.SemaphoreType.DMA((4,))],
        compiler_params=params(),
        cost_estimate=cost(10**6),
        name="mass_rows",
    )(*fixed(tracer_mass, intersection_weights, intersection_cells, rotation_codes))
    above = shift(mass_down, ROW_AXES, 1)
    below = shift(mass_up, ROW_AXES, -1)

    stencil, coef_down, coef_up = pl.pallas_call(
        coefficients,
        out_shape=(shape(OFFSETS, width, 128), shape(coef_edge, 128), shape(coef_edge, 128)),
        in_specs=[HBM] + [VMEM] * 3,
        out_specs=(VMEM,) * 3,
        scratch_shapes=[
            pltpu.SMEM(recon_table.shape, F32),
            scratch(TERMS, combos, 8, 128),
            scratch(25, combos, 8, 128),
            pltpu.SemaphoreType.DMA((1,)),
        ],
        compiler_params=params(),
        cost_estimate=cost(8 * 10**6),
        name="coefficients",
    )(*fixed(recon_table), weights, cells, codes)
    coef_above = shift(coef_down, ROW_AXES, 1)
    coef_below = shift(coef_up, ROW_AXES, -1)

    picks = jax.ShapeDtypeStruct((7, 256, 256), jnp.bfloat16)
    own_left, own_right, picks = pl.pallas_call(
        pack_own,
        out_shape=(shape(width * (tiles + 1), 128),) * 2 + (picks,),
        in_specs=[VMEM] * 2,
        out_specs=(VMEM,) * 3,
        compiler_params=params(),
        cost_estimate=cost(10**6),
        name="pack_own",
    )(mass, stencil)

    send = ((width + 12) * (tiles + 1), 128)
    mass_left, mass_right = pl.pallas_call(
        pack_mass,
        out_shape=(shape(*send),) * 2,
        in_specs=[VMEM] * 4,
        out_specs=(VMEM,) * 2,
        compiler_params=params(),
        cost_estimate=cost(10**6),
        name="pack_mass",
    )(own_left, own_right, above, below)
    send_a, send_b = pl.pallas_call(
        functools.partial(pack_all, width),
        out_shape=(shape(*send),) * 2,
        in_specs=[VMEM] * 4,
        out_specs=(VMEM,) * 2,
        scratch_shapes=[scratch(*send)] * 2,
        compiler_params=params(),
        cost_estimate=cost(10**6),
        name="pack_all",
    )(mass_left, mass_right, coef_above, coef_below)
    column_a = swap(send_a, COLUMN_AXES, False)
    column_b = swap(send_b, COLUMN_AXES, True)

    partial, wide, shifted, own_shifted = pl.pallas_call(
        step_one,
        out_shape=(
            shape(stacks, low, 128), shape(OFFSETS, low, 128), shape(OFFSETS, low, 128),
            shape(OFFSETS, width, 128),
        ),
        in_specs=[VMEM] * 6,
        out_specs=(VMEM,) * 4,
        scratch_shapes=[scratch(stacks, tall, 128)],
        compiler_params=params(),
        cost_estimate=cost(12 * 10**6),
        name="step_one",
    )(mass, stencil, above, below, coef_above, coef_below)

    sides = pl.pallas_call(
        side_coefficients,
        out_shape=(shape(tiles, tall, 128),) * 2 + (shape(OFFSETS, low, 128),) * 2,
        in_specs=[VMEM] * 6,
        out_specs=(VMEM,) * 4,
        scratch_shapes=[scratch(2, low, 128)] * 2 + [scratch(7, 7 * low, 128)],
        compiler_params=params(),
        cost_estimate=cost(4 * 10**6),
        name="side_coefficients",
    )(wide, send_a, send_b, column_a, column_b, picks)

    field, edges = pl.pallas_call(
        halo_steps,
        out_shape=(shape(stacks, low, 128), shape(stacks, width, 128)),
        in_specs=[VMEM] * 5,
        out_specs=(VMEM,) * 2,
        scratch_shapes=[scratch(tiles, low, 128), scratch(tiles, width, 128)] + [scratch(tiles, low, 128)] * 2,
        compiler_params=params(),
        cost_estimate=cost(4 * 10**6),
        name="halo_steps",
    )(*sides, partial)

    return pl.pallas_call(
        step_two,
        out_shape=shape(stacks, width, columns),
        in_specs=[VMEM] * 3,
        out_specs=HBM,
        scratch_shapes=[scratch(stacks, width, columns), pltpu.SemaphoreType.DMA((stacks // GROUP,))],
        compiler_params=params(),
        cost_estimate=cost(8 * 10**6),
        name="step_two",
    )(field, own_shifted, edges)


def solution(mesh):
    in_specs = (
        P(None, ("face", "px"), "py"),
        P(),
        P(None, None, ("face", "px"), "py"),
        P(None, ("face", "px"), "py"),
        P(None, ("face", "px"), "py"),
    )
    out_specs = P(None, ("face", "px"), "py")
    return jax.shard_map(local, mesh=mesh, in_specs=in_specs, out_specs=out_specs, check_vma=False)
```

```python
import functools

import jax
import jax.numpy as jnp
import numpy as np
from jax import lax
from jax.experimental import pallas as pl
from jax.experimental.pallas import tpu as pltpu
from jax.sharding import PartitionSpec as P

F32 = jnp.float32
ROW_AXES = ("face", "px")
COLUMN_AXES = "py"
SWAPPED = (0, 2, 1, 5, 4, 3, 9, 8, 7, 6)
POWERS = ((0, 0), (1, 0), (0, 1), (2, 0), (1, 1), (0, 2), (3, 0), (2, 1), (1, 2), (0, 3))
TERMS = 10
OFFSETS = 49
GROUP = 4
SPAN = 9
PER = 14
COEF_PER = 42
VMEM = pl.BlockSpec(memory_space=pltpu.VMEM)
ANY = pl.BlockSpec(memory_space=pl.ANY)
HBM = pl.BlockSpec(memory_space=pltpu.HBM)


def params():
    return pltpu.CompilerParams(vmem_limit_bytes=40 * 1024 * 1024)


def cost(operations):
    return pl.CostEstimate(flops=operations, bytes_accessed=1 << 20, transcendentals=0)


def swap(block, axes, odd_first):
    count = lax.axis_size(axes)
    partner = list(range(count))
    for low in range(1 if odd_first else 0, count, 2):
        high = (low + 1) % count
        partner[low], partner[high] = high, low
    return lax.ppermute(block, axes, list(enumerate(partner)))


def shift(block, axes, step):
    count = lax.axis_size(axes)
    return lax.ppermute(block, axes, [(index, (index + step) % count) for index in range(count)])


def ends(axes):
    index = lax.axis_index(axes)
    return index == 0, index == lax.axis_size(axes) - 1


def is_even(axes):
    return lax.rem(lax.axis_index(axes), 2) == 0


def turn(value, amount):
    amount %= 128
    return pltpu.roll(value, amount, 1) if amount else value


def lanes(rows=8):
    return lax.broadcasted_iota(jnp.int32, (rows, 128), 1)


def fill_stencil(recon, weights, cells, codes, turned, spread, stencil, tiles):
    zero = jnp.zeros((8, 128), F32)
    for g in range(tiles):
        rows = pl.ds(8 * g, 8)
        for m in range(4):
            code = codes[m, rows, :]
            odd = (code & 1) == 1
            sign_x = jnp.where(code >= 2, -1.0, 1.0).astype(F32)
            sign_y = jnp.where((code == 1) | (code == 2), -1.0, 1.0).astype(F32)
            sign_xy = sign_x * sign_y
            values = [weights[m, t, rows, :] for t in range(TERMS)]
            for t, (a, b) in enumerate(POWERS):
                value = values[t]
                if SWAPPED[t] != t:
                    value = jnp.where(odd, values[SWAPPED[t]], value)
                if a % 2 and b % 2:
                    value = value * sign_xy
                elif a % 2:
                    value = value * sign_x
                elif b % 2:
                    value = value * sign_y
                turned[t, m * tiles + g] = value

    combos = 4 * tiles

    def one_tap(tap, carry):
        total = [None] * combos
        for t in range(TERMS):
            scale = recon[t, tap]
            for c in range(combos):
                term = turned[t, c] * scale
                total[c] = term if t == 0 else total[c] + term
        for c in range(combos):
            spread[tap, c] = total[c]
        return carry

    lax.fori_loop(0, 25, one_tap, 0)

    for g in range(tiles):
        rows = pl.ds(8 * g, 8)
        masks = []
        for m in range(4):
            cell = cells[m, rows, :]
            first = jnp.where(cell < 3, 0, jnp.where(cell < 6, 3, 6))
            across = cell - first
            masks.append((cell < 3, cell < 6, across == 0, across <= 1))
        for ox in range(7):
            total = [None] * 7
            for m in range(4):
                low_x, mid_x, low_y, mid_y = masks[m]

                def tap(jx, jy):
                    if 0 <= jx < 5 and 0 <= jy < 5:
                        return spread[jx * 5 + jy, m * tiles + g]
                    return zero

                line = [
                    jnp.where(low_x, tap(ox, jy), jnp.where(mid_x, tap(ox - 1, jy), tap(ox - 2, jy)))
                    for jy in range(5)
                ]
                padded = [zero, zero] + line + [zero, zero]
                for oy in range(7):
                    value = jnp.where(
                        low_y, padded[oy + 2], jnp.where(mid_y, padded[oy + 1], padded[oy])
                    )
                    total[oy] = value if m == 0 else total[oy] + value
            for oy in range(7):
                stencil[ox * 7 + oy, rows, :] = total[oy]


def edge_rows(
    recon_hbm, mass_hbm, weights_hbm, cells_hbm, codes_hbm,
    mass, weights, cells, codes, send_down, send_up,
    recon, edge_weights, edge_cells, edge_codes, edge_stencil, turned, spread, sems,
):
    sources = (recon_hbm, codes_hbm, weights_hbm, cells_hbm, mass_hbm)
    targets = (recon, codes, weights, cells, mass)
    copies = [pltpu.make_async_copy(a, b, sems.at[i]) for i, (a, b) in enumerate(zip(sources, targets))]
    for copy in copies:
        copy.start()
    for copy in copies:
        copy.wait()
    stacks, width = mass.shape[:2]
    for target, source in ((edge_weights, weights), (edge_cells, cells), (edge_codes, codes)):
        for index in np.ndindex(*source.shape[:-2]):
            target[index + (slice(0, 3), slice(None))] = source[index + (slice(0, 3), slice(None))]
            target[index + (slice(3, 8), slice(None))] = source[index + (slice(width - 5, width), slice(None))]
    fill_stencil(recon, edge_weights, edge_cells, edge_codes, turned, spread, edge_stencil, 1)
    for send, mass_at, stencil_at in ((send_down, width - 6, 5), (send_up, 0, 0)):
        for s in range(stacks):
            send[6 * s : 6 * s + 6, :] = mass[s, mass_at : mass_at + 6, :]
        for o in range(OFFSETS):
            at = 6 * stacks + 3 * o
            send[at : at + 3, :] = edge_stencil[o, stencil_at : stencil_at + 3, :]


def coefficients(recon_hbm, weights, cells, codes, stencil, recon, turned, spread, sem):
    copy = pltpu.make_async_copy(recon_hbm, recon, sem.at[0])
    copy.start()
    copy.wait()
    fill_stencil(recon, weights, cells, codes, turned, spread, stencil, stencil.shape[1] // 8)


def pack_stacks(load, stacks, tile):
    lane = lanes()
    left = jnp.zeros((8, 128), F32)
    right = jnp.zeros((8, 128), F32)
    for s in range(PER * tile, min(stacks, PER * tile + PER)):
        at = SPAN * (s % PER)
        value = load(s)
        left = jnp.where((lane >= at + 3) & (lane < at + 9), turn(value, at + 3), left)
        right = jnp.where((lane >= at) & (lane < at + 6), turn(value, at - 122), right)
    return left, right


def pack_coefficients(load):
    lane = lanes()
    left = jnp.zeros((8, 128), F32)
    right = jnp.zeros((8, 128), F32)
    for o in range(COEF_PER):
        at = 3 * o
        here = (lane >= at) & (lane < at + 3)
        value = load(o)
        left = jnp.where(here, turn(value, at), left)
        right = jnp.where(here, turn(value, at - 125), right)
    return left, right


def add_spare(load, left, right):
    lane = lanes()
    for o in range(COEF_PER, OFFSETS):
        at = SPAN * (o - COEF_PER)
        value = load(o)
        left = jnp.where((lane >= at) & (lane < at + 3), turn(value, at), left)
        right = jnp.where((lane >= at + 6) & (lane < at + 9), turn(value, at - 119), right)
    return left, right


def fill_near(near):
    lane = lanes(1)
    group = (lane * 57) >> 9
    at = lane - SPAN * group
    source = lax.broadcasted_iota(jnp.int32, (128, 128), 0)
    for dy in range(-3, 4):
        q = at - dy
        right = jnp.where((at >= 3) & (q >= 0) & (q < 6), 122 + q, -1)
        left = jnp.where((at < 6) & (q >= 3) & (q < 9), q - 3, -1)
        for side, wanted in enumerate((right, left)):
            wanted = jnp.where(group < PER, wanted, -1)
            picked = jnp.where(source == wanted, 1.0, 0.0).astype(jnp.bfloat16)
            near[dy + 3, 0:128, 128 * side : 128 * side + 128] = picked
            near[dy + 3, 128:256, 128 * side : 128 * side + 128] = picked


def replicate(value, picks):
    high = value.astype(jnp.bfloat16)
    low = (value - high.astype(F32)).astype(jnp.bfloat16)
    return jnp.dot(jnp.concatenate([high, low], axis=1), picks, preferred_element_type=F32)


def fill_picks(picks):
    lane = lanes(1)
    group = (lane * 57) >> 9
    at = lane - SPAN * group
    source = lax.broadcasted_iota(jnp.int32, (128, 128), 0)
    for dy in range(-3, 4):
        q = at - dy
        halo = (q >= 3) & (q < 6)
        right = jnp.where(halo, 57 + q, jnp.where((q >= 0) & (q < 3) & (at >= 3), 125 + q, -1))
        left = jnp.where(halo, 61 + q, jnp.where((q >= 6) & (q < 9) & (at < 6), q - 6, -1))
        for side, wanted in enumerate((right, left)):
            wanted = jnp.where(group < PER, wanted, -1)
            picked = jnp.where(source == wanted, 1.0, 0.0).astype(jnp.bfloat16)
            picks[dy + 3, 0:128, 128 * side : 128 * side + 128] = picked
            picks[dy + 3, 128:256, 128 * side : 128 * side + 128] = picked


def pack_own(mass, stencil, left, right, picks, near):
    fill_picks(picks)
    fill_near(near)
    stacks, width = mass.shape[:2]
    tiles = -(-stacks // PER)
    for half in range(width // 8):
        rows = pl.ds(8 * half, 8)
        for tile in range(tiles):
            at = width * tile + 8 * half
            values = pack_stacks(lambda s: mass[s, rows, :], stacks, tile)
            if tile == 0:
                values = add_spare(lambda o: stencil[o, rows, :], *values)
            left[at : at + 8, :], right[at : at + 8, :] = values
        at = width * tiles + 8 * half
        left[at : at + 8, :], right[at : at + 8, :] = pack_coefficients(lambda o: stencil[o, rows, :])


def pack_all(stacks, own_left, own_right, above, below, middle, send_a, send_b, left, right):
    tiles = -(-stacks // PER)
    width = own_left.shape[0] // (tiles + 1)
    tall = width + 12
    for send, own in ((left, own_left), (right, own_right)):
        for tile in range(tiles + 1):
            send[tall * tile : tall * tile + width, :] = own[width * tile : width * tile + width, :]
        end = tall * tiles + width + 6
        send[end:, :] = jnp.zeros((send.shape[0] - end, 128), F32)
    first, last = ends(ROW_AXES)
    for got, outside, place, coef_place in (
        (above, first, width, width), (below, last, width + 6, width + 3)
    ):
        coef = lambda o: got[6 * stacks + 3 * o : 6 * stacks + 3 * o + 8, :]
        for tile in range(tiles):
            at = tall * tile + place
            packed = pack_stacks(lambda s: got[6 * s : 6 * s + 8, :], stacks, tile)
            if tile == 0:
                spare = add_spare(coef, *packed)
                packed = [
                    jnp.where(lax.broadcasted_iota(jnp.int32, (8, 128), 0) < 3, with_spare, without)
                    for with_spare, without in zip(spare, packed)
                ]
            left[at : at + 6, :] = jnp.where(outside, 0.0, packed[0][0:6])
            right[at : at + 6, :] = jnp.where(outside, 0.0, packed[1][0:6])
        at = tall * tiles + coef_place
        packed = pack_coefficients(coef)
        left[at : at + 3, :] = jnp.where(outside, 0.0, packed[0][0:3])
        right[at : at + 3, :] = jnp.where(outside, 0.0, packed[1][0:3])
    choose(is_even(COLUMN_AXES), right, left, send_a, send_b)


def choose(even, first, second, first_out, second_out):
    @pl.when(even)
    def _():
        first_out[...] = first[...]
        second_out[...] = second[...]

    @pl.when(jnp.logical_not(even))
    def _():
        first_out[...] = second[...]
        second_out[...] = first[...]


def main_sum(load, coef, coef_at, tile):
    fields = [[load(k, 8 * tile + dx) for k in range(GROUP)] for dx in range(7)]
    total = [None] * GROUP
    for dy in range(7):
        part = [None] * GROUP
        for dx in range(7):
            at = coef_at + 8 * tile
            scale = coef[dx * 7 + dy, at : at + 8, :]
            for k in range(GROUP):
                term = scale * fields[dx][k]
                part[k] = term if dx == 0 else part[k] + term
        for k in range(GROUP):
            moved = turn(part[k], 3 - dy)
            total[k] = moved if dy == 0 else total[k] + moved
    return total


def shift_rows(load, store, dys=range(-3, 4)):
    lane = lanes()
    for dy in dys:
        values = [turn(load(dx * 7 + dy + 3), dy) for dx in range(7)]
        if dy > 0:
            values = [jnp.where(lane >= dy, value, 0.0) for value in values]
        elif dy < 0:
            values = [jnp.where(lane < 128 + dy, value, 0.0) for value in values]
        for dx in range(7):
            store(dx * 7 + dy + 3, values[dx])


def own_part(mass, stencil, near, middle, own_shifted, right_near, left_near):
    stacks, width = mass.shape[:2]
    for tile in range(width // 8):
        rows = pl.ds(8 * tile, 8)

        def store(o, value):
            own_shifted[o, rows, :] = value

        shift_rows(lambda o: stencil[o, rows, :], store)

    def some_stacks(group, carry):
        for tile in range((width - 8) // 8):
            total = main_sum(lambda k, at: mass[group * GROUP + k, 2 + at : 10 + at, :], own_shifted, 5, tile)
            for k in range(GROUP):
                middle[group * GROUP + k, 8 * tile : 8 * tile + 8, :] = total[k]
        return carry

    lax.fori_loop(0, stacks // GROUP, some_stacks, 0)
    for dy in range(7):
        value = jnp.concatenate([stencil[dx * 7 + dy, :, :] for dx in range(7)], axis=0)
        spread = replicate(value, near[dy])
        for dx in range(7):
            right_near[dx * 7 + dy, :, :] = spread[width * dx : width * dx + width, 0:128]
            left_near[dx * 7 + dy, :, :] = spread[width * dx : width * dx + width, 128:256]


def both_steps(mass, stencil, above, below, middle, own_shifted, second, wide, shifted, field, partial):
    stacks, width = mass.shape[:2]
    first, last = ends(ROW_AXES)
    for s in range(stacks):
        at = 6 * s
        field[s, 0:6, :] = jnp.where(first, 0.0, above[at : at + 6, :])
        field[s, 6 : width + 6, :] = mass[s, :, :]
        field[s, width + 6 : width + 12, :] = jnp.where(last, 0.0, below[at : at + 6, :])
        field[s, width + 12 : width + 16, :] = jnp.zeros((4, 128), F32)
    for o in range(OFFSETS):
        at = 6 * stacks + 3 * o
        wide[o, 0:3, :] = jnp.where(first, 0.0, above[at : at + 3, :])
        wide[o, 3 : width + 3, :] = stencil[o, :, :]
        wide[o, width + 3 : width + 6, :] = jnp.where(last, 0.0, below[at : at + 3, :])
        wide[o, width + 6 : width + 8, :] = jnp.zeros((2, 128), F32)
    tiles = (0, width // 8)
    for tile in tiles:
        rows = pl.ds(8 * tile, 8)

        def store(o, value):
            shifted[o, rows, :] = value

        shift_rows(lambda o: wide[o, rows, :], store)

    def some_stacks(group, carry):
        for k in range(GROUP):
            partial[k, 8:width, :] = middle[group * GROUP + k, :, :]
        for tile in tiles:
            total = main_sum(lambda k, at: field[group * GROUP + k, at : at + 8, :], shifted, 0, tile)
            for k in range(GROUP):
                partial[k, 8 * tile : 8 * tile + 8, :] = total[k]
        for tile in range(width // 8):
            total = main_sum(lambda k, at: partial[k, at : at + 8, :], own_shifted, 0, tile)
            for k in range(GROUP):
                second[group * GROUP + k, 8 * tile : 8 * tile + 8, :] = total[k]
        return carry

    lax.fori_loop(0, stacks // GROUP, some_stacks, 0)


def packed_sum(load, coef, coef_at, tile, tiles, dys):
    fields = [[load(t, 8 * tile + dx) for t in range(tiles)] for dx in range(7)]
    total = [None] * tiles
    for dy in dys:
        part = [None] * tiles
        for dx in range(7):
            at = coef_at + 8 * tile
            scale = coef[dx * 7 + dy + 3, at : at + 8, :]
            for t in range(tiles):
                term = scale * fields[dx][t]
                part[t] = term if dx == 0 else part[t] + term
        for t in range(tiles):
            moved = turn(part[t], -dy)
            total[t] = moved if total[t] is None else total[t] + moved
    return total


def place_in_group(rows=8):
    lane = lanes(rows)
    return lane - SPAN * ((lane * 57) >> 9)


def side_coefficients(
    wide, send_a, send_b, got_a, got_b, picks,
    right_set, left_set, right_coef, left_coef, right_halo, left_halo, rows_of,
):
    tall = wide.shape[1]
    width = tall - 8
    tiles = right_set.shape[0]
    lane = lanes()

    first, last = ends(COLUMN_AXES)

    def gather(sent_right, sent_left, got_right, got_left):
        part = width + 12
        place = place_in_group(part)
        rows = [slice(part * tile, part * tile + part) for tile in range(tiles)]
        from_right = [jnp.where(last, 0.0, got_right[at, :]) for at in rows]
        from_left = [jnp.where(first, 0.0, got_left[at, :]) for at in rows]
        for tile, at in enumerate(rows):
            right = jnp.where(place < 3, turn(sent_right[at, :], -3), from_right[tile])
            left = jnp.where(place >= 6, turn(sent_left[at, :], 3), from_left[tile])
            for target, value in ((right_set, right), (left_set, left)):
                target[tile, 6 : width + 6, :] = value[0:width]
                target[tile, 0:6, :] = value[width : width + 6]
                target[tile, width + 6 : width + 12, :] = value[width + 6 : width + 12]
                target[tile, width + 12 : width + 16, :] = jnp.zeros((4, 128), F32)
        coefs = slice(part * tiles, part * tiles + width + 6)
        for target, source, got, outside in (
            (right_halo, from_right, got_right, last), (left_halo, from_left, got_left, first)
        ):
            value = jnp.where(outside, 0.0, got[coefs, :])
            spare = source[0]
            for tile, own, above, below in (
                (0, value[0:width], value[width : width + 3], value[width + 3 : width + 6]),
                (1, spare[0:width], spare[width : width + 3], spare[width + 6 : width + 9]),
            ):
                target[tile, 3 : width + 3, :] = own
                target[tile, 0:3, :] = above
                target[tile, width + 3 : width + 6, :] = below
                target[tile, width + 6 : width + 8, :] = jnp.zeros((2, 128), F32)

    even = is_even(COLUMN_AXES)

    @pl.when(even)
    def _():
        gather(send_a, send_b, got_a, got_b)

    @pl.when(jnp.logical_not(even))
    def _():
        gather(send_b, send_a, got_b, got_a)

    from_right = (lane >= 60) & (lane < 63)
    from_left = (lane >= 64) & (lane < 67)
    for tile in range(tall // 8):
        rows = pl.ds(8 * tile, 8)
        right_rows = [right_halo[t, rows, :] for t in range(2)]
        left_rows = [left_halo[t, rows, :] for t in range(2)]
        for dy in range(7):
            values = []
            for dx in range(7):
                o = dx * 7 + dy
                if o < COEF_PER:
                    right = turn(right_rows[0], 60 - 3 * o)
                    left = turn(left_rows[0], 64 - 3 * o)
                else:
                    at = SPAN * (o - COEF_PER)
                    right = turn(right_rows[1], 60 - at)
                    left = turn(left_rows[1], 58 - at)
                values.append(
                    jnp.where(from_right, right, jnp.where(from_left, left, wide[o, rows, :]))
                )
            for dx in range(7):
                at = tall * dx + 8 * tile
                rows_of[dy, at : at + 8, :] = values[dx]

    for dy in range(7):
        spread = replicate(rows_of[dy], picks[dy])
        for dx in range(7):
            right_coef[dx * 7 + dy, :, :] = spread[tall * dx : tall * dx + tall, 0:128]
            left_coef[dx * 7 + dy, :, :] = spread[tall * dx : tall * dx + tall, 128:256]


def halo_steps(
    right_set, left_set, right_coef, left_coef, right_near, left_near, second, out_hbm,
    right_next, left_next, right_out, left_out, out, sems,
):
    tiles = right_set.shape[0]
    stacks, width = out.shape[:2]
    place = place_in_group()
    everywhere = range(-3, 4)
    for tile in range(right_next.shape[1] // 8):
        rows = pl.ds(8 * tile, 8)
        right = packed_sum(
            lambda t, at: right_set[t, at : at + 8, :], right_coef, 0, tile, tiles, everywhere
        )
        left = packed_sum(
            lambda t, at: left_set[t, at : at + 8, :], left_coef, 0, tile, tiles, everywhere
        )
        for t in range(tiles):
            right_next[t, rows, :] = jnp.where(place >= 3, turn(right[t], 3), 0.0)
            left_next[t, rows, :] = jnp.where(place < 6, turn(left[t], -3), 0.0)
    for tile in range(width // 8):
        rows = pl.ds(8 * tile, 8)
        right = packed_sum(
            lambda t, at: right_next[t, at : at + 8, :], right_near, 0, tile, tiles, everywhere
        )
        left = packed_sum(
            lambda t, at: left_next[t, at : at + 8, :], left_near, 0, tile, tiles, everywhere
        )
        for t in range(tiles):
            right_out[t, rows, :] = right[t]
            left_out[t, rows, :] = left[t]

    lane = lanes()
    copies = []
    for t in range(tiles):
        low, high = PER * t, min(stacks, PER * t + PER)
        for tile in range(width // 8):
            rows = pl.ds(8 * tile, 8)
            right, left = right_out[t, rows, :], left_out[t, rows, :]
            values = []
            for s in range(low, high):
                at = SPAN * (s - low)
                change = jnp.where(lane < 6, turn(left, -at - 3), 0.0)
                change = jnp.where(lane >= 122, turn(right, 122 - at), change)
                values.append(second[s, rows, :] + change)
            for s, value in zip(range(low, high), values):
                out[s, rows, :] = value
        piece = pl.ds(low, high - low)
        copies.append(pltpu.make_async_copy(out.at[piece], out_hbm.at[piece], sems.at[t]))
        copies[-1].start()
    for copy in copies:
        copy.wait()


def local(tracer_mass, recon_table, intersection_weights, intersection_cells, rotation_codes):
    stacks, width, columns = tracer_mass.shape
    shape = lambda *sizes: jax.ShapeDtypeStruct(sizes, F32)
    scratch = lambda *sizes: pltpu.VMEM(sizes, F32)
    tiles = -(-stacks // PER)
    combos = 4 * (width // 8)
    tall, low = width + 16, width + 8
    fixed = lambda *values: [pltpu.with_memory_space_constraint(value, pltpu.HBM) for value in values]
    whole = lambda value: jax.ShapeDtypeStruct(value.shape, value.dtype)
    edge = -(-(6 * stacks + 3 * OFFSETS + 5) // 8) * 8
    integers = lambda *sizes: pltpu.VMEM(sizes, jnp.int32)
    picks = jax.ShapeDtypeStruct((7, 256, 256), jnp.bfloat16)
    regions = intersection_cells.shape[0]

    mass, weights, cells, codes, send_down, send_up = pl.pallas_call(
        edge_rows,
        out_shape=(
            whole(tracer_mass), whole(intersection_weights), whole(intersection_cells),
            whole(rotation_codes), shape(edge, 128), shape(edge, 128),
        ),
        in_specs=[HBM] * 5,
        out_specs=(VMEM,) * 6,
        scratch_shapes=[
            pltpu.SMEM(recon_table.shape, F32),
            scratch(regions, TERMS, 8, 128),
            integers(regions, 8, 128),
            integers(regions, 8, 128),
            scratch(OFFSETS, 8, 128),
            scratch(TERMS, regions, 8, 128),
            scratch(25, regions, 8, 128),
            pltpu.SemaphoreType.DMA((5,)),
        ],
        compiler_params=params(),
        cost_estimate=cost(4 * 10**6),
        name="edge_rows",
    )(*fixed(recon_table, tracer_mass, intersection_weights, intersection_cells, rotation_codes))
    above = shift(send_down, ROW_AXES, 1)
    below = shift(send_up, ROW_AXES, -1)

    stencil = pl.pallas_call(
        coefficients,
        out_shape=shape(OFFSETS, width, 128),
        in_specs=[HBM] + [VMEM] * 3,
        out_specs=VMEM,
        scratch_shapes=[
            pltpu.SMEM(recon_table.shape, F32),
            scratch(TERMS, combos, 8, 128),
            scratch(25, combos, 8, 128),
            pltpu.SemaphoreType.DMA((1,)),
        ],
        compiler_params=params(),
        cost_estimate=cost(8 * 10**6),
        name="coefficients",
    )(*fixed(recon_table), weights, cells, codes)

    own_left, own_right, picks, near = pl.pallas_call(
        pack_own,
        out_shape=(shape(width * (tiles + 1), 128),) * 2 + (picks, picks),
        in_specs=[VMEM] * 2,
        out_specs=(VMEM,) * 4,
        compiler_params=params(),
        cost_estimate=cost(10**6),
        name="pack_own",
    )(mass, stencil)

    middle, own_shifted, right_near, left_near = pl.pallas_call(
        own_part,
        out_shape=(shape(stacks, width - 8, 128),) + (shape(OFFSETS, width, 128),) * 3,
        in_specs=[VMEM] * 3,
        out_specs=(VMEM,) * 4,
        compiler_params=params(),
        cost_estimate=cost(4 * 10**6),
        name="own_part",
    )(mass, stencil, near)

    send = ((width + 12) * (tiles + 1), 128)
    send_a, send_b = pl.pallas_call(
        functools.partial(pack_all, stacks),
        out_shape=(shape(*send),) * 2,
        in_specs=[VMEM] * 4 + [ANY],
        out_specs=(VMEM,) * 2,
        scratch_shapes=[scratch(*send)] * 2,
        compiler_params=params(),
        cost_estimate=cost(10**6),
        name="pack_all",
    )(own_left, own_right, above, below, middle)
    column_a = swap(send_a, COLUMN_AXES, False)
    column_b = swap(send_b, COLUMN_AXES, True)

    second, wide = pl.pallas_call(
        both_steps,
        out_shape=(shape(stacks, width, 128), shape(OFFSETS, low, 128)),
        in_specs=[VMEM] * 6,
        out_specs=(VMEM,) * 2,
        scratch_shapes=[scratch(OFFSETS, low, 128), scratch(stacks, tall, 128), scratch(GROUP, low, 128)],
        compiler_params=params(),
        cost_estimate=cost(12 * 10**6),
        name="both_steps",
    )(mass, stencil, above, below, middle, own_shifted)

    sides = pl.pallas_call(
        side_coefficients,
        out_shape=(shape(tiles, tall, 128),) * 2 + (shape(OFFSETS, low, 128),) * 2,
        in_specs=[VMEM] * 6,
        out_specs=(VMEM,) * 4,
        scratch_shapes=[scratch(2, low, 128)] * 2 + [scratch(7, 7 * low, 128)],
        compiler_params=params(),
        cost_estimate=cost(4 * 10**6),
        name="side_coefficients",
    )(wide, send_a, send_b, column_a, column_b, picks)

    return pl.pallas_call(
        halo_steps,
        out_shape=shape(stacks, width, columns),
        in_specs=[VMEM] * 7,
        out_specs=HBM,
        scratch_shapes=[scratch(tiles, low, 128)] * 2 + [scratch(tiles, width, 128)] * 2
        + [scratch(stacks, width, columns), pltpu.SemaphoreType.DMA((tiles,))],
        compiler_params=params(),
        cost_estimate=cost(4 * 10**6),
        name="halo_steps",
    )(*sides, right_near, left_near, second)


def solution(mesh):
    in_specs = (
        P(None, ("face", "px"), "py"),
        P(),
        P(None, None, ("face", "px"), "py"),
        P(None, ("face", "px"), "py"),
        P(None, ("face", "px"), "py"),
    )
    out_specs = P(None, ("face", "px"), "py")
    return jax.shard_map(local, mesh=mesh, in_specs=in_specs, out_specs=out_specs, check_vma=False)
```

```python
import functools

import jax
import jax.numpy as jnp
import numpy as np
from jax import lax
from jax.experimental import pallas as pl
from jax.experimental.pallas import tpu as pltpu
from jax.sharding import PartitionSpec as P

F32 = jnp.float32
ROW_AXES = ("face", "px")
COLUMN_AXES = "py"
SWAPPED = (0, 2, 1, 5, 4, 3, 9, 8, 7, 6)
POWERS = ((0, 0), (1, 0), (0, 1), (2, 0), (1, 1), (0, 2), (3, 0), (2, 1), (1, 2), (0, 3))
TERMS = 10
OFFSETS = 49
GROUP = 4
SPAN = 9
PER = 14
COEF_PER = 42
VMEM = pl.BlockSpec(memory_space=pltpu.VMEM)
ANY = pl.BlockSpec(memory_space=pl.ANY)
HBM = pl.BlockSpec(memory_space=pltpu.HBM)


def params():
    return pltpu.CompilerParams(vmem_limit_bytes=40 * 1024 * 1024)


def cost(operations):
    return pl.CostEstimate(flops=operations, bytes_accessed=1 << 20, transcendentals=0)


def swap(block, axes, odd_first):
    count = lax.axis_size(axes)
    partner = list(range(count))
    for low in range(1 if odd_first else 0, count, 2):
        high = (low + 1) % count
        partner[low], partner[high] = high, low
    return lax.ppermute(block, axes, list(enumerate(partner)))


def shift(block, axes, step):
    count = lax.axis_size(axes)
    return lax.ppermute(block, axes, [(index, (index + step) % count) for index in range(count)])


def ends(axes):
    index = lax.axis_index(axes)
    return index == 0, index == lax.axis_size(axes) - 1


def is_even(axes):
    return lax.rem(lax.axis_index(axes), 2) == 0


def turn(value, amount):
    amount %= 128
    return pltpu.roll(value, amount, 1) if amount else value


def lanes(rows=8):
    return lax.broadcasted_iota(jnp.int32, (rows, 128), 1)


def fill_stencil(recon, weights, cells, codes, turned, spread, stencil, tiles):
    zero = jnp.zeros((8, 128), F32)
    for g in range(tiles):
        rows = pl.ds(8 * g, 8)
        for m in range(4):
            code = codes[m, rows, :]
            odd = (code & 1) == 1
            sign_x = jnp.where(code >= 2, -1.0, 1.0).astype(F32)
            sign_y = jnp.where((code == 1) | (code == 2), -1.0, 1.0).astype(F32)
            sign_xy = sign_x * sign_y
            values = [weights[m, t, rows, :] for t in range(TERMS)]
            for t, (a, b) in enumerate(POWERS):
                value = values[t]
                if SWAPPED[t] != t:
                    value = jnp.where(odd, values[SWAPPED[t]], value)
                if a % 2 and b % 2:
                    value = value * sign_xy
                elif a % 2:
                    value = value * sign_x
                elif b % 2:
                    value = value * sign_y
                turned[t, m * tiles + g] = value

    combos = 4 * tiles

    def five_taps(jx, carry):
        total = [[None] * combos for jy in range(5)]
        for t in range(TERMS):
            values = [turned[t, c] for c in range(combos)]
            for jy in range(5):
                scale = recon[t, 5 * jx + jy]
                for c in range(combos):
                    term = values[c] * scale
                    total[jy][c] = term if t == 0 else total[jy][c] + term
        for jy in range(5):
            for c in range(combos):
                spread[5 * jx + jy, c] = total[jy][c]
        return carry

    lax.fori_loop(0, 5, five_taps, 0)

    for g in range(tiles):
        rows = pl.ds(8 * g, 8)
        masks = []
        for m in range(4):
            cell = cells[m, rows, :]
            first = jnp.where(cell < 3, 0, jnp.where(cell < 6, 3, 6))
            across = cell - first
            masks.append((cell < 3, cell < 6, across == 0, across <= 1))
        for ox in range(7):
            total = [None] * 7
            for m in range(4):
                low_x, mid_x, low_y, mid_y = masks[m]

                def tap(jx, jy):
                    if 0 <= jx < 5 and 0 <= jy < 5:
                        return spread[jx * 5 + jy, m * tiles + g]
                    return zero

                line = [
                    jnp.where(low_x, tap(ox, jy), jnp.where(mid_x, tap(ox - 1, jy), tap(ox - 2, jy)))
                    for jy in range(5)
                ]
                padded = [zero, zero] + line + [zero, zero]
                for oy in range(7):
                    value = jnp.where(
                        low_y, padded[oy + 2], jnp.where(mid_y, padded[oy + 1], padded[oy])
                    )
                    total[oy] = value if m == 0 else total[oy] + value
            for oy in range(7):
                stencil[ox * 7 + oy, rows, :] = total[oy]


def edge_rows(
    recon_hbm, mass_hbm, weights_hbm, cells_hbm, codes_hbm,
    mass, weights, cells, codes, send_down, send_up,
    recon, edge_weights, edge_cells, edge_codes, edge_stencil, turned, spread, sems,
):
    sources = (recon_hbm, codes_hbm, weights_hbm, cells_hbm, mass_hbm)
    targets = (recon, codes, weights, cells, mass)
    copies = [pltpu.make_async_copy(a, b, sems.at[i]) for i, (a, b) in enumerate(zip(sources, targets))]
    for copy in copies:
        copy.start()
    for copy in copies:
        copy.wait()
    stacks, width = mass.shape[:2]
    for target, source in ((edge_weights, weights), (edge_cells, cells), (edge_codes, codes)):
        for index in np.ndindex(*source.shape[:-2]):
            target[index + (slice(0, 3), slice(None))] = source[index + (slice(0, 3), slice(None))]
            target[index + (slice(3, 8), slice(None))] = source[index + (slice(width - 5, width), slice(None))]
    fill_stencil(recon, edge_weights, edge_cells, edge_codes, turned, spread, edge_stencil, 1)
    for send, mass_at, stencil_at in ((send_down, width - 6, 5), (send_up, 0, 0)):
        for s in range(stacks):
            send[6 * s : 6 * s + 6, :] = mass[s, mass_at : mass_at + 6, :]
        for o in range(OFFSETS):
            at = 6 * stacks + 3 * o
            send[at : at + 3, :] = edge_stencil[o, stencil_at : stencil_at + 3, :]


def coefficients(recon_hbm, weights, cells, codes, stencil, recon, turned, spread, sem):
    copy = pltpu.make_async_copy(recon_hbm, recon, sem.at[0])
    copy.start()
    copy.wait()
    fill_stencil(recon, weights, cells, codes, turned, spread, stencil, stencil.shape[1] // 8)


def pack_stacks(load, stacks, tile):
    lane = lanes()
    left = jnp.zeros((8, 128), F32)
    right = jnp.zeros((8, 128), F32)
    for s in range(PER * tile, min(stacks, PER * tile + PER)):
        at = SPAN * (s % PER)
        moved = turn(load(s), at - 122)
        right = jnp.where((lane >= at) & (lane < at + 6), moved, right)
        left = jnp.where(on_ring(lane, at + 6, at + 12), moved, left)
    return turn(left, -3), right


def on_ring(lane, low, high):
    return (lane >= low) | (lane < high - 128) if high > 128 else (lane >= low) & (lane < high)


def pack_coefficients(load):
    lane = lanes()
    left = jnp.zeros((8, 128), F32)
    right = jnp.zeros((8, 128), F32)
    for o in range(COEF_PER):
        at = 3 * o
        moved = turn(load(o), at - 125)
        right = jnp.where((lane >= at) & (lane < at + 3), moved, right)
        left = jnp.where(on_ring(lane, at + 3, at + 6), moved, left)
    return turn(left, -3), right


def add_spare(load, left, right):
    lane = lanes()
    for o in range(COEF_PER, OFFSETS):
        at = SPAN * (o - COEF_PER)
        value = load(o)
        left = jnp.where((lane >= at) & (lane < at + 3), turn(value, at), left)
        right = jnp.where((lane >= at + 6) & (lane < at + 9), turn(value, at - 119), right)
    return left, right


def fill_near(near):
    lane = lanes(1)
    group = (lane * 57) >> 9
    at = lane - SPAN * group
    source = lax.broadcasted_iota(jnp.int32, (128, 128), 0)
    for dy in range(-3, 4):
        q = at - dy
        right = jnp.where((at >= 3) & (q >= 0) & (q < 6), 122 + q, -1)
        left = jnp.where((at < 6) & (q >= 3) & (q < 9), q - 3, -1)
        for side, wanted in enumerate((right, left)):
            wanted = jnp.where(group < PER, wanted, -1)
            picked = jnp.where(source == wanted, 1.0, 0.0).astype(jnp.bfloat16)
            near[dy + 3, 0:128, 128 * side : 128 * side + 128] = picked
            near[dy + 3, 128:256, 128 * side : 128 * side + 128] = picked


def replicate(value, picks):
    high = value.astype(jnp.bfloat16)
    low = (value - high.astype(F32)).astype(jnp.bfloat16)
    return jnp.dot(jnp.concatenate([high, low], axis=1), picks, preferred_element_type=F32)


def fill_picks(picks):
    lane = lanes(1)
    group = (lane * 57) >> 9
    at = lane - SPAN * group
    source = lax.broadcasted_iota(jnp.int32, (128, 128), 0)
    for dy in range(-3, 4):
        q = at - dy
        halo = (q >= 3) & (q < 6)
        right = jnp.where(halo, 57 + q, jnp.where((q >= 0) & (q < 3) & (at >= 3), 125 + q, -1))
        left = jnp.where(halo, 61 + q, jnp.where((q >= 6) & (q < 9) & (at < 6), q - 6, -1))
        for side, wanted in enumerate((right, left)):
            wanted = jnp.where(group < PER, wanted, -1)
            picked = jnp.where(source == wanted, 1.0, 0.0).astype(jnp.bfloat16)
            picks[dy + 3, 0:128, 128 * side : 128 * side + 128] = picked
            picks[dy + 3, 128:256, 128 * side : 128 * side + 128] = picked


def pack_own(mass, stencil, left, right, picks, near):
    fill_picks(picks)
    fill_near(near)
    stacks, width = mass.shape[:2]
    tiles = -(-stacks // PER)
    for half in range(width // 8):
        rows = pl.ds(8 * half, 8)
        for tile in range(tiles):
            at = width * tile + 8 * half
            values = pack_stacks(lambda s: mass[s, rows, :], stacks, tile)
            if tile == 0:
                values = add_spare(lambda o: stencil[o, rows, :], *values)
            left[at : at + 8, :], right[at : at + 8, :] = values
        at = width * tiles + 8 * half
        left[at : at + 8, :], right[at : at + 8, :] = pack_coefficients(lambda o: stencil[o, rows, :])


def pack_all(stacks, own_left, own_right, above, below, middle, send_a, send_b, left, right):
    tiles = -(-stacks // PER)
    width = own_left.shape[0] // (tiles + 1)
    tall = width + 12
    for send, own in ((left, own_left), (right, own_right)):
        for tile in range(tiles + 1):
            send[tall * tile : tall * tile + width, :] = own[width * tile : width * tile + width, :]
        end = tall * tiles + width + 6
        send[end:, :] = jnp.zeros((send.shape[0] - end, 128), F32)
    first, last = ends(ROW_AXES)
    for got, outside, place, coef_place in (
        (above, first, width, width), (below, last, width + 6, width + 3)
    ):
        coef = lambda o: got[6 * stacks + 3 * o : 6 * stacks + 3 * o + 8, :]
        for tile in range(tiles):
            at = tall * tile + place
            packed = pack_stacks(lambda s: got[6 * s : 6 * s + 8, :], stacks, tile)
            if tile == 0:
                spare = add_spare(coef, *packed)
                packed = [
                    jnp.where(lax.broadcasted_iota(jnp.int32, (8, 128), 0) < 3, with_spare, without)
                    for with_spare, without in zip(spare, packed)
                ]
            left[at : at + 6, :] = jnp.where(outside, 0.0, packed[0][0:6])
            right[at : at + 6, :] = jnp.where(outside, 0.0, packed[1][0:6])
        at = tall * tiles + coef_place
        packed = pack_coefficients(coef)
        left[at : at + 3, :] = jnp.where(outside, 0.0, packed[0][0:3])
        right[at : at + 3, :] = jnp.where(outside, 0.0, packed[1][0:3])
    choose(is_even(COLUMN_AXES), right, left, send_a, send_b)


def choose(even, first, second, first_out, second_out):
    @pl.when(even)
    def _():
        first_out[...] = first[...]
        second_out[...] = second[...]

    @pl.when(jnp.logical_not(even))
    def _():
        first_out[...] = second[...]
        second_out[...] = first[...]


def main_sum(load, coef, coef_at, tile):
    fields = [[load(k, 8 * tile + dx) for k in range(GROUP)] for dx in range(7)]
    total = [None] * GROUP
    for dy in range(7):
        part = [None] * GROUP
        for dx in range(7):
            at = coef_at + 8 * tile
            scale = coef[dx * 7 + dy, at : at + 8, :]
            for k in range(GROUP):
                term = scale * fields[dx][k]
                part[k] = term if dx == 0 else part[k] + term
        for k in range(GROUP):
            moved = turn(part[k], 3 - dy)
            total[k] = moved if dy == 0 else total[k] + moved
    return total


def shift_rows(load, store, dys=range(-3, 4)):
    lane = lanes()
    for dy in dys:
        values = [turn(load(dx * 7 + dy + 3), dy) for dx in range(7)]
        if dy > 0:
            values = [jnp.where(lane >= dy, value, 0.0) for value in values]
        elif dy < 0:
            values = [jnp.where(lane < 128 + dy, value, 0.0) for value in values]
        for dx in range(7):
            store(dx * 7 + dy + 3, values[dx])


def own_part(mass, stencil, near, middle, own_shifted, right_near, left_near):
    stacks, width = mass.shape[:2]
    for tile in range(width // 8):
        rows = pl.ds(8 * tile, 8)

        def store(o, value):
            own_shifted[o, rows, :] = value

        shift_rows(lambda o: stencil[o, rows, :], store)

    def some_stacks(group, carry):
        for tile in range((width - 8) // 8):
            total = main_sum(lambda k, at: mass[group * GROUP + k, 2 + at : 10 + at, :], own_shifted, 5, tile)
            for k in range(GROUP):
                middle[group * GROUP + k, 8 * tile : 8 * tile + 8, :] = total[k]
        return carry

    lax.fori_loop(0, stacks // GROUP, some_stacks, 0)
    for dy in range(7):
        value = jnp.concatenate([stencil[dx * 7 + dy, :, :] for dx in range(7)], axis=0)
        spread = replicate(value, near[dy])
        for dx in range(7):
            right_near[dx * 7 + dy, :, :] = spread[width * dx : width * dx + width, 0:128]
            left_near[dx * 7 + dy, :, :] = spread[width * dx : width * dx + width, 128:256]


def both_steps(mass, stencil, above, below, middle, own_shifted, second, wide, shifted, field, partial):
    stacks, width = mass.shape[:2]
    first, last = ends(ROW_AXES)
    for s in range(stacks):
        at = 6 * s
        field[s, 0:6, :] = jnp.where(first, 0.0, above[at : at + 6, :])
        field[s, 6 : width + 6, :] = mass[s, :, :]
        field[s, width + 6 : width + 12, :] = jnp.where(last, 0.0, below[at : at + 6, :])
        field[s, width + 12 : width + 16, :] = jnp.zeros((4, 128), F32)
    for o in range(OFFSETS):
        at = 6 * stacks + 3 * o
        wide[o, 0:3, :] = jnp.where(first, 0.0, above[at : at + 3, :])
        wide[o, 3 : width + 3, :] = stencil[o, :, :]
        wide[o, width + 3 : width + 6, :] = jnp.where(last, 0.0, below[at : at + 3, :])
        wide[o, width + 6 : width + 8, :] = jnp.zeros((2, 128), F32)
    tiles = (0, width // 8)
    for tile in tiles:
        rows = pl.ds(8 * tile, 8)

        def store(o, value):
            shifted[o, rows, :] = value

        shift_rows(lambda o: wide[o, rows, :], store)

    def first_step(group, carry):
        totals = [
            main_sum(lambda k, at: field[group * GROUP + k, at : at + 8, :], shifted, 0, tile)
            for tile in tiles
        ]
        for k in range(GROUP):
            s = group * GROUP + k
            partial[s, 8:width, :] = middle[s, :, :]
            for tile, total in zip(tiles, totals):
                partial[s, 8 * tile : 8 * tile + 8, :] = total[k]
        return carry

    lax.fori_loop(0, stacks // GROUP, first_step, 0)

    def second_step(group, carry):
        totals = [
            main_sum(lambda k, at: partial[group * GROUP + k, at : at + 8, :], own_shifted, 0, tile)
            for tile in range(width // 8)
        ]
        for k in range(GROUP):
            for tile, total in enumerate(totals):
                second[group * GROUP + k, 8 * tile : 8 * tile + 8, :] = total[k]
        return carry

    lax.fori_loop(0, stacks // GROUP, second_step, 0)


def packed_sum(load, coef, coef_at, tile, tiles, dys):
    fields = [[load(t, 8 * tile + dx) for t in range(tiles)] for dx in range(7)]
    total = [None] * tiles
    for dy in dys:
        part = [None] * tiles
        for dx in range(7):
            at = coef_at + 8 * tile
            scale = coef[dx * 7 + dy + 3, at : at + 8, :]
            for t in range(tiles):
                term = scale * fields[dx][t]
                part[t] = term if dx == 0 else part[t] + term
        for t in range(tiles):
            moved = turn(part[t], -dy)
            total[t] = moved if total[t] is None else total[t] + moved
    return total


def place_in_group(rows=8):
    lane = lanes(rows)
    return lane - SPAN * ((lane * 57) >> 9)


def side_coefficients(
    wide, send_a, send_b, got_a, got_b, picks,
    right_set, left_set, right_coef, left_coef, right_halo, left_halo, rows_of,
):
    tall = wide.shape[1]
    width = tall - 8
    tiles = right_set.shape[0]
    lane = lanes()

    first, last = ends(COLUMN_AXES)

    def gather(sent_right, sent_left, got_right, got_left):
        part = width + 12
        place = place_in_group(part)
        rows = [slice(part * tile, part * tile + part) for tile in range(tiles)]
        from_right = [jnp.where(last, 0.0, got_right[at, :]) for at in rows]
        from_left = [jnp.where(first, 0.0, got_left[at, :]) for at in rows]
        for tile, at in enumerate(rows):
            right = jnp.where(place < 3, turn(sent_right[at, :], -3), from_right[tile])
            left = jnp.where(place >= 6, turn(sent_left[at, :], 3), from_left[tile])
            for target, value in ((right_set, right), (left_set, left)):
                target[tile, 6 : width + 6, :] = value[0:width]
                target[tile, 0:6, :] = value[width : width + 6]
                target[tile, width + 6 : width + 12, :] = value[width + 6 : width + 12]
                target[tile, width + 12 : width + 16, :] = jnp.zeros((4, 128), F32)
        coefs = slice(part * tiles, part * tiles + width + 6)
        for target, source, got, outside in (
            (right_halo, from_right, got_right, last), (left_halo, from_left, got_left, first)
        ):
            value = jnp.where(outside, 0.0, got[coefs, :])
            spare = source[0]
            for tile, own, above, below in (
                (0, value[0:width], value[width : width + 3], value[width + 3 : width + 6]),
                (1, spare[0:width], spare[width : width + 3], spare[width + 6 : width + 9]),
            ):
                target[tile, 3 : width + 3, :] = own
                target[tile, 0:3, :] = above
                target[tile, width + 3 : width + 6, :] = below
                target[tile, width + 6 : width + 8, :] = jnp.zeros((2, 128), F32)

    even = is_even(COLUMN_AXES)

    @pl.when(even)
    def _():
        gather(send_a, send_b, got_a, got_b)

    @pl.when(jnp.logical_not(even))
    def _():
        gather(send_b, send_a, got_b, got_a)

    from_right = (lane >= 60) & (lane < 63)
    from_left = (lane >= 64) & (lane < 67)
    for tile in range(tall // 8):
        rows = pl.ds(8 * tile, 8)
        right_rows = [right_halo[t, rows, :] for t in range(2)]
        left_rows = [left_halo[t, rows, :] for t in range(2)]
        for dy in range(7):
            values = []
            for dx in range(7):
                o = dx * 7 + dy
                if o < COEF_PER:
                    right = turn(right_rows[0], 60 - 3 * o)
                    left = turn(left_rows[0], 64 - 3 * o)
                else:
                    at = SPAN * (o - COEF_PER)
                    right = turn(right_rows[1], 60 - at)
                    left = turn(left_rows[1], 58 - at)
                values.append(
                    jnp.where(from_right, right, jnp.where(from_left, left, wide[o, rows, :]))
                )
            for dx in range(7):
                at = tall * dx + 8 * tile
                rows_of[dy, at : at + 8, :] = values[dx]

    for dy in range(7):
        spread = replicate(rows_of[dy], picks[dy])
        for dx in range(7):
            right_coef[dx * 7 + dy, :, :] = spread[tall * dx : tall * dx + tall, 0:128]
            left_coef[dx * 7 + dy, :, :] = spread[tall * dx : tall * dx + tall, 128:256]


def halo_steps(
    right_set, left_set, right_coef, left_coef, right_near, left_near, second, out_hbm,
    right_next, left_next, right_out, left_out, out, sems,
):
    tiles = right_set.shape[0]
    stacks, width = out.shape[:2]
    place = place_in_group()
    everywhere = range(-3, 4)
    for tile in range(right_next.shape[1] // 8):
        rows = pl.ds(8 * tile, 8)
        right = packed_sum(
            lambda t, at: right_set[t, at : at + 8, :], right_coef, 0, tile, tiles, everywhere
        )
        left = packed_sum(
            lambda t, at: left_set[t, at : at + 8, :], left_coef, 0, tile, tiles, everywhere
        )
        for t in range(tiles):
            right_next[t, rows, :] = jnp.where(place >= 3, turn(right[t], 3), 0.0)
            left_next[t, rows, :] = jnp.where(place < 6, turn(left[t], -3), 0.0)
    for tile in range(width // 8):
        rows = pl.ds(8 * tile, 8)
        right = packed_sum(
            lambda t, at: right_next[t, at : at + 8, :], right_near, 0, tile, tiles, everywhere
        )
        left = packed_sum(
            lambda t, at: left_next[t, at : at + 8, :], left_near, 0, tile, tiles, everywhere
        )
        for t in range(tiles):
            right_out[t, rows, :] = right[t]
            left_out[t, rows, :] = left[t]

    lane = lanes()
    copies = []
    for t in range(tiles):
        low, high = PER * t, min(stacks, PER * t + PER)
        for tile in range(width // 8):
            rows = pl.ds(8 * tile, 8)
            right, left = right_out[t, rows, :], left_out[t, rows, :]
            values = []
            for s in range(low, high):
                at = SPAN * (s - low)
                change = jnp.where(lane < 6, turn(left, -at - 3), 0.0)
                change = jnp.where(lane >= 122, turn(right, 122 - at), change)
                values.append(second[s, rows, :] + change)
            for s, value in zip(range(low, high), values):
                out[s, rows, :] = value
        piece = pl.ds(low, high - low)
        copies.append(pltpu.make_async_copy(out.at[piece], out_hbm.at[piece], sems.at[t]))
        copies[-1].start()
    for copy in copies:
        copy.wait()


def local(tracer_mass, recon_table, intersection_weights, intersection_cells, rotation_codes):
    stacks, width, columns = tracer_mass.shape
    shape = lambda *sizes: jax.ShapeDtypeStruct(sizes, F32)
    scratch = lambda *sizes: pltpu.VMEM(sizes, F32)
    tiles = -(-stacks // PER)
    combos = 4 * (width // 8)
    tall, low = width + 16, width + 8
    fixed = lambda *values: [pltpu.with_memory_space_constraint(value, pltpu.HBM) for value in values]
    whole = lambda value: jax.ShapeDtypeStruct(value.shape, value.dtype)
    edge = -(-(6 * stacks + 3 * OFFSETS + 5) // 8) * 8
    integers = lambda *sizes: pltpu.VMEM(sizes, jnp.int32)
    picks = jax.ShapeDtypeStruct((7, 256, 256), jnp.bfloat16)
    regions = intersection_cells.shape[0]

    mass, weights, cells, codes, send_down, send_up = pl.pallas_call(
        edge_rows,
        out_shape=(
            whole(tracer_mass), whole(intersection_weights), whole(intersection_cells),
            whole(rotation_codes), shape(edge, 128), shape(edge, 128),
        ),
        in_specs=[HBM] * 5,
        out_specs=(VMEM,) * 6,
        scratch_shapes=[
            pltpu.SMEM(recon_table.shape, F32),
            scratch(regions, TERMS, 8, 128),
            integers(regions, 8, 128),
            integers(regions, 8, 128),
            scratch(OFFSETS, 8, 128),
            scratch(TERMS, regions, 8, 128),
            scratch(25, regions, 8, 128),
            pltpu.SemaphoreType.DMA((5,)),
        ],
        compiler_params=params(),
        cost_estimate=cost(4 * 10**6),
        name="edge_rows",
    )(*fixed(recon_table, tracer_mass, intersection_weights, intersection_cells, rotation_codes))
    above = shift(send_down, ROW_AXES, 1)
    below = shift(send_up, ROW_AXES, -1)

    stencil = pl.pallas_call(
        coefficients,
        out_shape=shape(OFFSETS, width, 128),
        in_specs=[HBM] + [VMEM] * 3,
        out_specs=VMEM,
        scratch_shapes=[
            pltpu.SMEM(recon_table.shape, F32),
            scratch(TERMS, combos, 8, 128),
            scratch(25, combos, 8, 128),
            pltpu.SemaphoreType.DMA((1,)),
        ],
        compiler_params=params(),
        cost_estimate=cost(8 * 10**6),
        name="coefficients",
    )(*fixed(recon_table), weights, cells, codes)

    own_left, own_right, picks, near = pl.pallas_call(
        pack_own,
        out_shape=(shape(width * (tiles + 1), 128),) * 2 + (picks, picks),
        in_specs=[VMEM] * 2,
        out_specs=(VMEM,) * 4,
        compiler_params=params(),
        cost_estimate=cost(10**6),
        name="pack_own",
    )(mass, stencil)

    middle, own_shifted, right_near, left_near = pl.pallas_call(
        own_part,
        out_shape=(shape(stacks, width - 8, 128),) + (shape(OFFSETS, width, 128),) * 3,
        in_specs=[VMEM] * 3,
        out_specs=(VMEM,) * 4,
        compiler_params=params(),
        cost_estimate=cost(4 * 10**6),
        name="own_part",
    )(mass, stencil, near)

    send = ((width + 12) * (tiles + 1), 128)
    send_a, send_b = pl.pallas_call(
        functools.partial(pack_all, stacks),
        out_shape=(shape(*send),) * 2,
        in_specs=[VMEM] * 4 + [ANY],
        out_specs=(VMEM,) * 2,
        scratch_shapes=[scratch(*send)] * 2,
        compiler_params=params(),
        cost_estimate=cost(10**6),
        name="pack_all",
    )(own_left, own_right, above, below, middle)
    column_a = swap(send_a, COLUMN_AXES, False)
    column_b = swap(send_b, COLUMN_AXES, True)

    second, wide = pl.pallas_call(
        both_steps,
        out_shape=(shape(stacks, width, 128), shape(OFFSETS, low, 128)),
        in_specs=[VMEM] * 6,
        out_specs=(VMEM,) * 2,
        scratch_shapes=[scratch(OFFSETS, low, 128), scratch(stacks, tall, 128), scratch(stacks, low, 128)],
        compiler_params=params(),
        cost_estimate=cost(12 * 10**6),
        name="both_steps",
    )(mass, stencil, above, below, middle, own_shifted)

    sides = pl.pallas_call(
        side_coefficients,
        out_shape=(shape(tiles, tall, 128),) * 2 + (shape(OFFSETS, low, 128),) * 2,
        in_specs=[VMEM] * 6,
        out_specs=(VMEM,) * 4,
        scratch_shapes=[scratch(2, low, 128)] * 2 + [scratch(7, 7 * low, 128)],
        compiler_params=params(),
        cost_estimate=cost(4 * 10**6),
        name="side_coefficients",
    )(wide, send_a, send_b, column_a, column_b, picks)

    return pl.pallas_call(
        halo_steps,
        out_shape=shape(stacks, width, columns),
        in_specs=[VMEM] * 7,
        out_specs=HBM,
        scratch_shapes=[scratch(tiles, low, 128)] * 2 + [scratch(tiles, width, 128)] * 2
        + [scratch(stacks, width, columns), pltpu.SemaphoreType.DMA((tiles,))],
        compiler_params=params(),
        cost_estimate=cost(4 * 10**6),
        name="halo_steps",
    )(*sides, right_near, left_near, second)


def solution(mesh):
    in_specs = (
        P(None, ("face", "px"), "py"),
        P(),
        P(None, None, ("face", "px"), "py"),
        P(None, ("face", "px"), "py"),
        P(None, ("face", "px"), "py"),
    )
    out_specs = P(None, ("face", "px"), "py")
    return jax.shard_map(local, mesh=mesh, in_specs=in_specs, out_specs=out_specs, check_vma=False)
```

```python
import functools

import jax
import jax.numpy as jnp
import numpy as np
from jax import lax
from jax.experimental import pallas as pl
from jax.experimental.pallas import tpu as pltpu
from jax.sharding import PartitionSpec as P

F32 = jnp.float32
ROW_AXES = ("face", "px")
COLUMN_AXES = "py"
SWAPPED = (0, 2, 1, 5, 4, 3, 9, 8, 7, 6)
POWERS = ((0, 0), (1, 0), (0, 1), (2, 0), (1, 1), (0, 2), (3, 0), (2, 1), (1, 2), (0, 3))
TERMS = 10
OFFSETS = 49
GROUP = 4
SPAN = 9
PER = 14
COEF_PER = 42
VMEM = pl.BlockSpec(memory_space=pltpu.VMEM)
ANY = pl.BlockSpec(memory_space=pl.ANY)
HBM = pl.BlockSpec(memory_space=pltpu.HBM)


def params():
    return pltpu.CompilerParams(vmem_limit_bytes=40 * 1024 * 1024)


def cost(operations):
    return pl.CostEstimate(flops=operations, bytes_accessed=1 << 20, transcendentals=0)


def column_swap(block, odd_first):
    chains, count = lax.axis_size(ROW_AXES), lax.axis_size(COLUMN_AXES)
    column = list(range(count))
    for low in range(1 if odd_first else 0, count - 1, 2):
        column[low], column[low + 1] = low + 1, low
    pairs = []
    for chain in range(chains):
        for place in range(count):
            target = (chain, column[place])
            if column[place] == place and chains % 2 == 0:
                target = (chain ^ 1, place)
            pairs.append((chain * count + place, target[0] * count + target[1]))
    return lax.ppermute(block, ROW_AXES + (COLUMN_AXES,), pairs)


def shift(block, axes, step):
    count = lax.axis_size(axes)
    return lax.ppermute(block, axes, [(index, (index + step) % count) for index in range(count)])


def ends(axes):
    index = lax.axis_index(axes)
    return index == 0, index == lax.axis_size(axes) - 1


def is_even(axes):
    return lax.rem(lax.axis_index(axes), 2) == 0


def turn(value, amount):
    amount %= 128
    return pltpu.roll(value, amount, 1) if amount else value


def lanes(rows=8):
    return lax.broadcasted_iota(jnp.int32, (rows, 128), 1)


def fill_stencil(recon, weights, cells, codes, turned, spread, stencil, tiles):
    zero = jnp.zeros((8, 128), F32)
    for g in range(tiles):
        rows = pl.ds(8 * g, 8)
        for m in range(4):
            code = codes[m, rows, :]
            odd = (code & 1) == 1
            sign_x = jnp.where(code >= 2, -1.0, 1.0).astype(F32)
            sign_y = jnp.where((code == 1) | (code == 2), -1.0, 1.0).astype(F32)
            sign_xy = sign_x * sign_y
            values = [weights[m, t, rows, :] for t in range(TERMS)]
            for t, (a, b) in enumerate(POWERS):
                value = values[t]
                if SWAPPED[t] != t:
                    value = jnp.where(odd, values[SWAPPED[t]], value)
                if a % 2 and b % 2:
                    value = value * sign_xy
                elif a % 2:
                    value = value * sign_x
                elif b % 2:
                    value = value * sign_y
                turned[t, m * tiles + g] = value

    combos = 4 * tiles

    def five_taps(jx, carry):
        total = [[None] * combos for jy in range(5)]
        for t in range(TERMS):
            values = [turned[t, c] for c in range(combos)]
            for jy in range(5):
                scale = recon[t, 5 * jx + jy]
                for c in range(combos):
                    term = values[c] * scale
                    total[jy][c] = term if t == 0 else total[jy][c] + term
        for jy in range(5):
            for c in range(combos):
                spread[5 * jx + jy, c] = total[jy][c]
        return carry

    lax.fori_loop(0, 5, five_taps, 0)

    for g in range(tiles):
        rows = pl.ds(8 * g, 8)
        masks = []
        for m in range(4):
            cell = cells[m, rows, :]
            first = jnp.where(cell < 3, 0, jnp.where(cell < 6, 3, 6))
            across = cell - first
            masks.append((cell < 3, cell < 6, across == 0, across <= 1))
        for ox in range(7):
            total = [None] * 7
            for m in range(4):
                low_x, mid_x, low_y, mid_y = masks[m]

                def tap(jx, jy):
                    if 0 <= jx < 5 and 0 <= jy < 5:
                        return spread[jx * 5 + jy, m * tiles + g]
                    return zero

                line = [
                    jnp.where(low_x, tap(ox, jy), jnp.where(mid_x, tap(ox - 1, jy), tap(ox - 2, jy)))
                    for jy in range(5)
                ]
                padded = [zero, zero] + line + [zero, zero]
                for oy in range(7):
                    value = jnp.where(
                        low_y, padded[oy + 2], jnp.where(mid_y, padded[oy + 1], padded[oy])
                    )
                    total[oy] = value if m == 0 else total[oy] + value
            for oy in range(7):
                stencil[ox * 7 + oy, rows, :] = total[oy]


def edge_rows(
    recon_hbm, mass_hbm, weights_hbm, cells_hbm, codes_hbm,
    mass, weights, cells, codes, send_down, send_up,
    recon, edge_weights, edge_cells, edge_codes, edge_stencil, turned, spread, sems,
):
    sources = (recon_hbm, codes_hbm, weights_hbm, cells_hbm, mass_hbm)
    targets = (recon, codes, weights, cells, mass)
    copies = [pltpu.make_async_copy(a, b, sems.at[i]) for i, (a, b) in enumerate(zip(sources, targets))]
    for copy in copies:
        copy.start()
    for copy in copies:
        copy.wait()
    stacks, width = mass.shape[:2]
    for target, source in ((edge_weights, weights), (edge_cells, cells), (edge_codes, codes)):
        for index in np.ndindex(*source.shape[:-2]):
            target[index + (slice(0, 3), slice(None))] = source[index + (slice(0, 3), slice(None))]
            target[index + (slice(3, 8), slice(None))] = source[index + (slice(width - 5, width), slice(None))]
    fill_stencil(recon, edge_weights, edge_cells, edge_codes, turned, spread, edge_stencil, 1)
    for send, mass_at, stencil_at in ((send_down, width - 6, 5), (send_up, 0, 0)):
        for s in range(stacks):
            send[6 * s : 6 * s + 6, :] = mass[s, mass_at : mass_at + 6, :]
        for o in range(OFFSETS):
            at = 6 * stacks + 3 * o
            send[at : at + 3, :] = edge_stencil[o, stencil_at : stencil_at + 3, :]


def coefficients(recon_hbm, weights, cells, codes, stencil, recon, turned, spread, sem):
    copy = pltpu.make_async_copy(recon_hbm, recon, sem.at[0])
    copy.start()
    copy.wait()
    fill_stencil(recon, weights, cells, codes, turned, spread, stencil, stencil.shape[1] // 8)


def pack_stacks(load, stacks, tile):
    lane = lanes()
    left = jnp.zeros((8, 128), F32)
    right = jnp.zeros((8, 128), F32)
    for s in range(PER * tile, min(stacks, PER * tile + PER)):
        at = SPAN * (s % PER)
        moved = turn(load(s), at - 122)
        right = jnp.where(lane >= at, moved, right)
        left = jnp.where(from_place(lane, at + 6, at + 12), moved, left)
    return turn(left, -3), right


def from_place(lane, low, high):
    return (lane >= low) | (lane < high - 128) if high > 128 else lane >= low


def pack_coefficients(load):
    lane = lanes()
    left = jnp.zeros((8, 128), F32)
    right = jnp.zeros((8, 128), F32)
    for o in range(COEF_PER):
        at = 3 * o
        moved = turn(load(o), at - 125)
        right = jnp.where(lane >= at, moved, right)
        left = jnp.where(from_place(lane, at + 3, at + 6), moved, left)
    return turn(left, -3), right


def add_spare(load, left, right):
    lane = lanes()
    for o in range(COEF_PER, OFFSETS):
        at = SPAN * (o - COEF_PER)
        value = load(o)
        left = jnp.where((lane >= at) & (lane < at + 3), turn(value, at), left)
        right = jnp.where((lane >= at + 6) & (lane < at + 9), turn(value, at - 119), right)
    return left, right


def fill_near(near):
    lane = lanes(1)
    group = (lane * 57) >> 9
    at = lane - SPAN * group
    source = lax.broadcasted_iota(jnp.int32, (128, 128), 0)
    for dy in range(-3, 4):
        q = at - dy
        right = jnp.where((at >= 3) & (q >= 0) & (q < 6), 122 + q, -1)
        left = jnp.where((at < 6) & (q >= 3) & (q < 9), q - 3, -1)
        for side, wanted in enumerate((right, left)):
            wanted = jnp.where(group < PER, wanted, -1)
            picked = jnp.where(source == wanted, 1.0, 0.0).astype(jnp.bfloat16)
            near[dy + 3, 0:128, 128 * side : 128 * side + 128] = picked
            near[dy + 3, 128:256, 128 * side : 128 * side + 128] = picked


def replicate(value, picks):
    high = value.astype(jnp.bfloat16)
    low = (value - high.astype(F32)).astype(jnp.bfloat16)
    return jnp.dot(jnp.concatenate([high, low], axis=1), picks, preferred_element_type=F32)


def fill_picks(picks):
    lane = lanes(1)
    group = (lane * 57) >> 9
    at = lane - SPAN * group
    source = lax.broadcasted_iota(jnp.int32, (128, 128), 0)
    for dy in range(-3, 4):
        q = at - dy
        halo = (q >= 3) & (q < 6)
        right = jnp.where(halo, 57 + q, jnp.where((q >= 0) & (q < 3) & (at >= 3), 125 + q, -1))
        left = jnp.where(halo, 61 + q, jnp.where((q >= 6) & (q < 9) & (at < 6), q - 6, -1))
        for side, wanted in enumerate((right, left)):
            wanted = jnp.where(group < PER, wanted, -1)
            picked = jnp.where(source == wanted, 1.0, 0.0).astype(jnp.bfloat16)
            picks[dy + 3, 0:128, 128 * side : 128 * side + 128] = picked
            picks[dy + 3, 128:256, 128 * side : 128 * side + 128] = picked


def pack_own(mass, stencil, left, right, picks, near):
    fill_picks(picks)
    fill_near(near)
    stacks, width = mass.shape[:2]
    tiles = -(-stacks // PER)
    for half in range(width // 8):
        rows = pl.ds(8 * half, 8)
        for tile in range(tiles):
            at = width * tile + 8 * half
            values = pack_stacks(lambda s: mass[s, rows, :], stacks, tile)
            if tile == 0:
                values = add_spare(lambda o: stencil[o, rows, :], *values)
            left[at : at + 8, :], right[at : at + 8, :] = values
        at = width * tiles + 8 * half
        left[at : at + 8, :], right[at : at + 8, :] = pack_coefficients(lambda o: stencil[o, rows, :])


def pack_all(stacks, own_left, own_right, above, below, middle, send_a, send_b, left, right):
    tiles = -(-stacks // PER)
    width = own_left.shape[0] // (tiles + 1)
    tall = width + 12
    for send, own in ((left, own_left), (right, own_right)):
        for tile in range(tiles + 1):
            send[tall * tile : tall * tile + width, :] = own[width * tile : width * tile + width, :]
        end = tall * tiles + width + 6
        send[end:, :] = jnp.zeros((send.shape[0] - end, 128), F32)
    first, last = ends(ROW_AXES)
    for got, outside, place, coef_place in (
        (above, first, width, width), (below, last, width + 6, width + 3)
    ):
        coef = lambda o: got[6 * stacks + 3 * o : 6 * stacks + 3 * o + 8, :]
        for tile in range(tiles):
            at = tall * tile + place
            packed = pack_stacks(lambda s: got[6 * s : 6 * s + 8, :], stacks, tile)
            if tile == 0:
                spare = add_spare(coef, *packed)
                packed = [
                    jnp.where(lax.broadcasted_iota(jnp.int32, (8, 128), 0) < 3, with_spare, without)
                    for with_spare, without in zip(spare, packed)
                ]
            left[at : at + 6, :] = jnp.where(outside, 0.0, packed[0][0:6])
            right[at : at + 6, :] = jnp.where(outside, 0.0, packed[1][0:6])
        at = tall * tiles + coef_place
        packed = pack_coefficients(coef)
        left[at : at + 3, :] = jnp.where(outside, 0.0, packed[0][0:3])
        right[at : at + 3, :] = jnp.where(outside, 0.0, packed[1][0:3])
    choose(is_even(COLUMN_AXES), right, left, send_a, send_b)


def choose(even, first, second, first_out, second_out):
    @pl.when(even)
    def _():
        first_out[...] = first[...]
        second_out[...] = second[...]

    @pl.when(jnp.logical_not(even))
    def _():
        first_out[...] = second[...]
        second_out[...] = first[...]


def main_sum(load, coef, coef_at, tile):
    fields = [[load(k, 8 * tile + dx) for k in range(GROUP)] for dx in range(7)]
    total = [None] * GROUP
    for dy in range(7):
        part = [None] * GROUP
        for dx in range(7):
            at = coef_at + 8 * tile
            scale = coef[dx * 7 + dy, at : at + 8, :]
            for k in range(GROUP):
                term = scale * fields[dx][k]
                part[k] = term if dx == 0 else part[k] + term
        for k in range(GROUP):
            moved = turn(part[k], 3 - dy)
            total[k] = moved if dy == 0 else total[k] + moved
    return total


def shift_rows(load, store, dys=range(-3, 4)):
    lane = lanes()
    for dy in dys:
        values = [turn(load(dx * 7 + dy + 3), dy) for dx in range(7)]
        if dy > 0:
            values = [jnp.where(lane >= dy, value, 0.0) for value in values]
        elif dy < 0:
            values = [jnp.where(lane < 128 + dy, value, 0.0) for value in values]
        for dx in range(7):
            store(dx * 7 + dy + 3, values[dx])


def own_part(mass, stencil, near, middle, own_shifted, right_near, left_near):
    stacks, width = mass.shape[:2]
    for tile in range(width // 8):
        rows = pl.ds(8 * tile, 8)

        def store(o, value):
            own_shifted[o, rows, :] = value

        shift_rows(lambda o: stencil[o, rows, :], store)

    def some_stacks(turn_at, carry):
        for_groups(
            turn_at, stacks, range((width - 8) // 8), own_shifted, 5,
            lambda s, tile, at: mass[s, 2 + at : 10 + at, :],
            lambda s, tile, value: store_rows(middle, s, 8 * tile, value),
        )
        return carry

    lax.fori_loop(0, turns(stacks), some_stacks, 0)
    for dy in range(7):
        value = jnp.concatenate([stencil[dx * 7 + dy, :, :] for dx in range(7)], axis=0)
        spread = replicate(value, near[dy])
        for dx in range(7):
            right_near[dx * 7 + dy, :, :] = spread[width * dx : width * dx + width, 0:128]
            left_near[dx * 7 + dy, :, :] = spread[width * dx : width * dx + width, 128:256]


def both_steps(mass, stencil, above, below, middle, own_shifted, second, wide, shifted, field, partial):
    stacks, width = mass.shape[:2]
    first, last = ends(ROW_AXES)
    coefs = 6 * stacks
    for s in range(stacks):
        field[0, s, 2:8, :] = above[6 * s : 6 * s + 6, :]
        field[0, s, 8:16, :] = mass[s, 0:8, :]
        field[1, s, 0:8, :] = mass[s, width - 8 : width, :]
        field[1, s, 8:16, :] = below[6 * s : 6 * s + 8, :]
    for o in range(OFFSETS):
        at = coefs + 3 * o
        wide[o, 0:3, :] = above[at : at + 3, :]
        wide[o, 3 : width + 3, :] = stencil[o, :, :]
        wide[o, width + 3 : width + 6, :] = below[at : at + 3, :]
        wide[o, width + 6 : width + 8, :] = jnp.zeros((2, 128), F32)

    @pl.when(first)
    def _():
        for s in range(stacks):
            field[0, s, 2:8, :] = jnp.zeros((6, 128), F32)
        for o in range(OFFSETS):
            wide[o, 0:3, :] = jnp.zeros((3, 128), F32)

    @pl.when(last)
    def _():
        for s in range(stacks):
            field[1, s, 8:16, :] = jnp.zeros((8, 128), F32)
        for o in range(OFFSETS):
            wide[o, width + 3 : width + 6, :] = jnp.zeros((3, 128), F32)

    for end, tile in enumerate((0, width // 8)):
        rows = pl.ds(8 * tile, 8)

        def store(o, value):
            shifted[end, o, :, :] = value

        shift_rows(lambda o: wide[o, rows, :], store)

    def first_step(turn_at, carry):
        sums = [
            for_groups(
                turn_at, stacks, (0,), shifted.at[end], 0, lambda s, tile, at: field[end, s, 2 + at : 10 + at, :]
            )
            for end in range(2)
        ]
        for end, tile in enumerate((0, width // 8)):
            for s, _, value in sums[end]:
                store_rows(partial, s, 8 * tile, value)
        for s, _, _ in sums[0]:
            partial[s, 8:width, :] = middle[s, :, :]
        return carry

    lax.fori_loop(0, turns(stacks), first_step, 0)

    def second_step(turn_at, carry):
        for_groups(
            turn_at, stacks, range(width // 8), own_shifted, 0,
            lambda s, tile, at: partial[s, at : at + 8, :],
            lambda s, tile, value: store_rows(second, s, 8 * tile, value),
        )
        return carry

    lax.fori_loop(0, turns(stacks), second_step, 0)


def store_rows(target, s, at, value):
    target[s, at : at + 8, :] = value


def per_turn(stacks):
    return 2 * GROUP if stacks % (2 * GROUP) == 0 else GROUP


def turns(stacks):
    return stacks // per_turn(stacks)


def for_groups(turn_at, stacks, tiles, coef, coef_at, load, store=None):
    sums = []
    for part in range(per_turn(stacks) // GROUP):
        start = turn_at * per_turn(stacks) + part * GROUP
        for tile in tiles:
            total = main_sum(lambda k, at: load(start + k, tile, at), coef, coef_at, tile)
            sums += [(start + k, tile, total[k]) for k in range(GROUP)]
    if store is not None:
        for s, tile, value in sums:
            store(s, tile, value)
    return sums


def packed_sum(load, coef, coef_at, tile, tiles, dys):
    fields = [[load(t, 8 * tile + dx) for t in range(tiles)] for dx in range(7)]
    total = [None] * tiles
    for dy in dys:
        part = [None] * tiles
        for dx in range(7):
            at = coef_at + 8 * tile
            scale = coef[dx * 7 + dy + 3, at : at + 8, :]
            for t in range(tiles):
                term = scale * fields[dx][t]
                part[t] = term if dx == 0 else part[t] + term
        for t in range(tiles):
            moved = turn(part[t], -dy)
            total[t] = moved if total[t] is None else total[t] + moved
    return total


def place_in_group(rows=8):
    lane = lanes(rows)
    return lane - SPAN * ((lane * 57) >> 9)


def side_coefficients(
    wide, send_a, send_b, got_a, got_b, picks,
    right_set, left_set, right_coef, left_coef, right_halo, left_halo, rows_of,
):
    tall = wide.shape[1]
    width = tall - 8
    tiles = right_set.shape[0]
    lane = lanes()

    first, last = ends(COLUMN_AXES)

    def gather(sent_right, sent_left, got_right, got_left):
        part = width + 12
        place = place_in_group(part)
        rows = [slice(part * tile, part * tile + part) for tile in range(tiles)]
        from_right = [jnp.where(last, 0.0, got_right[at, :]) for at in rows]
        from_left = [jnp.where(first, 0.0, got_left[at, :]) for at in rows]
        for tile, at in enumerate(rows):
            right = jnp.where(place < 3, turn(sent_right[at, :], -3), from_right[tile])
            left = jnp.where(place >= 6, turn(sent_left[at, :], 3), from_left[tile])
            for target, value in ((right_set, right), (left_set, left)):
                target[tile, 6 : width + 6, :] = value[0:width]
                target[tile, 0:6, :] = value[width : width + 6]
                target[tile, width + 6 : width + 12, :] = value[width + 6 : width + 12]
                target[tile, width + 12 : width + 16, :] = jnp.zeros((4, 128), F32)
        coefs = slice(part * tiles, part * tiles + width + 6)
        for target, source, got, outside in (
            (right_halo, from_right, got_right, last), (left_halo, from_left, got_left, first)
        ):
            value = jnp.where(outside, 0.0, got[coefs, :])
            spare = source[0]
            for tile, own, above, below in (
                (0, value[0:width], value[width : width + 3], value[width + 3 : width + 6]),
                (1, spare[0:width], spare[width : width + 3], spare[width + 6 : width + 9]),
            ):
                target[tile, 3 : width + 3, :] = own
                target[tile, 0:3, :] = above
                target[tile, width + 3 : width + 6, :] = below
                target[tile, width + 6 : width + 8, :] = jnp.zeros((2, 128), F32)

    even = is_even(COLUMN_AXES)

    @pl.when(even)
    def _():
        gather(send_a, send_b, got_a, got_b)

    @pl.when(jnp.logical_not(even))
    def _():
        gather(send_b, send_a, got_b, got_a)

    from_right = (lane >= 60) & (lane < 63)
    from_left = (lane >= 64) & (lane < 67)
    for tile in range(tall // 8):
        rows = pl.ds(8 * tile, 8)
        right_rows = [right_halo[t, rows, :] for t in range(2)]
        left_rows = [left_halo[t, rows, :] for t in range(2)]
        for dy in range(7):
            values = []
            for dx in range(7):
                o = dx * 7 + dy
                if o < COEF_PER:
                    right = turn(right_rows[0], 60 - 3 * o)
                    left = turn(left_rows[0], 64 - 3 * o)
                else:
                    at = SPAN * (o - COEF_PER)
                    right = turn(right_rows[1], 60 - at)
                    left = turn(left_rows[1], 58 - at)
                values.append(
                    jnp.where(from_right, right, jnp.where(from_left, left, wide[o, rows, :]))
                )
            for dx in range(7):
                at = tall * dx + 8 * tile
                rows_of[dy, at : at + 8, :] = values[dx]

    for dy in range(7):
        spread = replicate(rows_of[dy], picks[dy])
        for dx in range(7):
            right_coef[dx * 7 + dy, :, :] = spread[tall * dx : tall * dx + tall, 0:128]
            left_coef[dx * 7 + dy, :, :] = spread[tall * dx : tall * dx + tall, 128:256]


def halo_steps(
    right_set, left_set, right_coef, left_coef, right_near, left_near, second, out_hbm,
    right_next, left_next, right_out, left_out, out, sems,
):
    tiles = right_set.shape[0]
    stacks, width = out.shape[:2]
    place = place_in_group()
    everywhere = range(-3, 4)
    for tile in range(right_next.shape[1] // 8):
        rows = pl.ds(8 * tile, 8)
        right = packed_sum(
            lambda t, at: right_set[t, at : at + 8, :], right_coef, 0, tile, tiles, everywhere
        )
        left = packed_sum(
            lambda t, at: left_set[t, at : at + 8, :], left_coef, 0, tile, tiles, everywhere
        )
        for t in range(tiles):
            right_next[t, rows, :] = jnp.where(place >= 3, turn(right[t], 3), 0.0)
            left_next[t, rows, :] = jnp.where(place < 6, turn(left[t], -3), 0.0)
    for tile in range(width // 8):
        rows = pl.ds(8 * tile, 8)
        right = packed_sum(
            lambda t, at: right_next[t, at : at + 8, :], right_near, 0, tile, tiles, everywhere
        )
        left = packed_sum(
            lambda t, at: left_next[t, at : at + 8, :], left_near, 0, tile, tiles, everywhere
        )
        for t in range(tiles):
            right_out[t, rows, :] = right[t]
            left_out[t, rows, :] = left[t]

    lane = lanes()
    copies = []
    for t in range(tiles):
        low, high = PER * t, min(stacks, PER * t + PER)
        for tile in range(width // 8):
            rows = pl.ds(8 * tile, 8)
            right, left = right_out[t, rows, :], left_out[t, rows, :]
            values = []
            for s in range(low, high):
                at = SPAN * (s - low)
                change = jnp.where(lane < 6, turn(left, -at - 3), 0.0)
                change = jnp.where(lane >= 122, turn(right, 122 - at), change)
                values.append(second[s, rows, :] + change)
            for s, value in zip(range(low, high), values):
                out[s, rows, :] = value
        piece = pl.ds(low, high - low)
        copies.append(pltpu.make_async_copy(out.at[piece], out_hbm.at[piece], sems.at[t]))
        copies[-1].start()
    for copy in copies:
        copy.wait()


def local(tracer_mass, recon_table, intersection_weights, intersection_cells, rotation_codes):
    stacks, width, columns = tracer_mass.shape
    shape = lambda *sizes: jax.ShapeDtypeStruct(sizes, F32)
    scratch = lambda *sizes: pltpu.VMEM(sizes, F32)
    tiles = -(-stacks // PER)
    combos = 4 * (width // 8)
    tall, low = width + 16, width + 8
    fixed = lambda *values: [pltpu.with_memory_space_constraint(value, pltpu.HBM) for value in values]
    whole = lambda value: jax.ShapeDtypeStruct(value.shape, value.dtype)
    edge = -(-(6 * stacks + 3 * OFFSETS + 5) // 8) * 8
    integers = lambda *sizes: pltpu.VMEM(sizes, jnp.int32)
    picks = jax.ShapeDtypeStruct((7, 256, 256), jnp.bfloat16)
    regions = intersection_cells.shape[0]

    mass, weights, cells, codes, send_down, send_up = pl.pallas_call(
        edge_rows,
        out_shape=(
            whole(tracer_mass), whole(intersection_weights), whole(intersection_cells),
            whole(rotation_codes), shape(edge, 128), shape(edge, 128),
        ),
        in_specs=[HBM] * 5,
        out_specs=(VMEM,) * 6,
        scratch_shapes=[
            pltpu.SMEM(recon_table.shape, F32),
            scratch(regions, TERMS, 8, 128),
            integers(regions, 8, 128),
            integers(regions, 8, 128),
            scratch(OFFSETS, 8, 128),
            scratch(TERMS, regions, 8, 128),
            scratch(25, regions, 8, 128),
            pltpu.SemaphoreType.DMA((5,)),
        ],
        compiler_params=params(),
        cost_estimate=cost(4 * 10**6),
        name="edge_rows",
    )(*fixed(recon_table, tracer_mass, intersection_weights, intersection_cells, rotation_codes))
    above = shift(send_down, ROW_AXES, 1)
    below = shift(send_up, ROW_AXES, -1)

    stencil = pl.pallas_call(
        coefficients,
        out_shape=shape(OFFSETS, width, 128),
        in_specs=[HBM] + [VMEM] * 3,
        out_specs=VMEM,
        scratch_shapes=[
            pltpu.SMEM(recon_table.shape, F32),
            scratch(TERMS, combos, 8, 128),
            scratch(25, combos, 8, 128),
            pltpu.SemaphoreType.DMA((1,)),
        ],
        compiler_params=params(),
        cost_estimate=cost(8 * 10**6),
        name="coefficients",
    )(*fixed(recon_table), weights, cells, codes)

    own_left, own_right, picks, near = pl.pallas_call(
        pack_own,
        out_shape=(shape(width * (tiles + 1), 128),) * 2 + (picks, picks),
        in_specs=[VMEM] * 2,
        out_specs=(VMEM,) * 4,
        compiler_params=params(),
        cost_estimate=cost(10**6),
        name="pack_own",
    )(mass, stencil)

    middle, own_shifted, right_near, left_near = pl.pallas_call(
        own_part,
        out_shape=(shape(stacks, width - 8, 128),) + (shape(OFFSETS, width, 128),) * 3,
        in_specs=[VMEM] * 3,
        out_specs=(VMEM,) * 4,
        compiler_params=params(),
        cost_estimate=cost(4 * 10**6),
        name="own_part",
    )(mass, stencil, near)

    send = ((width + 12) * (tiles + 1), 128)
    send_a, send_b = pl.pallas_call(
        functools.partial(pack_all, stacks),
        out_shape=(shape(*send),) * 2,
        in_specs=[VMEM] * 4 + [ANY],
        out_specs=(VMEM,) * 2,
        scratch_shapes=[scratch(*send)] * 2,
        compiler_params=params(),
        cost_estimate=cost(10**6),
        name="pack_all",
    )(own_left, own_right, above, below, middle)
    column_a = column_swap(send_a, False)
    column_b = column_swap(send_b, True)

    second, wide = pl.pallas_call(
        both_steps,
        out_shape=(shape(stacks, width, 128), shape(OFFSETS, low, 128)),
        in_specs=[VMEM] * 6,
        out_specs=(VMEM,) * 2,
        scratch_shapes=[scratch(2, OFFSETS, 8, 128), scratch(2, stacks, 16, 128), scratch(stacks, low, 128)],
        compiler_params=params(),
        cost_estimate=cost(12 * 10**6),
        name="both_steps",
    )(mass, stencil, above, below, middle, own_shifted)

    sides = pl.pallas_call(
        side_coefficients,
        out_shape=(shape(tiles, tall, 128),) * 2 + (shape(OFFSETS, low, 128),) * 2,
        in_specs=[VMEM] * 6,
        out_specs=(VMEM,) * 4,
        scratch_shapes=[scratch(2, low, 128)] * 2 + [scratch(7, 7 * low, 128)],
        compiler_params=params(),
        cost_estimate=cost(4 * 10**6),
        name="side_coefficients",
    )(wide, send_a, send_b, column_a, column_b, picks)

    return pl.pallas_call(
        halo_steps,
        out_shape=shape(stacks, width, columns),
        in_specs=[VMEM] * 7,
        out_specs=HBM,
        scratch_shapes=[scratch(tiles, low, 128)] * 2 + [scratch(tiles, width, 128)] * 2
        + [scratch(stacks, width, columns), pltpu.SemaphoreType.DMA((tiles,))],
        compiler_params=params(),
        cost_estimate=cost(4 * 10**6),
        name="halo_steps",
    )(*sides, right_near, left_near, second)


def solution(mesh):
    in_specs = (
        P(None, ("face", "px"), "py"),
        P(),
        P(None, None, ("face", "px"), "py"),
        P(None, ("face", "px"), "py"),
        P(None, ("face", "px"), "py"),
    )
    out_specs = P(None, ("face", "px"), "py")
    return jax.shard_map(local, mesh=mesh, in_specs=in_specs, out_specs=out_specs, check_vma=False)
```

```python
import functools

import jax
import jax.numpy as jnp
import numpy as np
from jax import lax
from jax.experimental import pallas as pl
from jax.experimental.pallas import tpu as pltpu
from jax.sharding import PartitionSpec as P

F32 = jnp.float32
ROW_AXES = ("face", "px")
COLUMN_AXES = "py"
SWAPPED = (0, 2, 1, 5, 4, 3, 9, 8, 7, 6)
POWERS = ((0, 0), (1, 0), (0, 1), (2, 0), (1, 1), (0, 2), (3, 0), (2, 1), (1, 2), (0, 3))
TERMS = 10
OFFSETS = 49
GROUP = 4
SPAN = 9
PER = 14
COEF_PER = 42
VMEM = pl.BlockSpec(memory_space=pltpu.VMEM)
ANY = pl.BlockSpec(memory_space=pl.ANY)
HBM = pl.BlockSpec(memory_space=pltpu.HBM)


def params():
    return pltpu.CompilerParams(vmem_limit_bytes=40 * 1024 * 1024)


def cost(operations):
    return pl.CostEstimate(flops=operations, bytes_accessed=1 << 20, transcendentals=0)


def column_swap(block, odd_first):
    chains, count = lax.axis_size(ROW_AXES), lax.axis_size(COLUMN_AXES)
    column = list(range(count))
    for low in range(1 if odd_first else 0, count - 1, 2):
        column[low], column[low + 1] = low + 1, low
    pairs = []
    for chain in range(chains):
        for place in range(count):
            target = (chain, column[place])
            if column[place] == place and chains % 2 == 0:
                target = (chain ^ 1, place)
            pairs.append((chain * count + place, target[0] * count + target[1]))
    return lax.ppermute(block, ROW_AXES + (COLUMN_AXES,), pairs)


def shift(block, axes, step):
    count = lax.axis_size(axes)
    return lax.ppermute(block, axes, [(index, (index + step) % count) for index in range(count)])


def ends(axes):
    index = lax.axis_index(axes)
    return index == 0, index == lax.axis_size(axes) - 1


def is_even(axes):
    return lax.rem(lax.axis_index(axes), 2) == 0


def turn(value, amount):
    amount %= 128
    return pltpu.roll(value, amount, 1) if amount else value


def lanes(rows=8):
    return lax.broadcasted_iota(jnp.int32, (rows, 128), 1)


def fill_stencil(recon, weights, cells, codes, turned, spread, stencil, tiles, before_taps):
    zero = jnp.zeros((8, 128), F32)
    for g in range(tiles):
        rows = pl.ds(8 * g, 8)
        for m in range(4):
            code = codes[m, rows, :]
            odd = (code & 1) == 1
            sign_x = jnp.where(code >= 2, -1.0, 1.0).astype(F32)
            sign_y = jnp.where((code == 1) | (code == 2), -1.0, 1.0).astype(F32)
            sign_xy = sign_x * sign_y
            values = [weights[m, t, rows, :] for t in range(TERMS)]
            for t, (a, b) in enumerate(POWERS):
                value = values[t]
                if SWAPPED[t] != t:
                    value = jnp.where(odd, values[SWAPPED[t]], value)
                if a % 2 and b % 2:
                    value = value * sign_xy
                elif a % 2:
                    value = value * sign_x
                elif b % 2:
                    value = value * sign_y
                turned[t, m * tiles + g] = value

    combos = 4 * tiles
    before_taps()

    def five_taps(jx, carry):
        total = [[None] * combos for jy in range(5)]
        for t in range(TERMS):
            values = [turned[t, c] for c in range(combos)]
            for jy in range(5):
                scale = recon[t, 5 * jx + jy]
                for c in range(combos):
                    term = values[c] * scale
                    total[jy][c] = term if t == 0 else total[jy][c] + term
        for jy in range(5):
            for c in range(combos):
                spread[5 * jx + jy, c] = total[jy][c]
        return carry

    lax.fori_loop(0, 5, five_taps, 0)

    for g in range(tiles):
        rows = pl.ds(8 * g, 8)
        masks = []
        for m in range(4):
            cell = cells[m, rows, :]
            first = jnp.where(cell < 3, 0, jnp.where(cell < 6, 3, 6))
            across = cell - first
            masks.append((cell < 3, cell < 6, across == 0, across <= 1))
        for ox in range(7):
            total = [None] * 7
            for m in range(4):
                low_x, mid_x, low_y, mid_y = masks[m]

                def tap(jx, jy):
                    if 0 <= jx < 5 and 0 <= jy < 5:
                        return spread[jx * 5 + jy, m * tiles + g]
                    return zero

                line = [
                    jnp.where(low_x, tap(ox, jy), jnp.where(mid_x, tap(ox - 1, jy), tap(ox - 2, jy)))
                    for jy in range(5)
                ]
                padded = [zero, zero] + line + [zero, zero]
                for oy in range(7):
                    value = jnp.where(
                        low_y, padded[oy + 2], jnp.where(mid_y, padded[oy + 1], padded[oy])
                    )
                    total[oy] = value if m == 0 else total[oy] + value
            for oy in range(7):
                stencil[ox * 7 + oy, rows, :] = total[oy]


def edge_rows(
    recon_hbm, mass_hbm, weights_hbm, cells_hbm, codes_hbm,
    mass, weights, cells, codes, send_down, send_up,
    recon, edge_weights, edge_cells, edge_codes, edge_stencil, turned, spread, sems,
):
    sources = (recon_hbm, codes_hbm, weights_hbm, cells_hbm, mass_hbm)
    targets = (recon, codes, weights, cells, mass)
    copies = [pltpu.make_async_copy(a, b, sems.at[i]) for i, (a, b) in enumerate(zip(sources, targets))]
    for copy in copies:
        copy.start()
    for copy in copies[1:4]:
        copy.wait()
    stacks, width = mass.shape[:2]
    for target, source in ((edge_weights, weights), (edge_cells, cells), (edge_codes, codes)):
        for index in np.ndindex(*source.shape[:-2]):
            target[index + (slice(0, 3), slice(None))] = source[index + (slice(0, 3), slice(None))]
            target[index + (slice(3, 8), slice(None))] = source[index + (slice(width - 5, width), slice(None))]
    fill_stencil(
        recon, edge_weights, edge_cells, edge_codes, turned, spread, edge_stencil, 1, copies[0].wait
    )
    copies[4].wait()
    for send, mass_at, stencil_at in ((send_down, width - 6, 5), (send_up, 0, 0)):
        for s in range(stacks):
            send[6 * s : 6 * s + 6, :] = mass[s, mass_at : mass_at + 6, :]
        for o in range(OFFSETS):
            at = 6 * stacks + 3 * o
            send[at : at + 3, :] = edge_stencil[o, stencil_at : stencil_at + 3, :]


def coefficients(recon_hbm, weights, cells, codes, stencil, recon, turned, spread, sem):
    copy = pltpu.make_async_copy(recon_hbm, recon, sem.at[0])
    copy.start()
    fill_stencil(recon, weights, cells, codes, turned, spread, stencil, stencil.shape[1] // 8, copy.wait)


def pack_stacks(load, stacks, tile):
    lane = lanes()
    left = jnp.zeros((8, 128), F32)
    right = jnp.zeros((8, 128), F32)
    for s in range(PER * tile, min(stacks, PER * tile + PER)):
        at = SPAN * (s % PER)
        moved = turn(load(s), at - 122)
        right = jnp.where(lane >= at, moved, right)
        left = jnp.where(from_place(lane, at + 6, at + 12), moved, left)
    return turn(left, -3), right


def from_place(lane, low, high):
    return (lane >= low) | (lane < high - 128) if high > 128 else lane >= low


def pack_coefficients(load):
    lane = lanes()
    left = jnp.zeros((8, 128), F32)
    right = jnp.zeros((8, 128), F32)
    for o in range(COEF_PER):
        at = 3 * o
        moved = turn(load(o), at - 125)
        right = jnp.where(lane >= at, moved, right)
        left = jnp.where(from_place(lane, at + 3, at + 6), moved, left)
    return turn(left, -3), right


def add_spare(load, left, right):
    lane = lanes()
    for o in range(COEF_PER, OFFSETS):
        at = SPAN * (o - COEF_PER)
        value = load(o)
        left = jnp.where((lane >= at) & (lane < at + 3), turn(value, at), left)
        right = jnp.where((lane >= at + 6) & (lane < at + 9), turn(value, at - 119), right)
    return left, right


def fill_near(near):
    lane = lanes(1)
    group = (lane * 57) >> 9
    at = lane - SPAN * group
    source = lax.broadcasted_iota(jnp.int32, (128, 128), 0)
    for dy in range(-3, 4):
        q = at - dy
        right = jnp.where((at >= 3) & (q >= 0) & (q < 6), 122 + q, -1)
        left = jnp.where((at < 6) & (q >= 3) & (q < 9), q - 3, -1)
        for side, wanted in enumerate((right, left)):
            wanted = jnp.where(group < PER, wanted, -1)
            picked = jnp.where(source == wanted, 1.0, 0.0).astype(jnp.bfloat16)
            near[dy + 3, 0:128, 128 * side : 128 * side + 128] = picked
            near[dy + 3, 128:256, 128 * side : 128 * side + 128] = picked


def replicate(value, picks):
    high = value.astype(jnp.bfloat16)
    low = (value - high.astype(F32)).astype(jnp.bfloat16)
    return jnp.dot(jnp.concatenate([high, low], axis=1), picks, preferred_element_type=F32)


def fill_picks(picks):
    lane = lanes(1)
    group = (lane * 57) >> 9
    at = lane - SPAN * group
    source = lax.broadcasted_iota(jnp.int32, (128, 128), 0)
    for dy in range(-3, 4):
        q = at - dy
        halo = (q >= 3) & (q < 6)
        right = jnp.where(halo, 57 + q, jnp.where((q >= 0) & (q < 3) & (at >= 3), 125 + q, -1))
        left = jnp.where(halo, 61 + q, jnp.where((q >= 6) & (q < 9) & (at < 6), q - 6, -1))
        for side, wanted in enumerate((right, left)):
            wanted = jnp.where(group < PER, wanted, -1)
            picked = jnp.where(source == wanted, 1.0, 0.0).astype(jnp.bfloat16)
            picks[dy + 3, 0:128, 128 * side : 128 * side + 128] = picked
            picks[dy + 3, 128:256, 128 * side : 128 * side + 128] = picked


def pack_own(mass, stencil, left, right, picks, near):
    fill_picks(picks)
    fill_near(near)
    stacks, width = mass.shape[:2]
    tiles = -(-stacks // PER)
    for half in range(width // 8):
        rows = pl.ds(8 * half, 8)
        for tile in range(tiles):
            at = width * tile + 8 * half
            values = pack_stacks(lambda s: mass[s, rows, :], stacks, tile)
            if tile == 0:
                values = add_spare(lambda o: stencil[o, rows, :], *values)
            left[at : at + 8, :], right[at : at + 8, :] = values
        at = width * tiles + 8 * half
        left[at : at + 8, :], right[at : at + 8, :] = pack_coefficients(lambda o: stencil[o, rows, :])


def pack_all(stacks, own_left, own_right, above, below, middle, send_a, send_b, left, right):
    tiles = -(-stacks // PER)
    width = own_left.shape[0] // (tiles + 1)
    tall = width + 12
    first, last = ends(ROW_AXES)
    top_rows = lax.broadcasted_iota(jnp.int32, (8, 128), 0) < 3
    ready = []
    for got, outside, place, coef_place in (
        (above, first, width, width), (below, last, width + 6, width + 3)
    ):
        coef = lambda o: got[6 * stacks + 3 * o : 6 * stacks + 3 * o + 8, :]
        for tile in range(tiles):
            packed = pack_stacks(lambda s: got[6 * s : 6 * s + 8, :], stacks, tile)
            if tile == 0:
                spare = add_spare(coef, *packed)
                packed = [jnp.where(top_rows, new, old) for new, old in zip(spare, packed)]
            ready.append((tall * tile + place, 6, outside, packed))
        ready.append((tall * tiles + coef_place, 3, outside, pack_coefficients(coef)))
    for at, count, outside, packed in ready:
        for send, value in zip((left, right), packed):
            send[at : at + count, :] = jnp.where(outside, 0.0, value[0:count])
    for send, own in ((left, own_left), (right, own_right)):
        for tile in range(tiles + 1):
            send[tall * tile : tall * tile + width, :] = own[width * tile : width * tile + width, :]
        end = tall * tiles + width + 6
        send[end:, :] = jnp.zeros((send.shape[0] - end, 128), F32)
    choose(is_even(COLUMN_AXES), right, left, send_a, send_b)


def choose(even, first, second, first_out, second_out):
    @pl.when(even)
    def _():
        first_out[...] = first[...]
        second_out[...] = second[...]

    @pl.when(jnp.logical_not(even))
    def _():
        first_out[...] = second[...]
        second_out[...] = first[...]


def main_sum(load, coef, coef_at, tile):
    fields = [[load(k, 8 * tile + dx) for k in range(GROUP)] for dx in range(7)]
    total = [None] * GROUP
    for dy in range(7):
        part = [None] * GROUP
        for dx in range(7):
            at = coef_at + 8 * tile
            scale = coef[dx * 7 + dy, at : at + 8, :]
            for k in range(GROUP):
                term = scale * fields[dx][k]
                part[k] = term if dx == 0 else part[k] + term
        for k in range(GROUP):
            moved = turn(part[k], 3 - dy)
            total[k] = moved if dy == 0 else total[k] + moved
    return total


def shift_rows(load, store):
    lane = lanes()
    values = []
    for o in range(OFFSETS):
        dy = o % 7 - 3
        value = turn(load(o), dy)
        if dy > 0:
            value = jnp.where(lane >= dy, value, 0.0)
        elif dy < 0:
            value = jnp.where(lane < 128 + dy, value, 0.0)
        values.append(value)
    for o, value in enumerate(values):
        store(o, value)


def own_part(mass, stencil, near, middle, own_shifted, right_near, left_near):
    stacks, width = mass.shape[:2]
    for tile in range(width // 8):
        rows = pl.ds(8 * tile, 8)

        def store(o, value):
            own_shifted[o, rows, :] = value

        shift_rows(lambda o: stencil[o, rows, :], store)

    def some_stacks(turn_at, carry):
        for_groups(
            turn_at, stacks, range((width - 8) // 8), own_shifted, 5,
            lambda s, tile, at: mass[s, 2 + at : 10 + at, :],
            lambda s, tile, value: store_rows(middle, s, 8 * tile, value),
        )
        return carry

    lax.fori_loop(0, turns(stacks), some_stacks, 0)
    for dy in range(7):
        value = jnp.concatenate([stencil[dx * 7 + dy, :, :] for dx in range(7)], axis=0)
        spread = replicate(value, near[dy])
        for dx in range(7):
            right_near[dx * 7 + dy, :, :] = spread[width * dx : width * dx + width, 0:128]
            left_near[dx * 7 + dy, :, :] = spread[width * dx : width * dx + width, 128:256]


def both_steps(mass, stencil, above, below, middle, own_shifted, second, wide, shifted, field, partial):
    stacks, width = mass.shape[:2]
    first, last = ends(ROW_AXES)
    coefs = 6 * stacks
    for s in range(stacks):
        field[0, s, 2:8, :] = above[6 * s : 6 * s + 6, :]
        field[0, s, 8:16, :] = mass[s, 0:8, :]
        field[1, s, 0:8, :] = mass[s, width - 8 : width, :]
        field[1, s, 8:16, :] = below[6 * s : 6 * s + 8, :]
    for o in range(OFFSETS):
        at = coefs + 3 * o
        wide[o, 0:3, :] = above[at : at + 3, :]
        wide[o, 3 : width + 3, :] = stencil[o, :, :]
        wide[o, width + 3 : width + 6, :] = below[at : at + 3, :]
        wide[o, width + 6 : width + 8, :] = jnp.zeros((2, 128), F32)

    @pl.when(first)
    def _():
        for s in range(stacks):
            field[0, s, 2:8, :] = jnp.zeros((6, 128), F32)
        for o in range(OFFSETS):
            wide[o, 0:3, :] = jnp.zeros((3, 128), F32)

    @pl.when(last)
    def _():
        for s in range(stacks):
            field[1, s, 8:16, :] = jnp.zeros((8, 128), F32)
        for o in range(OFFSETS):
            wide[o, width + 3 : width + 6, :] = jnp.zeros((3, 128), F32)

    for end, tile in enumerate((0, width // 8)):
        rows = pl.ds(8 * tile, 8)

        def store(o, value):
            shifted[end, o, :, :] = value

        shift_rows(lambda o: wide[o, rows, :], store)

    def first_step(turn_at, carry):
        sums = [
            for_groups(
                turn_at, stacks, (0,), shifted.at[end], 0, lambda s, tile, at: field[end, s, 2 + at : 10 + at, :]
            )
            for end in range(2)
        ]
        for end, tile in enumerate((0, width // 8)):
            for s, _, value in sums[end]:
                store_rows(partial, s, 8 * tile, value)
        for s, _, _ in sums[0]:
            partial[s, 8:width, :] = middle[s, :, :]
        return carry

    lax.fori_loop(0, turns(stacks), first_step, 0)

    def second_step(turn_at, carry):
        for_groups(
            turn_at, stacks, range(width // 8), own_shifted, 0,
            lambda s, tile, at: partial[s, at : at + 8, :],
            lambda s, tile, value: store_rows(second, s, 8 * tile, value),
        )
        return carry

    lax.fori_loop(0, turns(stacks), second_step, 0)


def store_rows(target, s, at, value):
    target[s, at : at + 8, :] = value


def per_turn(stacks):
    return 2 * GROUP if stacks % (2 * GROUP) == 0 else GROUP


def turns(stacks):
    return stacks // per_turn(stacks)


def for_groups(turn_at, stacks, tiles, coef, coef_at, load, store=None):
    sums = []
    for part in range(per_turn(stacks) // GROUP):
        start = turn_at * per_turn(stacks) + part * GROUP
        for tile in tiles:
            total = main_sum(lambda k, at: load(start + k, tile, at), coef, coef_at, tile)
            sums += [(start + k, tile, total[k]) for k in range(GROUP)]
    if store is not None:
        for s, tile, value in sums:
            store(s, tile, value)
    return sums


def packed_sum(load, coef, coef_at, tile, tiles, dys):
    fields = [[load(t, 8 * tile + dx) for t in range(tiles)] for dx in range(7)]
    total = [None] * tiles
    for dy in dys:
        part = [None] * tiles
        for dx in range(7):
            at = coef_at + 8 * tile
            scale = coef[dx * 7 + dy + 3, at : at + 8, :]
            for t in range(tiles):
                term = scale * fields[dx][t]
                part[t] = term if dx == 0 else part[t] + term
        for t in range(tiles):
            moved = turn(part[t], -dy)
            total[t] = moved if total[t] is None else total[t] + moved
    return total


def place_in_group(rows=8):
    lane = lanes(rows)
    return lane - SPAN * ((lane * 57) >> 9)


def side_coefficients(
    wide, send_a, send_b, got_a, got_b, picks,
    right_set, left_set, right_coef, left_coef, right_halo, left_halo, rows_of,
):
    tall = wide.shape[1]
    width = tall - 8
    tiles = right_set.shape[0]
    lane = lanes()

    first, last = ends(COLUMN_AXES)

    def gather(sent_right, sent_left, got_right, got_left):
        part = width + 12
        place = place_in_group(part)
        rows = [slice(part * tile, part * tile + part) for tile in range(tiles)]
        from_right = [jnp.where(last, 0.0, got_right[at, :]) for at in rows]
        from_left = [jnp.where(first, 0.0, got_left[at, :]) for at in rows]
        for tile, at in enumerate(rows):
            right = jnp.where(place < 3, turn(sent_right[at, :], -3), from_right[tile])
            left = jnp.where(place >= 6, turn(sent_left[at, :], 3), from_left[tile])
            for target, value in ((right_set, right), (left_set, left)):
                target[tile, 6 : width + 6, :] = value[0:width]
                target[tile, 0:6, :] = value[width : width + 6]
                target[tile, width + 6 : width + 12, :] = value[width + 6 : width + 12]
                target[tile, width + 12 : width + 16, :] = jnp.zeros((4, 128), F32)
        coefs = slice(part * tiles, part * tiles + width + 6)
        for target, source, got, outside in (
            (right_halo, from_right, got_right, last), (left_halo, from_left, got_left, first)
        ):
            value = jnp.where(outside, 0.0, got[coefs, :])
            spare = source[0]
            for tile, own, above, below in (
                (0, value[0:width], value[width : width + 3], value[width + 3 : width + 6]),
                (1, spare[0:width], spare[width : width + 3], spare[width + 6 : width + 9]),
            ):
                target[tile, 3 : width + 3, :] = own
                target[tile, 0:3, :] = above
                target[tile, width + 3 : width + 6, :] = below
                target[tile, width + 6 : width + 8, :] = jnp.zeros((2, 128), F32)

    even = is_even(COLUMN_AXES)

    @pl.when(even)
    def _():
        gather(send_a, send_b, got_a, got_b)

    @pl.when(jnp.logical_not(even))
    def _():
        gather(send_b, send_a, got_b, got_a)

    from_right = (lane >= 60) & (lane < 63)
    from_left = (lane >= 64) & (lane < 67)
    for tile in range(tall // 8):
        rows = pl.ds(8 * tile, 8)
        right_rows = [right_halo[t, rows, :] for t in range(2)]
        left_rows = [left_halo[t, rows, :] for t in range(2)]
        values = []
        for o in range(OFFSETS):
            if o < COEF_PER:
                right = turn(right_rows[0], 60 - 3 * o)
                left = turn(left_rows[0], 64 - 3 * o)
            else:
                at = SPAN * (o - COEF_PER)
                right = turn(right_rows[1], 60 - at)
                left = turn(left_rows[1], 58 - at)
            values.append(jnp.where(from_right, right, jnp.where(from_left, left, wide[o, rows, :])))
        for o, value in enumerate(values):
            at = tall * (o // 7) + 8 * tile
            rows_of[o % 7, at : at + 8, :] = value

    for dy in range(7):
        spread = replicate(rows_of[dy], picks[dy])
        for dx in range(7):
            right_coef[dx * 7 + dy, :, :] = spread[tall * dx : tall * dx + tall, 0:128]
            left_coef[dx * 7 + dy, :, :] = spread[tall * dx : tall * dx + tall, 128:256]


def halo_steps(
    right_set, left_set, right_coef, left_coef, right_near, left_near, second, out_hbm,
    right_next, left_next, out, sems,
):
    tiles = right_set.shape[0]
    stacks, width = out.shape[:2]
    place = place_in_group()
    everywhere = range(-3, 4)
    row_tiles = range(right_next.shape[1] // 8)
    sums = [
        [
            packed_sum(lambda t, at: side[t, at : at + 8, :], coef, 0, tile, tiles, everywhere)
            for side, coef in ((right_set, right_coef), (left_set, left_coef))
        ]
        for tile in row_tiles
    ]
    for tile in row_tiles:
        right, left = sums[tile]
        rows = pl.ds(8 * tile, 8)
        for t in range(tiles):
            right_next[t, rows, :] = jnp.where(place >= 3, turn(right[t], 3), 0.0)
            left_next[t, rows, :] = jnp.where(place < 6, turn(left[t], -3), 0.0)
    changes = [
        [
            packed_sum(lambda t, at: side[t, at : at + 8, :], coef, 0, tile, tiles, everywhere)
            for side, coef in ((right_next, right_near), (left_next, left_near))
        ]
        for tile in range(width // 8)
    ]

    lane = lanes()
    copies = []
    for t in range(tiles):
        low, high = PER * t, min(stacks, PER * t + PER)
        for tile in range(width // 8):
            rows = pl.ds(8 * tile, 8)
            right, left = (side[t] for side in changes[tile])
            values = []
            for s in range(low, high):
                at = SPAN * (s - low)
                change = jnp.where(lane < 6, turn(left, -at - 3), 0.0)
                change = jnp.where(lane >= 122, turn(right, 122 - at), change)
                values.append(second[s, rows, :] + change)
            for s, value in zip(range(low, high), values):
                out[s, rows, :] = value
        piece = pl.ds(low, high - low)
        copies.append(pltpu.make_async_copy(out.at[piece], out_hbm.at[piece], sems.at[t]))
        copies[-1].start()
    for copy in copies:
        copy.wait()


def local(tracer_mass, recon_table, intersection_weights, intersection_cells, rotation_codes):
    stacks, width, columns = tracer_mass.shape
    shape = lambda *sizes: jax.ShapeDtypeStruct(sizes, F32)
    scratch = lambda *sizes: pltpu.VMEM(sizes, F32)
    tiles = -(-stacks // PER)
    combos = 4 * (width // 8)
    tall, low = width + 16, width + 8
    fixed = lambda *values: [pltpu.with_memory_space_constraint(value, pltpu.HBM) for value in values]
    whole = lambda value: jax.ShapeDtypeStruct(value.shape, value.dtype)
    edge = -(-(6 * stacks + 3 * OFFSETS + 5) // 8) * 8
    integers = lambda *sizes: pltpu.VMEM(sizes, jnp.int32)
    picks = jax.ShapeDtypeStruct((7, 256, 256), jnp.bfloat16)
    regions = intersection_cells.shape[0]

    mass, weights, cells, codes, send_down, send_up = pl.pallas_call(
        edge_rows,
        out_shape=(
            whole(tracer_mass), whole(intersection_weights), whole(intersection_cells),
            whole(rotation_codes), shape(edge, 128), shape(edge, 128),
        ),
        in_specs=[HBM] * 5,
        out_specs=(VMEM,) * 6,
        scratch_shapes=[
            pltpu.SMEM(recon_table.shape, F32),
            scratch(regions, TERMS, 8, 128),
            integers(regions, 8, 128),
            integers(regions, 8, 128),
            scratch(OFFSETS, 8, 128),
            scratch(TERMS, regions, 8, 128),
            scratch(25, regions, 8, 128),
            pltpu.SemaphoreType.DMA((5,)),
        ],
        compiler_params=params(),
        cost_estimate=cost(4 * 10**6),
        name="edge_rows",
    )(*fixed(recon_table, tracer_mass, intersection_weights, intersection_cells, rotation_codes))
    above = shift(send_down, ROW_AXES, 1)
    below = shift(send_up, ROW_AXES, -1)

    stencil = pl.pallas_call(
        coefficients,
        out_shape=shape(OFFSETS, width, 128),
        in_specs=[HBM] + [VMEM] * 3,
        out_specs=VMEM,
        scratch_shapes=[
            pltpu.SMEM(recon_table.shape, F32),
            scratch(TERMS, combos, 8, 128),
            scratch(25, combos, 8, 128),
            pltpu.SemaphoreType.DMA((1,)),
        ],
        compiler_params=params(),
        cost_estimate=cost(8 * 10**6),
        name="coefficients",
    )(*fixed(recon_table), weights, cells, codes)

    own_left, own_right, picks, near = pl.pallas_call(
        pack_own,
        out_shape=(shape(width * (tiles + 1), 128),) * 2 + (picks, picks),
        in_specs=[VMEM] * 2,
        out_specs=(VMEM,) * 4,
        compiler_params=params(),
        cost_estimate=cost(10**6),
        name="pack_own",
    )(mass, stencil)

    middle, own_shifted, right_near, left_near = pl.pallas_call(
        own_part,
        out_shape=(shape(stacks, width - 8, 128),) + (shape(OFFSETS, width, 128),) * 3,
        in_specs=[VMEM] * 3,
        out_specs=(VMEM,) * 4,
        compiler_params=params(),
        cost_estimate=cost(4 * 10**6),
        name="own_part",
    )(mass, stencil, near)

    send = ((width + 12) * (tiles + 1), 128)
    send_a, send_b = pl.pallas_call(
        functools.partial(pack_all, stacks),
        out_shape=(shape(*send),) * 2,
        in_specs=[VMEM] * 4 + [ANY],
        out_specs=(VMEM,) * 2,
        scratch_shapes=[scratch(*send)] * 2,
        compiler_params=params(),
        cost_estimate=cost(10**6),
        name="pack_all",
    )(own_left, own_right, above, below, middle)
    column_a = column_swap(send_a, False)
    column_b = column_swap(send_b, True)

    second, wide = pl.pallas_call(
        both_steps,
        out_shape=(shape(stacks, width, 128), shape(OFFSETS, low, 128)),
        in_specs=[VMEM] * 6,
        out_specs=(VMEM,) * 2,
        scratch_shapes=[scratch(2, OFFSETS, 8, 128), scratch(2, stacks, 16, 128), scratch(stacks, low, 128)],
        compiler_params=params(),
        cost_estimate=cost(12 * 10**6),
        name="both_steps",
    )(mass, stencil, above, below, middle, own_shifted)

    sides = pl.pallas_call(
        side_coefficients,
        out_shape=(shape(tiles, tall, 128),) * 2 + (shape(OFFSETS, low, 128),) * 2,
        in_specs=[VMEM] * 6,
        out_specs=(VMEM,) * 4,
        scratch_shapes=[scratch(2, low, 128)] * 2 + [scratch(7, 7 * low, 128)],
        compiler_params=params(),
        cost_estimate=cost(4 * 10**6),
        name="side_coefficients",
    )(wide, send_a, send_b, column_a, column_b, picks)

    return pl.pallas_call(
        halo_steps,
        out_shape=shape(stacks, width, columns),
        in_specs=[VMEM] * 7,
        out_specs=HBM,
        scratch_shapes=[scratch(tiles, low, 128)] * 2
        + [scratch(stacks, width, columns), pltpu.SemaphoreType.DMA((tiles,))],
        compiler_params=params(),
        cost_estimate=cost(4 * 10**6),
        name="halo_steps",
    )(*sides, right_near, left_near, second)


def solution(mesh):
    in_specs = (
        P(None, ("face", "px"), "py"),
        P(),
        P(None, None, ("face", "px"), "py"),
        P(None, ("face", "px"), "py"),
        P(None, ("face", "px"), "py"),
    )
    out_specs = P(None, ("face", "px"), "py")
    return jax.shard_map(local, mesh=mesh, in_specs=in_specs, out_specs=out_specs, check_vma=False)
```

```python
import functools

import jax
import jax.numpy as jnp
import numpy as np
from jax import lax
from jax.experimental import pallas as pl
from jax.experimental.pallas import tpu as pltpu
from jax.sharding import PartitionSpec as P

F32 = jnp.float32
ROW_AXES = ("face", "px")
COLUMN_AXES = "py"
SWAPPED = (0, 2, 1, 5, 4, 3, 9, 8, 7, 6)
POWERS = ((0, 0), (1, 0), (0, 1), (2, 0), (1, 1), (0, 2), (3, 0), (2, 1), (1, 2), (0, 3))
TERMS = 10
OFFSETS = 49
GROUP = 4
SPAN = 9
PER = 14
COEF_PER = 42
VMEM = pl.BlockSpec(memory_space=pltpu.VMEM)
ANY = pl.BlockSpec(memory_space=pl.ANY)
HBM = pl.BlockSpec(memory_space=pltpu.HBM)


def params():
    return pltpu.CompilerParams(vmem_limit_bytes=40 * 1024 * 1024)


def cost(operations):
    return pl.CostEstimate(flops=operations, bytes_accessed=1 << 20, transcendentals=0)


def column_swap(block, odd_first):
    chains, count = lax.axis_size(ROW_AXES), lax.axis_size(COLUMN_AXES)
    column = list(range(count))
    for low in range(1 if odd_first else 0, count - 1, 2):
        column[low], column[low + 1] = low + 1, low
    pairs = []
    for chain in range(chains):
        for place in range(count):
            target = (chain, column[place])
            if column[place] == place and chains % 2 == 0:
                target = (chain ^ 1, place)
            pairs.append((chain * count + place, target[0] * count + target[1]))
    return lax.ppermute(block, ROW_AXES + (COLUMN_AXES,), pairs)


def shift(block, axes, step):
    count = lax.axis_size(axes)
    return lax.ppermute(block, axes, [(index, (index + step) % count) for index in range(count)])


def ends(axes):
    index = lax.axis_index(axes)
    return index == 0, index == lax.axis_size(axes) - 1


def is_even(axes):
    return lax.rem(lax.axis_index(axes), 2) == 0


def turn(value, amount):
    amount %= 128
    return pltpu.roll(value, amount, 1) if amount else value


def lanes(rows=8):
    return lax.broadcasted_iota(jnp.int32, (rows, 128), 1)


def fill_stencil(recon, weights, cells, codes, turned, spread, stencil, tiles, before_taps):
    zero = jnp.zeros((8, 128), F32)
    for g in range(tiles):
        rows = pl.ds(8 * g, 8)
        for m in range(4):
            code = codes[m, rows, :]
            odd = (code & 1) == 1
            sign_x = jnp.where(code >= 2, -1.0, 1.0).astype(F32)
            sign_y = jnp.where((code == 1) | (code == 2), -1.0, 1.0).astype(F32)
            sign_xy = sign_x * sign_y
            values = [weights[m, t, rows, :] for t in range(TERMS)]
            for t, (a, b) in enumerate(POWERS):
                value = values[t]
                if SWAPPED[t] != t:
                    value = jnp.where(odd, values[SWAPPED[t]], value)
                if a % 2 and b % 2:
                    value = value * sign_xy
                elif a % 2:
                    value = value * sign_x
                elif b % 2:
                    value = value * sign_y
                turned[t, m * tiles + g] = value

    combos = 4 * tiles
    before_taps()

    def five_taps(jx, carry):
        total = [[None] * combos for jy in range(5)]
        for t in range(TERMS):
            values = [turned[t, c] for c in range(combos)]
            for jy in range(5):
                scale = recon[t, 5 * jx + jy]
                for c in range(combos):
                    term = values[c] * scale
                    total[jy][c] = term if t == 0 else total[jy][c] + term
        for jy in range(5):
            for c in range(combos):
                spread[5 * jx + jy, c] = total[jy][c]
        return carry

    lax.fori_loop(0, 5, five_taps, 0)

    for g in range(tiles):
        rows = pl.ds(8 * g, 8)
        masks = []
        for m in range(4):
            cell = cells[m, rows, :]
            first = jnp.where(cell < 3, 0, jnp.where(cell < 6, 3, 6))
            across = cell - first
            masks.append((cell < 3, cell < 6, across == 0, across <= 1))
        for ox in range(7):
            total = [None] * 7
            for m in range(4):
                low_x, mid_x, low_y, mid_y = masks[m]

                def tap(jx, jy):
                    if 0 <= jx < 5 and 0 <= jy < 5:
                        return spread[jx * 5 + jy, m * tiles + g]
                    return zero

                line = [
                    jnp.where(low_x, tap(ox, jy), jnp.where(mid_x, tap(ox - 1, jy), tap(ox - 2, jy)))
                    for jy in range(5)
                ]
                padded = [zero, zero] + line + [zero, zero]
                for oy in range(7):
                    value = jnp.where(
                        low_y, padded[oy + 2], jnp.where(mid_y, padded[oy + 1], padded[oy])
                    )
                    total[oy] = value if m == 0 else total[oy] + value
            for oy in range(7):
                stencil[ox * 7 + oy, rows, :] = total[oy]


def edge_rows(
    recon_hbm, mass_hbm, weights_hbm, cells_hbm, codes_hbm,
    mass, weights, cells, codes, send_down, send_up,
    recon, edge_weights, edge_cells, edge_codes, edge_stencil, turned, spread, sems,
):
    sources = (recon_hbm, codes_hbm, weights_hbm, cells_hbm, mass_hbm)
    targets = (recon, codes, weights, cells, mass)
    copies = [pltpu.make_async_copy(a, b, sems.at[i]) for i, (a, b) in enumerate(zip(sources, targets))]
    for copy in copies:
        copy.start()
    for copy in copies[1:4]:
        copy.wait()
    stacks, width = mass.shape[:2]
    for target, source in ((edge_weights, weights), (edge_cells, cells), (edge_codes, codes)):
        for index in np.ndindex(*source.shape[:-2]):
            target[index + (slice(0, 3), slice(None))] = source[index + (slice(0, 3), slice(None))]
            target[index + (slice(3, 8), slice(None))] = source[index + (slice(width - 5, width), slice(None))]
    fill_stencil(
        recon, edge_weights, edge_cells, edge_codes, turned, spread, edge_stencil, 1, copies[0].wait
    )
    copies[4].wait()
    for send, mass_at, stencil_at in ((send_down, width - 6, 5), (send_up, 0, 0)):
        for s in range(stacks):
            send[6 * s : 6 * s + 6, :] = mass[s, mass_at : mass_at + 6, :]
        for o in range(OFFSETS):
            at = 6 * stacks + 3 * o
            send[at : at + 3, :] = edge_stencil[o, stencil_at : stencil_at + 3, :]


def coefficients(recon_hbm, weights, cells, codes, stencil, recon, turned, spread, sem):
    copy = pltpu.make_async_copy(recon_hbm, recon, sem.at[0])
    copy.start()
    fill_stencil(recon, weights, cells, codes, turned, spread, stencil, stencil.shape[1] // 8, copy.wait)


def pack_stacks(load, stacks, tile):
    lane = lanes()
    left = jnp.zeros((8, 128), F32)
    right = jnp.zeros((8, 128), F32)
    for s in range(PER * tile, min(stacks, PER * tile + PER)):
        at = SPAN * (s % PER)
        moved = turn(load(s), at - 122)
        right = jnp.where(lane >= at, moved, right)
        left = jnp.where(from_place(lane, at + 6, at + 12), moved, left)
    return turn(left, -3), right


def from_place(lane, low, high):
    return (lane >= low) | (lane < high - 128) if high > 128 else lane >= low


def pack_coefficients(load):
    lane = lanes()
    left = jnp.zeros((8, 128), F32)
    right = jnp.zeros((8, 128), F32)
    for o in range(COEF_PER):
        at = 3 * o
        moved = turn(load(o), at - 125)
        right = jnp.where(lane >= at, moved, right)
        left = jnp.where(from_place(lane, at + 3, at + 6), moved, left)
    return turn(left, -3), right


def add_spare(load, left, right):
    lane = lanes()
    for o in range(COEF_PER, OFFSETS):
        at = SPAN * (o - COEF_PER)
        value = load(o)
        left = jnp.where((lane >= at) & (lane < at + 3), turn(value, at), left)
        right = jnp.where((lane >= at + 6) & (lane < at + 9), turn(value, at - 119), right)
    return left, right


def fill_near(near):
    lane = lanes(1)
    group = (lane * 57) >> 9
    at = lane - SPAN * group
    source = lax.broadcasted_iota(jnp.int32, (128, 128), 0)
    for dy in range(-3, 4):
        q = at - dy
        right = jnp.where((at >= 3) & (q >= 0) & (q < 6), 122 + q, -1)
        left = jnp.where((at < 6) & (q >= 3) & (q < 9), q - 3, -1)
        for side, wanted in enumerate((right, left)):
            wanted = jnp.where(group < PER, wanted, -1)
            picked = jnp.where(source == wanted, 1.0, 0.0).astype(jnp.bfloat16)
            near[dy + 3, 0:128, 128 * side : 128 * side + 128] = picked
            near[dy + 3, 128:256, 128 * side : 128 * side + 128] = picked


def replicate(value, picks):
    high = value.astype(jnp.bfloat16)
    low = (value - high.astype(F32)).astype(jnp.bfloat16)
    return jnp.dot(jnp.concatenate([high, low], axis=1), picks, preferred_element_type=F32)


def fill_picks(picks):
    lane = lanes(1)
    group = (lane * 57) >> 9
    at = lane - SPAN * group
    source = lax.broadcasted_iota(jnp.int32, (128, 128), 0)
    for dy in range(-3, 4):
        q = at - dy
        halo = (q >= 3) & (q < 6)
        right = jnp.where(halo, 57 + q, jnp.where((q >= 0) & (q < 3) & (at >= 3), 125 + q, -1))
        left = jnp.where(halo, 61 + q, jnp.where((q >= 6) & (q < 9) & (at < 6), q - 6, -1))
        for side, wanted in enumerate((right, left)):
            wanted = jnp.where(group < PER, wanted, -1)
            picked = jnp.where(source == wanted, 1.0, 0.0).astype(jnp.bfloat16)
            picks[dy + 3, 0:128, 128 * side : 128 * side + 128] = picked
            picks[dy + 3, 128:256, 128 * side : 128 * side + 128] = picked


def pack_own(mass, stencil, left, right, picks, near):
    fill_picks(picks)
    fill_near(near)
    stacks, width = mass.shape[:2]
    tiles = -(-stacks // PER)
    for half in range(width // 8):
        rows = pl.ds(8 * half, 8)
        for tile in range(tiles):
            at = width * tile + 8 * half
            values = pack_stacks(lambda s: mass[s, rows, :], stacks, tile)
            if tile == 0:
                values = add_spare(lambda o: stencil[o, rows, :], *values)
            left[at : at + 8, :], right[at : at + 8, :] = values
        at = width * tiles + 8 * half
        left[at : at + 8, :], right[at : at + 8, :] = pack_coefficients(lambda o: stencil[o, rows, :])


def pack_all(stacks, own_left, own_right, above, below, middle, send_a, send_b, left, right):
    tiles = -(-stacks // PER)
    width = own_left.shape[0] // (tiles + 1)
    tall = width + 12
    first, last = ends(ROW_AXES)
    top_rows = lax.broadcasted_iota(jnp.int32, (8, 128), 0) < 3
    ready = []
    for got, outside, place, coef_place in (
        (above, first, width, width), (below, last, width + 6, width + 3)
    ):
        coef = lambda o: got[6 * stacks + 3 * o : 6 * stacks + 3 * o + 8, :]
        for tile in range(tiles):
            packed = pack_stacks(lambda s: got[6 * s : 6 * s + 8, :], stacks, tile)
            if tile == 0:
                spare = add_spare(coef, *packed)
                packed = [jnp.where(top_rows, new, old) for new, old in zip(spare, packed)]
            ready.append((tall * tile + place, 6, outside, packed))
        ready.append((tall * tiles + coef_place, 3, outside, pack_coefficients(coef)))
    for at, count, outside, packed in ready:
        for send, value in zip((left, right), packed):
            send[at : at + count, :] = jnp.where(outside, 0.0, value[0:count])
    for send, own in ((left, own_left), (right, own_right)):
        for tile in range(tiles + 1):
            send[tall * tile : tall * tile + width, :] = own[width * tile : width * tile + width, :]
        end = tall * tiles + width + 6
        send[end:, :] = jnp.zeros((send.shape[0] - end, 128), F32)
    choose(is_even(COLUMN_AXES), right, left, send_a, send_b)


def choose(even, first, second, first_out, second_out):
    @pl.when(even)
    def _():
        first_out[...] = first[...]
        second_out[...] = second[...]

    @pl.when(jnp.logical_not(even))
    def _():
        first_out[...] = second[...]
        second_out[...] = first[...]


def main_sum(load, coef, coef_at, tile):
    fields = [[load(k, 8 * tile + dx) for k in range(GROUP)] for dx in range(7)]
    total = [None] * GROUP
    for dy in range(7):
        part = [None] * GROUP
        for dx in range(7):
            at = coef_at + 8 * tile
            scale = coef[dx * 7 + dy, at : at + 8, :]
            for k in range(GROUP):
                term = scale * fields[dx][k]
                part[k] = term if dx == 0 else part[k] + term
        for k in range(GROUP):
            moved = turn(part[k], 3 - dy)
            total[k] = moved if dy == 0 else total[k] + moved
    return total


def shift_rows(load, store):
    lane = lanes()
    values = []
    for o in range(OFFSETS):
        dy = o % 7 - 3
        value = turn(load(o), dy)
        if dy > 0:
            value = jnp.where(lane >= dy, value, 0.0)
        elif dy < 0:
            value = jnp.where(lane < 128 + dy, value, 0.0)
        values.append(value)
    for o, value in enumerate(values):
        store(o, value)


def own_part(mass, stencil, near, middle, own_shifted, right_near, left_near):
    stacks, width = mass.shape[:2]
    for tile in range(width // 8):
        rows = pl.ds(8 * tile, 8)

        def store(o, value):
            own_shifted[o, rows, :] = value

        shift_rows(lambda o: stencil[o, rows, :], store)

    def some_stacks(turn_at, carry):
        for_groups(
            turn_at, stacks, range((width - 8) // 8), own_shifted, 5,
            lambda s, tile, at: mass[s, 2 + at : 10 + at, :],
            lambda s, tile, value: store_rows(middle, s, 8 * tile, value),
        )
        return carry

    lax.fori_loop(0, turns(stacks), some_stacks, 0)
    for dy in range(7):
        value = jnp.concatenate([stencil[dx * 7 + dy, :, :] for dx in range(7)], axis=0)
        spread = replicate(value, near[dy])
        for dx in range(7):
            right_near[dx * 7 + dy, :, :] = spread[width * dx : width * dx + width, 0:128]
            left_near[dx * 7 + dy, :, :] = spread[width * dx : width * dx + width, 128:256]


def both_steps(mass, stencil, above, below, middle, own_shifted, second, wide, shifted, field, partial):
    stacks, width = mass.shape[:2]
    first, last = ends(ROW_AXES)
    coefs = 6 * stacks
    for s in range(stacks):
        field[0, s, 2:8, :] = above[6 * s : 6 * s + 6, :]
        field[0, s, 8:16, :] = mass[s, 0:8, :]
        field[1, s, 0:8, :] = mass[s, width - 8 : width, :]
        field[1, s, 8:16, :] = below[6 * s : 6 * s + 8, :]
    for o in range(OFFSETS):
        at = coefs + 3 * o
        wide[o, 0:3, :] = above[at : at + 3, :]
        wide[o, 3 : width + 3, :] = stencil[o, :, :]
        wide[o, width + 3 : width + 6, :] = below[at : at + 3, :]
        wide[o, width + 6 : width + 8, :] = jnp.zeros((2, 128), F32)

    @pl.when(first)
    def _():
        for s in range(stacks):
            field[0, s, 2:8, :] = jnp.zeros((6, 128), F32)
        for o in range(OFFSETS):
            wide[o, 0:3, :] = jnp.zeros((3, 128), F32)

    @pl.when(last)
    def _():
        for s in range(stacks):
            field[1, s, 8:16, :] = jnp.zeros((8, 128), F32)
        for o in range(OFFSETS):
            wide[o, width + 3 : width + 6, :] = jnp.zeros((3, 128), F32)

    for end, tile in enumerate((0, width // 8)):
        rows = pl.ds(8 * tile, 8)

        def store(o, value):
            shifted[end, o, :, :] = value

        shift_rows(lambda o: wide[o, rows, :], store)

    def first_step(turn_at, carry):
        sums = [
            for_groups(
                turn_at, stacks, (0,), shifted.at[end], 0, lambda s, tile, at: field[end, s, 2 + at : 10 + at, :]
            )
            for end in range(2)
        ]
        for end, tile in enumerate((0, width // 8)):
            for s, _, value in sums[end]:
                store_rows(partial, s, 8 * tile, value)
        for s, _, _ in sums[0]:
            partial[s, 8:width, :] = middle[s, :, :]
        return carry

    lax.fori_loop(0, turns(stacks), first_step, 0)

    def second_step(turn_at, carry):
        for_groups(
            turn_at, stacks, range(width // 8), own_shifted, 0,
            lambda s, tile, at: partial[s, at : at + 8, :],
            lambda s, tile, value: store_rows(second, s, 8 * tile, value),
        )
        return carry

    lax.fori_loop(0, turns(stacks), second_step, 0)


def store_rows(target, s, at, value):
    target[s, at : at + 8, :] = value


def per_turn(stacks):
    return next(GROUP * groups for groups in (5, 2, 1) if stacks % (GROUP * groups) == 0)


def turns(stacks):
    return stacks // per_turn(stacks)


def for_groups(turn_at, stacks, tiles, coef, coef_at, load, store=None):
    sums = []
    for part in range(per_turn(stacks) // GROUP):
        start = turn_at * per_turn(stacks) + part * GROUP
        for tile in tiles:
            total = main_sum(lambda k, at: load(start + k, tile, at), coef, coef_at, tile)
            sums += [(start + k, tile, total[k]) for k in range(GROUP)]
    if store is not None:
        for s, tile, value in sums:
            store(s, tile, value)
    return sums


def packed_sum(load, coef, coef_at, tile, tiles, dys):
    fields = [[load(t, 8 * tile + dx) for t in range(tiles)] for dx in range(7)]
    total = [None] * tiles
    for dy in dys:
        part = [None] * tiles
        for dx in range(7):
            at = coef_at + 8 * tile
            scale = coef[dx * 7 + dy + 3, at : at + 8, :]
            for t in range(tiles):
                term = scale * fields[dx][t]
                part[t] = term if dx == 0 else part[t] + term
        for t in range(tiles):
            moved = turn(part[t], -dy)
            total[t] = moved if total[t] is None else total[t] + moved
    return total


def place_in_group(rows=8):
    lane = lanes(rows)
    return lane - SPAN * ((lane * 57) >> 9)


def side_coefficients(
    wide, send_a, send_b, got_b, got_a, picks,
    right_set, left_set, right_coef, left_coef, right_halo, left_halo, rows_of,
):
    tall = wide.shape[1]
    width = tall - 8
    tiles = right_set.shape[0]
    lane = lanes()

    first, last = ends(COLUMN_AXES)

    def gather(sent_right, sent_left, got_right, got_left):
        part = width + 12
        place = place_in_group(part)
        rows = [slice(part * tile, part * tile + part) for tile in range(tiles)]
        from_right = [jnp.where(last, 0.0, got_right[at, :]) for at in rows]
        from_left = [jnp.where(first, 0.0, got_left[at, :]) for at in rows]
        for tile, at in enumerate(rows):
            right = jnp.where(place < 3, turn(sent_right[at, :], -3), from_right[tile])
            left = jnp.where(place >= 6, turn(sent_left[at, :], 3), from_left[tile])
            for target, value in ((right_set, right), (left_set, left)):
                target[tile, 6 : width + 6, :] = value[0:width]
                target[tile, 0:6, :] = value[width : width + 6]
                target[tile, width + 6 : width + 12, :] = value[width + 6 : width + 12]
                target[tile, width + 12 : width + 16, :] = jnp.zeros((4, 128), F32)
        coefs = slice(part * tiles, part * tiles + width + 6)
        for target, source, got, outside in (
            (right_halo, from_right, got_right, last), (left_halo, from_left, got_left, first)
        ):
            value = jnp.where(outside, 0.0, got[coefs, :])
            spare = source[0]
            for tile, own, above, below in (
                (0, value[0:width], value[width : width + 3], value[width + 3 : width + 6]),
                (1, spare[0:width], spare[width : width + 3], spare[width + 6 : width + 9]),
            ):
                target[tile, 3 : width + 3, :] = own
                target[tile, 0:3, :] = above
                target[tile, width + 3 : width + 6, :] = below
                target[tile, width + 6 : width + 8, :] = jnp.zeros((2, 128), F32)

    even = is_even(COLUMN_AXES)

    @pl.when(even)
    def _():
        gather(send_a, send_b, got_a, got_b)

    @pl.when(jnp.logical_not(even))
    def _():
        gather(send_b, send_a, got_b, got_a)

    from_right = (lane >= 60) & (lane < 63)
    from_left = (lane >= 64) & (lane < 67)
    for tile in range(tall // 8):
        rows = pl.ds(8 * tile, 8)
        right_rows = [right_halo[t, rows, :] for t in range(2)]
        left_rows = [left_halo[t, rows, :] for t in range(2)]
        values = []
        for o in range(OFFSETS):
            if o < COEF_PER:
                right = turn(right_rows[0], 60 - 3 * o)
                left = turn(left_rows[0], 64 - 3 * o)
            else:
                at = SPAN * (o - COEF_PER)
                right = turn(right_rows[1], 60 - at)
                left = turn(left_rows[1], 58 - at)
            values.append(jnp.where(from_right, right, jnp.where(from_left, left, wide[o, rows, :])))
        for o, value in enumerate(values):
            at = tall * (o // 7) + 8 * tile
            rows_of[o % 7, at : at + 8, :] = value

    for dy in range(7):
        spread = replicate(rows_of[dy], picks[dy])
        for dx in range(7):
            right_coef[dx * 7 + dy, :, :] = spread[tall * dx : tall * dx + tall, 0:128]
            left_coef[dx * 7 + dy, :, :] = spread[tall * dx : tall * dx + tall, 128:256]


def halo_steps(
    right_set, left_set, right_coef, left_coef, right_near, left_near, second, out_hbm,
    right_next, left_next, out, sems,
):
    tiles = right_set.shape[0]
    stacks, width = out.shape[:2]
    place = place_in_group()
    everywhere = range(-3, 4)
    row_tiles = range(right_next.shape[1] // 8)
    sums = [
        [
            packed_sum(lambda t, at: side[t, at : at + 8, :], coef, 0, tile, tiles, everywhere)
            for side, coef in ((right_set, right_coef), (left_set, left_coef))
        ]
        for tile in row_tiles
    ]
    for tile in row_tiles:
        right, left = sums[tile]
        rows = pl.ds(8 * tile, 8)
        for t in range(tiles):
            right_next[t, rows, :] = jnp.where(place >= 3, turn(right[t], 3), 0.0)
            left_next[t, rows, :] = jnp.where(place < 6, turn(left[t], -3), 0.0)
    changes = [
        [
            packed_sum(lambda t, at: side[t, at : at + 8, :], coef, 0, tile, tiles, everywhere)
            for side, coef in ((right_next, right_near), (left_next, left_near))
        ]
        for tile in range(width // 8)
    ]

    lane = lanes()
    copies = []
    for t in range(tiles):
        low, high = PER * t, min(stacks, PER * t + PER)
        for tile in range(width // 8):
            rows = pl.ds(8 * tile, 8)
            right, left = (side[t] for side in changes[tile])
            values = []
            for s in range(low, high):
                at = SPAN * (s - low)
                change = jnp.where(lane < 6, turn(left, -at - 3), 0.0)
                change = jnp.where(lane >= 122, turn(right, 122 - at), change)
                values.append(second[s, rows, :] + change)
            for s, value in zip(range(low, high), values):
                out[s, rows, :] = value
        piece = pl.ds(low, high - low)
        copies.append(pltpu.make_async_copy(out.at[piece], out_hbm.at[piece], sems.at[t]))
        copies[-1].start()
    for copy in copies:
        copy.wait()


def local(tracer_mass, recon_table, intersection_weights, intersection_cells, rotation_codes):
    stacks, width, columns = tracer_mass.shape
    shape = lambda *sizes: jax.ShapeDtypeStruct(sizes, F32)
    scratch = lambda *sizes: pltpu.VMEM(sizes, F32)
    tiles = -(-stacks // PER)
    combos = 4 * (width // 8)
    tall, low = width + 16, width + 8
    fixed = lambda *values: [pltpu.with_memory_space_constraint(value, pltpu.HBM) for value in values]
    whole = lambda value: jax.ShapeDtypeStruct(value.shape, value.dtype)
    edge = -(-(6 * stacks + 3 * OFFSETS + 5) // 8) * 8
    integers = lambda *sizes: pltpu.VMEM(sizes, jnp.int32)
    picks = jax.ShapeDtypeStruct((7, 256, 256), jnp.bfloat16)
    regions = intersection_cells.shape[0]

    mass, weights, cells, codes, send_down, send_up = pl.pallas_call(
        edge_rows,
        out_shape=(
            whole(tracer_mass), whole(intersection_weights), whole(intersection_cells),
            whole(rotation_codes), shape(edge, 128), shape(edge, 128),
        ),
        in_specs=[HBM] * 5,
        out_specs=(VMEM,) * 6,
        scratch_shapes=[
            pltpu.SMEM(recon_table.shape, F32),
            scratch(regions, TERMS, 8, 128),
            integers(regions, 8, 128),
            integers(regions, 8, 128),
            scratch(OFFSETS, 8, 128),
            scratch(TERMS, regions, 8, 128),
            scratch(25, regions, 8, 128),
            pltpu.SemaphoreType.DMA((5,)),
        ],
        compiler_params=params(),
        cost_estimate=cost(4 * 10**6),
        name="edge_rows",
    )(*fixed(recon_table, tracer_mass, intersection_weights, intersection_cells, rotation_codes))
    above = shift(send_down, ROW_AXES, 1)
    below = shift(send_up, ROW_AXES, -1)

    stencil = pl.pallas_call(
        coefficients,
        out_shape=shape(OFFSETS, width, 128),
        in_specs=[HBM] + [VMEM] * 3,
        out_specs=VMEM,
        scratch_shapes=[
            pltpu.SMEM(recon_table.shape, F32),
            scratch(TERMS, combos, 8, 128),
            scratch(25, combos, 8, 128),
            pltpu.SemaphoreType.DMA((1,)),
        ],
        compiler_params=params(),
        cost_estimate=cost(8 * 10**6),
        name="coefficients",
    )(*fixed(recon_table), weights, cells, codes)

    own_left, own_right, picks, near = pl.pallas_call(
        pack_own,
        out_shape=(shape(width * (tiles + 1), 128),) * 2 + (picks, picks),
        in_specs=[VMEM] * 2,
        out_specs=(VMEM,) * 4,
        compiler_params=params(),
        cost_estimate=cost(10**6),
        name="pack_own",
    )(mass, stencil)

    middle, own_shifted, right_near, left_near = pl.pallas_call(
        own_part,
        out_shape=(shape(stacks, width - 8, 128),) + (shape(OFFSETS, width, 128),) * 3,
        in_specs=[VMEM] * 3,
        out_specs=(VMEM,) * 4,
        compiler_params=params(),
        cost_estimate=cost(4 * 10**6),
        name="own_part",
    )(mass, stencil, near)

    send = ((width + 12) * (tiles + 1), 128)
    send_a, send_b = pl.pallas_call(
        functools.partial(pack_all, stacks),
        out_shape=(shape(*send),) * 2,
        in_specs=[VMEM] * 4 + [ANY],
        out_specs=(VMEM,) * 2,
        scratch_shapes=[scratch(*send)] * 2,
        compiler_params=params(),
        cost_estimate=cost(10**6),
        name="pack_all",
    )(own_left, own_right, above, below, middle)
    column_b = column_swap(send_b, True)
    column_a = column_swap(send_a, False)

    second, wide = pl.pallas_call(
        both_steps,
        out_shape=(shape(stacks, width, 128), shape(OFFSETS, low, 128)),
        in_specs=[VMEM] * 6,
        out_specs=(VMEM,) * 2,
        scratch_shapes=[scratch(2, OFFSETS, 8, 128), scratch(2, stacks, 16, 128), scratch(stacks, low, 128)],
        compiler_params=params(),
        cost_estimate=cost(12 * 10**6),
        name="both_steps",
    )(mass, stencil, above, below, middle, own_shifted)

    sides = pl.pallas_call(
        side_coefficients,
        out_shape=(shape(tiles, tall, 128),) * 2 + (shape(OFFSETS, low, 128),) * 2,
        in_specs=[VMEM] * 6,
        out_specs=(VMEM,) * 4,
        scratch_shapes=[scratch(2, low, 128)] * 2 + [scratch(7, 7 * low, 128)],
        compiler_params=params(),
        cost_estimate=cost(4 * 10**6),
        name="side_coefficients",
    )(wide, send_a, send_b, column_b, column_a, picks)

    return pl.pallas_call(
        halo_steps,
        out_shape=shape(stacks, width, columns),
        in_specs=[VMEM] * 7,
        out_specs=HBM,
        scratch_shapes=[scratch(tiles, low, 128)] * 2
        + [scratch(stacks, width, columns), pltpu.SemaphoreType.DMA((tiles,))],
        compiler_params=params(),
        cost_estimate=cost(4 * 10**6),
        name="halo_steps",
    )(*sides, right_near, left_near, second)


def solution(mesh):
    in_specs = (
        P(None, ("face", "px"), "py"),
        P(),
        P(None, None, ("face", "px"), "py"),
        P(None, ("face", "px"), "py"),
        P(None, ("face", "px"), "py"),
    )
    out_specs = P(None, ("face", "px"), "py")
    return jax.shard_map(local, mesh=mesh, in_specs=in_specs, out_specs=out_specs, check_vma=False)
```

```python
import functools

import jax
import jax.numpy as jnp
import numpy as np
from jax import lax
from jax.experimental import pallas as pl
from jax.experimental.pallas import tpu as pltpu
from jax.sharding import PartitionSpec as P

F32 = jnp.float32
ROW_AXES = ("face", "px")
COLUMN_AXES = "py"
SWAPPED = (0, 2, 1, 5, 4, 3, 9, 8, 7, 6)
POWERS = ((0, 0), (1, 0), (0, 1), (2, 0), (1, 1), (0, 2), (3, 0), (2, 1), (1, 2), (0, 3))
TERMS = 10
OFFSETS = 49
GROUP = 4
SPAN = 9
PER = 14
COEF_PER = 42
VMEM = pl.BlockSpec(memory_space=pltpu.VMEM)
ANY = pl.BlockSpec(memory_space=pl.ANY)
HBM = pl.BlockSpec(memory_space=pltpu.HBM)


def params():
    return pltpu.CompilerParams(vmem_limit_bytes=40 * 1024 * 1024)


def cost(operations):
    return pl.CostEstimate(flops=operations, bytes_accessed=1 << 20, transcendentals=0)


def column_swap(block, odd_first):
    chains, count = lax.axis_size(ROW_AXES), lax.axis_size(COLUMN_AXES)
    column = list(range(count))
    for low in range(1 if odd_first else 0, count - 1, 2):
        column[low], column[low + 1] = low + 1, low
    pairs = []
    for chain in range(chains):
        for place in range(count):
            target = (chain, column[place])
            if column[place] == place and chains % 2 == 0:
                target = (chain ^ 1, place)
            pairs.append((chain * count + place, target[0] * count + target[1]))
    return lax.ppermute(block, ROW_AXES + (COLUMN_AXES,), pairs)


def shift(block, axes, step):
    count = lax.axis_size(axes)
    return lax.ppermute(block, axes, [(index, (index + step) % count) for index in range(count)])


def ends(axes):
    index = lax.axis_index(axes)
    return index == 0, index == lax.axis_size(axes) - 1


def is_even(axes):
    return lax.rem(lax.axis_index(axes), 2) == 0


def turn(value, amount):
    amount %= 128
    return pltpu.roll(value, amount, 1) if amount else value


def lanes(rows=8):
    return lax.broadcasted_iota(jnp.int32, (rows, 128), 1)


def fill_stencil(recon, weights, cells, codes, turned, spread, stencil, tiles, before_taps):
    zero = jnp.zeros((8, 128), F32)
    for g in range(tiles):
        rows = pl.ds(8 * g, 8)
        for m in range(4):
            code = codes[m, rows, :]
            odd = (code & 1) == 1
            sign_x = jnp.where(code >= 2, -1.0, 1.0).astype(F32)
            sign_y = jnp.where((code == 1) | (code == 2), -1.0, 1.0).astype(F32)
            sign_xy = sign_x * sign_y
            values = [weights[m, t, rows, :] for t in range(TERMS)]
            for t, (a, b) in enumerate(POWERS):
                value = values[t]
                if SWAPPED[t] != t:
                    value = jnp.where(odd, values[SWAPPED[t]], value)
                if a % 2 and b % 2:
                    value = value * sign_xy
                elif a % 2:
                    value = value * sign_x
                elif b % 2:
                    value = value * sign_y
                turned[t, m * tiles + g] = value

    combos = 4 * tiles
    before_taps()

    def five_taps(jx, carry):
        total = [[None] * combos for jy in range(5)]
        for t in range(TERMS):
            values = [turned[t, c] for c in range(combos)]
            for jy in range(5):
                scale = recon[t, 5 * jx + jy]
                for c in range(combos):
                    term = values[c] * scale
                    total[jy][c] = term if t == 0 else total[jy][c] + term
        for jy in range(5):
            for c in range(combos):
                spread[5 * jx + jy, c] = total[jy][c]
        return carry

    lax.fori_loop(0, 5, five_taps, 0)

    for g in range(tiles):
        rows = pl.ds(8 * g, 8)
        masks = []
        for m in range(4):
            cell = cells[m, rows, :]
            first = jnp.where(cell < 3, 0, jnp.where(cell < 6, 3, 6))
            across = cell - first
            masks.append((cell < 3, cell < 6, across == 0, across <= 1))
        for ox in range(7):
            total = [None] * 7
            for m in range(4):
                low_x, mid_x, low_y, mid_y = masks[m]

                def tap(jx, jy):
                    if 0 <= jx < 5 and 0 <= jy < 5:
                        return spread[jx * 5 + jy, m * tiles + g]
                    return zero

                line = [
                    jnp.where(low_x, tap(ox, jy), jnp.where(mid_x, tap(ox - 1, jy), tap(ox - 2, jy)))
                    for jy in range(5)
                ]
                padded = [zero, zero] + line + [zero, zero]
                for oy in range(7):
                    value = jnp.where(
                        low_y, padded[oy + 2], jnp.where(mid_y, padded[oy + 1], padded[oy])
                    )
                    total[oy] = value if m == 0 else total[oy] + value
            for oy in range(7):
                stencil[ox * 7 + oy, rows, :] = total[oy]


def edge_rows(
    recon_hbm, mass_hbm, weights_hbm, cells_hbm, codes_hbm,
    mass, weights, cells, codes, send_down, send_up,
    recon, edge_weights, edge_cells, edge_codes, edge_stencil, turned, spread, sems,
):
    sources = (recon_hbm, codes_hbm, weights_hbm, cells_hbm, mass_hbm)
    targets = (recon, codes, weights, cells, mass)
    copies = [pltpu.make_async_copy(a, b, sems.at[i]) for i, (a, b) in enumerate(zip(sources, targets))]
    for copy in copies:
        copy.start()
    for copy in copies[1:4]:
        copy.wait()
    stacks, width = mass.shape[:2]
    for target, source in ((edge_weights, weights), (edge_cells, cells), (edge_codes, codes)):
        for index in np.ndindex(*source.shape[:-2]):
            target[index + (slice(0, 3), slice(None))] = source[index + (slice(0, 3), slice(None))]
            target[index + (slice(3, 8), slice(None))] = source[index + (slice(width - 5, width), slice(None))]
    fill_stencil(
        recon, edge_weights, edge_cells, edge_codes, turned, spread, edge_stencil, 1, copies[0].wait
    )
    copies[4].wait()
    for send, mass_at, stencil_at in ((send_down, width - 6, 5), (send_up, 0, 0)):
        for s in range(stacks):
            send[6 * s : 6 * s + 6, :] = mass[s, mass_at : mass_at + 6, :]
        for o in range(OFFSETS):
            at = 6 * stacks + 3 * o
            send[at : at + 3, :] = edge_stencil[o, stencil_at : stencil_at + 3, :]


def coefficients(recon_hbm, weights, cells, codes, stencil, recon, turned, spread, sem):
    copy = pltpu.make_async_copy(recon_hbm, recon, sem.at[0])
    copy.start()
    fill_stencil(recon, weights, cells, codes, turned, spread, stencil, stencil.shape[1] // 8, copy.wait)


def pack_stacks(load, stacks, tile):
    lane = lanes()
    left = jnp.zeros((8, 128), F32)
    right = jnp.zeros((8, 128), F32)
    for s in range(PER * tile, min(stacks, PER * tile + PER)):
        at = SPAN * (s % PER)
        moved = turn(load(s), at - 122)
        right = jnp.where(lane >= at, moved, right)
        left = jnp.where(from_place(lane, at + 6, at + 12), moved, left)
    return turn(left, -3), right


def from_place(lane, low, high):
    return (lane >= low) | (lane < high - 128) if high > 128 else lane >= low


def pack_coefficients(load):
    lane = lanes()
    left = jnp.zeros((8, 128), F32)
    right = jnp.zeros((8, 128), F32)
    for o in range(COEF_PER):
        at = 3 * o
        moved = turn(load(o), at - 125)
        right = jnp.where(lane >= at, moved, right)
        left = jnp.where(from_place(lane, at + 3, at + 6), moved, left)
    return turn(left, -3), right


def add_spare(load, left, right):
    lane = lanes()
    for o in range(COEF_PER, OFFSETS):
        at = SPAN * (o - COEF_PER)
        value = load(o)
        left = jnp.where((lane >= at) & (lane < at + 3), turn(value, at), left)
        right = jnp.where((lane >= at + 6) & (lane < at + 9), turn(value, at - 119), right)
    return left, right


def fill_near(near):
    lane = lanes(1)
    group = (lane * 57) >> 9
    at = lane - SPAN * group
    source = lax.broadcasted_iota(jnp.int32, (128, 128), 0)
    for dy in range(-3, 4):
        q = at - dy
        right = jnp.where((at >= 3) & (q >= 0) & (q < 6), 122 + q, -1)
        left = jnp.where((at < 6) & (q >= 3) & (q < 9), q - 3, -1)
        for side, wanted in enumerate((right, left)):
            wanted = jnp.where(group < PER, wanted, -1)
            picked = jnp.where(source == wanted, 1.0, 0.0).astype(jnp.bfloat16)
            near[dy + 3, 0:128, 128 * side : 128 * side + 128] = picked
            near[dy + 3, 128:256, 128 * side : 128 * side + 128] = picked


def replicate(value, picks):
    high = value.astype(jnp.bfloat16)
    low = (value - high.astype(F32)).astype(jnp.bfloat16)
    return jnp.dot(jnp.concatenate([high, low], axis=1), picks, preferred_element_type=F32)


def fill_picks(picks):
    lane = lanes(1)
    group = (lane * 57) >> 9
    at = lane - SPAN * group
    source = lax.broadcasted_iota(jnp.int32, (128, 128), 0)
    for dy in range(-3, 4):
        q = at - dy
        halo = (q >= 3) & (q < 6)
        right = jnp.where(halo, 57 + q, jnp.where((q >= 0) & (q < 3) & (at >= 3), 125 + q, -1))
        left = jnp.where(halo, 61 + q, jnp.where((q >= 6) & (q < 9) & (at < 6), q - 6, -1))
        for side, wanted in enumerate((right, left)):
            wanted = jnp.where(group < PER, wanted, -1)
            picked = jnp.where(source == wanted, 1.0, 0.0).astype(jnp.bfloat16)
            picks[dy + 3, 0:128, 128 * side : 128 * side + 128] = picked
            picks[dy + 3, 128:256, 128 * side : 128 * side + 128] = picked


def pack_own(mass, stencil, left, right, picks, near):
    fill_picks(picks)
    fill_near(near)
    stacks, width = mass.shape[:2]
    tiles = -(-stacks // PER)
    for half in range(width // 8):
        rows = pl.ds(8 * half, 8)
        for tile in range(tiles):
            at = width * tile + 8 * half
            values = pack_stacks(lambda s: mass[s, rows, :], stacks, tile)
            if tile == 0:
                values = add_spare(lambda o: stencil[o, rows, :], *values)
            left[at : at + 8, :], right[at : at + 8, :] = values
        at = width * tiles + 8 * half
        left[at : at + 8, :], right[at : at + 8, :] = pack_coefficients(lambda o: stencil[o, rows, :])


def pack_all(stacks, own_left, own_right, above, below, middle, send_a, send_b, left, right):
    tiles = -(-stacks // PER)
    width = own_left.shape[0] // (tiles + 1)
    tall = width + 12
    first, last = ends(ROW_AXES)
    top_rows = lax.broadcasted_iota(jnp.int32, (8, 128), 0) < 3
    ready = []
    for got, outside, place, coef_place in (
        (above, first, width, width), (below, last, width + 6, width + 3)
    ):
        coef = lambda o: got[6 * stacks + 3 * o : 6 * stacks + 3 * o + 8, :]
        for tile in range(tiles):
            packed = pack_stacks(lambda s: got[6 * s : 6 * s + 8, :], stacks, tile)
            if tile == 0:
                spare = add_spare(coef, *packed)
                packed = [jnp.where(top_rows, new, old) for new, old in zip(spare, packed)]
            ready.append((tall * tile + place, 6, outside, packed))
        ready.append((tall * tiles + coef_place, 3, outside, pack_coefficients(coef)))
    for at, count, outside, packed in ready:
        for send, value in zip((left, right), packed):
            send[at : at + count, :] = jnp.where(outside, 0.0, value[0:count])
    for send, own in ((left, own_left), (right, own_right)):
        for tile in range(tiles + 1):
            send[tall * tile : tall * tile + width, :] = own[width * tile : width * tile + width, :]
        end = tall * tiles + width + 6
        send[end:, :] = jnp.zeros((send.shape[0] - end, 128), F32)
    choose(is_even(COLUMN_AXES), right, left, send_a, send_b)


def choose(even, first, second, first_out, second_out):
    @pl.when(even)
    def _():
        first_out[...] = first[...]
        second_out[...] = second[...]

    @pl.when(jnp.logical_not(even))
    def _():
        first_out[...] = second[...]
        second_out[...] = first[...]


def main_sum(load, coef, coef_at, tile):
    fields = [[load(k, 8 * tile + dx) for k in range(GROUP)] for dx in range(7)]
    total = [None] * GROUP
    for dy in range(7):
        part = [None] * GROUP
        for dx in range(7):
            at = coef_at + 8 * tile
            scale = coef[dx * 7 + dy, at : at + 8, :]
            for k in range(GROUP):
                term = scale * fields[dx][k]
                part[k] = term if dx == 0 else part[k] + term
        for k in range(GROUP):
            moved = turn(part[k], 3 - dy)
            total[k] = moved if dy == 0 else total[k] + moved
    return total


def shift_rows(load, store):
    lane = lanes()
    values = []
    for o in range(OFFSETS):
        dy = o % 7 - 3
        value = turn(load(o), dy)
        if dy > 0:
            value = jnp.where(lane >= dy, value, 0.0)
        elif dy < 0:
            value = jnp.where(lane < 128 + dy, value, 0.0)
        values.append(value)
    for o, value in enumerate(values):
        store(o, value)


def own_part(mass, stencil, near, middle, own_shifted, right_near, left_near):
    stacks, width = mass.shape[:2]
    for tile in range(width // 8):
        rows = pl.ds(8 * tile, 8)

        def store(o, value):
            own_shifted[o, rows, :] = value

        shift_rows(lambda o: stencil[o, rows, :], store)

    def some_stacks(turn_at, carry):
        for_groups(
            turn_at, stacks, range((width - 8) // 8), own_shifted, 5,
            lambda s, tile, at: mass[s, 2 + at : 10 + at, :],
            lambda s, tile, value: store_rows(middle, s, 8 * tile, value),
        )
        return carry

    lax.fori_loop(0, turns(stacks), some_stacks, 0)
    for dy in range(7):
        value = jnp.concatenate([stencil[dx * 7 + dy, :, :] for dx in range(7)], axis=0)
        spread = replicate(value, near[dy])
        for dx in range(7):
            right_near[dx * 7 + dy, :, :] = spread[width * dx : width * dx + width, 0:128]
            left_near[dx * 7 + dy, :, :] = spread[width * dx : width * dx + width, 128:256]


def both_steps(mass, stencil, above, below, middle, own_shifted, second, wide, shifted, field, partial):
    stacks, width = mass.shape[:2]
    first, last = ends(ROW_AXES)
    coefs = 6 * stacks
    for s in range(stacks):
        field[0, s, 2:8, :] = above[6 * s : 6 * s + 6, :]
        field[0, s, 8:16, :] = mass[s, 0:8, :]
        field[1, s, 0:8, :] = mass[s, width - 8 : width, :]
        field[1, s, 8:16, :] = below[6 * s : 6 * s + 8, :]
    for o in range(OFFSETS):
        at = coefs + 3 * o
        wide[o, 0:3, :] = above[at : at + 3, :]
        wide[o, 3 : width + 3, :] = stencil[o, :, :]
        wide[o, width + 3 : width + 6, :] = below[at : at + 3, :]
        wide[o, width + 6 : width + 8, :] = jnp.zeros((2, 128), F32)

    @pl.when(first)
    def _():
        for s in range(stacks):
            field[0, s, 2:8, :] = jnp.zeros((6, 128), F32)
        for o in range(OFFSETS):
            wide[o, 0:3, :] = jnp.zeros((3, 128), F32)

    @pl.when(last)
    def _():
        for s in range(stacks):
            field[1, s, 8:16, :] = jnp.zeros((8, 128), F32)
        for o in range(OFFSETS):
            wide[o, width + 3 : width + 6, :] = jnp.zeros((3, 128), F32)

    for end, tile in enumerate((0, width // 8)):
        rows = pl.ds(8 * tile, 8)

        def store(o, value):
            shifted[end, o, :, :] = value

        shift_rows(lambda o: wide[o, rows, :], store)

    def first_step(turn_at, carry):
        sums = [
            for_groups(
                turn_at, stacks, (0,), shifted.at[end], 0, lambda s, tile, at: field[end, s, 2 + at : 10 + at, :]
            )
            for end in range(2)
        ]
        for end, tile in enumerate((0, width // 8)):
            for s, _, value in sums[end]:
                store_rows(partial, s, 8 * tile, value)
        for s, _, _ in sums[0]:
            partial[s, 8:width, :] = middle[s, :, :]
        return carry

    lax.fori_loop(0, turns(stacks), first_step, 0)

    def second_step(turn_at, carry):
        for_groups(
            turn_at, stacks, range(width // 8), own_shifted, 0,
            lambda s, tile, at: partial[s, at : at + 8, :],
            lambda s, tile, value: store_rows(second, s, 8 * tile, value),
        )
        return carry

    lax.fori_loop(0, turns(stacks), second_step, 0)


def store_rows(target, s, at, value):
    target[s, at : at + 8, :] = value


def per_turn(stacks):
    return next(GROUP * groups for groups in (5, 2, 1) if stacks % (GROUP * groups) == 0)


def turns(stacks):
    return stacks // per_turn(stacks)


def for_groups(turn_at, stacks, tiles, coef, coef_at, load, store=None):
    sums = []
    for part in range(per_turn(stacks) // GROUP):
        start = turn_at * per_turn(stacks) + part * GROUP
        for tile in tiles:
            total = main_sum(lambda k, at: load(start + k, tile, at), coef, coef_at, tile)
            sums += [(start + k, tile, total[k]) for k in range(GROUP)]
    if store is not None:
        for s, tile, value in sums:
            store(s, tile, value)
    return sums


def take_first(got, after, out):
    out[...] = got[...]


def packed_sum(load, coef, coef_at, tile, tiles, dys):
    fields = [[load(t, 8 * tile + dx) for t in range(tiles)] for dx in range(7)]
    total = [None] * tiles
    for dy in dys:
        part = [None] * tiles
        for dx in range(7):
            at = coef_at + 8 * tile
            scale = coef[dx * 7 + dy + 3, at : at + 8, :]
            for t in range(tiles):
                term = scale * fields[dx][t]
                part[t] = term if dx == 0 else part[t] + term
        for t in range(tiles):
            moved = turn(part[t], -dy)
            total[t] = moved if total[t] is None else total[t] + moved
    return total


def place_in_group(rows=8):
    lane = lanes(rows)
    return lane - SPAN * ((lane * 57) >> 9)


def side_coefficients(
    wide, send_a, send_b, got_b, got_a, picks,
    right_set, left_set, right_coef, left_coef, right_halo, left_halo, rows_of,
):
    tall = wide.shape[1]
    width = tall - 8
    tiles = right_set.shape[0]
    lane = lanes()

    first, last = ends(COLUMN_AXES)

    def gather(sent_right, sent_left, got_right, got_left):
        part = width + 12
        place = place_in_group(part)
        rows = [slice(part * tile, part * tile + part) for tile in range(tiles)]
        from_right = [jnp.where(last, 0.0, got_right[at, :]) for at in rows]
        from_left = [jnp.where(first, 0.0, got_left[at, :]) for at in rows]
        for tile, at in enumerate(rows):
            right = jnp.where(place < 3, turn(sent_right[at, :], -3), from_right[tile])
            left = jnp.where(place >= 6, turn(sent_left[at, :], 3), from_left[tile])
            for target, value in ((right_set, right), (left_set, left)):
                target[tile, 6 : width + 6, :] = value[0:width]
                target[tile, 0:6, :] = value[width : width + 6]
                target[tile, width + 6 : width + 12, :] = value[width + 6 : width + 12]
                target[tile, width + 12 : width + 16, :] = jnp.zeros((4, 128), F32)
        coefs = slice(part * tiles, part * tiles + width + 6)
        for target, source, got, outside in (
            (right_halo, from_right, got_right, last), (left_halo, from_left, got_left, first)
        ):
            value = jnp.where(outside, 0.0, got[coefs, :])
            spare = source[0]
            for tile, own, above, below in (
                (0, value[0:width], value[width : width + 3], value[width + 3 : width + 6]),
                (1, spare[0:width], spare[width : width + 3], spare[width + 6 : width + 9]),
            ):
                target[tile, 3 : width + 3, :] = own
                target[tile, 0:3, :] = above
                target[tile, width + 3 : width + 6, :] = below
                target[tile, width + 6 : width + 8, :] = jnp.zeros((2, 128), F32)

    even = is_even(COLUMN_AXES)

    @pl.when(even)
    def _():
        gather(send_a, send_b, got_a, got_b)

    @pl.when(jnp.logical_not(even))
    def _():
        gather(send_b, send_a, got_b, got_a)

    from_right = (lane >= 60) & (lane < 63)
    from_left = (lane >= 64) & (lane < 67)
    for tile in range(tall // 8):
        rows = pl.ds(8 * tile, 8)
        right_rows = [right_halo[t, rows, :] for t in range(2)]
        left_rows = [left_halo[t, rows, :] for t in range(2)]
        values = []
        for o in range(OFFSETS):
            if o < COEF_PER:
                right = turn(right_rows[0], 60 - 3 * o)
                left = turn(left_rows[0], 64 - 3 * o)
            else:
                at = SPAN * (o - COEF_PER)
                right = turn(right_rows[1], 60 - at)
                left = turn(left_rows[1], 58 - at)
            values.append(jnp.where(from_right, right, jnp.where(from_left, left, wide[o, rows, :])))
        for o, value in enumerate(values):
            at = tall * (o // 7) + 8 * tile
            rows_of[o % 7, at : at + 8, :] = value

    for dy in range(7):
        spread = replicate(rows_of[dy], picks[dy])
        for dx in range(7):
            right_coef[dx * 7 + dy, :, :] = spread[tall * dx : tall * dx + tall, 0:128]
            left_coef[dx * 7 + dy, :, :] = spread[tall * dx : tall * dx + tall, 128:256]


def halo_steps(
    right_set, left_set, right_coef, left_coef, right_near, left_near, second, out_hbm,
    right_next, left_next, out, sems,
):
    tiles = right_set.shape[0]
    stacks, width = out.shape[:2]
    place = place_in_group()
    everywhere = range(-3, 4)
    row_tiles = range(right_next.shape[1] // 8)
    sums = [
        [
            packed_sum(lambda t, at: side[t, at : at + 8, :], coef, 0, tile, tiles, everywhere)
            for side, coef in ((right_set, right_coef), (left_set, left_coef))
        ]
        for tile in row_tiles
    ]
    for tile in row_tiles:
        right, left = sums[tile]
        rows = pl.ds(8 * tile, 8)
        for t in range(tiles):
            right_next[t, rows, :] = jnp.where(place >= 3, turn(right[t], 3), 0.0)
            left_next[t, rows, :] = jnp.where(place < 6, turn(left[t], -3), 0.0)
    changes = [
        [
            packed_sum(lambda t, at: side[t, at : at + 8, :], coef, 0, tile, tiles, everywhere)
            for side, coef in ((right_next, right_near), (left_next, left_near))
        ]
        for tile in range(width // 8)
    ]

    lane = lanes()
    copies = []
    for t in range(tiles):
        low, high = PER * t, min(stacks, PER * t + PER)
        for tile in range(width // 8):
            rows = pl.ds(8 * tile, 8)
            right, left = (side[t] for side in changes[tile])
            values = []
            for s in range(low, high):
                at = SPAN * (s - low)
                change = jnp.where(lane < 6, turn(left, -at - 3), 0.0)
                change = jnp.where(lane >= 122, turn(right, 122 - at), change)
                values.append(second[s, rows, :] + change)
            for s, value in zip(range(low, high), values):
                out[s, rows, :] = value
        piece = pl.ds(low, high - low)
        copies.append(pltpu.make_async_copy(out.at[piece], out_hbm.at[piece], sems.at[t]))
        copies[-1].start()
    for copy in copies:
        copy.wait()


def local(tracer_mass, recon_table, intersection_weights, intersection_cells, rotation_codes):
    stacks, width, columns = tracer_mass.shape
    shape = lambda *sizes: jax.ShapeDtypeStruct(sizes, F32)
    scratch = lambda *sizes: pltpu.VMEM(sizes, F32)
    tiles = -(-stacks // PER)
    combos = 4 * (width // 8)
    tall, low = width + 16, width + 8
    fixed = lambda *values: [pltpu.with_memory_space_constraint(value, pltpu.HBM) for value in values]
    whole = lambda value: jax.ShapeDtypeStruct(value.shape, value.dtype)
    edge = -(-(6 * stacks + 3 * OFFSETS + 5) // 8) * 8
    integers = lambda *sizes: pltpu.VMEM(sizes, jnp.int32)
    picks = jax.ShapeDtypeStruct((7, 256, 256), jnp.bfloat16)
    regions = intersection_cells.shape[0]

    mass, weights, cells, codes, send_down, send_up = pl.pallas_call(
        edge_rows,
        out_shape=(
            whole(tracer_mass), whole(intersection_weights), whole(intersection_cells),
            whole(rotation_codes), shape(edge, 128), shape(edge, 128),
        ),
        in_specs=[HBM] * 5,
        out_specs=(VMEM,) * 6,
        scratch_shapes=[
            pltpu.SMEM(recon_table.shape, F32),
            scratch(regions, TERMS, 8, 128),
            integers(regions, 8, 128),
            integers(regions, 8, 128),
            scratch(OFFSETS, 8, 128),
            scratch(TERMS, regions, 8, 128),
            scratch(25, regions, 8, 128),
            pltpu.SemaphoreType.DMA((5,)),
        ],
        compiler_params=params(),
        cost_estimate=cost(4 * 10**6),
        name="edge_rows",
    )(*fixed(recon_table, tracer_mass, intersection_weights, intersection_cells, rotation_codes))
    above = shift(send_down, ROW_AXES, 1)
    below = shift(send_up, ROW_AXES, -1)

    stencil = pl.pallas_call(
        coefficients,
        out_shape=shape(OFFSETS, width, 128),
        in_specs=[HBM] + [VMEM] * 3,
        out_specs=VMEM,
        scratch_shapes=[
            pltpu.SMEM(recon_table.shape, F32),
            scratch(TERMS, combos, 8, 128),
            scratch(25, combos, 8, 128),
            pltpu.SemaphoreType.DMA((1,)),
        ],
        compiler_params=params(),
        cost_estimate=cost(8 * 10**6),
        name="coefficients",
    )(*fixed(recon_table), weights, cells, codes)

    own_left, own_right, picks, near = pl.pallas_call(
        pack_own,
        out_shape=(shape(width * (tiles + 1), 128),) * 2 + (picks, picks),
        in_specs=[VMEM] * 2,
        out_specs=(VMEM,) * 4,
        compiler_params=params(),
        cost_estimate=cost(10**6),
        name="pack_own",
    )(mass, stencil)

    middle, own_shifted, right_near, left_near = pl.pallas_call(
        own_part,
        out_shape=(shape(stacks, width - 8, 128),) + (shape(OFFSETS, width, 128),) * 3,
        in_specs=[VMEM] * 3,
        out_specs=(VMEM,) * 4,
        compiler_params=params(),
        cost_estimate=cost(4 * 10**6),
        name="own_part",
    )(mass, stencil, near)

    send = ((width + 12) * (tiles + 1), 128)
    send_a, send_b = pl.pallas_call(
        functools.partial(pack_all, stacks),
        out_shape=(shape(*send),) * 2,
        in_specs=[VMEM] * 4 + [ANY],
        out_specs=(VMEM,) * 2,
        scratch_shapes=[scratch(*send)] * 2,
        compiler_params=params(),
        cost_estimate=cost(10**6),
        name="pack_all",
    )(own_left, own_right, above, below, middle)
    column_b = column_swap(send_b, True)
    column_a = column_swap(send_a, False)

    second, wide = pl.pallas_call(
        both_steps,
        out_shape=(shape(stacks, width, 128), shape(OFFSETS, low, 128)),
        in_specs=[VMEM] * 6,
        out_specs=(VMEM,) * 2,
        scratch_shapes=[scratch(2, OFFSETS, 8, 128), scratch(2, stacks, 16, 128), scratch(stacks, low, 128)],
        compiler_params=params(),
        cost_estimate=cost(12 * 10**6),
        name="both_steps",
    )(mass, stencil, above, below, middle, own_shifted)

    column_b = pl.pallas_call(
        take_first,
        out_shape=shape(*send),
        in_specs=[VMEM, ANY],
        out_specs=VMEM,
        compiler_params=params(),
        cost_estimate=cost(10**4),
        name="take_first",
    )(column_b, second)

    sides = pl.pallas_call(
        side_coefficients,
        out_shape=(shape(tiles, tall, 128),) * 2 + (shape(OFFSETS, low, 128),) * 2,
        in_specs=[VMEM] * 6,
        out_specs=(VMEM,) * 4,
        scratch_shapes=[scratch(2, low, 128)] * 2 + [scratch(7, 7 * low, 128)],
        compiler_params=params(),
        cost_estimate=cost(4 * 10**6),
        name="side_coefficients",
    )(wide, send_a, send_b, column_b, column_a, picks)

    return pl.pallas_call(
        halo_steps,
        out_shape=shape(stacks, width, columns),
        in_specs=[VMEM] * 7,
        out_specs=HBM,
        scratch_shapes=[scratch(tiles, low, 128)] * 2
        + [scratch(stacks, width, columns), pltpu.SemaphoreType.DMA((tiles,))],
        compiler_params=params(),
        cost_estimate=cost(4 * 10**6),
        name="halo_steps",
    )(*sides, right_near, left_near, second)


def solution(mesh):
    in_specs = (
        P(None, ("face", "px"), "py"),
        P(),
        P(None, None, ("face", "px"), "py"),
        P(None, ("face", "px"), "py"),
        P(None, ("face", "px"), "py"),
    )
    out_specs = P(None, ("face", "px"), "py")
    return jax.shard_map(local, mesh=mesh, in_specs=in_specs, out_specs=out_specs, check_vma=False)
```

```python
import functools

import jax
import jax.numpy as jnp
import numpy as np
from jax import lax
from jax.experimental import pallas as pl
from jax.experimental.pallas import tpu as pltpu
from jax.sharding import PartitionSpec as P

F32 = jnp.float32
ROW_AXES = ("face", "px")
COLUMN_AXES = "py"
SWAPPED = (0, 2, 1, 5, 4, 3, 9, 8, 7, 6)
POWERS = ((0, 0), (1, 0), (0, 1), (2, 0), (1, 1), (0, 2), (3, 0), (2, 1), (1, 2), (0, 3))
TERMS = 10
OFFSETS = 49
GROUP = 4
SPAN = 9
PER = 14
COEF_PER = 42
VMEM = pl.BlockSpec(memory_space=pltpu.VMEM)
ANY = pl.BlockSpec(memory_space=pl.ANY)
HBM = pl.BlockSpec(memory_space=pltpu.HBM)


def params():
    return pltpu.CompilerParams(vmem_limit_bytes=40 * 1024 * 1024)


def cost(operations):
    return pl.CostEstimate(flops=operations, bytes_accessed=1 << 20, transcendentals=0)


def column_swap(block, odd_first):
    chains, count = lax.axis_size(ROW_AXES), lax.axis_size(COLUMN_AXES)
    column = list(range(count))
    for low in range(1 if odd_first else 0, count - 1, 2):
        column[low], column[low + 1] = low + 1, low
    pairs = []
    for chain in range(chains):
        for place in range(count):
            target = (chain, column[place])
            if column[place] == place and chains % 2 == 0:
                target = (chain ^ 1, place)
            pairs.append((chain * count + place, target[0] * count + target[1]))
    return lax.ppermute(block, ROW_AXES + (COLUMN_AXES,), pairs)


def row_swap(block, odd_first):
    chains, count = lax.axis_size(ROW_AXES), lax.axis_size(COLUMN_AXES)
    chain_of = list(range(chains))
    for low in range(1 if odd_first else 0, chains - 1, 2):
        chain_of[low], chain_of[low + 1] = low + 1, low
    pairs = []
    for chain in range(chains):
        for place in range(count):
            target = (chain_of[chain], place)
            if chain_of[chain] == chain and count % 2 == 0:
                target = (chain, place ^ 1)
            pairs.append((chain * count + place, target[0] * count + target[1]))
    return lax.ppermute(block, ROW_AXES + (COLUMN_AXES,), pairs)


def ends(axes):
    index = lax.axis_index(axes)
    return index == 0, index == lax.axis_size(axes) - 1


def is_even(axes):
    return lax.rem(lax.axis_index(axes), 2) == 0


def turn(value, amount):
    amount %= 128
    return pltpu.roll(value, amount, 1) if amount else value


def lanes(rows=8):
    return lax.broadcasted_iota(jnp.int32, (rows, 128), 1)


def fill_stencil(recon, weights, cells, codes, turned, spread, stencil, tiles, before_taps):
    zero = jnp.zeros((8, 128), F32)
    for g in range(tiles):
        rows = pl.ds(8 * g, 8)
        for m in range(4):
            code = codes[m, rows, :]
            odd = (code & 1) == 1
            sign_x = jnp.where(code >= 2, -1.0, 1.0).astype(F32)
            sign_y = jnp.where((code == 1) | (code == 2), -1.0, 1.0).astype(F32)
            sign_xy = sign_x * sign_y
            values = [weights[m, t, rows, :] for t in range(TERMS)]
            for t, (a, b) in enumerate(POWERS):
                value = values[t]
                if SWAPPED[t] != t:
                    value = jnp.where(odd, values[SWAPPED[t]], value)
                if a % 2 and b % 2:
                    value = value * sign_xy
                elif a % 2:
                    value = value * sign_x
                elif b % 2:
                    value = value * sign_y
                turned[t, m * tiles + g] = value

    combos = 4 * tiles
    before_taps()

    def five_taps(jx, carry):
        total = [[None] * combos for jy in range(5)]
        for t in range(TERMS):
            values = [turned[t, c] for c in range(combos)]
            for jy in range(5):
                scale = recon[t, 5 * jx + jy]
                for c in range(combos):
                    term = values[c] * scale
                    total[jy][c] = term if t == 0 else total[jy][c] + term
        for jy in range(5):
            for c in range(combos):
                spread[5 * jx + jy, c] = total[jy][c]
        return carry

    lax.fori_loop(0, 5, five_taps, 0)

    for g in range(tiles):
        rows = pl.ds(8 * g, 8)
        masks = []
        for m in range(4):
            cell = cells[m, rows, :]
            first = jnp.where(cell < 3, 0, jnp.where(cell < 6, 3, 6))
            across = cell - first
            masks.append((cell < 3, cell < 6, across == 0, across <= 1))
        for ox in range(7):
            total = [None] * 7
            for m in range(4):
                low_x, mid_x, low_y, mid_y = masks[m]

                def tap(jx, jy):
                    if 0 <= jx < 5 and 0 <= jy < 5:
                        return spread[jx * 5 + jy, m * tiles + g]
                    return zero

                line = [
                    jnp.where(low_x, tap(ox, jy), jnp.where(mid_x, tap(ox - 1, jy), tap(ox - 2, jy)))
                    for jy in range(5)
                ]
                padded = [zero, zero] + line + [zero, zero]
                for oy in range(7):
                    value = jnp.where(
                        low_y, padded[oy + 2], jnp.where(mid_y, padded[oy + 1], padded[oy])
                    )
                    total[oy] = value if m == 0 else total[oy] + value
            for oy in range(7):
                stencil[ox * 7 + oy, rows, :] = total[oy]


def edge_rows(
    recon_hbm, mass_hbm, weights_hbm, cells_hbm, codes_hbm,
    mass, weights, cells, codes, send_a, send_b,
    recon, edge_weights, edge_cells, edge_codes, edge_stencil, turned, spread, sems,
):
    sources = (recon_hbm, codes_hbm, weights_hbm, cells_hbm, mass_hbm)
    targets = (recon, codes, weights, cells, mass)
    copies = [pltpu.make_async_copy(a, b, sems.at[i]) for i, (a, b) in enumerate(zip(sources, targets))]
    for copy in copies:
        copy.start()
    for copy in copies[1:4]:
        copy.wait()
    stacks, width = mass.shape[:2]
    for target, source in ((edge_weights, weights), (edge_cells, cells), (edge_codes, codes)):
        for index in np.ndindex(*source.shape[:-2]):
            target[index + (slice(0, 3), slice(None))] = source[index + (slice(0, 3), slice(None))]
            target[index + (slice(3, 8), slice(None))] = source[index + (slice(width - 5, width), slice(None))]
    fill_stencil(
        recon, edge_weights, edge_cells, edge_codes, turned, spread, edge_stencil, 1, copies[0].wait
    )
    copies[4].wait()
    even = is_even(ROW_AXES)
    for send, low_edge in ((send_a, jnp.logical_not(even)), (send_b, even)):
        mass_at = jnp.where(low_edge, 0, width - 6)
        stencil_at = jnp.where(low_edge, 0, 5)
        for s in range(stacks):
            send[6 * s : 6 * s + 6, :] = mass[s, pl.ds(mass_at, 6), :]
        for o in range(OFFSETS):
            at = 6 * stacks + 3 * o
            send[at : at + 3, :] = edge_stencil[o, pl.ds(stencil_at, 3), :]


def coefficients(recon_hbm, weights, cells, codes, stencil, recon, turned, spread, sem):
    copy = pltpu.make_async_copy(recon_hbm, recon, sem.at[0])
    copy.start()
    fill_stencil(recon, weights, cells, codes, turned, spread, stencil, stencil.shape[1] // 8, copy.wait)


def pack_stacks(load, stacks, tile):
    lane = lanes()
    left = jnp.zeros((8, 128), F32)
    right = jnp.zeros((8, 128), F32)
    for s in range(PER * tile, min(stacks, PER * tile + PER)):
        at = SPAN * (s % PER)
        moved = turn(load(s), at - 122)
        right = jnp.where(lane >= at, moved, right)
        left = jnp.where(from_place(lane, at + 6, at + 12), moved, left)
    return turn(left, -3), right


def from_place(lane, low, high):
    return (lane >= low) | (lane < high - 128) if high > 128 else lane >= low


def pack_coefficients(load):
    lane = lanes()
    left = jnp.zeros((8, 128), F32)
    right = jnp.zeros((8, 128), F32)
    for o in range(COEF_PER):
        at = 3 * o
        moved = turn(load(o), at - 125)
        right = jnp.where(lane >= at, moved, right)
        left = jnp.where(from_place(lane, at + 3, at + 6), moved, left)
    return turn(left, -3), right


def add_spare(load, left, right):
    lane = lanes()
    for o in range(COEF_PER, OFFSETS):
        at = SPAN * (o - COEF_PER)
        value = load(o)
        left = jnp.where((lane >= at) & (lane < at + 3), turn(value, at), left)
        right = jnp.where((lane >= at + 6) & (lane < at + 9), turn(value, at - 119), right)
    return left, right


def fill_near(near):
    lane = lanes(1)
    group = (lane * 57) >> 9
    at = lane - SPAN * group
    source = lax.broadcasted_iota(jnp.int32, (128, 128), 0)
    for dy in range(-3, 4):
        q = at - dy
        right = jnp.where((at >= 3) & (q >= 0) & (q < 6), 122 + q, -1)
        left = jnp.where((at < 6) & (q >= 3) & (q < 9), q - 3, -1)
        for side, wanted in enumerate((right, left)):
            wanted = jnp.where(group < PER, wanted, -1)
            picked = jnp.where(source == wanted, 1.0, 0.0).astype(jnp.bfloat16)
            near[dy + 3, 0:128, 128 * side : 128 * side + 128] = picked
            near[dy + 3, 128:256, 128 * side : 128 * side + 128] = picked


def replicate(value, picks):
    high = value.astype(jnp.bfloat16)
    low = (value - high.astype(F32)).astype(jnp.bfloat16)
    return jnp.dot(jnp.concatenate([high, low], axis=1), picks, preferred_element_type=F32)


def fill_picks(picks):
    lane = lanes(1)
    group = (lane * 57) >> 9
    at = lane - SPAN * group
    source = lax.broadcasted_iota(jnp.int32, (128, 128), 0)
    for dy in range(-3, 4):
        q = at - dy
        halo = (q >= 3) & (q < 6)
        right = jnp.where(halo, 57 + q, jnp.where((q >= 0) & (q < 3) & (at >= 3), 125 + q, -1))
        left = jnp.where(halo, 61 + q, jnp.where((q >= 6) & (q < 9) & (at < 6), q - 6, -1))
        for side, wanted in enumerate((right, left)):
            wanted = jnp.where(group < PER, wanted, -1)
            picked = jnp.where(source == wanted, 1.0, 0.0).astype(jnp.bfloat16)
            picks[dy + 3, 0:128, 128 * side : 128 * side + 128] = picked
            picks[dy + 3, 128:256, 128 * side : 128 * side + 128] = picked


def pack_own(mass, stencil, left, right, picks, near):
    fill_picks(picks)
    fill_near(near)
    stacks, width = mass.shape[:2]
    tiles = -(-stacks // PER)
    for half in range(width // 8):
        rows = pl.ds(8 * half, 8)
        for tile in range(tiles):
            at = width * tile + 8 * half
            values = pack_stacks(lambda s: mass[s, rows, :], stacks, tile)
            if tile == 0:
                values = add_spare(lambda o: stencil[o, rows, :], *values)
            left[at : at + 8, :], right[at : at + 8, :] = values
        at = width * tiles + 8 * half
        left[at : at + 8, :], right[at : at + 8, :] = pack_coefficients(lambda o: stencil[o, rows, :])


def pack_all(stacks, own_left, own_right, above, below, middle, send_a, send_b, left, right):
    tiles = -(-stacks // PER)
    width = own_left.shape[0] // (tiles + 1)
    tall = width + 12
    first, last = ends(ROW_AXES)
    top_rows = lax.broadcasted_iota(jnp.int32, (8, 128), 0) < 3
    ready = []
    for got, outside, place, coef_place in (
        (above, first, width, width), (below, last, width + 6, width + 3)
    ):
        coef = lambda o: got[6 * stacks + 3 * o : 6 * stacks + 3 * o + 8, :]
        for tile in range(tiles):
            packed = pack_stacks(lambda s: got[6 * s : 6 * s + 8, :], stacks, tile)
            if tile == 0:
                spare = add_spare(coef, *packed)
                packed = [jnp.where(top_rows, new, old) for new, old in zip(spare, packed)]
            ready.append((tall * tile + place, 6, outside, packed))
        ready.append((tall * tiles + coef_place, 3, outside, pack_coefficients(coef)))
    for at, count, outside, packed in ready:
        for send, value in zip((left, right), packed):
            send[at : at + count, :] = jnp.where(outside, 0.0, value[0:count])
    for send, own in ((left, own_left), (right, own_right)):
        for tile in range(tiles + 1):
            send[tall * tile : tall * tile + width, :] = own[width * tile : width * tile + width, :]
        end = tall * tiles + width + 6
        send[end:, :] = jnp.zeros((send.shape[0] - end, 128), F32)
    choose(is_even(COLUMN_AXES), right, left, send_a, send_b)


def choose(even, first, second, first_out, second_out):
    @pl.when(even)
    def _():
        first_out[...] = first[...]
        second_out[...] = second[...]

    @pl.when(jnp.logical_not(even))
    def _():
        first_out[...] = second[...]
        second_out[...] = first[...]


def main_sum(load, coef, coef_at, tile):
    fields = [[load(k, 8 * tile + dx) for k in range(GROUP)] for dx in range(7)]
    total = [None] * GROUP
    for dy in range(7):
        part = [None] * GROUP
        for dx in range(7):
            at = coef_at + 8 * tile
            scale = coef[dx * 7 + dy, at : at + 8, :]
            for k in range(GROUP):
                term = scale * fields[dx][k]
                part[k] = term if dx == 0 else part[k] + term
        for k in range(GROUP):
            moved = turn(part[k], 3 - dy)
            total[k] = moved if dy == 0 else total[k] + moved
    return total


def shift_rows(load, store):
    lane = lanes()
    values = []
    for o in range(OFFSETS):
        dy = o % 7 - 3
        value = turn(load(o), dy)
        if dy > 0:
            value = jnp.where(lane >= dy, value, 0.0)
        elif dy < 0:
            value = jnp.where(lane < 128 + dy, value, 0.0)
        values.append(value)
    for o, value in enumerate(values):
        store(o, value)


def own_part(mass, stencil, near, middle, own_shifted, right_near, left_near):
    stacks, width = mass.shape[:2]
    for tile in range(width // 8):
        rows = pl.ds(8 * tile, 8)

        def store(o, value):
            own_shifted[o, rows, :] = value

        shift_rows(lambda o: stencil[o, rows, :], store)

    def some_stacks(turn_at, carry):
        for_groups(
            turn_at, stacks, range((width - 8) // 8), own_shifted, 5,
            lambda s, tile, at: mass[s, 2 + at : 10 + at, :],
            lambda s, tile, value: store_rows(middle, s, 8 * tile, value),
        )
        return carry

    lax.fori_loop(0, turns(stacks), some_stacks, 0)
    for dy in range(7):
        value = jnp.concatenate([stencil[dx * 7 + dy, :, :] for dx in range(7)], axis=0)
        spread = replicate(value, near[dy])
        for dx in range(7):
            right_near[dx * 7 + dy, :, :] = spread[width * dx : width * dx + width, 0:128]
            left_near[dx * 7 + dy, :, :] = spread[width * dx : width * dx + width, 128:256]


def both_steps(mass, stencil, above, below, middle, own_shifted, second, wide, shifted, field, partial):
    stacks, width = mass.shape[:2]
    first, last = ends(ROW_AXES)
    coefs = 6 * stacks
    for s in range(stacks):
        field[0, s, 2:8, :] = above[6 * s : 6 * s + 6, :]
        field[0, s, 8:16, :] = mass[s, 0:8, :]
        field[1, s, 0:8, :] = mass[s, width - 8 : width, :]
        field[1, s, 8:16, :] = below[6 * s : 6 * s + 8, :]
    for o in range(OFFSETS):
        at = coefs + 3 * o
        wide[o, 0:3, :] = above[at : at + 3, :]
        wide[o, 3 : width + 3, :] = stencil[o, :, :]
        wide[o, width + 3 : width + 6, :] = below[at : at + 3, :]
        wide[o, width + 6 : width + 8, :] = jnp.zeros((2, 128), F32)

    @pl.when(first)
    def _():
        for s in range(stacks):
            field[0, s, 2:8, :] = jnp.zeros((6, 128), F32)
        for o in range(OFFSETS):
            wide[o, 0:3, :] = jnp.zeros((3, 128), F32)

    @pl.when(last)
    def _():
        for s in range(stacks):
            field[1, s, 8:16, :] = jnp.zeros((8, 128), F32)
        for o in range(OFFSETS):
            wide[o, width + 3 : width + 6, :] = jnp.zeros((3, 128), F32)

    for end, tile in enumerate((0, width // 8)):
        rows = pl.ds(8 * tile, 8)

        def store(o, value):
            shifted[end, o, :, :] = value

        shift_rows(lambda o: wide[o, rows, :], store)

    def first_step(turn_at, carry):
        sums = [
            for_groups(
                turn_at, stacks, (0,), shifted.at[end], 0, lambda s, tile, at: field[end, s, 2 + at : 10 + at, :]
            )
            for end in range(2)
        ]
        for end, tile in enumerate((0, width // 8)):
            for s, _, value in sums[end]:
                store_rows(partial, s, 8 * tile, value)
        for s, _, _ in sums[0]:
            partial[s, 8:width, :] = middle[s, :, :]
        return carry

    lax.fori_loop(0, turns(stacks), first_step, 0)

    def second_step(turn_at, carry):
        for_groups(
            turn_at, stacks, range(width // 8), own_shifted, 0,
            lambda s, tile, at: partial[s, at : at + 8, :],
            lambda s, tile, value: store_rows(second, s, 8 * tile, value),
        )
        return carry

    lax.fori_loop(0, turns(stacks), second_step, 0)


def store_rows(target, s, at, value):
    target[s, at : at + 8, :] = value


def per_turn(stacks):
    return next(GROUP * groups for groups in (5, 2, 1) if stacks % (GROUP * groups) == 0)


def turns(stacks):
    return stacks // per_turn(stacks)


def for_groups(turn_at, stacks, tiles, coef, coef_at, load, store=None):
    sums = []
    for part in range(per_turn(stacks) // GROUP):
        start = turn_at * per_turn(stacks) + part * GROUP
        for tile in tiles:
            total = main_sum(lambda k, at: load(start + k, tile, at), coef, coef_at, tile)
            sums += [(start + k, tile, total[k]) for k in range(GROUP)]
    if store is not None:
        for s, tile, value in sums:
            store(s, tile, value)
    return sums


def take_first(got, after, out):
    out[...] = got[...]


def in_order(got_a, got_b, above, below):
    choose(is_even(ROW_AXES), got_b, got_a, above, below)


def packed_sum(load, coef, coef_at, tile, tiles, dys):
    fields = [[load(t, 8 * tile + dx) for t in range(tiles)] for dx in range(7)]
    total = [None] * tiles
    for dy in dys:
        part = [None] * tiles
        for dx in range(7):
            at = coef_at + 8 * tile
            scale = coef[dx * 7 + dy + 3, at : at + 8, :]
            for t in range(tiles):
                term = scale * fields[dx][t]
                part[t] = term if dx == 0 else part[t] + term
        for t in range(tiles):
            moved = turn(part[t], -dy)
            total[t] = moved if total[t] is None else total[t] + moved
    return total


def place_in_group(rows=8):
    lane = lanes(rows)
    return lane - SPAN * ((lane * 57) >> 9)


def side_coefficients(
    wide, send_a, send_b, got_b, got_a, picks,
    right_set, left_set, right_coef, left_coef, right_halo, left_halo, rows_of,
):
    tall = wide.shape[1]
    width = tall - 8
    tiles = right_set.shape[0]
    lane = lanes()

    first, last = ends(COLUMN_AXES)

    def gather(sent_right, sent_left, got_right, got_left):
        part = width + 12
        place = place_in_group(part)
        rows = [slice(part * tile, part * tile + part) for tile in range(tiles)]
        from_right = [jnp.where(last, 0.0, got_right[at, :]) for at in rows]
        from_left = [jnp.where(first, 0.0, got_left[at, :]) for at in rows]
        for tile, at in enumerate(rows):
            right = jnp.where(place < 3, turn(sent_right[at, :], -3), from_right[tile])
            left = jnp.where(place >= 6, turn(sent_left[at, :], 3), from_left[tile])
            for target, value in ((right_set, right), (left_set, left)):
                target[tile, 6 : width + 6, :] = value[0:width]
                target[tile, 0:6, :] = value[width : width + 6]
                target[tile, width + 6 : width + 12, :] = value[width + 6 : width + 12]
                target[tile, width + 12 : width + 16, :] = jnp.zeros((4, 128), F32)
        coefs = slice(part * tiles, part * tiles + width + 6)
        for target, source, got, outside in (
            (right_halo, from_right, got_right, last), (left_halo, from_left, got_left, first)
        ):
            value = jnp.where(outside, 0.0, got[coefs, :])
            spare = source[0]
            for tile, own, above, below in (
                (0, value[0:width], value[width : width + 3], value[width + 3 : width + 6]),
                (1, spare[0:width], spare[width : width + 3], spare[width + 6 : width + 9]),
            ):
                target[tile, 3 : width + 3, :] = own
                target[tile, 0:3, :] = above
                target[tile, width + 3 : width + 6, :] = below
                target[tile, width + 6 : width + 8, :] = jnp.zeros((2, 128), F32)

    even = is_even(COLUMN_AXES)

    @pl.when(even)
    def _():
        gather(send_a, send_b, got_a, got_b)

    @pl.when(jnp.logical_not(even))
    def _():
        gather(send_b, send_a, got_b, got_a)

    from_right = (lane >= 60) & (lane < 63)
    from_left = (lane >= 64) & (lane < 67)
    for tile in range(tall // 8):
        rows = pl.ds(8 * tile, 8)
        right_rows = [right_halo[t, rows, :] for t in range(2)]
        left_rows = [left_halo[t, rows, :] for t in range(2)]
        values = []
        for o in range(OFFSETS):
            if o < COEF_PER:
                right = turn(right_rows[0], 60 - 3 * o)
                left = turn(left_rows[0], 64 - 3 * o)
            else:
                at = SPAN * (o - COEF_PER)
                right = turn(right_rows[1], 60 - at)
                left = turn(left_rows[1], 58 - at)
            values.append(jnp.where(from_right, right, jnp.where(from_left, left, wide[o, rows, :])))
        for o, value in enumerate(values):
            at = tall * (o // 7) + 8 * tile
            rows_of[o % 7, at : at + 8, :] = value

    for dy in range(7):
        spread = replicate(rows_of[dy], picks[dy])
        for dx in range(7):
            right_coef[dx * 7 + dy, :, :] = spread[tall * dx : tall * dx + tall, 0:128]
            left_coef[dx * 7 + dy, :, :] = spread[tall * dx : tall * dx + tall, 128:256]


def halo_steps(
    right_set, left_set, right_coef, left_coef, right_near, left_near, second, out_hbm,
    right_next, left_next, out, sems,
):
    tiles = right_set.shape[0]
    stacks, width = out.shape[:2]
    place = place_in_group()
    everywhere = range(-3, 4)
    row_tiles = range(right_next.shape[1] // 8)
    sums = [
        [
            packed_sum(lambda t, at: side[t, at : at + 8, :], coef, 0, tile, tiles, everywhere)
            for side, coef in ((right_set, right_coef), (left_set, left_coef))
        ]
        for tile in row_tiles
    ]
    for tile in row_tiles:
        right, left = sums[tile]
        rows = pl.ds(8 * tile, 8)
        for t in range(tiles):
            right_next[t, rows, :] = jnp.where(place >= 3, turn(right[t], 3), 0.0)
            left_next[t, rows, :] = jnp.where(place < 6, turn(left[t], -3), 0.0)
    changes = [
        [
            packed_sum(lambda t, at: side[t, at : at + 8, :], coef, 0, tile, tiles, everywhere)
            for side, coef in ((right_next, right_near), (left_next, left_near))
        ]
        for tile in range(width // 8)
    ]

    lane = lanes()
    copies = []
    for t in range(tiles):
        low, high = PER * t, min(stacks, PER * t + PER)
        for tile in range(width // 8):
            rows = pl.ds(8 * tile, 8)
            right, left = (side[t] for side in changes[tile])
            values = []
            for s in range(low, high):
                at = SPAN * (s - low)
                change = jnp.where(lane < 6, turn(left, -at - 3), 0.0)
                change = jnp.where(lane >= 122, turn(right, 122 - at), change)
                values.append(second[s, rows, :] + change)
            for s, value in zip(range(low, high), values):
                out[s, rows, :] = value
        piece = pl.ds(low, high - low)
        copies.append(pltpu.make_async_copy(out.at[piece], out_hbm.at[piece], sems.at[t]))
        copies[-1].start()
    for copy in copies:
        copy.wait()


def local(tracer_mass, recon_table, intersection_weights, intersection_cells, rotation_codes):
    stacks, width, columns = tracer_mass.shape
    shape = lambda *sizes: jax.ShapeDtypeStruct(sizes, F32)
    scratch = lambda *sizes: pltpu.VMEM(sizes, F32)
    tiles = -(-stacks // PER)
    combos = 4 * (width // 8)
    tall, low = width + 16, width + 8
    fixed = lambda *values: [pltpu.with_memory_space_constraint(value, pltpu.HBM) for value in values]
    whole = lambda value: jax.ShapeDtypeStruct(value.shape, value.dtype)
    edge = -(-(6 * stacks + 3 * OFFSETS + 5) // 8) * 8
    integers = lambda *sizes: pltpu.VMEM(sizes, jnp.int32)
    picks = jax.ShapeDtypeStruct((7, 256, 256), jnp.bfloat16)
    regions = intersection_cells.shape[0]

    mass, weights, cells, codes, send_a, send_b = pl.pallas_call(
        edge_rows,
        out_shape=(
            whole(tracer_mass), whole(intersection_weights), whole(intersection_cells),
            whole(rotation_codes), shape(edge, 128), shape(edge, 128),
        ),
        in_specs=[HBM] * 5,
        out_specs=(VMEM,) * 6,
        scratch_shapes=[
            pltpu.SMEM(recon_table.shape, F32),
            scratch(regions, TERMS, 8, 128),
            integers(regions, 8, 128),
            integers(regions, 8, 128),
            scratch(OFFSETS, 8, 128),
            scratch(TERMS, regions, 8, 128),
            scratch(25, regions, 8, 128),
            pltpu.SemaphoreType.DMA((5,)),
        ],
        compiler_params=params(),
        cost_estimate=cost(4 * 10**6),
        name="edge_rows",
    )(*fixed(recon_table, tracer_mass, intersection_weights, intersection_cells, rotation_codes))
    got_b = row_swap(send_b, True)
    got_a = row_swap(send_a, False)

    stencil = pl.pallas_call(
        coefficients,
        out_shape=shape(OFFSETS, width, 128),
        in_specs=[HBM] + [VMEM] * 3,
        out_specs=VMEM,
        scratch_shapes=[
            pltpu.SMEM(recon_table.shape, F32),
            scratch(TERMS, combos, 8, 128),
            scratch(25, combos, 8, 128),
            pltpu.SemaphoreType.DMA((1,)),
        ],
        compiler_params=params(),
        cost_estimate=cost(8 * 10**6),
        name="coefficients",
    )(*fixed(recon_table), weights, cells, codes)

    own_left, own_right, picks, near = pl.pallas_call(
        pack_own,
        out_shape=(shape(width * (tiles + 1), 128),) * 2 + (picks, picks),
        in_specs=[VMEM] * 2,
        out_specs=(VMEM,) * 4,
        compiler_params=params(),
        cost_estimate=cost(10**6),
        name="pack_own",
    )(mass, stencil)

    middle, own_shifted, right_near, left_near = pl.pallas_call(
        own_part,
        out_shape=(shape(stacks, width - 8, 128),) + (shape(OFFSETS, width, 128),) * 3,
        in_specs=[VMEM] * 3,
        out_specs=(VMEM,) * 4,
        compiler_params=params(),
        cost_estimate=cost(4 * 10**6),
        name="own_part",
    )(mass, stencil, near)

    got_b = pl.pallas_call(
        take_first,
        out_shape=shape(edge, 128),
        in_specs=[VMEM, ANY],
        out_specs=VMEM,
        compiler_params=params(),
        cost_estimate=cost(10**4),
        name="take_first",
    )(got_b, middle)
    above, below = pl.pallas_call(
        in_order,
        out_shape=(shape(edge, 128),) * 2,
        in_specs=[VMEM] * 2,
        out_specs=(VMEM,) * 2,
        compiler_params=params(),
        cost_estimate=cost(10**4),
        name="in_order",
    )(got_a, got_b)

    send = ((width + 12) * (tiles + 1), 128)
    send_a, send_b = pl.pallas_call(
        functools.partial(pack_all, stacks),
        out_shape=(shape(*send),) * 2,
        in_specs=[VMEM] * 4 + [ANY],
        out_specs=(VMEM,) * 2,
        scratch_shapes=[scratch(*send)] * 2,
        compiler_params=params(),
        cost_estimate=cost(10**6),
        name="pack_all",
    )(own_left, own_right, above, below, middle)
    column_b = column_swap(send_b, True)
    column_a = column_swap(send_a, False)

    second, wide = pl.pallas_call(
        both_steps,
        out_shape=(shape(stacks, width, 128), shape(OFFSETS, low, 128)),
        in_specs=[VMEM] * 6,
        out_specs=(VMEM,) * 2,
        scratch_shapes=[scratch(2, OFFSETS, 8, 128), scratch(2, stacks, 16, 128), scratch(stacks, low, 128)],
        compiler_params=params(),
        cost_estimate=cost(12 * 10**6),
        name="both_steps",
    )(mass, stencil, above, below, middle, own_shifted)

    sides = pl.pallas_call(
        side_coefficients,
        out_shape=(shape(tiles, tall, 128),) * 2 + (shape(OFFSETS, low, 128),) * 2,
        in_specs=[VMEM] * 6,
        out_specs=(VMEM,) * 4,
        scratch_shapes=[scratch(2, low, 128)] * 2 + [scratch(7, 7 * low, 128)],
        compiler_params=params(),
        cost_estimate=cost(4 * 10**6),
        name="side_coefficients",
    )(wide, send_a, send_b, column_b, column_a, picks)

    return pl.pallas_call(
        halo_steps,
        out_shape=shape(stacks, width, columns),
        in_specs=[VMEM] * 7,
        out_specs=HBM,
        scratch_shapes=[scratch(tiles, low, 128)] * 2
        + [scratch(stacks, width, columns), pltpu.SemaphoreType.DMA((tiles,))],
        compiler_params=params(),
        cost_estimate=cost(4 * 10**6),
        name="halo_steps",
    )(*sides, right_near, left_near, second)


def solution(mesh):
    in_specs = (
        P(None, ("face", "px"), "py"),
        P(),
        P(None, None, ("face", "px"), "py"),
        P(None, ("face", "px"), "py"),
        P(None, ("face", "px"), "py"),
    )
    out_specs = P(None, ("face", "px"), "py")
    return jax.shard_map(local, mesh=mesh, in_specs=in_specs, out_specs=out_specs, check_vma=False)
```

```python
import functools

import jax
import jax.numpy as jnp
import numpy as np
from jax import lax
from jax.experimental import pallas as pl
from jax.experimental.pallas import tpu as pltpu
from jax.sharding import PartitionSpec as P

F32 = jnp.float32
ROW_AXES = ("face", "px")
COLUMN_AXES = "py"
SWAPPED = (0, 2, 1, 5, 4, 3, 9, 8, 7, 6)
POWERS = ((0, 0), (1, 0), (0, 1), (2, 0), (1, 1), (0, 2), (3, 0), (2, 1), (1, 2), (0, 3))
TERMS = 10
OFFSETS = 49
GROUP = 4
SPAN = 9
PER = 14
COEF_PER = 42
VMEM = pl.BlockSpec(memory_space=pltpu.VMEM)
ANY = pl.BlockSpec(memory_space=pl.ANY)
HBM = pl.BlockSpec(memory_space=pltpu.HBM)


def params():
    return pltpu.CompilerParams(vmem_limit_bytes=40 * 1024 * 1024)


def cost(operations):
    return pl.CostEstimate(flops=operations, bytes_accessed=1 << 20, transcendentals=0)


def column_swap(block, odd_first):
    chains, count = lax.axis_size(ROW_AXES), lax.axis_size(COLUMN_AXES)
    column = list(range(count))
    for low in range(1 if odd_first else 0, count - 1, 2):
        column[low], column[low + 1] = low + 1, low
    pairs = []
    for chain in range(chains):
        for place in range(count):
            target = (chain, column[place])
            if column[place] == place and chains % 2 == 0:
                target = (chain ^ 1, place)
            pairs.append((chain * count + place, target[0] * count + target[1]))
    return lax.ppermute(block, ROW_AXES + (COLUMN_AXES,), pairs)


def row_swap(block, odd_first):
    chains, count = lax.axis_size(ROW_AXES), lax.axis_size(COLUMN_AXES)
    chain_of = list(range(chains))
    for low in range(1 if odd_first else 0, chains - 1, 2):
        chain_of[low], chain_of[low + 1] = low + 1, low
    pairs = []
    for chain in range(chains):
        for place in range(count):
            target = (chain_of[chain], place)
            if chain_of[chain] == chain and count % 2 == 0:
                target = (chain, place ^ 1)
            pairs.append((chain * count + place, target[0] * count + target[1]))
    return lax.ppermute(block, ROW_AXES + (COLUMN_AXES,), pairs)


def ends(axes):
    index = lax.axis_index(axes)
    return index == 0, index == lax.axis_size(axes) - 1


def is_even(axes):
    return lax.rem(lax.axis_index(axes), 2) == 0


def turn(value, amount):
    amount %= 128
    return pltpu.roll(value, amount, 1) if amount else value


def lanes(rows=8):
    return lax.broadcasted_iota(jnp.int32, (rows, 128), 1)


def fill_stencil(recon, weights, cells, codes, turned, spread, stencil, tiles, before_taps):
    zero = jnp.zeros((8, 128), F32)
    for g in range(tiles):
        rows = pl.ds(8 * g, 8)
        for m in range(4):
            code = codes[m, rows, :]
            odd = (code & 1) == 1
            sign_x = jnp.where(code >= 2, -1.0, 1.0).astype(F32)
            sign_y = jnp.where((code == 1) | (code == 2), -1.0, 1.0).astype(F32)
            sign_xy = sign_x * sign_y
            values = [weights[m, t, rows, :] for t in range(TERMS)]
            for t, (a, b) in enumerate(POWERS):
                value = values[t]
                if SWAPPED[t] != t:
                    value = jnp.where(odd, values[SWAPPED[t]], value)
                if a % 2 and b % 2:
                    value = value * sign_xy
                elif a % 2:
                    value = value * sign_x
                elif b % 2:
                    value = value * sign_y
                turned[t, m * tiles + g] = value

    combos = 4 * tiles
    before_taps()

    def five_taps(jx, carry):
        total = [[None] * combos for jy in range(5)]
        for t in range(TERMS):
            values = [turned[t, c] for c in range(combos)]
            for jy in range(5):
                scale = recon[t, 5 * jx + jy]
                for c in range(combos):
                    term = values[c] * scale
                    total[jy][c] = term if t == 0 else total[jy][c] + term
        for jy in range(5):
            for c in range(combos):
                spread[5 * jx + jy, c] = total[jy][c]
        return carry

    lax.fori_loop(0, 5, five_taps, 0)

    for g in range(tiles):
        rows = pl.ds(8 * g, 8)
        masks = []
        for m in range(4):
            cell = cells[m, rows, :]
            first = jnp.where(cell < 3, 0, jnp.where(cell < 6, 3, 6))
            across = cell - first
            masks.append((cell < 3, cell < 6, across == 0, across <= 1))
        for ox in range(7):
            total = [None] * 7
            for m in range(4):
                low_x, mid_x, low_y, mid_y = masks[m]

                def tap(jx, jy):
                    if 0 <= jx < 5 and 0 <= jy < 5:
                        return spread[jx * 5 + jy, m * tiles + g]
                    return zero

                line = [
                    jnp.where(low_x, tap(ox, jy), jnp.where(mid_x, tap(ox - 1, jy), tap(ox - 2, jy)))
                    for jy in range(5)
                ]
                padded = [zero, zero] + line + [zero, zero]
                for oy in range(7):
                    value = jnp.where(
                        low_y, padded[oy + 2], jnp.where(mid_y, padded[oy + 1], padded[oy])
                    )
                    total[oy] = value if m == 0 else total[oy] + value
            for oy in range(7):
                stencil[ox * 7 + oy, rows, :] = total[oy]


def edge_rows(
    recon_hbm, mass_hbm, weights_hbm, cells_hbm, codes_hbm,
    mass, weights, cells, codes, send_a, send_b,
    recon, edge_weights, edge_cells, edge_codes, edge_stencil, turned, spread, sems,
):
    sources = (recon_hbm, codes_hbm, weights_hbm, cells_hbm, mass_hbm)
    targets = (recon, codes, weights, cells, mass)
    copies = [pltpu.make_async_copy(a, b, sems.at[i]) for i, (a, b) in enumerate(zip(sources, targets))]
    for copy in copies:
        copy.start()
    for copy in copies[1:4]:
        copy.wait()
    stacks, width = mass.shape[:2]
    for target, source in ((edge_weights, weights), (edge_cells, cells), (edge_codes, codes)):
        for index in np.ndindex(*source.shape[:-2]):
            target[index + (slice(0, 3), slice(None))] = source[index + (slice(0, 3), slice(None))]
            target[index + (slice(3, 8), slice(None))] = source[index + (slice(width - 5, width), slice(None))]
    fill_stencil(
        recon, edge_weights, edge_cells, edge_codes, turned, spread, edge_stencil, 1, copies[0].wait
    )
    copies[4].wait()
    even = is_even(ROW_AXES)
    for send, low_edge in ((send_a, jnp.logical_not(even)), (send_b, even)):
        mass_at = jnp.where(low_edge, 0, width - 6)
        stencil_at = jnp.where(low_edge, 0, 5)
        for s in range(stacks):
            send[6 * s : 6 * s + 6, :] = mass[s, pl.ds(mass_at, 6), :]
        for o in range(OFFSETS):
            at = 6 * stacks + 3 * o
            send[at : at + 3, :] = edge_stencil[o, pl.ds(stencil_at, 3), :]


def coefficients(recon_hbm, weights, cells, codes, stencil, recon, turned, spread, sem):
    copy = pltpu.make_async_copy(recon_hbm, recon, sem.at[0])
    copy.start()
    fill_stencil(recon, weights, cells, codes, turned, spread, stencil, stencil.shape[1] // 8, copy.wait)


def pack_stacks(load, stacks, tile):
    lane = lanes()
    left = jnp.zeros((8, 128), F32)
    right = jnp.zeros((8, 128), F32)
    for s in range(PER * tile, min(stacks, PER * tile + PER)):
        at = SPAN * (s % PER)
        moved = turn(load(s), at - 122)
        right = jnp.where(lane >= at, moved, right)
        left = jnp.where(from_place(lane, at + 6, at + 12), moved, left)
    return turn(left, -3), right


def from_place(lane, low, high):
    return (lane >= low) | (lane < high - 128) if high > 128 else lane >= low


def pack_coefficients(load):
    lane = lanes()
    left = jnp.zeros((8, 128), F32)
    right = jnp.zeros((8, 128), F32)
    for o in range(COEF_PER):
        at = 3 * o
        moved = turn(load(o), at - 125)
        right = jnp.where(lane >= at, moved, right)
        left = jnp.where(from_place(lane, at + 3, at + 6), moved, left)
    return turn(left, -3), right


def add_spare(load, left, right):
    lane = lanes()
    for o in range(COEF_PER, OFFSETS):
        at = SPAN * (o - COEF_PER)
        value = load(o)
        left = jnp.where((lane >= at) & (lane < at + 3), turn(value, at), left)
        right = jnp.where((lane >= at + 6) & (lane < at + 9), turn(value, at - 119), right)
    return left, right


def fill_near(near):
    lane = lanes(1)
    group = (lane * 57) >> 9
    at = lane - SPAN * group
    source = lax.broadcasted_iota(jnp.int32, (128, 128), 0)
    for dy in range(-3, 4):
        q = at - dy
        right = jnp.where((at >= 3) & (q >= 0) & (q < 6), 122 + q, -1)
        left = jnp.where((at < 6) & (q >= 3) & (q < 9), q - 3, -1)
        for side, wanted in enumerate((right, left)):
            wanted = jnp.where(group < PER, wanted, -1)
            picked = jnp.where(source == wanted, 1.0, 0.0).astype(jnp.bfloat16)
            near[dy + 3, 0:128, 128 * side : 128 * side + 128] = picked
            near[dy + 3, 128:256, 128 * side : 128 * side + 128] = picked


def replicate(value, picks):
    high = value.astype(jnp.bfloat16)
    low = (value - high.astype(F32)).astype(jnp.bfloat16)
    return jnp.dot(jnp.concatenate([high, low], axis=1), picks, preferred_element_type=F32)


def fill_picks(picks):
    lane = lanes(1)
    group = (lane * 57) >> 9
    at = lane - SPAN * group
    source = lax.broadcasted_iota(jnp.int32, (128, 128), 0)
    for dy in range(-3, 4):
        q = at - dy
        halo = (q >= 3) & (q < 6)
        right = jnp.where(halo, 57 + q, jnp.where((q >= 0) & (q < 3) & (at >= 3), 125 + q, -1))
        left = jnp.where(halo, 61 + q, jnp.where((q >= 6) & (q < 9) & (at < 6), q - 6, -1))
        for side, wanted in enumerate((right, left)):
            wanted = jnp.where(group < PER, wanted, -1)
            picked = jnp.where(source == wanted, 1.0, 0.0).astype(jnp.bfloat16)
            picks[dy + 3, 0:128, 128 * side : 128 * side + 128] = picked
            picks[dy + 3, 128:256, 128 * side : 128 * side + 128] = picked


def pack_own(mass, stencil, left, right, picks, near):
    fill_picks(picks)
    fill_near(near)
    stacks, width = mass.shape[:2]
    tiles = -(-stacks // PER)
    for half in range(width // 8):
        rows = pl.ds(8 * half, 8)
        for tile in range(tiles):
            at = width * tile + 8 * half
            values = pack_stacks(lambda s: mass[s, rows, :], stacks, tile)
            if tile == 0:
                values = add_spare(lambda o: stencil[o, rows, :], *values)
            left[at : at + 8, :], right[at : at + 8, :] = values
        at = width * tiles + 8 * half
        left[at : at + 8, :], right[at : at + 8, :] = pack_coefficients(lambda o: stencil[o, rows, :])


def pack_all(stacks, own_left, own_right, above, below, middle, send_a, send_b, left, right):
    tiles = -(-stacks // PER)
    width = own_left.shape[0] // (tiles + 1)
    tall = width + 12
    first, last = ends(ROW_AXES)
    top_rows = lax.broadcasted_iota(jnp.int32, (8, 128), 0) < 3
    ready = []
    for got, outside, place, coef_place in (
        (above, first, width, width), (below, last, width + 6, width + 3)
    ):
        coef = lambda o: got[6 * stacks + 3 * o : 6 * stacks + 3 * o + 8, :]
        for tile in range(tiles):
            packed = pack_stacks(lambda s: got[6 * s : 6 * s + 8, :], stacks, tile)
            if tile == 0:
                spare = add_spare(coef, *packed)
                packed = [jnp.where(top_rows, new, old) for new, old in zip(spare, packed)]
            ready.append((tall * tile + place, 6, outside, packed))
        ready.append((tall * tiles + coef_place, 3, outside, pack_coefficients(coef)))
    for at, count, outside, packed in ready:
        for send, value in zip((left, right), packed):
            send[at : at + count, :] = jnp.where(outside, 0.0, value[0:count])
    for send, own in ((left, own_left), (right, own_right)):
        for tile in range(tiles + 1):
            send[tall * tile : tall * tile + width, :] = own[width * tile : width * tile + width, :]
        end = tall * tiles + width + 6
        send[end:, :] = jnp.zeros((send.shape[0] - end, 128), F32)
    choose(is_even(COLUMN_AXES), right, left, send_a, send_b)


def choose(even, first, second, first_out, second_out):
    @pl.when(even)
    def _():
        first_out[...] = first[...]
        second_out[...] = second[...]

    @pl.when(jnp.logical_not(even))
    def _():
        first_out[...] = second[...]
        second_out[...] = first[...]


def main_sum(load, coef, coef_at, tile):
    fields = [[load(k, 8 * tile + dx) for k in range(GROUP)] for dx in range(7)]
    total = [None] * GROUP
    for dy in range(7):
        part = [None] * GROUP
        for dx in range(7):
            at = coef_at + 8 * tile
            scale = coef[dx * 7 + dy, at : at + 8, :]
            for k in range(GROUP):
                term = scale * fields[dx][k]
                part[k] = term if dx == 0 else part[k] + term
        for k in range(GROUP):
            moved = turn(part[k], 3 - dy)
            total[k] = moved if dy == 0 else total[k] + moved
    return total


def shift_rows(load, store):
    lane = lanes()
    values = []
    for o in range(OFFSETS):
        dy = o % 7 - 3
        value = turn(load(o), dy)
        if dy > 0:
            value = jnp.where(lane >= dy, value, 0.0)
        elif dy < 0:
            value = jnp.where(lane < 128 + dy, value, 0.0)
        values.append(value)
    for o, value in enumerate(values):
        store(o, value)


def own_part(mass, stencil, near, middle, own_shifted, right_near, left_near):
    stacks, width = mass.shape[:2]
    for tile in range(width // 8):
        rows = pl.ds(8 * tile, 8)

        def store(o, value):
            own_shifted[o, rows, :] = value

        shift_rows(lambda o: stencil[o, rows, :], store)

    def some_stacks(turn_at, carry):
        for_groups(
            turn_at, stacks, range((width - 8) // 8), own_shifted, 5,
            lambda s, tile, at: mass[s, 2 + at : 10 + at, :],
            lambda s, tile, value: store_rows(middle, s, 8 * tile, value),
        )
        return carry

    lax.fori_loop(0, turns(stacks), some_stacks, 0)
    for dy in range(7):
        value = jnp.concatenate([stencil[dx * 7 + dy, :, :] for dx in range(7)], axis=0)
        spread = replicate(value, near[dy])
        for dx in range(7):
            right_near[dx * 7 + dy, :, :] = spread[width * dx : width * dx + width, 0:128]
            left_near[dx * 7 + dy, :, :] = spread[width * dx : width * dx + width, 128:256]


def both_steps(mass, stencil, above, below, middle, own_shifted, second, wide, shifted, field, partial):
    stacks, width = mass.shape[:2]
    first, last = ends(ROW_AXES)
    coefs = 6 * stacks
    for s in range(stacks):
        field[0, s, 2:8, :] = above[6 * s : 6 * s + 6, :]
        field[0, s, 8:16, :] = mass[s, 0:8, :]
        field[1, s, 0:8, :] = mass[s, width - 8 : width, :]
        field[1, s, 8:16, :] = below[6 * s : 6 * s + 8, :]
    for o in range(OFFSETS):
        at = coefs + 3 * o
        wide[o, 0:3, :] = above[at : at + 3, :]
        wide[o, 3 : width + 3, :] = stencil[o, :, :]
        wide[o, width + 3 : width + 6, :] = below[at : at + 3, :]
        wide[o, width + 6 : width + 8, :] = jnp.zeros((2, 128), F32)

    @pl.when(first)
    def _():
        for s in range(stacks):
            field[0, s, 2:8, :] = jnp.zeros((6, 128), F32)
        for o in range(OFFSETS):
            wide[o, 0:3, :] = jnp.zeros((3, 128), F32)

    @pl.when(last)
    def _():
        for s in range(stacks):
            field[1, s, 8:16, :] = jnp.zeros((8, 128), F32)
        for o in range(OFFSETS):
            wide[o, width + 3 : width + 6, :] = jnp.zeros((3, 128), F32)

    for end, tile in enumerate((0, width // 8)):
        rows = pl.ds(8 * tile, 8)

        def store(o, value):
            shifted[end, o, :, :] = value

        shift_rows(lambda o: wide[o, rows, :], store)

    def first_step(turn_at, carry):
        sums = [
            for_groups(
                turn_at, stacks, (0,), shifted.at[end], 0, lambda s, tile, at: field[end, s, 2 + at : 10 + at, :]
            )
            for end in range(2)
        ]
        for end, tile in enumerate((0, width // 8)):
            for s, _, value in sums[end]:
                store_rows(partial, s, 8 * tile, value)
        for s, _, _ in sums[0]:
            partial[s, 8:width, :] = middle[s, :, :]
        return carry

    lax.fori_loop(0, turns(stacks), first_step, 0)

    def second_step(turn_at, carry):
        for_groups(
            turn_at, stacks, range(width // 8), own_shifted, 0,
            lambda s, tile, at: partial[s, at : at + 8, :],
            lambda s, tile, value: store_rows(second, s, 8 * tile, value),
        )
        return carry

    lax.fori_loop(0, turns(stacks), second_step, 0)


def store_rows(target, s, at, value):
    target[s, at : at + 8, :] = value


def per_turn(stacks):
    return next(GROUP * groups for groups in (10, 5, 2, 1) if stacks % (GROUP * groups) == 0)


def turns(stacks):
    return stacks // per_turn(stacks)


def for_groups(turn_at, stacks, tiles, coef, coef_at, load, store=None):
    sums = []
    for part in range(per_turn(stacks) // GROUP):
        start = turn_at * per_turn(stacks) + part * GROUP
        for tile in tiles:
            total = main_sum(lambda k, at: load(start + k, tile, at), coef, coef_at, tile)
            sums += [(start + k, tile, total[k]) for k in range(GROUP)]
    if store is not None:
        for s, tile, value in sums:
            store(s, tile, value)
    return sums


def take_first(got, after, out):
    out[...] = got[...]


def in_order(got_a, got_b, above, below):
    choose(is_even(ROW_AXES), got_b, got_a, above, below)


def packed_sum(load, coef, coef_at, tile, tiles, dys):
    fields = [[load(t, 8 * tile + dx) for t in range(tiles)] for dx in range(7)]
    total = [None] * tiles
    for dy in dys:
        part = [None] * tiles
        for dx in range(7):
            at = coef_at + 8 * tile
            scale = coef[dx * 7 + dy + 3, at : at + 8, :]
            for t in range(tiles):
                term = scale * fields[dx][t]
                part[t] = term if dx == 0 else part[t] + term
        for t in range(tiles):
            moved = turn(part[t], -dy)
            total[t] = moved if total[t] is None else total[t] + moved
    return total


def place_in_group(rows=8):
    lane = lanes(rows)
    return lane - SPAN * ((lane * 57) >> 9)


def side_coefficients(
    wide, send_a, send_b, got_b, got_a, picks,
    right_set, left_set, right_coef, left_coef, right_halo, left_halo, rows_of,
):
    tall = wide.shape[1]
    width = tall - 8
    tiles = right_set.shape[0]
    lane = lanes()

    first, last = ends(COLUMN_AXES)

    def gather(sent_right, sent_left, got_right, got_left):
        part = width + 12
        place = place_in_group(part)
        rows = [slice(part * tile, part * tile + part) for tile in range(tiles)]
        from_right = [jnp.where(last, 0.0, got_right[at, :]) for at in rows]
        from_left = [jnp.where(first, 0.0, got_left[at, :]) for at in rows]
        for tile, at in enumerate(rows):
            right = jnp.where(place < 3, turn(sent_right[at, :], -3), from_right[tile])
            left = jnp.where(place >= 6, turn(sent_left[at, :], 3), from_left[tile])
            for target, value in ((right_set, right), (left_set, left)):
                target[tile, 6 : width + 6, :] = value[0:width]
                target[tile, 0:6, :] = value[width : width + 6]
                target[tile, width + 6 : width + 12, :] = value[width + 6 : width + 12]
                target[tile, width + 12 : width + 16, :] = jnp.zeros((4, 128), F32)
        coefs = slice(part * tiles, part * tiles + width + 6)
        for target, source, got, outside in (
            (right_halo, from_right, got_right, last), (left_halo, from_left, got_left, first)
        ):
            value = jnp.where(outside, 0.0, got[coefs, :])
            spare = source[0]
            for tile, own, above, below in (
                (0, value[0:width], value[width : width + 3], value[width + 3 : width + 6]),
                (1, spare[0:width], spare[width : width + 3], spare[width + 6 : width + 9]),
            ):
                target[tile, 3 : width + 3, :] = own
                target[tile, 0:3, :] = above
                target[tile, width + 3 : width + 6, :] = below
                target[tile, width + 6 : width + 8, :] = jnp.zeros((2, 128), F32)

    even = is_even(COLUMN_AXES)

    @pl.when(even)
    def _():
        gather(send_a, send_b, got_a, got_b)

    @pl.when(jnp.logical_not(even))
    def _():
        gather(send_b, send_a, got_b, got_a)

    from_right = (lane >= 60) & (lane < 63)
    from_left = (lane >= 64) & (lane < 67)
    for tile in range(tall // 8):
        rows = pl.ds(8 * tile, 8)
        right_rows = [right_halo[t, rows, :] for t in range(2)]
        left_rows = [left_halo[t, rows, :] for t in range(2)]
        values = []
        for o in range(OFFSETS):
            if o < COEF_PER:
                right = turn(right_rows[0], 60 - 3 * o)
                left = turn(left_rows[0], 64 - 3 * o)
            else:
                at = SPAN * (o - COEF_PER)
                right = turn(right_rows[1], 60 - at)
                left = turn(left_rows[1], 58 - at)
            values.append(jnp.where(from_right, right, jnp.where(from_left, left, wide[o, rows, :])))
        for o, value in enumerate(values):
            at = tall * (o // 7) + 8 * tile
            rows_of[o % 7, at : at + 8, :] = value

    for dy in range(7):
        spread = replicate(rows_of[dy], picks[dy])
        for dx in range(7):
            right_coef[dx * 7 + dy, :, :] = spread[tall * dx : tall * dx + tall, 0:128]
            left_coef[dx * 7 + dy, :, :] = spread[tall * dx : tall * dx + tall, 128:256]


def halo_steps(
    right_set, left_set, right_coef, left_coef, right_near, left_near, second, out_hbm,
    right_next, left_next, out, sems,
):
    tiles = right_set.shape[0]
    stacks, width = out.shape[:2]
    place = place_in_group()
    everywhere = range(-3, 4)
    row_tiles = range(right_next.shape[1] // 8)
    sums = [
        [
            packed_sum(lambda t, at: side[t, at : at + 8, :], coef, 0, tile, tiles, everywhere)
            for side, coef in ((right_set, right_coef), (left_set, left_coef))
        ]
        for tile in row_tiles
    ]
    for tile in row_tiles:
        right, left = sums[tile]
        rows = pl.ds(8 * tile, 8)
        for t in range(tiles):
            right_next[t, rows, :] = jnp.where(place >= 3, turn(right[t], 3), 0.0)
            left_next[t, rows, :] = jnp.where(place < 6, turn(left[t], -3), 0.0)
    changes = [
        [
            packed_sum(lambda t, at: side[t, at : at + 8, :], coef, 0, tile, tiles, everywhere)
            for side, coef in ((right_next, right_near), (left_next, left_near))
        ]
        for tile in range(width // 8)
    ]

    lane = lanes()
    copies = []
    for t in range(tiles):
        low, high = PER * t, min(stacks, PER * t + PER)
        for tile in range(width // 8):
            rows = pl.ds(8 * tile, 8)
            right, left = (side[t] for side in changes[tile])
            values = []
            for s in range(low, high):
                at = SPAN * (s - low)
                change = jnp.where(lane < 6, turn(left, -at - 3), 0.0)
                change = jnp.where(lane >= 122, turn(right, 122 - at), change)
                values.append(second[s, rows, :] + change)
            for s, value in zip(range(low, high), values):
                out[s, rows, :] = value
        piece = pl.ds(low, high - low)
        copies.append(pltpu.make_async_copy(out.at[piece], out_hbm.at[piece], sems.at[t]))
        copies[-1].start()
    for copy in copies:
        copy.wait()


def local(tracer_mass, recon_table, intersection_weights, intersection_cells, rotation_codes):
    stacks, width, columns = tracer_mass.shape
    shape = lambda *sizes: jax.ShapeDtypeStruct(sizes, F32)
    scratch = lambda *sizes: pltpu.VMEM(sizes, F32)
    tiles = -(-stacks // PER)
    combos = 4 * (width // 8)
    tall, low = width + 16, width + 8
    fixed = lambda *values: [pltpu.with_memory_space_constraint(value, pltpu.HBM) for value in values]
    whole = lambda value: jax.ShapeDtypeStruct(value.shape, value.dtype)
    edge = -(-(6 * stacks + 3 * OFFSETS + 5) // 8) * 8
    integers = lambda *sizes: pltpu.VMEM(sizes, jnp.int32)
    picks = jax.ShapeDtypeStruct((7, 256, 256), jnp.bfloat16)
    regions = intersection_cells.shape[0]

    mass, weights, cells, codes, send_a, send_b = pl.pallas_call(
        edge_rows,
        out_shape=(
            whole(tracer_mass), whole(intersection_weights), whole(intersection_cells),
            whole(rotation_codes), shape(edge, 128), shape(edge, 128),
        ),
        in_specs=[HBM] * 5,
        out_specs=(VMEM,) * 6,
        scratch_shapes=[
            pltpu.SMEM(recon_table.shape, F32),
            scratch(regions, TERMS, 8, 128),
            integers(regions, 8, 128),
            integers(regions, 8, 128),
            scratch(OFFSETS, 8, 128),
            scratch(TERMS, regions, 8, 128),
            scratch(25, regions, 8, 128),
            pltpu.SemaphoreType.DMA((5,)),
        ],
        compiler_params=params(),
        cost_estimate=cost(4 * 10**6),
        name="edge_rows",
    )(*fixed(recon_table, tracer_mass, intersection_weights, intersection_cells, rotation_codes))
    got_b = row_swap(send_b, True)
    got_a = row_swap(send_a, False)

    stencil = pl.pallas_call(
        coefficients,
        out_shape=shape(OFFSETS, width, 128),
        in_specs=[HBM] + [VMEM] * 3,
        out_specs=VMEM,
        scratch_shapes=[
            pltpu.SMEM(recon_table.shape, F32),
            scratch(TERMS, combos, 8, 128),
            scratch(25, combos, 8, 128),
            pltpu.SemaphoreType.DMA((1,)),
        ],
        compiler_params=params(),
        cost_estimate=cost(8 * 10**6),
        name="coefficients",
    )(*fixed(recon_table), weights, cells, codes)

    own_left, own_right, picks, near = pl.pallas_call(
        pack_own,
        out_shape=(shape(width * (tiles + 1), 128),) * 2 + (picks, picks),
        in_specs=[VMEM] * 2,
        out_specs=(VMEM,) * 4,
        compiler_params=params(),
        cost_estimate=cost(10**6),
        name="pack_own",
    )(mass, stencil)

    middle, own_shifted, right_near, left_near = pl.pallas_call(
        own_part,
        out_shape=(shape(stacks, width - 8, 128),) + (shape(OFFSETS, width, 128),) * 3,
        in_specs=[VMEM] * 3,
        out_specs=(VMEM,) * 4,
        compiler_params=params(),
        cost_estimate=cost(4 * 10**6),
        name="own_part",
    )(mass, stencil, near)

    got_b = pl.pallas_call(
        take_first,
        out_shape=shape(edge, 128),
        in_specs=[VMEM, ANY],
        out_specs=VMEM,
        compiler_params=params(),
        cost_estimate=cost(10**4),
        name="take_first",
    )(got_b, middle)
    above, below = pl.pallas_call(
        in_order,
        out_shape=(shape(edge, 128),) * 2,
        in_specs=[VMEM] * 2,
        out_specs=(VMEM,) * 2,
        compiler_params=params(),
        cost_estimate=cost(10**4),
        name="in_order",
    )(got_a, got_b)

    send = ((width + 12) * (tiles + 1), 128)
    send_a, send_b = pl.pallas_call(
        functools.partial(pack_all, stacks),
        out_shape=(shape(*send),) * 2,
        in_specs=[VMEM] * 4 + [ANY],
        out_specs=(VMEM,) * 2,
        scratch_shapes=[scratch(*send)] * 2,
        compiler_params=params(),
        cost_estimate=cost(10**6),
        name="pack_all",
    )(own_left, own_right, above, below, middle)
    column_b = column_swap(send_b, True)
    column_a = column_swap(send_a, False)

    second, wide = pl.pallas_call(
        both_steps,
        out_shape=(shape(stacks, width, 128), shape(OFFSETS, low, 128)),
        in_specs=[VMEM] * 6,
        out_specs=(VMEM,) * 2,
        scratch_shapes=[scratch(2, OFFSETS, 8, 128), scratch(2, stacks, 16, 128), scratch(stacks, low, 128)],
        compiler_params=params(),
        cost_estimate=cost(12 * 10**6),
        name="both_steps",
    )(mass, stencil, above, below, middle, own_shifted)

    sides = pl.pallas_call(
        side_coefficients,
        out_shape=(shape(tiles, tall, 128),) * 2 + (shape(OFFSETS, low, 128),) * 2,
        in_specs=[VMEM] * 6,
        out_specs=(VMEM,) * 4,
        scratch_shapes=[scratch(2, low, 128)] * 2 + [scratch(7, 7 * low, 128)],
        compiler_params=params(),
        cost_estimate=cost(4 * 10**6),
        name="side_coefficients",
    )(wide, send_a, send_b, column_b, column_a, picks)

    return pl.pallas_call(
        halo_steps,
        out_shape=shape(stacks, width, columns),
        in_specs=[VMEM] * 7,
        out_specs=HBM,
        scratch_shapes=[scratch(tiles, low, 128)] * 2
        + [scratch(stacks, width, columns), pltpu.SemaphoreType.DMA((tiles,))],
        compiler_params=params(),
        cost_estimate=cost(4 * 10**6),
        name="halo_steps",
    )(*sides, right_near, left_near, second)


def solution(mesh):
    in_specs = (
        P(None, ("face", "px"), "py"),
        P(),
        P(None, None, ("face", "px"), "py"),
        P(None, ("face", "px"), "py"),
        P(None, ("face", "px"), "py"),
    )
    out_specs = P(None, ("face", "px"), "py")
    return jax.shard_map(local, mesh=mesh, in_specs=in_specs, out_specs=out_specs, check_vma=False)
```

```python
import functools

import jax
import jax.numpy as jnp
import numpy as np
from jax import lax
from jax.experimental import pallas as pl
from jax.experimental.pallas import tpu as pltpu
from jax.sharding import PartitionSpec as P

F32 = jnp.float32
ROW_AXES = ("face", "px")
COLUMN_AXES = "py"
SWAPPED = (0, 2, 1, 5, 4, 3, 9, 8, 7, 6)
POWERS = ((0, 0), (1, 0), (0, 1), (2, 0), (1, 1), (0, 2), (3, 0), (2, 1), (1, 2), (0, 3))
TERMS = 10
OFFSETS = 49
GROUP = 4
SPAN = 9
PER = 14
COEF_PER = 42
VMEM = pl.BlockSpec(memory_space=pltpu.VMEM)
ANY = pl.BlockSpec(memory_space=pl.ANY)
HBM = pl.BlockSpec(memory_space=pltpu.HBM)


def params():
    return pltpu.CompilerParams(vmem_limit_bytes=40 * 1024 * 1024)


def cost(operations):
    return pl.CostEstimate(flops=operations, bytes_accessed=1 << 20, transcendentals=0)


def column_swap(block, odd_first):
    chains, count = lax.axis_size(ROW_AXES), lax.axis_size(COLUMN_AXES)
    column = list(range(count))
    for low in range(1 if odd_first else 0, count - 1, 2):
        column[low], column[low + 1] = low + 1, low
    pairs = []
    for chain in range(chains):
        for place in range(count):
            target = (chain, column[place])
            if column[place] == place and chains % 2 == 0:
                target = (chain ^ 1, place)
            pairs.append((chain * count + place, target[0] * count + target[1]))
    return lax.ppermute(block, ROW_AXES + (COLUMN_AXES,), pairs)


def row_swap(block, odd_first):
    chains, count = lax.axis_size(ROW_AXES), lax.axis_size(COLUMN_AXES)
    chain_of = list(range(chains))
    for low in range(1 if odd_first else 0, chains - 1, 2):
        chain_of[low], chain_of[low + 1] = low + 1, low
    pairs = []
    for chain in range(chains):
        for place in range(count):
            target = (chain_of[chain], place)
            if chain_of[chain] == chain and count % 2 == 0:
                target = (chain, place ^ 1)
            pairs.append((chain * count + place, target[0] * count + target[1]))
    return lax.ppermute(block, ROW_AXES + (COLUMN_AXES,), pairs)


def ends(axes):
    index = lax.axis_index(axes)
    return index == 0, index == lax.axis_size(axes) - 1


def is_even(axes):
    return lax.rem(lax.axis_index(axes), 2) == 0


def turn(value, amount):
    amount %= 128
    return pltpu.roll(value, amount, 1) if amount else value


def lanes(rows=8):
    return lax.broadcasted_iota(jnp.int32, (rows, 128), 1)


def fill_stencil(recon, weights, cells, codes, turned, spread, stencil, tiles, before_taps):
    zero = jnp.zeros((8, 128), F32)
    for g in range(tiles):
        rows = pl.ds(8 * g, 8)
        for m in range(4):
            code = codes[m, rows, :]
            odd = (code & 1) == 1
            sign_x = jnp.where(code >= 2, -1.0, 1.0).astype(F32)
            sign_y = jnp.where((code == 1) | (code == 2), -1.0, 1.0).astype(F32)
            sign_xy = sign_x * sign_y
            values = [weights[m, t, rows, :] for t in range(TERMS)]
            for t, (a, b) in enumerate(POWERS):
                value = values[t]
                if SWAPPED[t] != t:
                    value = jnp.where(odd, values[SWAPPED[t]], value)
                if a % 2 and b % 2:
                    value = value * sign_xy
                elif a % 2:
                    value = value * sign_x
                elif b % 2:
                    value = value * sign_y
                turned[t, m * tiles + g] = value

    combos = 4 * tiles
    before_taps()

    def five_taps(jx, carry):
        total = [[None] * combos for jy in range(5)]
        for t in range(TERMS):
            values = [turned[t, c] for c in range(combos)]
            for jy in range(5):
                scale = recon[t, 5 * jx + jy]
                for c in range(combos):
                    term = values[c] * scale
                    total[jy][c] = term if t == 0 else total[jy][c] + term
        for jy in range(5):
            for c in range(combos):
                spread[5 * jx + jy, c] = total[jy][c]
        return carry

    for jx in range(5):
        five_taps(jx, 0)

    for g in range(tiles):
        rows = pl.ds(8 * g, 8)
        masks = []
        for m in range(4):
            cell = cells[m, rows, :]
            first = jnp.where(cell < 3, 0, jnp.where(cell < 6, 3, 6))
            across = cell - first
            masks.append((cell < 3, cell < 6, across == 0, across <= 1))
        for ox in range(7):
            total = [None] * 7
            for m in range(4):
                low_x, mid_x, low_y, mid_y = masks[m]

                def tap(jx, jy):
                    if 0 <= jx < 5 and 0 <= jy < 5:
                        return spread[jx * 5 + jy, m * tiles + g]
                    return zero

                line = [
                    jnp.where(low_x, tap(ox, jy), jnp.where(mid_x, tap(ox - 1, jy), tap(ox - 2, jy)))
                    for jy in range(5)
                ]
                padded = [zero, zero] + line + [zero, zero]
                for oy in range(7):
                    value = jnp.where(
                        low_y, padded[oy + 2], jnp.where(mid_y, padded[oy + 1], padded[oy])
                    )
                    total[oy] = value if m == 0 else total[oy] + value
            for oy in range(7):
                stencil[ox * 7 + oy, rows, :] = total[oy]


def edge_rows(
    recon_hbm, mass_hbm, weights_hbm, cells_hbm, codes_hbm,
    mass, weights, cells, codes, send_a, send_b,
    recon, edge_weights, edge_cells, edge_codes, edge_stencil, turned, spread, sems,
):
    sources = (recon_hbm, codes_hbm, weights_hbm, cells_hbm, mass_hbm)
    targets = (recon, codes, weights, cells, mass)
    copies = [pltpu.make_async_copy(a, b, sems.at[i]) for i, (a, b) in enumerate(zip(sources, targets))]
    for copy in copies:
        copy.start()
    for copy in copies[1:4]:
        copy.wait()
    stacks, width = mass.shape[:2]
    for target, source in ((edge_weights, weights), (edge_cells, cells), (edge_codes, codes)):
        for index in np.ndindex(*source.shape[:-2]):
            target[index + (slice(0, 3), slice(None))] = source[index + (slice(0, 3), slice(None))]
            target[index + (slice(3, 8), slice(None))] = source[index + (slice(width - 5, width), slice(None))]
    fill_stencil(
        recon, edge_weights, edge_cells, edge_codes, turned, spread, edge_stencil, 1, copies[0].wait
    )
    copies[4].wait()
    even = is_even(ROW_AXES)
    for send, low_edge in ((send_a, jnp.logical_not(even)), (send_b, even)):
        mass_at = jnp.where(low_edge, 0, width - 6)
        stencil_at = jnp.where(low_edge, 0, 5)
        for s in range(stacks):
            send[6 * s : 6 * s + 6, :] = mass[s, pl.ds(mass_at, 6), :]
        for o in range(OFFSETS):
            at = 6 * stacks + 3 * o
            send[at : at + 3, :] = edge_stencil[o, pl.ds(stencil_at, 3), :]


def coefficients(recon_hbm, weights, cells, codes, stencil, recon, turned, spread, sem):
    copy = pltpu.make_async_copy(recon_hbm, recon, sem.at[0])
    copy.start()
    fill_stencil(recon, weights, cells, codes, turned, spread, stencil, stencil.shape[1] // 8, copy.wait)


def pack_stacks(load, stacks, tile):
    lane = lanes()
    left = jnp.zeros((8, 128), F32)
    right = jnp.zeros((8, 128), F32)
    for s in range(PER * tile, min(stacks, PER * tile + PER)):
        at = SPAN * (s % PER)
        moved = turn(load(s), at - 122)
        right = jnp.where(lane >= at, moved, right)
        left = jnp.where(from_place(lane, at + 6, at + 12), moved, left)
    return turn(left, -3), right


def from_place(lane, low, high):
    return (lane >= low) | (lane < high - 128) if high > 128 else lane >= low


def pack_coefficients(load):
    lane = lanes()
    left = jnp.zeros((8, 128), F32)
    right = jnp.zeros((8, 128), F32)
    for o in range(COEF_PER):
        at = 3 * o
        moved = turn(load(o), at - 125)
        right = jnp.where(lane >= at, moved, right)
        left = jnp.where(from_place(lane, at + 3, at + 6), moved, left)
    return turn(left, -3), right


def add_spare(load, left, right):
    lane = lanes()
    for o in range(COEF_PER, OFFSETS):
        at = SPAN * (o - COEF_PER)
        value = load(o)
        left = jnp.where((lane >= at) & (lane < at + 3), turn(value, at), left)
        right = jnp.where((lane >= at + 6) & (lane < at + 9), turn(value, at - 119), right)
    return left, right


def fill_near(near):
    lane = lanes(1)
    group = (lane * 57) >> 9
    at = lane - SPAN * group
    source = lax.broadcasted_iota(jnp.int32, (128, 128), 0)
    for dy in range(-3, 4):
        q = at - dy
        right = jnp.where((at >= 3) & (q >= 0) & (q < 6), 122 + q, -1)
        left = jnp.where((at < 6) & (q >= 3) & (q < 9), q - 3, -1)
        for side, wanted in enumerate((right, left)):
            wanted = jnp.where(group < PER, wanted, -1)
            picked = jnp.where(source == wanted, 1.0, 0.0).astype(jnp.bfloat16)
            near[dy + 3, 0:128, 128 * side : 128 * side + 128] = picked
            near[dy + 3, 128:256, 128 * side : 128 * side + 128] = picked


def replicate(value, picks):
    high = value.astype(jnp.bfloat16)
    low = (value - high.astype(F32)).astype(jnp.bfloat16)
    return jnp.dot(jnp.concatenate([high, low], axis=1), picks, preferred_element_type=F32)


def fill_picks(picks):
    lane = lanes(1)
    group = (lane * 57) >> 9
    at = lane - SPAN * group
    source = lax.broadcasted_iota(jnp.int32, (128, 128), 0)
    for dy in range(-3, 4):
        q = at - dy
        halo = (q >= 3) & (q < 6)
        right = jnp.where(halo, 57 + q, jnp.where((q >= 0) & (q < 3) & (at >= 3), 125 + q, -1))
        left = jnp.where(halo, 61 + q, jnp.where((q >= 6) & (q < 9) & (at < 6), q - 6, -1))
        for side, wanted in enumerate((right, left)):
            wanted = jnp.where(group < PER, wanted, -1)
            picked = jnp.where(source == wanted, 1.0, 0.0).astype(jnp.bfloat16)
            picks[dy + 3, 0:128, 128 * side : 128 * side + 128] = picked
            picks[dy + 3, 128:256, 128 * side : 128 * side + 128] = picked


def pack_own(mass, stencil, left, right, picks, near):
    fill_picks(picks)
    fill_near(near)
    stacks, width = mass.shape[:2]
    tiles = -(-stacks // PER)
    for half in range(width // 8):
        rows = pl.ds(8 * half, 8)
        for tile in range(tiles):
            at = width * tile + 8 * half
            values = pack_stacks(lambda s: mass[s, rows, :], stacks, tile)
            if tile == 0:
                values = add_spare(lambda o: stencil[o, rows, :], *values)
            left[at : at + 8, :], right[at : at + 8, :] = values
        at = width * tiles + 8 * half
        left[at : at + 8, :], right[at : at + 8, :] = pack_coefficients(lambda o: stencil[o, rows, :])


def pack_all(stacks, own_left, own_right, above, below, middle, send_a, send_b, left, right):
    tiles = -(-stacks // PER)
    width = own_left.shape[0] // (tiles + 1)
    tall = width + 12
    first, last = ends(ROW_AXES)
    top_rows = lax.broadcasted_iota(jnp.int32, (8, 128), 0) < 3
    ready = []
    for got, outside, place, coef_place in (
        (above, first, width, width), (below, last, width + 6, width + 3)
    ):
        coef = lambda o: got[6 * stacks + 3 * o : 6 * stacks + 3 * o + 8, :]
        for tile in range(tiles):
            packed = pack_stacks(lambda s: got[6 * s : 6 * s + 8, :], stacks, tile)
            if tile == 0:
                spare = add_spare(coef, *packed)
                packed = [jnp.where(top_rows, new, old) for new, old in zip(spare, packed)]
            ready.append((tall * tile + place, 6, outside, packed))
        ready.append((tall * tiles + coef_place, 3, outside, pack_coefficients(coef)))
    for at, count, outside, packed in ready:
        for send, value in zip((left, right), packed):
            send[at : at + count, :] = jnp.where(outside, 0.0, value[0:count])
    for send, own in ((left, own_left), (right, own_right)):
        for tile in range(tiles + 1):
            send[tall * tile : tall * tile + width, :] = own[width * tile : width * tile + width, :]
        end = tall * tiles + width + 6
        send[end:, :] = jnp.zeros((send.shape[0] - end, 128), F32)
    choose(is_even(COLUMN_AXES), right, left, send_a, send_b)


def choose(even, first, second, first_out, second_out):
    @pl.when(even)
    def _():
        first_out[...] = first[...]
        second_out[...] = second[...]

    @pl.when(jnp.logical_not(even))
    def _():
        first_out[...] = second[...]
        second_out[...] = first[...]


def main_sum(load, coef, coef_at, tile):
    fields = [[load(k, 8 * tile + dx) for k in range(GROUP)] for dx in range(7)]
    total = [None] * GROUP
    for dy in range(7):
        part = [None] * GROUP
        for dx in range(7):
            at = coef_at + 8 * tile
            scale = coef[dx * 7 + dy, at : at + 8, :]
            for k in range(GROUP):
                term = scale * fields[dx][k]
                part[k] = term if dx == 0 else part[k] + term
        for k in range(GROUP):
            moved = turn(part[k], 3 - dy)
            total[k] = moved if dy == 0 else total[k] + moved
    return total


def shift_rows(load, store):
    lane = lanes()
    values = []
    for o in range(OFFSETS):
        dy = o % 7 - 3
        value = turn(load(o), dy)
        if dy > 0:
            value = jnp.where(lane >= dy, value, 0.0)
        elif dy < 0:
            value = jnp.where(lane < 128 + dy, value, 0.0)
        values.append(value)
    for o, value in enumerate(values):
        store(o, value)


def own_part(mass, stencil, near, middle, own_shifted, right_near, left_near):
    stacks, width = mass.shape[:2]
    for tile in range(width // 8):
        rows = pl.ds(8 * tile, 8)

        def store(o, value):
            own_shifted[o, rows, :] = value

        shift_rows(lambda o: stencil[o, rows, :], store)

    def some_stacks(turn_at, carry):
        for_groups(
            turn_at, stacks, range((width - 8) // 8), own_shifted, 5,
            lambda s, tile, at: mass[s, 2 + at : 10 + at, :],
            lambda s, tile, value: store_rows(middle, s, 8 * tile, value),
        )
        return carry

    lax.fori_loop(0, turns(stacks), some_stacks, 0)
    for dy in range(7):
        value = jnp.concatenate([stencil[dx * 7 + dy, :, :] for dx in range(7)], axis=0)
        spread = replicate(value, near[dy])
        for dx in range(7):
            right_near[dx * 7 + dy, :, :] = spread[width * dx : width * dx + width, 0:128]
            left_near[dx * 7 + dy, :, :] = spread[width * dx : width * dx + width, 128:256]


def both_steps(mass, stencil, above, below, middle, own_shifted, second, wide, shifted, field, partial):
    stacks, width = mass.shape[:2]
    first, last = ends(ROW_AXES)
    coefs = 6 * stacks
    for s in range(stacks):
        field[0, s, 2:8, :] = above[6 * s : 6 * s + 6, :]
        field[0, s, 8:16, :] = mass[s, 0:8, :]
        field[1, s, 0:8, :] = mass[s, width - 8 : width, :]
        field[1, s, 8:16, :] = below[6 * s : 6 * s + 8, :]
    for o in range(OFFSETS):
        at = coefs + 3 * o
        wide[o, 0:3, :] = above[at : at + 3, :]
        wide[o, 3 : width + 3, :] = stencil[o, :, :]
        wide[o, width + 3 : width + 6, :] = below[at : at + 3, :]
        wide[o, width + 6 : width + 8, :] = jnp.zeros((2, 128), F32)

    @pl.when(first)
    def _():
        for s in range(stacks):
            field[0, s, 2:8, :] = jnp.zeros((6, 128), F32)
        for o in range(OFFSETS):
            wide[o, 0:3, :] = jnp.zeros((3, 128), F32)

    @pl.when(last)
    def _():
        for s in range(stacks):
            field[1, s, 8:16, :] = jnp.zeros((8, 128), F32)
        for o in range(OFFSETS):
            wide[o, width + 3 : width + 6, :] = jnp.zeros((3, 128), F32)

    for end, tile in enumerate((0, width // 8)):
        rows = pl.ds(8 * tile, 8)

        def store(o, value):
            shifted[end, o, :, :] = value

        shift_rows(lambda o: wide[o, rows, :], store)

    def first_step(turn_at, carry):
        sums = [
            for_groups(
                turn_at, stacks, (0,), shifted.at[end], 0, lambda s, tile, at: field[end, s, 2 + at : 10 + at, :]
            )
            for end in range(2)
        ]
        for end, tile in enumerate((0, width // 8)):
            for s, _, value in sums[end]:
                store_rows(partial, s, 8 * tile, value)
        for s, _, _ in sums[0]:
            partial[s, 8:width, :] = middle[s, :, :]
        return carry

    lax.fori_loop(0, turns(stacks), first_step, 0)

    def second_step(turn_at, carry):
        for_groups(
            turn_at, stacks, range(width // 8), own_shifted, 0,
            lambda s, tile, at: partial[s, at : at + 8, :],
            lambda s, tile, value: store_rows(second, s, 8 * tile, value),
        )
        return carry

    lax.fori_loop(0, turns(stacks), second_step, 0)


def store_rows(target, s, at, value):
    target[s, at : at + 8, :] = value


def per_turn(stacks):
    return next(GROUP * groups for groups in (10, 5, 2, 1) if stacks % (GROUP * groups) == 0)


def turns(stacks):
    return stacks // per_turn(stacks)


def for_groups(turn_at, stacks, tiles, coef, coef_at, load, store=None):
    sums = []
    for part in range(per_turn(stacks) // GROUP):
        start = turn_at * per_turn(stacks) + part * GROUP
        for tile in tiles:
            total = main_sum(lambda k, at: load(start + k, tile, at), coef, coef_at, tile)
            sums += [(start + k, tile, total[k]) for k in range(GROUP)]
    if store is not None:
        for s, tile, value in sums:
            store(s, tile, value)
    return sums


def take_first(got, after, out):
    out[...] = got[...]


def in_order(got_a, got_b, above, below):
    choose(is_even(ROW_AXES), got_b, got_a, above, below)


def packed_sum(load, coef, coef_at, tile, tiles, dys):
    fields = [[load(t, 8 * tile + dx) for t in range(tiles)] for dx in range(7)]
    total = [None] * tiles
    for dy in dys:
        part = [None] * tiles
        for dx in range(7):
            at = coef_at + 8 * tile
            scale = coef[dx * 7 + dy + 3, at : at + 8, :]
            for t in range(tiles):
                term = scale * fields[dx][t]
                part[t] = term if dx == 0 else part[t] + term
        for t in range(tiles):
            moved = turn(part[t], -dy)
            total[t] = moved if total[t] is None else total[t] + moved
    return total


def place_in_group(rows=8):
    lane = lanes(rows)
    return lane - SPAN * ((lane * 57) >> 9)


def side_coefficients(
    wide, send_a, send_b, got_b, got_a, picks,
    right_set, left_set, right_coef, left_coef, right_halo, left_halo, rows_of,
):
    tall = wide.shape[1]
    width = tall - 8
    tiles = right_set.shape[0]
    lane = lanes()

    first, last = ends(COLUMN_AXES)

    def gather(sent_right, sent_left, got_right, got_left):
        part = width + 12
        place = place_in_group(part)
        rows = [slice(part * tile, part * tile + part) for tile in range(tiles)]
        from_right = [jnp.where(last, 0.0, got_right[at, :]) for at in rows]
        from_left = [jnp.where(first, 0.0, got_left[at, :]) for at in rows]
        for tile, at in enumerate(rows):
            right = jnp.where(place < 3, turn(sent_right[at, :], -3), from_right[tile])
            left = jnp.where(place >= 6, turn(sent_left[at, :], 3), from_left[tile])
            for target, value in ((right_set, right), (left_set, left)):
                target[tile, 6 : width + 6, :] = value[0:width]
                target[tile, 0:6, :] = value[width : width + 6]
                target[tile, width + 6 : width + 12, :] = value[width + 6 : width + 12]
                target[tile, width + 12 : width + 16, :] = jnp.zeros((4, 128), F32)
        coefs = slice(part * tiles, part * tiles + width + 6)
        for target, source, got, outside in (
            (right_halo, from_right, got_right, last), (left_halo, from_left, got_left, first)
        ):
            value = jnp.where(outside, 0.0, got[coefs, :])
            spare = source[0]
            for tile, own, above, below in (
                (0, value[0:width], value[width : width + 3], value[width + 3 : width + 6]),
                (1, spare[0:width], spare[width : width + 3], spare[width + 6 : width + 9]),
            ):
                target[tile, 3 : width + 3, :] = own
                target[tile, 0:3, :] = above
                target[tile, width + 3 : width + 6, :] = below
                target[tile, width + 6 : width + 8, :] = jnp.zeros((2, 128), F32)

    even = is_even(COLUMN_AXES)

    @pl.when(even)
    def _():
        gather(send_a, send_b, got_a, got_b)

    @pl.when(jnp.logical_not(even))
    def _():
        gather(send_b, send_a, got_b, got_a)

    from_right = (lane >= 60) & (lane < 63)
    from_left = (lane >= 64) & (lane < 67)
    for tile in range(tall // 8):
        rows = pl.ds(8 * tile, 8)
        right_rows = [right_halo[t, rows, :] for t in range(2)]
        left_rows = [left_halo[t, rows, :] for t in range(2)]
        values = []
        for o in range(OFFSETS):
            if o < COEF_PER:
                right = turn(right_rows[0], 60 - 3 * o)
                left = turn(left_rows[0], 64 - 3 * o)
            else:
                at = SPAN * (o - COEF_PER)
                right = turn(right_rows[1], 60 - at)
                left = turn(left_rows[1], 58 - at)
            values.append(jnp.where(from_right, right, jnp.where(from_left, left, wide[o, rows, :])))
        for o, value in enumerate(values):
            at = tall * (o // 7) + 8 * tile
            rows_of[o % 7, at : at + 8, :] = value

    for dy in range(7):
        spread = replicate(rows_of[dy], picks[dy])
        for dx in range(7):
            right_coef[dx * 7 + dy, :, :] = spread[tall * dx : tall * dx + tall, 0:128]
            left_coef[dx * 7 + dy, :, :] = spread[tall * dx : tall * dx + tall, 128:256]


def halo_steps(
    right_set, left_set, right_coef, left_coef, right_near, left_near, second, out_hbm,
    right_next, left_next, out, sems,
):
    tiles = right_set.shape[0]
    stacks, width = out.shape[:2]
    place = place_in_group()
    everywhere = range(-3, 4)
    row_tiles = range(right_next.shape[1] // 8)
    sums = [
        [
            packed_sum(lambda t, at: side[t, at : at + 8, :], coef, 0, tile, tiles, everywhere)
            for side, coef in ((right_set, right_coef), (left_set, left_coef))
        ]
        for tile in row_tiles
    ]
    for tile in row_tiles:
        right, left = sums[tile]
        rows = pl.ds(8 * tile, 8)
        for t in range(tiles):
            right_next[t, rows, :] = jnp.where(place >= 3, turn(right[t], 3), 0.0)
            left_next[t, rows, :] = jnp.where(place < 6, turn(left[t], -3), 0.0)
    changes = [
        [
            packed_sum(lambda t, at: side[t, at : at + 8, :], coef, 0, tile, tiles, everywhere)
            for side, coef in ((right_next, right_near), (left_next, left_near))
        ]
        for tile in range(width // 8)
    ]

    lane = lanes()
    copies = []
    for t in range(tiles):
        low, high = PER * t, min(stacks, PER * t + PER)
        for tile in range(width // 8):
            rows = pl.ds(8 * tile, 8)
            right, left = (side[t] for side in changes[tile])
            values = []
            for s in range(low, high):
                at = SPAN * (s - low)
                change = jnp.where(lane < 6, turn(left, -at - 3), 0.0)
                change = jnp.where(lane >= 122, turn(right, 122 - at), change)
                values.append(second[s, rows, :] + change)
            for s, value in zip(range(low, high), values):
                out[s, rows, :] = value
        piece = pl.ds(low, high - low)
        copies.append(pltpu.make_async_copy(out.at[piece], out_hbm.at[piece], sems.at[t]))
        copies[-1].start()
    for copy in copies:
        copy.wait()


def local(tracer_mass, recon_table, intersection_weights, intersection_cells, rotation_codes):
    stacks, width, columns = tracer_mass.shape
    shape = lambda *sizes: jax.ShapeDtypeStruct(sizes, F32)
    scratch = lambda *sizes: pltpu.VMEM(sizes, F32)
    tiles = -(-stacks // PER)
    combos = 4 * (width // 8)
    tall, low = width + 16, width + 8
    fixed = lambda *values: [pltpu.with_memory_space_constraint(value, pltpu.HBM) for value in values]
    whole = lambda value: jax.ShapeDtypeStruct(value.shape, value.dtype)
    edge = -(-(6 * stacks + 3 * OFFSETS + 5) // 8) * 8
    integers = lambda *sizes: pltpu.VMEM(sizes, jnp.int32)
    picks = jax.ShapeDtypeStruct((7, 256, 256), jnp.bfloat16)
    regions = intersection_cells.shape[0]

    mass, weights, cells, codes, send_a, send_b = pl.pallas_call(
        edge_rows,
        out_shape=(
            whole(tracer_mass), whole(intersection_weights), whole(intersection_cells),
            whole(rotation_codes), shape(edge, 128), shape(edge, 128),
        ),
        in_specs=[HBM] * 5,
        out_specs=(VMEM,) * 6,
        scratch_shapes=[
            pltpu.SMEM(recon_table.shape, F32),
            scratch(regions, TERMS, 8, 128),
            integers(regions, 8, 128),
            integers(regions, 8, 128),
            scratch(OFFSETS, 8, 128),
            scratch(TERMS, regions, 8, 128),
            scratch(25, regions, 8, 128),
            pltpu.SemaphoreType.DMA((5,)),
        ],
        compiler_params=params(),
        cost_estimate=cost(4 * 10**6),
        name="edge_rows",
    )(*fixed(recon_table, tracer_mass, intersection_weights, intersection_cells, rotation_codes))
    got_b = row_swap(send_b, True)
    got_a = row_swap(send_a, False)

    stencil = pl.pallas_call(
        coefficients,
        out_shape=shape(OFFSETS, width, 128),
        in_specs=[HBM] + [VMEM] * 3,
        out_specs=VMEM,
        scratch_shapes=[
            pltpu.SMEM(recon_table.shape, F32),
            scratch(TERMS, combos, 8, 128),
            scratch(25, combos, 8, 128),
            pltpu.SemaphoreType.DMA((1,)),
        ],
        compiler_params=params(),
        cost_estimate=cost(8 * 10**6),
        name="coefficients",
    )(*fixed(recon_table), weights, cells, codes)

    own_left, own_right, picks, near = pl.pallas_call(
        pack_own,
        out_shape=(shape(width * (tiles + 1), 128),) * 2 + (picks, picks),
        in_specs=[VMEM] * 2,
        out_specs=(VMEM,) * 4,
        compiler_params=params(),
        cost_estimate=cost(10**6),
        name="pack_own",
    )(mass, stencil)

    middle, own_shifted, right_near, left_near = pl.pallas_call(
        own_part,
        out_shape=(shape(stacks, width - 8, 128),) + (shape(OFFSETS, width, 128),) * 3,
        in_specs=[VMEM] * 3,
        out_specs=(VMEM,) * 4,
        compiler_params=params(),
        cost_estimate=cost(4 * 10**6),
        name="own_part",
    )(mass, stencil, near)

    got_b = pl.pallas_call(
        take_first,
        out_shape=shape(edge, 128),
        in_specs=[VMEM, ANY],
        out_specs=VMEM,
        compiler_params=params(),
        cost_estimate=cost(10**4),
        name="take_first",
    )(got_b, middle)
    above, below = pl.pallas_call(
        in_order,
        out_shape=(shape(edge, 128),) * 2,
        in_specs=[VMEM] * 2,
        out_specs=(VMEM,) * 2,
        compiler_params=params(),
        cost_estimate=cost(10**4),
        name="in_order",
    )(got_a, got_b)

    send = ((width + 12) * (tiles + 1), 128)
    send_a, send_b = pl.pallas_call(
        functools.partial(pack_all, stacks),
        out_shape=(shape(*send),) * 2,
        in_specs=[VMEM] * 4 + [ANY],
        out_specs=(VMEM,) * 2,
        scratch_shapes=[scratch(*send)] * 2,
        compiler_params=params(),
        cost_estimate=cost(10**6),
        name="pack_all",
    )(own_left, own_right, above, below, middle)
    column_b = column_swap(send_b, True)
    column_a = column_swap(send_a, False)

    second, wide = pl.pallas_call(
        both_steps,
        out_shape=(shape(stacks, width, 128), shape(OFFSETS, low, 128)),
        in_specs=[VMEM] * 6,
        out_specs=(VMEM,) * 2,
        scratch_shapes=[scratch(2, OFFSETS, 8, 128), scratch(2, stacks, 16, 128), scratch(stacks, low, 128)],
        compiler_params=params(),
        cost_estimate=cost(12 * 10**6),
        name="both_steps",
    )(mass, stencil, above, below, middle, own_shifted)

    sides = pl.pallas_call(
        side_coefficients,
        out_shape=(shape(tiles, tall, 128),) * 2 + (shape(OFFSETS, low, 128),) * 2,
        in_specs=[VMEM] * 6,
        out_specs=(VMEM,) * 4,
        scratch_shapes=[scratch(2, low, 128)] * 2 + [scratch(7, 7 * low, 128)],
        compiler_params=params(),
        cost_estimate=cost(4 * 10**6),
        name="side_coefficients",
    )(wide, send_a, send_b, column_b, column_a, picks)

    return pl.pallas_call(
        halo_steps,
        out_shape=shape(stacks, width, columns),
        in_specs=[VMEM] * 7,
        out_specs=HBM,
        scratch_shapes=[scratch(tiles, low, 128)] * 2
        + [scratch(stacks, width, columns), pltpu.SemaphoreType.DMA((tiles,))],
        compiler_params=params(),
        cost_estimate=cost(4 * 10**6),
        name="halo_steps",
    )(*sides, right_near, left_near, second)


def solution(mesh):
    in_specs = (
        P(None, ("face", "px"), "py"),
        P(),
        P(None, None, ("face", "px"), "py"),
        P(None, ("face", "px"), "py"),
        P(None, ("face", "px"), "py"),
    )
    out_specs = P(None, ("face", "px"), "py")
    return jax.shard_map(local, mesh=mesh, in_specs=in_specs, out_specs=out_specs, check_vma=False)
```

```python
import functools

import jax
import jax.numpy as jnp
import numpy as np
from jax import lax
from jax.experimental import pallas as pl
from jax.experimental.pallas import tpu as pltpu
from jax.sharding import PartitionSpec as P

F32 = jnp.float32
ROW_AXES = ("face", "px")
COLUMN_AXES = "py"
SWAPPED = (0, 2, 1, 5, 4, 3, 9, 8, 7, 6)
POWERS = ((0, 0), (1, 0), (0, 1), (2, 0), (1, 1), (0, 2), (3, 0), (2, 1), (1, 2), (0, 3))
TERMS = 10
OFFSETS = 49
GROUP = 5
SPAN = 9
PER = 14
COEF_PER = 42
VMEM = pl.BlockSpec(memory_space=pltpu.VMEM)
ANY = pl.BlockSpec(memory_space=pl.ANY)
HBM = pl.BlockSpec(memory_space=pltpu.HBM)


def params():
    return pltpu.CompilerParams(vmem_limit_bytes=40 * 1024 * 1024)


def cost(operations):
    return pl.CostEstimate(flops=operations, bytes_accessed=1 << 20, transcendentals=0)


def column_swap(block, odd_first):
    chains, count = lax.axis_size(ROW_AXES), lax.axis_size(COLUMN_AXES)
    column = list(range(count))
    for low in range(1 if odd_first else 0, count - 1, 2):
        column[low], column[low + 1] = low + 1, low
    pairs = []
    for chain in range(chains):
        for place in range(count):
            target = (chain, column[place])
            if column[place] == place and chains % 2 == 0:
                target = (chain ^ 1, place)
            pairs.append((chain * count + place, target[0] * count + target[1]))
    return lax.ppermute(block, ROW_AXES + (COLUMN_AXES,), pairs)


def row_swap(block, odd_first):
    chains, count = lax.axis_size(ROW_AXES), lax.axis_size(COLUMN_AXES)
    chain_of = list(range(chains))
    for low in range(1 if odd_first else 0, chains - 1, 2):
        chain_of[low], chain_of[low + 1] = low + 1, low
    pairs = []
    for chain in range(chains):
        for place in range(count):
            target = (chain_of[chain], place)
            if chain_of[chain] == chain and count % 2 == 0:
                target = (chain, place ^ 1)
            pairs.append((chain * count + place, target[0] * count + target[1]))
    return lax.ppermute(block, ROW_AXES + (COLUMN_AXES,), pairs)


def ends(axes):
    index = lax.axis_index(axes)
    return index == 0, index == lax.axis_size(axes) - 1


def is_even(axes):
    return lax.rem(lax.axis_index(axes), 2) == 0


def turn(value, amount):
    amount %= 128
    return pltpu.roll(value, amount, 1) if amount else value


def lanes(rows=8):
    return lax.broadcasted_iota(jnp.int32, (rows, 128), 1)


def fill_stencil(recon, weights, cells, codes, turned, spread, stencil, tiles, before_taps):
    zero = jnp.zeros((8, 128), F32)
    for g in range(tiles):
        rows = pl.ds(8 * g, 8)
        for m in range(4):
            code = codes[m, rows, :]
            odd = (code & 1) == 1
            sign_x = jnp.where(code >= 2, -1.0, 1.0).astype(F32)
            sign_y = jnp.where((code == 1) | (code == 2), -1.0, 1.0).astype(F32)
            sign_xy = sign_x * sign_y
            values = [weights[m, t, rows, :] for t in range(TERMS)]
            for t, (a, b) in enumerate(POWERS):
                value = values[t]
                if SWAPPED[t] != t:
                    value = jnp.where(odd, values[SWAPPED[t]], value)
                if a % 2 and b % 2:
                    value = value * sign_xy
                elif a % 2:
                    value = value * sign_x
                elif b % 2:
                    value = value * sign_y
                turned[t, m * tiles + g] = value

    combos = 4 * tiles
    before_taps()

    def five_taps(jx, carry):
        total = [[None] * combos for jy in range(5)]
        for t in range(TERMS):
            values = [turned[t, c] for c in range(combos)]
            for jy in range(5):
                scale = recon[t, 5 * jx + jy]
                for c in range(combos):
                    term = values[c] * scale
                    total[jy][c] = term if t == 0 else total[jy][c] + term
        for jy in range(5):
            for c in range(combos):
                spread[5 * jx + jy, c] = total[jy][c]
        return carry

    for jx in range(5):
        five_taps(jx, 0)

    for g in range(tiles):
        rows = pl.ds(8 * g, 8)
        masks = []
        for m in range(4):
            cell = cells[m, rows, :]
            first = jnp.where(cell < 3, 0, jnp.where(cell < 6, 3, 6))
            across = cell - first
            masks.append((cell < 3, cell < 6, across == 0, across <= 1))
        for ox in range(7):
            total = [None] * 7
            for m in range(4):
                low_x, mid_x, low_y, mid_y = masks[m]

                def tap(jx, jy):
                    if 0 <= jx < 5 and 0 <= jy < 5:
                        return spread[jx * 5 + jy, m * tiles + g]
                    return zero

                line = [
                    jnp.where(low_x, tap(ox, jy), jnp.where(mid_x, tap(ox - 1, jy), tap(ox - 2, jy)))
                    for jy in range(5)
                ]
                padded = [zero, zero] + line + [zero, zero]
                for oy in range(7):
                    value = jnp.where(
                        low_y, padded[oy + 2], jnp.where(mid_y, padded[oy + 1], padded[oy])
                    )
                    total[oy] = value if m == 0 else total[oy] + value
            for oy in range(7):
                stencil[ox * 7 + oy, rows, :] = total[oy]


def edge_rows(
    recon_hbm, mass_hbm, weights_hbm, cells_hbm, codes_hbm,
    mass, weights, cells, codes, send_a, send_b,
    recon, edge_weights, edge_cells, edge_codes, edge_stencil, turned, spread, sems,
):
    sources = (recon_hbm, codes_hbm, weights_hbm, cells_hbm, mass_hbm)
    targets = (recon, codes, weights, cells, mass)
    copies = [pltpu.make_async_copy(a, b, sems.at[i]) for i, (a, b) in enumerate(zip(sources, targets))]
    for copy in copies:
        copy.start()
    for copy in copies[1:4]:
        copy.wait()
    stacks, width = mass.shape[:2]
    for target, source in ((edge_weights, weights), (edge_cells, cells), (edge_codes, codes)):
        for index in np.ndindex(*source.shape[:-2]):
            target[index + (slice(0, 3), slice(None))] = source[index + (slice(0, 3), slice(None))]
            target[index + (slice(3, 8), slice(None))] = source[index + (slice(width - 5, width), slice(None))]
    fill_stencil(
        recon, edge_weights, edge_cells, edge_codes, turned, spread, edge_stencil, 1, copies[0].wait
    )
    copies[4].wait()
    even = is_even(ROW_AXES)
    for send, low_edge in ((send_a, jnp.logical_not(even)), (send_b, even)):
        mass_at = jnp.where(low_edge, 0, width - 6)
        stencil_at = jnp.where(low_edge, 0, 5)
        for s in range(stacks):
            send[6 * s : 6 * s + 6, :] = mass[s, pl.ds(mass_at, 6), :]
        for o in range(OFFSETS):
            at = 6 * stacks + 3 * o
            send[at : at + 3, :] = edge_stencil[o, pl.ds(stencil_at, 3), :]


def coefficients(recon_hbm, weights, cells, codes, stencil, recon, turned, spread, sem):
    copy = pltpu.make_async_copy(recon_hbm, recon, sem.at[0])
    copy.start()
    fill_stencil(recon, weights, cells, codes, turned, spread, stencil, stencil.shape[1] // 8, copy.wait)


def pack_stacks(load, stacks, tile):
    lane = lanes()
    left = jnp.zeros((8, 128), F32)
    right = jnp.zeros((8, 128), F32)
    for s in range(PER * tile, min(stacks, PER * tile + PER)):
        at = SPAN * (s % PER)
        moved = turn(load(s), at - 122)
        right = jnp.where(lane >= at, moved, right)
        left = jnp.where(from_place(lane, at + 6, at + 12), moved, left)
    return turn(left, -3), right


def from_place(lane, low, high):
    return (lane >= low) | (lane < high - 128) if high > 128 else lane >= low


def pack_coefficients(load):
    lane = lanes()
    left = jnp.zeros((8, 128), F32)
    right = jnp.zeros((8, 128), F32)
    for o in range(COEF_PER):
        at = 3 * o
        moved = turn(load(o), at - 125)
        right = jnp.where(lane >= at, moved, right)
        left = jnp.where(from_place(lane, at + 3, at + 6), moved, left)
    return turn(left, -3), right


def add_spare(load, left, right):
    lane = lanes()
    for o in range(COEF_PER, OFFSETS):
        at = SPAN * (o - COEF_PER)
        value = load(o)
        left = jnp.where((lane >= at) & (lane < at + 3), turn(value, at), left)
        right = jnp.where((lane >= at + 6) & (lane < at + 9), turn(value, at - 119), right)
    return left, right


def fill_near(near):
    lane = lanes(1)
    group = (lane * 57) >> 9
    at = lane - SPAN * group
    source = lax.broadcasted_iota(jnp.int32, (128, 128), 0)
    for dy in range(-3, 4):
        q = at - dy
        right = jnp.where((at >= 3) & (q >= 0) & (q < 6), 122 + q, -1)
        left = jnp.where((at < 6) & (q >= 3) & (q < 9), q - 3, -1)
        for side, wanted in enumerate((right, left)):
            wanted = jnp.where(group < PER, wanted, -1)
            picked = jnp.where(source == wanted, 1.0, 0.0).astype(jnp.bfloat16)
            near[dy + 3, 0:128, 128 * side : 128 * side + 128] = picked
            near[dy + 3, 128:256, 128 * side : 128 * side + 128] = picked


def replicate(value, picks):
    high = value.astype(jnp.bfloat16)
    low = (value - high.astype(F32)).astype(jnp.bfloat16)
    return jnp.dot(jnp.concatenate([high, low], axis=1), picks, preferred_element_type=F32)


def fill_picks(picks):
    lane = lanes(1)
    group = (lane * 57) >> 9
    at = lane - SPAN * group
    source = lax.broadcasted_iota(jnp.int32, (128, 128), 0)
    for dy in range(-3, 4):
        q = at - dy
        halo = (q >= 3) & (q < 6)
        right = jnp.where(halo, 57 + q, jnp.where((q >= 0) & (q < 3) & (at >= 3), 125 + q, -1))
        left = jnp.where(halo, 61 + q, jnp.where((q >= 6) & (q < 9) & (at < 6), q - 6, -1))
        for side, wanted in enumerate((right, left)):
            wanted = jnp.where(group < PER, wanted, -1)
            picked = jnp.where(source == wanted, 1.0, 0.0).astype(jnp.bfloat16)
            picks[dy + 3, 0:128, 128 * side : 128 * side + 128] = picked
            picks[dy + 3, 128:256, 128 * side : 128 * side + 128] = picked


def pack_own(mass, stencil, left, right, picks, near):
    fill_picks(picks)
    fill_near(near)
    stacks, width = mass.shape[:2]
    tiles = -(-stacks // PER)
    for half in range(width // 8):
        rows = pl.ds(8 * half, 8)
        for tile in range(tiles):
            at = width * tile + 8 * half
            values = pack_stacks(lambda s: mass[s, rows, :], stacks, tile)
            if tile == 0:
                values = add_spare(lambda o: stencil[o, rows, :], *values)
            left[at : at + 8, :], right[at : at + 8, :] = values
        at = width * tiles + 8 * half
        left[at : at + 8, :], right[at : at + 8, :] = pack_coefficients(lambda o: stencil[o, rows, :])


def pack_all(stacks, own_left, own_right, above, below, middle, send_a, send_b, left, right):
    tiles = -(-stacks // PER)
    width = own_left.shape[0] // (tiles + 1)
    tall = width + 12
    first, last = ends(ROW_AXES)
    top_rows = lax.broadcasted_iota(jnp.int32, (8, 128), 0) < 3
    ready = []
    for got, outside, place, coef_place in (
        (above, first, width, width), (below, last, width + 6, width + 3)
    ):
        coef = lambda o: got[6 * stacks + 3 * o : 6 * stacks + 3 * o + 8, :]
        for tile in range(tiles):
            packed = pack_stacks(lambda s: got[6 * s : 6 * s + 8, :], stacks, tile)
            if tile == 0:
                spare = add_spare(coef, *packed)
                packed = [jnp.where(top_rows, new, old) for new, old in zip(spare, packed)]
            ready.append((tall * tile + place, 6, outside, packed))
        ready.append((tall * tiles + coef_place, 3, outside, pack_coefficients(coef)))
    for at, count, outside, packed in ready:
        for send, value in zip((left, right), packed):
            send[at : at + count, :] = jnp.where(outside, 0.0, value[0:count])
    for send, own in ((left, own_left), (right, own_right)):
        for tile in range(tiles + 1):
            send[tall * tile : tall * tile + width, :] = own[width * tile : width * tile + width, :]
        end = tall * tiles + width + 6
        send[end:, :] = jnp.zeros((send.shape[0] - end, 128), F32)
    choose(is_even(COLUMN_AXES), right, left, send_a, send_b)


def choose(even, first, second, first_out, second_out):
    @pl.when(even)
    def _():
        first_out[...] = first[...]
        second_out[...] = second[...]

    @pl.when(jnp.logical_not(even))
    def _():
        first_out[...] = second[...]
        second_out[...] = first[...]


def main_sum(load, coef, coef_at, tile):
    fields = [[load(k, 8 * tile + dx) for k in range(GROUP)] for dx in range(7)]
    total = [None] * GROUP
    for dy in range(7):
        part = [None] * GROUP
        for dx in range(7):
            at = coef_at + 8 * tile
            scale = coef[dx * 7 + dy, at : at + 8, :]
            for k in range(GROUP):
                term = scale * fields[dx][k]
                part[k] = term if dx == 0 else part[k] + term
        for k in range(GROUP):
            moved = turn(part[k], 3 - dy)
            total[k] = moved if dy == 0 else total[k] + moved
    return total


def shift_rows(load, store):
    lane = lanes()
    values = []
    for o in range(OFFSETS):
        dy = o % 7 - 3
        value = turn(load(o), dy)
        if dy > 0:
            value = jnp.where(lane >= dy, value, 0.0)
        elif dy < 0:
            value = jnp.where(lane < 128 + dy, value, 0.0)
        values.append(value)
    for o, value in enumerate(values):
        store(o, value)


def own_part(mass, stencil, near, middle, own_shifted, right_near, left_near):
    stacks, width = mass.shape[:2]
    for tile in range(width // 8):
        rows = pl.ds(8 * tile, 8)

        def store(o, value):
            own_shifted[o, rows, :] = value

        shift_rows(lambda o: stencil[o, rows, :], store)

    def some_stacks(turn_at, carry):
        for_groups(
            turn_at, stacks, range((width - 8) // 8), own_shifted, 5,
            lambda s, tile, at: mass[s, 2 + at : 10 + at, :],
            lambda s, tile, value: store_rows(middle, s, 8 * tile, value),
        )
        return carry

    lax.fori_loop(0, turns(stacks), some_stacks, 0)
    for dy in range(7):
        value = jnp.concatenate([stencil[dx * 7 + dy, :, :] for dx in range(7)], axis=0)
        spread = replicate(value, near[dy])
        for dx in range(7):
            right_near[dx * 7 + dy, :, :] = spread[width * dx : width * dx + width, 0:128]
            left_near[dx * 7 + dy, :, :] = spread[width * dx : width * dx + width, 128:256]


def both_steps(mass, stencil, above, below, middle, own_shifted, second, wide, shifted, field, partial):
    stacks, width = mass.shape[:2]
    first, last = ends(ROW_AXES)
    coefs = 6 * stacks
    for s in range(stacks):
        field[0, s, 2:8, :] = above[6 * s : 6 * s + 6, :]
        field[0, s, 8:16, :] = mass[s, 0:8, :]
        field[1, s, 0:8, :] = mass[s, width - 8 : width, :]
        field[1, s, 8:16, :] = below[6 * s : 6 * s + 8, :]
    for o in range(OFFSETS):
        at = coefs + 3 * o
        wide[o, 0:3, :] = above[at : at + 3, :]
        wide[o, 3 : width + 3, :] = stencil[o, :, :]
        wide[o, width + 3 : width + 6, :] = below[at : at + 3, :]
        wide[o, width + 6 : width + 8, :] = jnp.zeros((2, 128), F32)

    @pl.when(first)
    def _():
        for s in range(stacks):
            field[0, s, 2:8, :] = jnp.zeros((6, 128), F32)
        for o in range(OFFSETS):
            wide[o, 0:3, :] = jnp.zeros((3, 128), F32)

    @pl.when(last)
    def _():
        for s in range(stacks):
            field[1, s, 8:16, :] = jnp.zeros((8, 128), F32)
        for o in range(OFFSETS):
            wide[o, width + 3 : width + 6, :] = jnp.zeros((3, 128), F32)

    for end, tile in enumerate((0, width // 8)):
        rows = pl.ds(8 * tile, 8)

        def store(o, value):
            shifted[end, o, :, :] = value

        shift_rows(lambda o: wide[o, rows, :], store)

    def first_step(turn_at, carry):
        sums = [
            for_groups(
                turn_at, stacks, (0,), shifted.at[end], 0, lambda s, tile, at: field[end, s, 2 + at : 10 + at, :]
            )
            for end in range(2)
        ]
        for end, tile in enumerate((0, width // 8)):
            for s, _, value in sums[end]:
                store_rows(partial, s, 8 * tile, value)
        for s, _, _ in sums[0]:
            partial[s, 8:width, :] = middle[s, :, :]
        return carry

    lax.fori_loop(0, turns(stacks), first_step, 0)

    def second_step(turn_at, carry):
        for_groups(
            turn_at, stacks, range(width // 8), own_shifted, 0,
            lambda s, tile, at: partial[s, at : at + 8, :],
            lambda s, tile, value: store_rows(second, s, 8 * tile, value),
        )
        return carry

    lax.fori_loop(0, turns(stacks), second_step, 0)


def store_rows(target, s, at, value):
    target[s, at : at + 8, :] = value


def per_turn(stacks):
    return next(GROUP * groups for groups in (8, 4, 2, 1) if stacks % (GROUP * groups) == 0)


def turns(stacks):
    return stacks // per_turn(stacks)


def for_groups(turn_at, stacks, tiles, coef, coef_at, load, store=None):
    sums = []
    for part in range(per_turn(stacks) // GROUP):
        start = turn_at * per_turn(stacks) + part * GROUP
        for tile in tiles:
            total = main_sum(lambda k, at: load(start + k, tile, at), coef, coef_at, tile)
            sums += [(start + k, tile, total[k]) for k in range(GROUP)]
    if store is not None:
        for s, tile, value in sums:
            store(s, tile, value)
    return sums


def take_first(got, after, out):
    out[...] = got[...]


def in_order(got_a, got_b, above, below):
    choose(is_even(ROW_AXES), got_b, got_a, above, below)


def packed_sum(load, coef, coef_at, tile, tiles, dys):
    fields = [[load(t, 8 * tile + dx) for t in range(tiles)] for dx in range(7)]
    total = [None] * tiles
    for dy in dys:
        part = [None] * tiles
        for dx in range(7):
            at = coef_at + 8 * tile
            scale = coef[dx * 7 + dy + 3, at : at + 8, :]
            for t in range(tiles):
                term = scale * fields[dx][t]
                part[t] = term if dx == 0 else part[t] + term
        for t in range(tiles):
            moved = turn(part[t], -dy)
            total[t] = moved if total[t] is None else total[t] + moved
    return total


def place_in_group(rows=8):
    lane = lanes(rows)
    return lane - SPAN * ((lane * 57) >> 9)


def side_coefficients(
    wide, send_a, send_b, got_b, got_a, picks,
    right_set, left_set, right_coef, left_coef, right_halo, left_halo, rows_of,
):
    tall = wide.shape[1]
    width = tall - 8
    tiles = right_set.shape[0]
    lane = lanes()

    first, last = ends(COLUMN_AXES)

    def gather(sent_right, sent_left, got_right, got_left):
        part = width + 12
        place = place_in_group(part)
        rows = [slice(part * tile, part * tile + part) for tile in range(tiles)]
        from_right = [jnp.where(last, 0.0, got_right[at, :]) for at in rows]
        from_left = [jnp.where(first, 0.0, got_left[at, :]) for at in rows]
        for tile, at in enumerate(rows):
            right = jnp.where(place < 3, turn(sent_right[at, :], -3), from_right[tile])
            left = jnp.where(place >= 6, turn(sent_left[at, :], 3), from_left[tile])
            for target, value in ((right_set, right), (left_set, left)):
                target[tile, 6 : width + 6, :] = value[0:width]
                target[tile, 0:6, :] = value[width : width + 6]
                target[tile, width + 6 : width + 12, :] = value[width + 6 : width + 12]
                target[tile, width + 12 : width + 16, :] = jnp.zeros((4, 128), F32)
        coefs = slice(part * tiles, part * tiles + width + 6)
        for target, source, got, outside in (
            (right_halo, from_right, got_right, last), (left_halo, from_left, got_left, first)
        ):
            value = jnp.where(outside, 0.0, got[coefs, :])
            spare = source[0]
            for tile, own, above, below in (
                (0, value[0:width], value[width : width + 3], value[width + 3 : width + 6]),
                (1, spare[0:width], spare[width : width + 3], spare[width + 6 : width + 9]),
            ):
                target[tile, 3 : width + 3, :] = own
                target[tile, 0:3, :] = above
                target[tile, width + 3 : width + 6, :] = below
                target[tile, width + 6 : width + 8, :] = jnp.zeros((2, 128), F32)

    even = is_even(COLUMN_AXES)

    @pl.when(even)
    def _():
        gather(send_a, send_b, got_a, got_b)

    @pl.when(jnp.logical_not(even))
    def _():
        gather(send_b, send_a, got_b, got_a)

    from_right = (lane >= 60) & (lane < 63)
    from_left = (lane >= 64) & (lane < 67)
    for tile in range(tall // 8):
        rows = pl.ds(8 * tile, 8)
        right_rows = [right_halo[t, rows, :] for t in range(2)]
        left_rows = [left_halo[t, rows, :] for t in range(2)]
        values = []
        for o in range(OFFSETS):
            if o < COEF_PER:
                right = turn(right_rows[0], 60 - 3 * o)
                left = turn(left_rows[0], 64 - 3 * o)
            else:
                at = SPAN * (o - COEF_PER)
                right = turn(right_rows[1], 60 - at)
                left = turn(left_rows[1], 58 - at)
            values.append(jnp.where(from_right, right, jnp.where(from_left, left, wide[o, rows, :])))
        for o, value in enumerate(values):
            at = tall * (o // 7) + 8 * tile
            rows_of[o % 7, at : at + 8, :] = value

    for dy in range(7):
        spread = replicate(rows_of[dy], picks[dy])
        for dx in range(7):
            right_coef[dx * 7 + dy, :, :] = spread[tall * dx : tall * dx + tall, 0:128]
            left_coef[dx * 7 + dy, :, :] = spread[tall * dx : tall * dx + tall, 128:256]


def halo_steps(
    right_set, left_set, right_coef, left_coef, right_near, left_near, second, out_hbm,
    right_next, left_next, out, sems,
):
    tiles = right_set.shape[0]
    stacks, width = out.shape[:2]
    place = place_in_group()
    everywhere = range(-3, 4)
    row_tiles = range(right_next.shape[1] // 8)
    sums = [
        [
            packed_sum(lambda t, at: side[t, at : at + 8, :], coef, 0, tile, tiles, everywhere)
            for side, coef in ((right_set, right_coef), (left_set, left_coef))
        ]
        for tile in row_tiles
    ]
    for tile in row_tiles:
        right, left = sums[tile]
        rows = pl.ds(8 * tile, 8)
        for t in range(tiles):
            right_next[t, rows, :] = jnp.where(place >= 3, turn(right[t], 3), 0.0)
            left_next[t, rows, :] = jnp.where(place < 6, turn(left[t], -3), 0.0)
    changes = [
        [
            packed_sum(lambda t, at: side[t, at : at + 8, :], coef, 0, tile, tiles, everywhere)
            for side, coef in ((right_next, right_near), (left_next, left_near))
        ]
        for tile in range(width // 8)
    ]

    lane = lanes()
    copies = []
    for t in range(tiles):
        low, high = PER * t, min(stacks, PER * t + PER)
        for tile in range(width // 8):
            rows = pl.ds(8 * tile, 8)
            right, left = (side[t] for side in changes[tile])
            values = []
            for s in range(low, high):
                at = SPAN * (s - low)
                change = jnp.where(lane < 6, turn(left, -at - 3), 0.0)
                change = jnp.where(lane >= 122, turn(right, 122 - at), change)
                values.append(second[s, rows, :] + change)
            for s, value in zip(range(low, high), values):
                out[s, rows, :] = value
        piece = pl.ds(low, high - low)
        copies.append(pltpu.make_async_copy(out.at[piece], out_hbm.at[piece], sems.at[t]))
        copies[-1].start()
    for copy in copies:
        copy.wait()


def local(tracer_mass, recon_table, intersection_weights, intersection_cells, rotation_codes):
    stacks, width, columns = tracer_mass.shape
    shape = lambda *sizes: jax.ShapeDtypeStruct(sizes, F32)
    scratch = lambda *sizes: pltpu.VMEM(sizes, F32)
    tiles = -(-stacks // PER)
    combos = 4 * (width // 8)
    tall, low = width + 16, width + 8
    fixed = lambda *values: [pltpu.with_memory_space_constraint(value, pltpu.HBM) for value in values]
    whole = lambda value: jax.ShapeDtypeStruct(value.shape, value.dtype)
    edge = -(-(6 * stacks + 3 * OFFSETS + 5) // 8) * 8
    integers = lambda *sizes: pltpu.VMEM(sizes, jnp.int32)
    picks = jax.ShapeDtypeStruct((7, 256, 256), jnp.bfloat16)
    regions = intersection_cells.shape[0]

    mass, weights, cells, codes, send_a, send_b = pl.pallas_call(
        edge_rows,
        out_shape=(
            whole(tracer_mass), whole(intersection_weights), whole(intersection_cells),
            whole(rotation_codes), shape(edge, 128), shape(edge, 128),
        ),
        in_specs=[HBM] * 5,
        out_specs=(VMEM,) * 6,
        scratch_shapes=[
            pltpu.SMEM(recon_table.shape, F32),
            scratch(regions, TERMS, 8, 128),
            integers(regions, 8, 128),
            integers(regions, 8, 128),
            scratch(OFFSETS, 8, 128),
            scratch(TERMS, regions, 8, 128),
            scratch(25, regions, 8, 128),
            pltpu.SemaphoreType.DMA((5,)),
        ],
        compiler_params=params(),
        cost_estimate=cost(4 * 10**6),
        name="edge_rows",
    )(*fixed(recon_table, tracer_mass, intersection_weights, intersection_cells, rotation_codes))
    got_b = row_swap(send_b, True)
    got_a = row_swap(send_a, False)

    stencil = pl.pallas_call(
        coefficients,
        out_shape=shape(OFFSETS, width, 128),
        in_specs=[HBM] + [VMEM] * 3,
        out_specs=VMEM,
        scratch_shapes=[
            pltpu.SMEM(recon_table.shape, F32),
            scratch(TERMS, combos, 8, 128),
            scratch(25, combos, 8, 128),
            pltpu.SemaphoreType.DMA((1,)),
        ],
        compiler_params=params(),
        cost_estimate=cost(8 * 10**6),
        name="coefficients",
    )(*fixed(recon_table), weights, cells, codes)

    own_left, own_right, picks, near = pl.pallas_call(
        pack_own,
        out_shape=(shape(width * (tiles + 1), 128),) * 2 + (picks, picks),
        in_specs=[VMEM] * 2,
        out_specs=(VMEM,) * 4,
        compiler_params=params(),
        cost_estimate=cost(10**6),
        name="pack_own",
    )(mass, stencil)

    middle, own_shifted, right_near, left_near = pl.pallas_call(
        own_part,
        out_shape=(shape(stacks, width - 8, 128),) + (shape(OFFSETS, width, 128),) * 3,
        in_specs=[VMEM] * 3,
        out_specs=(VMEM,) * 4,
        compiler_params=params(),
        cost_estimate=cost(4 * 10**6),
        name="own_part",
    )(mass, stencil, near)

    got_b = pl.pallas_call(
        take_first,
        out_shape=shape(edge, 128),
        in_specs=[VMEM, ANY],
        out_specs=VMEM,
        compiler_params=params(),
        cost_estimate=cost(10**4),
        name="take_first",
    )(got_b, middle)
    above, below = pl.pallas_call(
        in_order,
        out_shape=(shape(edge, 128),) * 2,
        in_specs=[VMEM] * 2,
        out_specs=(VMEM,) * 2,
        compiler_params=params(),
        cost_estimate=cost(10**4),
        name="in_order",
    )(got_a, got_b)

    send = ((width + 12) * (tiles + 1), 128)
    send_a, send_b = pl.pallas_call(
        functools.partial(pack_all, stacks),
        out_shape=(shape(*send),) * 2,
        in_specs=[VMEM] * 4 + [ANY],
        out_specs=(VMEM,) * 2,
        scratch_shapes=[scratch(*send)] * 2,
        compiler_params=params(),
        cost_estimate=cost(10**6),
        name="pack_all",
    )(own_left, own_right, above, below, middle)
    column_b = column_swap(send_b, True)
    column_a = column_swap(send_a, False)

    second, wide = pl.pallas_call(
        both_steps,
        out_shape=(shape(stacks, width, 128), shape(OFFSETS, low, 128)),
        in_specs=[VMEM] * 6,
        out_specs=(VMEM,) * 2,
        scratch_shapes=[scratch(2, OFFSETS, 8, 128), scratch(2, stacks, 16, 128), scratch(stacks, low, 128)],
        compiler_params=params(),
        cost_estimate=cost(12 * 10**6),
        name="both_steps",
    )(mass, stencil, above, below, middle, own_shifted)

    sides = pl.pallas_call(
        side_coefficients,
        out_shape=(shape(tiles, tall, 128),) * 2 + (shape(OFFSETS, low, 128),) * 2,
        in_specs=[VMEM] * 6,
        out_specs=(VMEM,) * 4,
        scratch_shapes=[scratch(2, low, 128)] * 2 + [scratch(7, 7 * low, 128)],
        compiler_params=params(),
        cost_estimate=cost(4 * 10**6),
        name="side_coefficients",
    )(wide, send_a, send_b, column_b, column_a, picks)

    return pl.pallas_call(
        halo_steps,
        out_shape=shape(stacks, width, columns),
        in_specs=[VMEM] * 7,
        out_specs=HBM,
        scratch_shapes=[scratch(tiles, low, 128)] * 2
        + [scratch(stacks, width, columns), pltpu.SemaphoreType.DMA((tiles,))],
        compiler_params=params(),
        cost_estimate=cost(4 * 10**6),
        name="halo_steps",
    )(*sides, right_near, left_near, second)


def solution(mesh):
    in_specs = (
        P(None, ("face", "px"), "py"),
        P(),
        P(None, None, ("face", "px"), "py"),
        P(None, ("face", "px"), "py"),
        P(None, ("face", "px"), "py"),
    )
    out_specs = P(None, ("face", "px"), "py")
    return jax.shard_map(local, mesh=mesh, in_specs=in_specs, out_specs=out_specs, check_vma=False)
```
